32 devices in a mesh: blk: 8 (over z, core), head: 4 (over y, x).
Axes of the slice: x: 2, y: 2, z: 4, core: 2. Of those that a mesh axis runs over, the one named last changes fastest.
Arguments:
- hidden_in: bfloat16 [4096, 2304], P(('blk', 'head')), may hold values from -6 to 6
- out_grad: bfloat16 [4096, 2304], P(('blk', 'head')), may hold values from -6 to 6
- span_order: int32 [16], replicated, may hold values from 0 to 15, as said below
- w_query: bfloat16 [2304, 2048], P('blk', 'head'), may hold values from -0.5 to 0.5
- w_key: bfloat16 [2304, 1024], P('blk'), may hold values from -0.125 to 0.125
- w_value: bfloat16 [2304, 1024], P('blk'), may hold values from -0.125 to 0.125
- w_output: bfloat16 [2048, 2304], P('head', 'blk'), may hold values from -0.125 to 0.125
- w_gate: bfloat16 [2304, 9216], P('blk', 'head'), may hold values from -0.125 to 0.125
- w_up: bfloat16 [2304, 9216], P('blk', 'head'), may hold values from -0.125 to 0.125
- w_down: bfloat16 [9216, 2304], P('head', 'blk'), may hold values from -0.0625 to 0.0625
- norm_scales: bfloat16 [4, 2304], P(None, 'blk'), may hold values from 0.5 to 1.5
Outputs:
- layer_out: bfloat16 [4096, 2304], P(('blk', 'head'))
- grad_in: float32 [4096, 2304], P(('blk', 'head'))
- grad_query: float32 [2304, 2048], P('blk', 'head')
- grad_key: float32 [2304, 1024], P('blk')
- grad_value: float32 [2304, 1024], P('blk')
- grad_output: float32 [2048, 2304], P('head', 'blk')
- grad_gate: float32 [2304, 9216], P('blk', 'head')
- grad_up: float32 [2304, 9216], P('blk', 'head')
- grad_down: float32 [9216, 2304], P('head', 'blk')
- grad_scales: float32 [4, 2304], P(None, 'blk')
The draws below stay inside these ranges and needn't reach their ends.
Inputs may be any that keep to these rules, and one draw needn't show every extreme that they name: span_order is a permutation of 0 to 15 in which entries 2 i and 2 i + 1 sum to 15.
All inputs are finite; a program needn't handle non-finite values.
Results may differ from the reference program's by a relative error of at most 0.03.
The reference program's roundings to bfloat16 on the way count: a program that leaves them out, or rounds other values in their place, can miss the bound.
Values may be sent and summed in bfloat16 or wider, within the bound.
No kernel may reach another device: no remote copies, remote signals or barrier semaphores. Data moves between devices by JAX's collectives and lax.ppermute only.
A program may use at most 256 MiB of HBM per device.

```python
import math
import jax
import jax.numpy as jnp
from jax import lax

D = 2304
H = 8
KVH = 4
HD = 256
FF = 9216
SPAN = 256
SPANS = 16
LENGTH = 4096


def draw_span_order(key, part):
    key = jax.random.fold_in(key, 7)
    leading = jax.random.permutation(key, SPANS // 2).astype(jnp.int32)
    mirror = SPANS - 1 - leading
    return jnp.stack([leading, mirror], axis=1).reshape(SPANS).astype(jnp.int32)


def draw_w_query(key, part):
    key = jax.random.fold_in(key, 11)
    head_key = jax.random.fold_in(key, 1)
    entry_key = jax.random.fold_in(key, 2)
    chosen = jax.random.permutation(head_key, H).astype(jnp.int32)[:2]
    column_head = jnp.arange(H * HD, dtype=jnp.int32) // HD
    picked = jnp.any(column_head[:, None] == chosen[None, :], axis=1)
    factor = jnp.where(picked, 6.0, 1.0).astype(jnp.float32)
    normal_part = jax.random.truncated_normal(entry_key, -4.0, 4.0, (D, H * HD), jnp.float32)
    return (normal_part * factor[None, :] * D ** (-0.5)).astype(jnp.bfloat16)


def block_levels(stream_key, extent, shards, low, high):
    loudness = 1.0
    for axis_at, shards_of in shards:
        draws = jax.random.uniform(jax.random.fold_in(jax.random.fold_in(stream_key, 6), axis_at), (shards_of,), jnp.float32, low / len(shards), high / len(shards))
        loudness = loudness * jnp.repeat(jnp.exp(draws), extent[axis_at] // shards_of).reshape((-1,) + (1,) * (len(extent) - 1 - axis_at))
    return loudness


def normal_values(key, shape, spread, most, shards=(), held_as=jnp.bfloat16):
    array = spread * jax.random.normal(key, shape, jnp.float32)
    if shards:
        array = array * block_levels(key, shape, shards, -0.22, 0.18)
    return jnp.clip(array, -most, most).astype(held_as)


def setup_inputs(seed: int = 0) -> dict:
    arg_keys = jax.random.split(jax.random.key(seed), 12)
    hidden_in = normal_values(arg_keys[0], (LENGTH, D), 1.0, 6.0, ((0, 32),))
    out_grad = normal_values(arg_keys[1], (LENGTH, D), 1.0, 6.0, ((0, 32),))
    span_order = draw_span_order(jax.random.fold_in(arg_keys[11], 71), 0)
    w_query = draw_w_query(jax.random.fold_in(arg_keys[11], 71), 0)
    w_key = normal_values(arg_keys[4], (D, KVH * HD), D ** -0.5, 0.125, ((0, 8),))
    w_value = normal_values(arg_keys[5], (D, KVH * HD), D ** -0.5, 0.125, ((0, 8),))
    w_output = normal_values(arg_keys[6], (H * HD, D), (H * HD) ** -0.5, 0.125, ((0, 4), (1, 8)))
    w_gate = normal_values(arg_keys[7], (D, FF), D ** -0.5, 0.125, ((0, 8), (1, 4)))
    w_up = normal_values(arg_keys[8], (D, FF), D ** -0.5, 0.125, ((0, 8), (1, 4)))
    w_down = normal_values(arg_keys[9], (FF, D), FF ** -0.5, 0.0625, ((0, 4), (1, 8)))
    norm_scales = jnp.clip(1.0 + 0.1 * jax.random.normal(arg_keys[10], (4, D), jnp.float32), 0.5, 1.5).astype(jnp.bfloat16)
    return {"hidden_in": hidden_in, "out_grad": out_grad, "span_order": span_order, "w_query": w_query, "w_key": w_key, "w_value": w_value, "w_output": w_output, "w_gate": w_gate, "w_up": w_up, "w_down": w_down, "norm_scales": norm_scales}


@jax.custom_vjp
def low(v):
    return lax.optimization_barrier(v.astype(jnp.bfloat16)).astype(jnp.float32)

@jax.custom_vjp
def low_back(v):
    return v

def low_keep(v):
    return (low(v), None)

def low_pass(kept, grad):
    return (grad,)

def back_keep(v):
    return (v, None)

def back_low(kept, grad):
    return (low(grad),)
low.defvjp(low_keep, low_pass)
low_back.defvjp(back_keep, back_low)
norm_eps = 1e-06
cap_value = 50.0
theta_base = 10000.0
masked_value = -1e+30

def matmul(left, right):
    return jnp.dot(left, right, precision=lax.Precision.HIGHEST)

def rms_scale(value, scale):
    inverse = lax.rsqrt(lax.optimization_barrier(jnp.mean(value * value, axis=-1, keepdims=True)) + norm_eps)
    return value * inverse * scale

def rotate(value, position, first_half, sign):
    row_count, total_width = value.shape
    quarter = HD // 4
    groups = total_width // (2 * quarter)
    shaped = value.reshape(row_count, groups, 2, quarter)
    halves = (first_half + jnp.arange(groups, dtype=jnp.int32)) % 2
    pair_index = halves[:, None] * quarter + jnp.arange(quarter, dtype=jnp.int32)[None, :]
    frequency = jnp.power(theta_base, -2.0 * pair_index.astype(jnp.float32) / HD)
    angles = position.astype(jnp.float32)[:, None, None] * frequency[None, :, :]
    cosine = jnp.cos(angles)
    sine_part = jnp.sin(angles)
    first_part = shaped[:, :, 0]
    second_part = shaped[:, :, 1]
    new_first = first_part * cosine - sign * second_part * sine_part
    new_second = sign * first_part * sine_part + second_part * cosine
    return jnp.stack([new_first, new_second], axis=2).reshape(row_count, total_width)

def attention_tile(query_tile, query_pos, key_rows, value_rows, key_pos):
    raw_score = low_back(jnp.einsum('qkgd,mkgd->qkgm', query_tile, key_rows, precision=lax.Precision.HIGHEST))
    capped = cap_value * jnp.tanh(raw_score / (cap_value * math.sqrt(HD)))
    visible = (key_pos[None, :] <= query_pos[:, None])[:, None, None, :]
    masked = jnp.where(visible, capped, masked_value)
    row_top = lax.optimization_barrier(jnp.max(masked, axis=-1, keepdims=True))
    weights = jnp.where(visible, jnp.exp(masked - row_top), 0.0)
    probability = low(weights / lax.optimization_barrier(jnp.sum(weights, axis=-1, keepdims=True)))
    mixed = jnp.einsum('qkgm,mkgd->qkgd', probability, value_rows, precision=lax.Precision.HIGHEST)
    return low(low_back(mixed))

def reference(hidden_in, out_grad, span_order, w_query, w_key, w_value, w_output, w_gate, w_up, w_down, norm_scales):
    row_index = jnp.arange(LENGTH, dtype=jnp.int32)
    position = span_order[row_index // SPAN] * SPAN + row_index % SPAN
    group_size = H // KVH
    qblock = math.gcd(512, LENGTH)

    def copies(lin):
        shaped = lin.reshape(LENGTH, KVH, 1, HD)
        return jnp.broadcast_to(shaped, (LENGTH, KVH, group_size, HD)).reshape(LENGTH, H * HD)

    def forward(inputs, wq_full, wk_full, wv_full, wo_full, wg_full, wu_full, wd_full, scales):
        normed = low(rms_scale(inputs, scales[0]))
        query_lin = low_back(matmul(normed, wq_full))
        queries = low(rotate(query_lin, position, 0, 1.0))
        key_copies = low_back(copies(matmul(normed, wk_full)))
        key_rows = low(rotate(key_copies, position, 0, 1.0)).reshape(LENGTH, KVH, group_size, HD)
        value_rows = low(low_back(copies(matmul(normed, wv_full)))).reshape(LENGTH, KVH, group_size, HD)
        query_tiles = queries.reshape(LENGTH // qblock, qblock, KVH, group_size, HD)
        pos_tiles = position.reshape(LENGTH // qblock, qblock)

        def attend(tile_pair):
            return attention_tile(tile_pair[0], tile_pair[1], key_rows, value_rows, position)
        mixed = lax.map(jax.checkpoint(attend), (query_tiles, pos_tiles)).reshape(LENGTH, H * HD)
        attn = low_back(matmul(mixed, wo_full))
        resid = inputs + rms_scale(attn, scales[1])
        ffn_in = low(rms_scale(resid, scales[2]))
        gate = low_back(matmul(ffn_in, wg_full))
        up_value = low_back(matmul(ffn_in, wu_full))
        hidden = low(jax.nn.gelu(gate, approximate=True) * up_value)
        ffn_out = low_back(matmul(hidden, wd_full))
        return resid + rms_scale(ffn_out, scales[3])
    layer_out, pullback = jax.vjp(forward, hidden_in.astype(jnp.float32), w_query.astype(jnp.float32), w_key.astype(jnp.float32), w_value.astype(jnp.float32), w_output.astype(jnp.float32), w_gate.astype(jnp.float32), w_up.astype(jnp.float32), w_down.astype(jnp.float32), norm_scales.astype(jnp.float32))
    grads = pullback(out_grad.astype(jnp.float32))
    return (layer_out.astype(jnp.bfloat16), grads[0], grads[1], grads[2], grads[3], grads[4], grads[5], grads[6], grads[7], grads[8])
```

```python
import functools
import math

import jax
import jax.numpy as jnp
from jax import lax
from jax.experimental import pallas as pl
from jax.experimental.pallas import tpu as pltpu
from jax.sharding import PartitionSpec as P

H = 8
KVH = 4
HD = 256

norm_eps = 1e-06
cap_value = 50.0
theta_base = 10000.0
f32 = jnp.float32
bf16 = jnp.bfloat16


def rms_scale(value, scale):
    inverse = lax.rsqrt(jnp.mean(value * value, axis=-1, keepdims=True) + norm_eps)
    return value * inverse * scale


def rms_back(value, scale, grad):
    inverse = lax.rsqrt(jnp.mean(value * value, axis=-1, keepdims=True) + norm_eps)
    scaled = grad * scale
    inner = jnp.mean(scaled * value, axis=-1, keepdims=True)
    grad_value = inverse * scaled - value * (inverse * inverse * inverse) * inner
    grad_scale = jnp.sum(grad * value * inverse, axis=0)
    return (grad_value, grad_scale)


def rotation(position, head_dim):
    quarter = head_dim // 4
    pair_index = jnp.arange(2, dtype=jnp.int32)[:, None] * quarter + jnp.arange(quarter, dtype=jnp.int32)[None, :]
    frequency = jnp.power(theta_base, -2.0 * pair_index.astype(f32) / head_dim)
    angles = position.astype(f32)[:, None, None] * frequency[None, :, :]
    return jnp.cos(angles), jnp.sin(angles)


def rotate(value, table, sign):
    cosine, sine = table
    row_count, total_width = value.shape
    quarter = cosine.shape[2]
    copies = total_width // (4 * quarter)
    shaped = value.reshape(row_count, copies, 2, 2, quarter)
    first = shaped[:, :, :, 0]
    second = shaped[:, :, :, 1]
    cosine = cosine[:, None]
    sine = sign * sine[:, None]
    new_first = first * cosine - second * sine
    new_second = first * sine + second * cosine
    return jnp.stack([new_first, new_second], axis=3).reshape(row_count, total_width)


def gelu_tanh(value):
    return jax.nn.gelu(value, approximate=True)


def swap(value, axis):
    blk_mask, head_mask = axis
    block_count, head_count = lax.axis_size("blk"), lax.axis_size("head")
    if blk_mask == 0:
        return lax.ppermute(value, "head", [(i, i ^ head_mask) for i in range(head_count)])
    return lax.ppermute(value, "blk", [(i, i ^ blk_mask) for i in range(block_count)])


def bits(count):
    return [1 << i for i in range(count.bit_length() - 1)]


def route(subset, axis_total):
    members = [i for i in range(axis_total) if subset >> i & 1]
    if len(members) >= 2 and len(members) == axis_total:
        return members
    if len(members) == 2 and members[1] - members[0] != 1:
        return members[1:]
    return members[:1]


def shares(row_total, parts):
    unit = row_total // 16
    cuts = [unit * i // parts * 16 for i in range(parts + 1)]
    cuts[-1] = row_total
    return list(zip(cuts[:-1], cuts[1:]))


def gather_rows(value, axes):
    pieces = [value]
    total = len(axes)
    for subset in sorted(range(1, 1 << total), key=lambda t: (bin(t).count("1"), t)):
        pieces.append(None)
    for subset in sorted(range(1, 1 << total), key=lambda t: (bin(t).count("1"), t)):
        ways = route(subset, total)
        parts = []
        for way, (low, high) in zip(ways, shares(value.shape[0], len(ways))):
            source = pieces[subset ^ (1 << way)]
            parts.append(swap(source if len(ways) == 1 else source[low:high], axes[way]))
        pieces[subset] = parts[0] if len(parts) == 1 else jnp.concatenate(parts, 0)
    return pieces


def joined(left, right):
    return (left.astype(f32) + right.astype(f32)).astype(bf16)


def scatter_rows(pieces, axes):
    total = len(axes)
    pieces = list(pieces)
    rows = pieces[0].shape[0]
    last = []
    for subset in sorted(range(1, 1 << total), key=lambda t: (-bin(t).count("1"), t)):
        ways = route(subset, total)
        for way, (low, high) in zip(ways, shares(rows, len(ways))):
            target = subset ^ (1 << way)
            if len(ways) == 1:
                moved = swap(pieces[subset], axes[way])
                if target == 0:
                    last.append(moved)
                else:
                    pieces[target] = joined(pieces[target], moved)
            else:
                moved = swap(pieces[subset][low:high], axes[way])
                old = pieces[target]
                cut = [old[:low], joined(old[low:high], moved), old[high:]]
                pieces[target] = jnp.concatenate([c for c in cut if c.shape[0]], 0)
    result = pieces[0].astype(f32)
    for moved in last:
        result = result + moved.astype(f32)
    return result


def gather_blocks(value, masks):
    held = {0: value}
    for mask in masks:
        for have in list(held):
            held[have ^ mask] = swap(held[have], (mask, 0))
    return held


def stack_rows(held, block_index):
    rows, columns = held[0].shape
    whole = jnp.zeros((len(held) * rows, columns), held[0].dtype)
    for mask, piece in held.items():
        whole = lax.dynamic_update_slice(whole, piece, ((block_index ^ mask) * rows, 0))
    return whole


def scatter_blocks(pick, masks):
    pending = {}

    def term(target):
        value = pick(target)
        return value

    terms = {}
    every = [0]
    for mask in masks:
        every = every + [t ^ mask for t in every]
    for target in every:
        terms[target] = term(target)
    left = list(every)
    for step, mask in enumerate(masks):
        rest = masks[step + 1 :]
        keep = [0]
        for other in rest:
            keep = keep + [t ^ other for t in keep]
        final = not rest
        for target in keep:
            moved = swap(terms[target ^ mask].astype(bf16), (mask, 0))
            total = terms[target].astype(f32) + moved.astype(f32)
            terms[target] = total if final else total.astype(bf16)
        left = keep
    return terms[0]


def scores(query, key, score_scale):
    raw = lax.dot_general(query, key, (((1,), (1,)), ((), ())), preferred_element_type=f32)
    return jnp.tanh(raw * (score_scale / cap_value))


def forward_kernel(group, span_len, tiles, spans_ref, q_ref, kv_ref, mixed_ref, exact_ref, lse_ref, q_all, acc, total):
    step = pl.program_id(0)
    score_scale = 1.0 / math.sqrt(HD)
    rows = group * span_len

    @pl.when(step == 0)
    def _():
        for half in range(2):
            for g in range(group):
                q_all[half, g * span_len : (g + 1) * span_len, :] = q_ref[
                    half * span_len : (half + 1) * span_len, g * HD : (g + 1) * HD
                ]
        acc[...] = jnp.zeros_like(acc)
        total[...] = jnp.zeros_like(total)

    tile_span = spans_ref[step]
    key = kv_ref[:, :HD]
    value = kv_ref[:, HD:]

    def visit(half, diagonal):
        weights = jnp.exp(cap_value * scores(q_all[half], key, score_scale))
        if diagonal:
            flip = spans_ref[tiles + 2]
            shape = (rows, span_len)
            q_pos = (lax.broadcasted_iota(jnp.int32, shape, 0) % span_len) ^ flip
            k_pos = lax.broadcasted_iota(jnp.int32, shape, 1) ^ flip
            weights = jnp.where(k_pos <= q_pos, weights, 0.0)
        part = weights[:, :128]
        for at in range(128, span_len, 128):
            part = part + weights[:, at : at + 128]
        total[half] += part
        acc[half] += jnp.dot(weights.astype(bf16), value, preferred_element_type=f32)

    for half in range(2):
        own = spans_ref[tiles + half]

        @pl.when(tile_span < own)
        def _():
            visit(half, False)

        @pl.when(tile_span == own)
        def _():
            visit(half, True)

    @pl.when(step == tiles - 1)
    def _():
        for half in range(2):
            sums = jnp.sum(total[half], axis=1, keepdims=True)
            exact = acc[half] / sums
            lse_ref[half] = jnp.log(jnp.sum(total[half].T, axis=0, keepdims=True))
            for g in range(group):
                piece = exact[g * span_len : (g + 1) * span_len]
                place = (slice(half * span_len, (half + 1) * span_len), slice(g * HD, (g + 1) * HD))
                exact_ref[place] = piece
                mixed_ref[place] = piece.astype(bf16)


def backward_kernel(
    group, span_len, tiles, spans_ref, q_ref, g_ref, exact_ref, lse_ref, kv_ref, dq_ref, dkv_ref, q_all, g_all, delta, dq_acc
):
    step = pl.program_id(0)
    score_scale = 1.0 / math.sqrt(HD)
    rows = group * span_len

    @pl.when(step == 0)
    def _():
        for half in range(2):
            for g in range(group):
                place = (slice(half * span_len, (half + 1) * span_len), slice(g * HD, (g + 1) * HD))
                here = slice(g * span_len, (g + 1) * span_len)
                q_all[half, here, :] = q_ref[place]
                g_all[half, here, :] = g_ref[place]
                product = g_ref[place].astype(f32) * exact_ref[place]
                folded = product[:, :128] + product[:, 128:]
                delta[half, :, here] = jnp.sum(folded.T, axis=0, keepdims=True)
        dq_acc[...] = jnp.zeros_like(dq_acc)

    tile_span = spans_ref[step]
    key = kv_ref[:, :HD]
    value = kv_ref[:, HD:]

    def visit(half, diagonal):
        query = q_all[half]
        grad = g_all[half]
        tangent = scores(key, query, score_scale)
        probability = jnp.exp(cap_value * tangent - lse_ref[half])
        if diagonal:
            flip = spans_ref[tiles + 2]
            shape = (span_len, rows)
            q_pos = (lax.broadcasted_iota(jnp.int32, shape, 1) % span_len) ^ flip
            k_pos = lax.broadcasted_iota(jnp.int32, shape, 0) ^ flip
            probability = jnp.where(k_pos <= q_pos, probability, 0.0)
        grad_prob = lax.dot_general(value, grad, (((1,), (1,)), ((), ())), preferred_element_type=f32)
        grad_raw = probability * (grad_prob - delta[half]) * ((1.0 - tangent * tangent) * score_scale)
        grad_raw = grad_raw.astype(bf16)
        dv = jnp.dot(probability.astype(bf16), grad, preferred_element_type=f32)
        dk = jnp.dot(grad_raw, query, preferred_element_type=f32)
        dq_acc[half] += lax.dot_general(grad_raw, key, (((0,), (0,)), ((), ())), preferred_element_type=f32)
        return dk, dv

    low, high = spans_ref[tiles], spans_ref[tiles + 1]

    @pl.when(jnp.logical_and(tile_span > low, tile_span > high))
    def _():
        dkv_ref[...] = jnp.zeros_like(dkv_ref)

    for half in range(2):
        own = spans_ref[tiles + half]
        other = spans_ref[tiles + 1 - half]

        def store(diagonal, half=half, own=own, other=other):
            dk, dv = visit(half, diagonal)

            @pl.when(jnp.logical_and(half == 1, tile_span <= other))
            def _():
                dkv_ref[:, :HD] = (dkv_ref[:, :HD].astype(f32) + dk).astype(dkv_ref.dtype)
                dkv_ref[:, HD:] = (dkv_ref[:, HD:].astype(f32) + dv).astype(dkv_ref.dtype)

            @pl.when(jnp.logical_or(half == 0, tile_span > other))
            def _():
                dkv_ref[:, :HD] = dk.astype(dkv_ref.dtype)
                dkv_ref[:, HD:] = dv.astype(dkv_ref.dtype)

        @pl.when(tile_span < own)
        def _():
            store(False)

        @pl.when(tile_span == own)
        def _():
            store(True)

    @pl.when(step == tiles - 1)
    def _():
        for half in range(2):
            for g in range(group):
                dq_ref[half * span_len : (half + 1) * span_len, g * HD : (g + 1) * HD] = dq_acc[
                    half, g * span_len : (g + 1) * span_len
                ]


def attention_forward(spans, queries, kv, span_len):
    tiles = kv.shape[0] // span_len
    width = queries.shape[1]
    group = width // HD
    rows = group * span_len
    whole = lambda s, t: (0, 0)
    visits = tiles + 1
    return pl.pallas_call(
        functools.partial(forward_kernel, group, span_len, tiles),
        grid_spec=pltpu.PrefetchScalarGridSpec(
            num_scalar_prefetch=1,
            grid=(tiles,),
            in_specs=[
                pl.BlockSpec(queries.shape, whole),
                pl.BlockSpec((span_len, 2 * HD), lambda s, t: (s, 0)),
            ],
            out_specs=[
                pl.BlockSpec(queries.shape, whole),
                pl.BlockSpec(queries.shape, whole),
                pl.BlockSpec((2, 1, rows), lambda s, t: (0, 0, 0)),
            ],
            scratch_shapes=[
                pltpu.VMEM((2, rows, HD), bf16),
                pltpu.VMEM((2, rows, HD), f32),
                pltpu.VMEM((2, rows, 128), f32),
            ],
        ),
        out_shape=[
            jax.ShapeDtypeStruct(queries.shape, bf16),
            jax.ShapeDtypeStruct(queries.shape, f32),
            jax.ShapeDtypeStruct((2, 1, rows), f32),
        ],
        compiler_params=pltpu.CompilerParams(vmem_limit_bytes=40 * 1024 * 1024),
        cost_estimate=pl.CostEstimate(
            flops=visits * rows * span_len * HD * 4,
            bytes_accessed=kv.size * 2 + queries.size * 12,
            transcendentals=visits * rows * span_len * 2,
        ),
        name="attention_forward",
    )(spans, queries, kv)


def attention_backward(spans, queries, grads, exact, lse, kv, span_len):
    tiles = kv.shape[0] // span_len
    width = queries.shape[1]
    group = width // HD
    rows = group * span_len
    whole = lambda s, t: (0, 0)
    visits = tiles + 1
    return pl.pallas_call(
        functools.partial(backward_kernel, group, span_len, tiles),
        grid_spec=pltpu.PrefetchScalarGridSpec(
            num_scalar_prefetch=1,
            grid=(tiles,),
            in_specs=[
                pl.BlockSpec(queries.shape, whole),
                pl.BlockSpec(queries.shape, whole),
                pl.BlockSpec(queries.shape, whole),
                pl.BlockSpec((2, 1, rows), lambda s, t: (0, 0, 0)),
                pl.BlockSpec((span_len, 2 * HD), lambda s, t: (s, 0)),
            ],
            out_specs=[
                pl.BlockSpec(queries.shape, whole),
                pl.BlockSpec((span_len, 2 * HD), lambda s, t: (s, 0)),
            ],
            scratch_shapes=[
                pltpu.VMEM((2, rows, HD), bf16),
                pltpu.VMEM((2, rows, HD), bf16),
                pltpu.VMEM((2, 1, rows), f32),
                pltpu.VMEM((2, rows, HD), f32),
            ],
        ),
        out_shape=[
            jax.ShapeDtypeStruct(queries.shape, f32),
            jax.ShapeDtypeStruct(kv.shape, bf16),
        ],
        compiler_params=pltpu.CompilerParams(vmem_limit_bytes=40 * 1024 * 1024),
        cost_estimate=pl.CostEstimate(
            flops=visits * rows * span_len * HD * 10,
            bytes_accessed=kv.size * 4 + queries.size * 16,
            transcendentals=visits * rows * span_len * 2,
        ),
        name="attention_backward",
    )(spans, queries, grads, exact, lse, kv)


def product(left, right, left_dim, right_dim, out=f32):
    result = lax.dot_general(left, right, (((left_dim,), (right_dim,)), ((), ())), preferred_element_type=f32)
    return result.astype(out)


def on_device(
    hidden_in,
    out_grad,
    span_order,
    w_query,
    w_key,
    w_value,
    w_output,
    w_gate,
    w_up,
    w_down,
    norm_scales,
):
    local_rows = hidden_in.shape[0]
    head_count = lax.axis_size("head")
    block_count = lax.axis_size("blk")
    block_index = lax.axis_index("blk")
    head_index = lax.axis_index("head")
    group_rows = local_rows * head_count
    span_len = group_rows // 2
    model_rows, query_width = w_query.shape
    model_width = hidden_in.shape[1]
    query_heads = query_width // HD
    half_units = w_gate.shape[1] // 2

    chip_masks = bits(block_count)[1:]
    pair = chip_masks[0]
    down_masks = chip_masks[::-1] + [1]
    head_axes = [(0, mask) for mask in bits(head_count)]
    unit_axes = head_axes + [(pair, 0)]
    unit_side = (block_index // pair) % 2

    held = gather_blocks(norm_scales, down_masks)
    scale_rows = jnp.zeros((block_count,) + norm_scales.shape, norm_scales.dtype)
    for mask, piece in held.items():
        scale_rows = lax.dynamic_update_slice(scale_rows, piece[None], (block_index ^ mask, 0, 0))
    scale_rows = scale_rows.transpose(1, 0, 2).reshape(norm_scales.shape[0], model_width).astype(f32)

    kv_at = head_index * query_heads // (H // KVH) * HD
    kv_local = jnp.concatenate(
        [
            lax.dynamic_slice_in_dim(w_key, kv_at, HD, 1),
            lax.dynamic_slice_in_dim(w_value, kv_at, HD, 1),
        ],
        1,
    )
    kv_weight = stack_rows(gather_blocks(kv_local, down_masks), block_index)
    query_weight = stack_rows(gather_blocks(w_query, down_masks), block_index)
    output_weight = stack_rows(gather_blocks(w_output.T, down_masks), block_index)

    def unit_weight(local):
        mine = lax.dynamic_slice_in_dim(local, unit_side * half_units, half_units, 1)
        theirs = lax.dynamic_slice_in_dim(local, (1 - unit_side) * half_units, half_units, 1)
        held = {0: mine, pair: swap(theirs, (pair, 0))}
        for mask in [m for m in down_masks if m != pair]:
            for have in list(held):
                held[have ^ mask] = swap(held[have], (mask, 0))
        return stack_rows(held, block_index)

    gate_weight = unit_weight(w_gate)
    up_weight = unit_weight(w_up)
    down_weight = unit_weight(w_down.T)

    def unit_gradient(partial):
        shaped = partial.reshape(block_count, model_rows, half_units)

        def pick(mask):
            return lax.dynamic_index_in_dim(shaped, block_index ^ mask, 0, keepdims=False)

        masks = [1] + [m for m in down_masks if m not in (1, pair)]

        mine = scatter_blocks(pick, masks)
        theirs = scatter_blocks(lambda mask: pick(mask ^ pair), masks)
        other = swap(theirs.astype(bf16), (pair, 0))
        mine = mine.astype(bf16)
        low = jnp.where(unit_side == 0, mine, other)
        high = jnp.where(unit_side == 0, other, mine)
        return jnp.concatenate([low, high], 1).astype(f32)

    def block_gradient(partial):
        shaped = partial.reshape(block_count, model_rows, partial.shape[1])
        return scatter_blocks(
            lambda mask: lax.dynamic_index_in_dim(shaped, block_index ^ mask, 0, keepdims=False),
            [1] + chip_masks[::-1],
        )

    hidden_full = jnp.concatenate(gather_rows(hidden_in, head_axes), 0).astype(f32)
    slot = jnp.arange(head_count, dtype=jnp.int32) ^ head_index
    in_block = (slot[:, None] * local_rows + jnp.arange(local_rows, dtype=jnp.int32)[None, :]).reshape(-1)
    side = head_index // (head_count // 2)
    own_spans = jnp.stack([span_order[2 * block_index + side], span_order[2 * block_index + 1 - side]])
    row_spans = jnp.repeat(own_spans, span_len)
    position = row_spans * span_len + in_block % span_len
    tile_blocks = jnp.arange(block_count, dtype=jnp.int32) ^ block_index
    tile_slots = (2 * tile_blocks[:, None] + jnp.stack([side, 1 - side])[None, :]).reshape(-1)
    flip = (head_index % (head_count // 2)) * local_rows
    spans = jnp.concatenate([span_order[tile_slots], own_spans, flip[None]]).astype(jnp.int32)
    table = rotation(position, HD)

    residual_in = hidden_in.astype(f32)
    normed_full = rms_scale(hidden_full, scale_rows[0]).astype(bf16)
    kv_lin = product(normed_full, kv_weight, 1, 0)
    kv_rows = jnp.concatenate(
        [rotate(kv_lin[:, :HD], table, 1.0).astype(bf16), kv_lin[:, HD:].astype(bf16)], 1
    )
    kv_held = gather_blocks(kv_rows, down_masks)
    kv = jnp.concatenate([kv_held[mask] for mask in range(block_count)], 0)
    query_lin = product(normed_full, query_weight, 1, 0)
    queries = rotate(query_lin, table, 1.0).astype(bf16)

    mixed, exact, lse = attention_forward(spans, queries, kv, span_len)

    def row_sum(partial, axes):
        shaped = partial.reshape(1 << len(axes), local_rows, model_width)
        return scatter_rows([shaped[i] for i in range(1 << len(axes))], axes)

    attn_out = row_sum(product(mixed, output_weight, 1, 1, bf16), head_axes)
    resid = residual_in + rms_scale(attn_out, scale_rows[1])
    ffn_in = rms_scale(resid, scale_rows[2]).astype(bf16)
    ffn_full = jnp.concatenate(gather_rows(ffn_in, unit_axes), 0)
    gate = product(ffn_full, gate_weight, 1, 0)
    up_value = product(ffn_full, up_weight, 1, 0)
    activated, gelu_back = jax.vjp(gelu_tanh, gate)
    hidden = (activated * up_value).astype(bf16)
    ffn_out = row_sum(product(hidden, down_weight, 1, 1, bf16), unit_axes)
    layer_out = (resid + rms_scale(ffn_out, scale_rows[3])).astype(bf16)

    grad_top = out_grad.astype(f32)
    grad_ffn_out, scale_grad3 = rms_back(ffn_out, scale_rows[3], grad_top)
    grad_ffn_full = jnp.concatenate(gather_rows(grad_ffn_out.astype(bf16), unit_axes), 0)
    grad_hidden = product(grad_ffn_full, down_weight, 1, 0)
    grad_down = product(grad_ffn_full, hidden, 0, 0, bf16)
    grad_gate_act = gelu_back(grad_hidden * up_value)[0].astype(bf16)
    grad_up_act = (grad_hidden * activated).astype(bf16)
    grad_ffn_part = product(grad_gate_act, gate_weight, 1, 1) + product(grad_up_act, up_weight, 1, 1)
    grad_ffn_in = row_sum(grad_ffn_part.astype(bf16), unit_axes)
    grad_wgate = product(ffn_full, grad_gate_act, 0, 0, bf16)
    grad_wup = product(ffn_full, grad_up_act, 0, 0, bf16)
    out_down = unit_gradient(grad_down).T
    out_gate = unit_gradient(grad_wgate)
    out_up = unit_gradient(grad_wup)

    grad_resid_part, scale_grad2 = rms_back(resid, scale_rows[2], grad_ffn_in)
    grad_resid = grad_top + grad_resid_part
    grad_attn, scale_grad1 = rms_back(attn_out, scale_rows[1], grad_resid)
    grad_attn_full = jnp.concatenate(gather_rows(grad_attn.astype(bf16), head_axes), 0)
    grad_mixed = product(grad_attn_full, output_weight, 1, 0, bf16)
    grad_woutput = product(grad_attn_full, mixed, 0, 0, bf16)
    out_output = block_gradient(grad_woutput).T

    grad_query, grad_kv = attention_backward(spans, queries, grad_mixed, exact, lse, kv, span_len)
    grad_query_lin = rotate(grad_query, table, -1.0).astype(bf16)
    grad_wquery = product(normed_full, grad_query_lin, 0, 0, bf16)
    out_query = block_gradient(grad_wquery)
    kv_shaped = grad_kv.reshape(block_count, group_rows, 2 * HD)
    kv_grad_rows = scatter_blocks(lambda mask: kv_shaped[mask], [1] + chip_masks[::-1])
    grad_kv_lin = jnp.concatenate(
        [rotate(kv_grad_rows[:, :HD], table, -1.0).astype(bf16), kv_grad_rows[:, HD:].astype(bf16)], 1
    )
    grad_wkv = block_gradient(product(normed_full, grad_kv_lin, 0, 0, bf16))
    grad_normed_part = product(grad_query_lin, query_weight, 1, 1) + product(grad_kv_lin, kv_weight, 1, 1)
    grad_normed = row_sum(grad_normed_part.astype(bf16), head_axes)
    grad_in_part, scale_grad0 = rms_back(residual_in, scale_rows[0], grad_normed)
    grad_in = grad_resid + grad_in_part

    kv_pieces = jnp.stack(gather_rows(grad_wkv.astype(bf16), head_axes))
    kv_ordered = jnp.zeros_like(kv_pieces)
    for mask in range(head_count):
        kv_ordered = lax.dynamic_update_slice(kv_ordered, kv_pieces[mask][None], (head_index ^ mask, 0, 0))
    kv_ordered = kv_ordered.astype(f32).reshape(KVH, head_count // KVH, model_rows, 2, HD).sum(1)
    out_key = kv_ordered[:, :, 0].transpose(1, 0, 2).reshape(model_rows, KVH * HD)
    out_value = kv_ordered[:, :, 1].transpose(1, 0, 2).reshape(model_rows, KVH * HD)

    scale_grad = jnp.stack([scale_grad0, scale_grad1, scale_grad2, scale_grad3])
    scale_shaped = scale_grad.reshape(4, block_count, model_rows).transpose(1, 0, 2)
    scale_total = scatter_blocks(
        lambda mask: lax.dynamic_index_in_dim(scale_shaped, block_index ^ mask, 0, keepdims=False),
        [1] + chip_masks[::-1],
    )
    for axis in head_axes:
        scale_total = scale_total + swap(scale_total, axis)

    return (
        layer_out,
        grad_in,
        out_query,
        out_key,
        out_value,
        out_output,
        out_gate,
        out_up,
        out_down,
        scale_total,
    )


def solution(mesh):
    placed = (
        P(("blk", "head"), None),
        P(("blk", "head"), None),
        P(),
        P("blk", "head"),
        P("blk", None),
        P("blk", None),
        P("head", "blk"),
        P("blk", "head"),
        P("blk", "head"),
        P("head", "blk"),
        P(None, "blk"),
    )
    return jax.shard_map(
        on_device,
        mesh=mesh,
        in_specs=placed,
        out_specs=(
            P(("blk", "head"), None),
            P(("blk", "head"), None),
            P("blk", "head"),
            P("blk", None),
            P("blk", None),
            P("head", "blk"),
            P("blk", "head"),
            P("blk", "head"),
            P("head", "blk"),
            P(None, "blk"),
        ),
        check_vma=False,
    )
```

```python
import functools
import math

import jax
import jax.numpy as jnp
from jax import lax
from jax.experimental import pallas as pl
from jax.experimental.pallas import tpu as pltpu
from jax.sharding import PartitionSpec as P

H = 8
KVH = 4
HD = 256

norm_eps = 1e-06
cap_value = 50.0
theta_base = 10000.0
f32 = jnp.float32
bf16 = jnp.bfloat16


def inverse_rms(value):
    return lax.rsqrt(jnp.mean(value * value, axis=-1, keepdims=True) + norm_eps)


def rms_back(value, scale, grad):
    inverse = inverse_rms(value)
    scaled = grad * scale
    inner = jnp.mean(scaled * value, axis=-1, keepdims=True)
    grad_value = inverse * scaled - value * (inverse * inverse * inverse) * inner
    grad_scale = jnp.sum(grad * value * inverse, axis=0, keepdims=True)
    return (grad_value, grad_scale)


def rotation(position):
    entry = jnp.arange(HD, dtype=jnp.int32)
    quarter = HD // 4
    pair_index = entry // (2 * quarter) * quarter + entry % quarter
    frequency = jnp.power(theta_base, -2.0 * pair_index.astype(f32) / HD)
    angles = position.astype(f32)[:, None] * frequency[None, :]
    sign = jnp.where(entry % (2 * quarter) < quarter, -1.0, 1.0)
    return jnp.cos(angles), jnp.sin(angles) * sign[None, :]


def rotated(value, cosine, sine, sign):
    half = HD // 2
    parts = []
    for at in range(0, HD, half):
        piece = value[:, at : at + half]
        partner = pltpu.roll(piece, half // 2, 1)
        parts.append(piece * cosine[:, at : at + half] + partner * (sign * sine[:, at : at + half]))
    return jnp.concatenate(parts, 1)


def swap(value, axis):
    blk_mask, head_mask = axis
    block_count, head_count = lax.axis_size("blk"), lax.axis_size("head")
    if blk_mask == 0:
        return lax.ppermute(value, "head", [(i, i ^ head_mask) for i in range(head_count)])
    return lax.ppermute(value, "blk", [(i, i ^ blk_mask) for i in range(block_count)])


def bits(count):
    return [1 << i for i in range(count.bit_length() - 1)]


def route(subset, total, light):
    members = [i for i in range(total) if subset >> i & 1]
    if light and len(members) > 1 and members[-1] == total - 1:
        members = members[:-1]
        return members if len(members) == total - 1 else members[:1]
    if len(members) >= 2 and len(members) == total - light:
        return members
    if not light and len(members) == 2 and members[1] - members[0] != 1:
        return members[1:]
    return members[:1]


def hops(total, light):
    size = lambda t: bin(t).count("1")
    last = 1 << (total - 1)
    subsets = range(1, 1 << total)
    if not light:
        return [[t for t in subsets if size(t) == n] for n in range(1, total + 1)]
    result = [[t for t in subsets if size(t) == 1]]
    for high in (0, last):
        for n in range(2, total + 1):
            result.append([t for t in subsets if size(t) == n and t & last == high])
    return [hop for hop in result if hop]


def shares(row_total, parts):
    unit = row_total // 16
    cuts = [unit * i // parts * 16 for i in range(parts + 1)]
    cuts[-1] = row_total
    return list(zip(cuts[:-1], cuts[1:]))


def gather_hop(parts, axes, light, subsets, before=()):
    rows = parts[0][0].shape[0]
    came = {}
    for subset in subsets:
        ways = route(subset, len(axes), light)
        cuts = shares(rows, len(ways)) if len(ways) > 1 else [(0, rows)]
        came[subset] = []
        for way, (low, high) in zip(ways, cuts):
            source = parts[subset ^ (1 << way)][0]
            came[subset].append(swap(tie(source[low:high] if len(ways) > 1 else source, *before), axes[way]))
    return came


def gather_rows(value, axes, light=False, parts=None):
    last = 1 << (len(axes) - 1)
    parts, before = parts or {0: [value]}, ()
    for subsets in hops(len(axes), light):
        if subsets[0] in parts:
            continue
        if light and last in parts:
            before = [x for x in before if x is not parts[last][0]]
            before += parts[last] * any(t & last for t in subsets)
        came = gather_hop(parts, axes, light, subsets, before)
        parts = parts | came
        before = [part for pieces in came.values() for part in pieces]
    return parts


def join_kernel(plan, *refs):
    step = pl.program_id(0)
    out = refs[-1]
    for at, (slot, first, rows) in enumerate(plan):

        @pl.when(step == slot)
        def _():
            out[first : first + rows, :] = refs[at][...]


def join_rows(parts):
    plan, arrays = [], []
    for slot in sorted(parts):
        first = 0
        for array in parts[slot]:
            plan.append((slot, first, array.shape[0]))
            arrays.append(array)
            first += array.shape[0]
    rows, columns = parts[0][0].shape
    return pl.pallas_call(
        functools.partial(join_kernel, plan),
        grid=(len(parts),),
        in_specs=[pl.BlockSpec(a.shape, lambda m: (0, 0), pipeline_mode=pl.Buffered(1)) for a in arrays],
        out_specs=pl.BlockSpec((rows, columns), lambda m: (m, 0)),
        out_shape=jax.ShapeDtypeStruct((len(parts) * rows, columns), arrays[0].dtype),
        compiler_params=pltpu.CompilerParams(vmem_limit_bytes=32 * 1024 * 1024),
        cost_estimate=pl.CostEstimate(flops=0, bytes_accessed=4 * len(parts) * rows * columns, transcendentals=0),
        name="join_rows",
    )(*arrays)


def two_products_kernel(a_ref, u_ref, b_ref, v_ref, out_ref):
    nt = (((1,), (1,)), ((), ()))
    total = lax.dot_general(a_ref[...], u_ref[...], nt, preferred_element_type=f32)
    total += lax.dot_general(b_ref[...], v_ref[...], nt, preferred_element_type=f32)
    out_ref[...] = total.astype(out_ref.dtype)


def two_products(a, u, b, v):
    rows, depth = a.shape
    columns = u.shape[0]
    step = 256
    resident = pl.BlockSpec((rows, depth), lambda n: (0, 0), pipeline_mode=pl.Buffered(1))
    return pl.pallas_call(
        two_products_kernel,
        grid=(columns // step,),
        in_specs=[resident, pl.BlockSpec((step, depth), lambda n: (n, 0))] * 2,
        out_specs=pl.BlockSpec((rows, step), lambda n: (0, n)),
        out_shape=jax.ShapeDtypeStruct((rows, columns), bf16),
        compiler_params=pltpu.CompilerParams(vmem_limit_bytes=40 * 1024 * 1024),
        cost_estimate=pl.CostEstimate(
            flops=4 * rows * columns * depth,
            bytes_accessed=4 * (rows * depth + columns * depth) + 2 * rows * columns,
            transcendentals=0,
        ),
        name="two_products",
    )(a, u, b, v)


def joined(left, right):
    return (left.astype(f32) + right.astype(f32)).astype(bf16)


def scatter_plan(total, light):
    plan = [list(hop) for hop in hops(total, light)[::-1]]
    last = 1 << (total - 1)
    if light:
        plan[-1].remove(last)
        plan[next(i for i, hop in enumerate(plan) if not any(t & last for t in hop))].append(last)
    return plan


def scatter_hop(pieces, axes, light, subsets, before=(), beside=None):
    last = 1 << (len(axes) - 1)
    pieces = dict(pieces)
    rows = pieces[0][0].shape[0]
    sent, result = [], None
    for subset in subsets:
        (piece,) = pieces.pop(subset)
        ways = route(subset, len(axes), light)
        cuts = shares(rows, len(ways)) if len(ways) > 1 else [(0, rows)]
        for way, (low, high) in zip(ways, cuts):
            part = piece if len(ways) == 1 else piece[low:high]
            sent.append((subset, subset ^ (1 << way), low, high, swap(tie(part, *before), axes[way])))
    if beside:
        result, came = beside([item[4] for item in sent])
        sent = [item[:4] + (moved,) for item, moved in zip(sent, came)]
    for subset, target, low, high, moved in sent:
        if target == 0:
            pieces[0] = pieces[0] + [moved]
        elif high - low == rows:
            pieces[target] = [joined(pieces[target][0], moved)]
        else:
            old = pieces[target][0]
            cut = [old[:low], joined(old[low:high], moved), old[high:]]
            pieces[target] = [jnp.concatenate([c for c in cut if c.shape[0]], 0)]
    came = [item[4] for item in sent if not (light and item[0] == last)]
    return pieces, came, result


def scatter_rows(pieces, axes, light=False):
    pieces, came = {t: [piece] for t, piece in enumerate(pieces)}, ()
    for subsets in scatter_plan(len(axes), light):
        pieces, came, _ = scatter_hop(pieces, axes, light, subsets, came)
    return pieces[0]


def tie(value, *after):
    return lax.optimization_barrier((value, *after))[0] if after else value


def tie_all(held, *after):
    return {mask: tie(block, *after) for mask, block in held.items()}


def scale_kernel(count, index_ref, *refs):
    step = pl.program_id(0)
    for at in range(count):

        @pl.when(step == at)
        def _():
            refs[count][...] = refs[at][...]


def place_scales(held, rows, block_index):
    count = len(held)
    shape = (16, held[0].shape[1])
    return pl.pallas_call(
        functools.partial(scale_kernel, count),
        grid_spec=pltpu.PrefetchScalarGridSpec(
            num_scalar_prefetch=1,
            grid=(count,),
            in_specs=[pl.BlockSpec(shape, lambda m, b: (rows // 16, 0), pipeline_mode=pl.Buffered(1))] * count,
            out_specs=pl.BlockSpec(shape, lambda m, b: (b[0] ^ m, 0)),
        ),
        out_shape=jax.ShapeDtypeStruct((count * 16, shape[1]), bf16),
        cost_estimate=pl.CostEstimate(flops=0, bytes_accessed=4 * count * 16 * shape[1], transcendentals=0),
        name="place_scales",
    )(block_index[None].astype(jnp.int32), *[held[mask] for mask in range(count)])


def placed_kernel(body, plans, counts, steps, index_ref, *refs):
    refs = list(refs)
    arrays, inputs, outs, wholes, weights = [[refs.pop(0) for _ in range(count)] for count in counts]
    in_sems, out_sems = refs
    step = pl.program_id(0)
    came, at = [], 0
    for weight, plan in zip(weights, plans):
        copies = []
        rows = weight.shape[0] // len(plan)
        for mask, (source, column) in enumerate(plan):
            row = pl.multiple_of((index_ref[0] ^ mask) * rows, 16)
            block = arrays[source].at[pl.ds(0, rows)]
            if arrays[source].shape[1] != weight.shape[1]:
                block = arrays[source].at[pl.ds(0, rows), pl.ds(column, weight.shape[1])]
            copies.append(pltpu.make_async_copy(block, weight.at[pl.ds(row, rows)], in_sems.at[at]))
            at += 1
        came.append(copies)
    gone = [
        pltpu.make_async_copy(weight, whole, out_sems.at[n]) for n, (weight, whole) in enumerate(zip(weights, wholes))
    ]

    @pl.when(step == 0)
    def _():
        for copies in came:
            for copy in copies:
                copy.start()
        for copies, copy_out in zip(came, gone):
            for copy in copies:
                copy.wait()
            copy_out.start()

    body(step, inputs, outs, weights)

    @pl.when(step == steps - 1)
    def _():
        for copy_out in gone:
            copy_out.wait()


def placed(body, steps, held, columns, inputs, in_specs, outs, out_specs, block_index, name, flops):
    arrays, plans = [], []
    for blocks, width in zip(held, columns):
        plan = []
        for mask in range(len(blocks)):
            array, column = blocks[mask]
            if width % 128 or column % 128:
                array, column = array[:, column : column + width], 0
            where = next((n for n, known in enumerate(arrays) if known is array), len(arrays))
            if where == len(arrays):
                arrays.append(array)
            plan.append((where, column))
        plans.append(plan)
    rows = min(array.shape[0] for array in arrays) // 16 * 16
    rows = rows - (16 if name == "key_rows" else 0)
    shapes = [(len(plan) * rows, width) for plan, width in zip(plans, columns)]
    anywhere = pl.BlockSpec(memory_space=pl.ANY)
    counts = (len(arrays), len(inputs), len(outs), len(plans), len(plans))
    return pl.pallas_call(
        functools.partial(placed_kernel, body, plans, counts, steps),
        grid_spec=pltpu.PrefetchScalarGridSpec(
            num_scalar_prefetch=1,
            grid=(steps,),
            in_specs=[anywhere] * len(arrays) + in_specs,
            out_specs=out_specs + [anywhere] * len(plans),
            scratch_shapes=[pltpu.VMEM(shape, bf16) for shape in shapes]
            + [
                pltpu.SemaphoreType.DMA((sum(len(plan) for plan in plans),)),
                pltpu.SemaphoreType.DMA((len(plans),)),
            ],
        ),
        out_shape=outs + [jax.ShapeDtypeStruct(shape, bf16) for shape in shapes],
        compiler_params=pltpu.CompilerParams(vmem_limit_bytes=56 * 1024 * 1024),
        cost_estimate=pl.CostEstimate(
            flops=flops, bytes_accessed=4 * sum(h * w for h, w in shapes), transcendentals=0
        ),
        name=name,
    )(block_index[None].astype(jnp.int32), *arrays, *inputs)


def in_turn(held):
    came = []
    for block in held.values():
        came.append(swap(tie(block, *came[-2:-1]), (1, 0)))
    return dict(zip(held, came))


def both_cores(held):
    return held | {mask ^ 1: swap(block, (1, 0)) for mask, block in held.items()}


def pick(value, dim, index):
    return lax.dynamic_index_in_dim(value, index, dim, keepdims=False)


def plus(left, right):
    return left.astype(f32) + right.astype(f32)


def whole_call(body, outs, *inputs, name):
    size = sum(x.size * x.dtype.itemsize for x in inputs)
    return pl.pallas_call(
        body,
        out_shape=[jax.ShapeDtypeStruct(shape, dtype) for shape, dtype in outs],
        compiler_params=pltpu.CompilerParams(vmem_limit_bytes=40 * 1024 * 1024),
        cost_estimate=pl.CostEstimate(flops=0, bytes_accessed=2 * size, transcendentals=0),
        name=name,
    )(*inputs)


def summed(refs):
    total = refs[0][...].astype(f32)
    for ref in refs[1:]:
        total = total + ref[...].astype(f32)
    return total


def norm_full_kernel(count, *refs):
    parts, (scale, normed, inverse) = refs[:count], refs[count:]
    first = 0
    for part in parts:
        value = part[...].astype(f32)
        here = slice(first, first + part.shape[0])
        first += part.shape[0]
        factor = inverse_rms(value)
        inverse[here, :] = factor
        normed[here, :] = (value * factor * scale[0:1, :]).astype(bf16)


def after_attention_kernel(count, *refs):
    terms, (hidden, scales, attn_out, resid_out, ffn_in) = refs[:count], refs[count:]
    attn = summed(terms)
    attn_out[...] = attn
    resid = hidden[...].astype(f32) + attn * inverse_rms(attn) * scales[1:2, :]
    resid_out[...] = resid
    ffn_in[...] = (resid * inverse_rms(resid) * scales[2:3, :]).astype(bf16)


def after_ffn_kernel(count, *refs):
    terms, (resid, out_grad, scales, layer_out, grad_out, grad_scale) = refs[:count], refs[count:]
    ffn_out = summed(terms)
    grad, grad_scale[...] = rms_back(ffn_out, scales[3:4, :], out_grad[...].astype(f32))
    grad_out[...] = grad.astype(bf16)
    layer_out[...] = (resid[...] + ffn_out * inverse_rms(ffn_out) * scales[3:4, :]).astype(bf16)


def after_ffn_back_kernel(count, *refs):
    terms, (resid, attn, out_grad, scales, grad_resid, grad_attn, grad_scale2, grad_scale1) = refs[:count], refs[count:]
    grad, grad_scale2[...] = rms_back(resid[...], scales[2:3, :], summed(terms))
    grad = out_grad[...].astype(f32) + grad
    grad_resid[...] = grad
    back, grad_scale1[...] = rms_back(attn[...], scales[1:2, :], grad)
    grad_attn[...] = back.astype(bf16)


def after_all_kernel(count, *refs):
    terms, (hidden, grad_resid, scales, grad_in) = refs[:count], refs[count:]
    grad, _ = rms_back(hidden[...].astype(f32), scales[0:1, :], summed(terms))
    grad_in[...] = grad_resid[...] + grad


def key_value_grad_kernel(kept, came, cosine, sine, out):
    total = kept[...].astype(f32) + came[...].astype(f32)
    out[:, :HD] = rotated(total[:, :HD], cosine[...], sine[...], -1.0).astype(bf16)
    out[:, HD:] = total[:, HD:].astype(bf16)


def project(rows, held, columns, table, turning, block_index, name):
    count, depth = rows.shape
    heads = columns[0] // HD
    fixed = lambda n, b: (0, 0)
    once = pl.Buffered(1)

    def body(step, inputs, outs, weights):
        rows_ref, cosine_ref, sine_ref = inputs
        (out_ref,) = outs
        here = pl.ds(pl.multiple_of(step * HD, HD), HD)
        value = jnp.dot(rows_ref[...], weights[0][:, here], preferred_element_type=f32)

        @pl.when(step < turning)
        def _():
            out_ref[...] = rotated(value, cosine_ref[...], sine_ref[...], 1.0).astype(bf16)

        @pl.when(step >= turning)
        def _():
            out_ref[...] = value.astype(bf16)

    return placed(
        body,
        heads,
        held,
        columns,
        [rows, *table],
        [
            pl.BlockSpec((count, depth), fixed, pipeline_mode=once),
            pl.BlockSpec((count, HD), fixed, pipeline_mode=once),
            pl.BlockSpec((count, HD), fixed, pipeline_mode=once),
        ],
        [jax.ShapeDtypeStruct((count, columns[0]), bf16)],
        [pl.BlockSpec((count, HD), lambda n, b: (0, n))],
        block_index,
        name,
        2 * rows.size * columns[0],
    )


def hidden_units(rows, held, width, block_index):
    count, depth = rows.shape
    step = 256

    def body(number, inputs, outs, weights):
        hidden_ref, active_ref, slope_ref = outs
        gate = jnp.dot(inputs[0][...], weights[0][...], preferred_element_type=f32)
        up = jnp.dot(inputs[0][...], weights[1][...], preferred_element_type=f32)
        inner = math.sqrt(2.0 / math.pi)
        square = gate * gate
        tangent = jnp.tanh(inner * gate * (1.0 + 0.044715 * square))
        share = 0.5 * (1.0 + tangent)
        active = gate * share
        slope = share + (0.5 * inner) * gate * (1.0 - tangent * tangent) * (1.0 + (3 * 0.044715) * square)
        hidden_ref[...] = (active * up).astype(bf16)
        active_ref[...] = active
        slope_ref[...] = slope * up

    return placed(
        body,
        count // step,
        held,
        [width, width],
        [rows],
        [pl.BlockSpec((step, depth), lambda n, b: (n, 0))],
        [jax.ShapeDtypeStruct((count, width), dtype) for dtype in (bf16, f32, f32)],
        [pl.BlockSpec((step, width), lambda n, b: (n, 0))] * 3,
        block_index,
        "hidden_units",
        4 * rows.size * width,
    )


def down_rows(hidden, held, block_index):
    count, width = hidden.shape
    depth = len(held) * held[0][0].shape[0]
    step = 768 if depth % 768 == 0 else 256

    def body(number, inputs, outs, weights):
        here = pl.ds(pl.multiple_of(number * step, step), step)
        value = lax.dot_general(
            inputs[0][...], weights[0][here, :], (((1,), (1,)), ((), ())), preferred_element_type=f32
        )
        outs[0][...] = value.astype(bf16)

    return placed(
        body,
        depth // step,
        [held],
        [width],
        [hidden],
        [pl.BlockSpec((count, width), lambda n, b: (0, 0), pipeline_mode=pl.Buffered(1))],
        [jax.ShapeDtypeStruct((count, depth), bf16)],
        [pl.BlockSpec((count, step), lambda n, b: (0, n))],
        block_index,
        "down_rows",
        2 * hidden.size * depth,
    )


def outer_kernel(*refs):
    pairs, out = refs[:-1], refs[-1]
    width = 0
    for left, right in zip(pairs[::2], pairs[1::2]):
        columns = right.shape[1]
        value = lax.dot_general(left[...], right[...], (((0,), (0,)), ((), ())), preferred_element_type=f32)
        out[:, width : width + columns] = value.astype(bf16)
        width += columns


def outer(*pairs):
    rows, depth = pairs[0][0].shape
    width = sum(right.shape[1] for _, right in pairs)
    step = depth // 2
    specs = []
    for _, right in pairs:
        specs.append(pl.BlockSpec((rows, step), lambda n: (0, n)))
        specs.append(pl.BlockSpec(right.shape, lambda n: (0, 0), pipeline_mode=pl.Buffered(1)))
    return pl.pallas_call(
        outer_kernel,
        grid=(depth // step,),
        in_specs=specs,
        out_specs=pl.BlockSpec((step, width), lambda n: (n, 0)),
        out_shape=jax.ShapeDtypeStruct((depth, width), bf16),
        compiler_params=pltpu.CompilerParams(vmem_limit_bytes=40 * 1024 * 1024),
        cost_estimate=pl.CostEstimate(
            flops=2 * rows * depth * width, bytes_accessed=2 * (rows * depth * len(pairs) + depth * width), transcendentals=0
        ),
        name="outer",
    )(*[x for pair in pairs for x in pair])


def normed_back_kernel(count, q_ref, wq_ref, kv_ref, wkv_ref, inverse_ref, *refs):
    hidden, (out_ref, scale_ref) = refs[:count], refs[count:]
    nt = (((1,), (1,)), ((), ()))
    total = lax.dot_general(q_ref[...], wq_ref[...], nt, preferred_element_type=f32)
    total += lax.dot_general(kv_ref[...], wkv_ref[...], nt, preferred_element_type=f32)
    out_ref[...] = total.astype(bf16)
    grad_scale, first = jnp.zeros((1, total.shape[1]), f32), 0
    for part in hidden:
        here = slice(first, first + part.shape[0])
        first += part.shape[0]
        unit = part[...].astype(f32) * inverse_ref[here, :]
        grad_scale += jnp.sum(total[here, :] * unit, axis=0, keepdims=True)
    scale_ref[...] = grad_scale


def normed_back(grad_query, query_weight, grad_kv, kv_weight, inverse, hidden):
    rows, width = grad_query.shape
    kv_width = grad_kv.shape[1]
    columns = query_weight.shape[0]
    step = 768 if columns % 768 == 0 else 256
    fixed = lambda n: (0, 0)
    once = pl.Buffered(1)
    return pl.pallas_call(
        functools.partial(normed_back_kernel, len(hidden)),
        grid=(columns // step,),
        in_specs=[
            pl.BlockSpec((rows, width), fixed, pipeline_mode=once),
            pl.BlockSpec((step, width), lambda n: (n, 0)),
            pl.BlockSpec((rows, kv_width), fixed, pipeline_mode=once),
            pl.BlockSpec((step, kv_width), lambda n: (n, 0)),
            pl.BlockSpec((rows, 1), fixed, pipeline_mode=once),
        ]
        + [pl.BlockSpec((part.shape[0], step), lambda n: (0, n)) for part in hidden],
        out_specs=[pl.BlockSpec((rows, step), lambda n: (0, n)), pl.BlockSpec((1, step), lambda n: (0, n))],
        out_shape=[jax.ShapeDtypeStruct((rows, columns), bf16), jax.ShapeDtypeStruct((1, columns), f32)],
        compiler_params=pltpu.CompilerParams(vmem_limit_bytes=40 * 1024 * 1024),
        cost_estimate=pl.CostEstimate(
            flops=2 * rows * columns * (width + kv_width), bytes_accessed=4 * rows * columns, transcendentals=0
        ),
        name="normed_back",
    )(grad_query, query_weight, grad_kv, kv_weight, inverse, *hidden)


def scores(query, key, score_scale):
    raw = lax.dot_general(query, key, (((1,), (1,)), ((), ())), preferred_element_type=f32)
    return jnp.tanh(raw * (score_scale / cap_value))


def load_pieces(step, pieces, kv_all, sems):
    copies = [pltpu.make_async_copy(piece, kv_all.at[at], sems.at[at]) for at, piece in enumerate(pieces)]

    @pl.when(step == 0)
    def _():
        for copy in copies:
            copy.start()

    for at, copy in enumerate(copies):

        @pl.when(step == 2 * at)
        def _():
            copy.wait()


def forward_kernel(group, span_len, tiles, spans_ref, q_ref, *refs):
    pieces, (mixed_ref, exact_ref, lse_ref, q_all, acc, total, kv_all, sems) = refs[: tiles // 2], refs[tiles // 2 :]
    step = pl.program_id(0)
    load_pieces(step, pieces, kv_all, sems)
    score_scale = 1.0 / math.sqrt(HD)
    rows = group * span_len

    @pl.when(step == 0)
    def _():
        for half in range(2):
            for g in range(group):
                q_all[half, g * span_len : (g + 1) * span_len, :] = q_ref[
                    half * span_len : (half + 1) * span_len, g * HD : (g + 1) * HD
                ]
        acc[...] = jnp.zeros_like(acc)
        total[...] = jnp.zeros_like(total)

    tile_span = spans_ref[step]
    here = pl.ds(pl.multiple_of((step % 2) * span_len, span_len), span_len)
    key = kv_all[step // 2, here, :HD]
    value = kv_all[step // 2, here, HD:]

    def visit(half, diagonal):
        weights = jnp.exp(cap_value * scores(q_all[half], key, score_scale))
        if diagonal:
            flip = spans_ref[tiles + 2]
            shape = (rows, span_len)
            q_pos = (lax.broadcasted_iota(jnp.int32, shape, 0) % span_len) ^ flip
            k_pos = lax.broadcasted_iota(jnp.int32, shape, 1) ^ flip
            weights = jnp.where(k_pos <= q_pos, weights, 0.0)
        part = weights[:, :128]
        for at in range(128, span_len, 128):
            part = part + weights[:, at : at + 128]
        total[half] += part
        acc[half] += jnp.dot(weights.astype(bf16), value, preferred_element_type=f32)

    for half in range(2):
        own = spans_ref[tiles + half]

        @pl.when(tile_span < own)
        def _():
            visit(half, False)

        @pl.when(tile_span == own)
        def _():
            visit(half, True)

    @pl.when(step == tiles - 1)
    def _():
        for half in range(2):
            sums = jnp.sum(total[half], axis=1, keepdims=True)
            exact = acc[half] / sums
            lse_ref[half] = jnp.log(jnp.sum(total[half].T, axis=0, keepdims=True))
            for g in range(group):
                piece = exact[g * span_len : (g + 1) * span_len]
                place = (slice(half * span_len, (half + 1) * span_len), slice(g * HD, (g + 1) * HD))
                exact_ref[place] = piece
                mixed_ref[place] = piece.astype(bf16)


def backward_kernel(group, span_len, tiles, spans_ref, q_ref, g_ref, exact_ref, lse_ref, cosine_ref, sine_ref, *refs):
    pieces, rest = refs[: tiles // 2], refs[tiles // 2 :]
    dq_ref, near_ref, far_ref, q_all, g_all, delta, dq_acc, kv_all, sems = rest
    step = pl.program_id(0)
    load_pieces(step, pieces, kv_all, sems)
    score_scale = 1.0 / math.sqrt(HD)
    rows = group * span_len

    @pl.when(step == 0)
    def _():
        for half in range(2):
            for g in range(group):
                place = (slice(half * span_len, (half + 1) * span_len), slice(g * HD, (g + 1) * HD))
                here = slice(g * span_len, (g + 1) * span_len)
                q_all[half, here, :] = q_ref[place]
                g_all[half, here, :] = g_ref[place]
                product = g_ref[place].astype(f32) * exact_ref[place]
                folded = product[:, :128] + product[:, 128:]
                delta[half, :, here] = jnp.sum(folded.T, axis=0, keepdims=True)
        dq_acc[...] = jnp.zeros_like(dq_acc)

    tile_span = spans_ref[step]
    here = pl.ds(pl.multiple_of((step % 2) * span_len, span_len), span_len)
    key = kv_all[step // 2, here, :HD]
    value = kv_all[step // 2, here, HD:]

    def visit(half, diagonal):
        query = q_all[half]
        grad = g_all[half]
        tangent = scores(key, query, score_scale)
        probability = jnp.exp(cap_value * tangent - lse_ref[half])
        if diagonal:
            flip = spans_ref[tiles + 2]
            shape = (span_len, rows)
            q_pos = (lax.broadcasted_iota(jnp.int32, shape, 1) % span_len) ^ flip
            k_pos = lax.broadcasted_iota(jnp.int32, shape, 0) ^ flip
            probability = jnp.where(k_pos <= q_pos, probability, 0.0)
        grad_prob = lax.dot_general(value, grad, (((1,), (1,)), ((), ())), preferred_element_type=f32)
        grad_raw = probability * (grad_prob - delta[half]) * ((1.0 - tangent * tangent) * score_scale)
        grad_raw = grad_raw.astype(bf16)
        dv = jnp.dot(probability.astype(bf16), grad, preferred_element_type=f32)
        dk = jnp.dot(grad_raw, query, preferred_element_type=f32)
        dq_acc[half] += lax.dot_general(grad_raw, key, (((0,), (0,)), ((), ())), preferred_element_type=f32)
        return dk, dv

    def put(dk, dv):
        @pl.when(step < tiles // 2)
        def _():
            near_ref[:, :HD] = dk.astype(bf16)
            near_ref[:, HD:] = dv.astype(bf16)

        @pl.when(step >= tiles // 2)
        def _():
            far_ref[:, :HD] = dk.astype(bf16)
            far_ref[:, HD:] = dv.astype(bf16)

    low, high = spans_ref[tiles], spans_ref[tiles + 1]
    first, second = tile_span <= low, tile_span <= high

    @pl.when(jnp.logical_not(jnp.logical_or(first, second)))
    def _():
        put(jnp.zeros((span_len, HD), f32), jnp.zeros((span_len, HD), f32))

    for half, own, other in ((0, low, high), (1, high, low)):
        for diagonal in (False, True):
            here = tile_span == own if diagonal else tile_span < own

            @pl.when(jnp.logical_and(here, tile_span > other))
            def _(half=half, diagonal=diagonal):
                put(*visit(half, diagonal))

    for half, own, other in ((0, low, high), (1, high, low)):
        for diagonal in (False, True):
            here = tile_span == own if diagonal else tile_span < own

            @pl.when(jnp.logical_and(here, own < other))
            def _(half=half, diagonal=diagonal):
                dk_low, dv_low = visit(half, diagonal)
                dk_high, dv_high = visit(1 - half, False)
                put(dk_low + dk_high, dv_low + dv_high)

    @pl.when(step == tiles - 1)
    def _():
        for half in range(2):
            for g in range(group):
                here = slice(half * span_len, (half + 1) * span_len)
                turned = rotated(
                    dq_acc[half, g * span_len : (g + 1) * span_len], cosine_ref[here, :], sine_ref[here, :], -1.0
                )
                dq_ref[here, g * HD : (g + 1) * HD] = turned.astype(bf16)


def attention_forward(spans, queries, pieces, span_len):
    tiles = 2 * len(pieces)
    kv_size = len(pieces) * pieces[0].size
    width = queries.shape[1]
    group = width // HD
    rows = group * span_len
    whole = lambda s, t: (0, 0)
    visits = tiles + 1
    return pl.pallas_call(
        functools.partial(forward_kernel, group, span_len, tiles),
        grid_spec=pltpu.PrefetchScalarGridSpec(
            num_scalar_prefetch=1,
            grid=(tiles,),
            in_specs=[
                pl.BlockSpec(queries.shape, whole),
            ]
            + [pl.BlockSpec(memory_space=pl.ANY)] * len(pieces),
            out_specs=[
                pl.BlockSpec(queries.shape, whole),
                pl.BlockSpec(queries.shape, whole),
                pl.BlockSpec((2, 1, rows), lambda s, t: (0, 0, 0)),
            ],
            scratch_shapes=[
                pltpu.VMEM((2, rows, HD), bf16),
                pltpu.VMEM((2, rows, HD), f32),
                pltpu.VMEM((2, rows, 128), f32),
                pltpu.VMEM((len(pieces),) + pieces[0].shape, bf16),
                pltpu.SemaphoreType.DMA((len(pieces),)),
            ],
        ),
        out_shape=[
            jax.ShapeDtypeStruct(queries.shape, bf16),
            jax.ShapeDtypeStruct(queries.shape, f32),
            jax.ShapeDtypeStruct((2, 1, rows), f32),
        ],
        compiler_params=pltpu.CompilerParams(vmem_limit_bytes=40 * 1024 * 1024),
        cost_estimate=pl.CostEstimate(
            flops=visits * rows * span_len * HD * 4,
            bytes_accessed=kv_size * 2 + queries.size * 12,
            transcendentals=visits * rows * span_len * 2,
        ),
        name="attention_forward",
    )(spans, queries, *pieces)


def attention_backward(spans, queries, grads, exact, lse, table, pieces, span_len):
    tiles = 2 * len(pieces)
    kv_size = len(pieces) * pieces[0].size
    width = queries.shape[1]
    group = width // HD
    rows = group * span_len
    whole = lambda s, t: (0, 0)
    visits = tiles + 1
    return pl.pallas_call(
        functools.partial(backward_kernel, group, span_len, tiles),
        grid_spec=pltpu.PrefetchScalarGridSpec(
            num_scalar_prefetch=1,
            grid=(tiles,),
            in_specs=[
                pl.BlockSpec(queries.shape, whole),
                pl.BlockSpec(queries.shape, whole),
                pl.BlockSpec(queries.shape, whole),
                pl.BlockSpec((2, 1, rows), lambda s, t: (0, 0, 0)),
                pl.BlockSpec(table[0].shape, whole),
                pl.BlockSpec(table[0].shape, whole),
            ]
            + [pl.BlockSpec(memory_space=pl.ANY)] * len(pieces),
            out_specs=[
                pl.BlockSpec(queries.shape, whole),
                pl.BlockSpec((span_len, 2 * HD), lambda s, t: (jnp.minimum(s, tiles // 2 - 1), 0)),
                pl.BlockSpec((span_len, 2 * HD), lambda s, t: (jnp.maximum(s - tiles // 2, 0), 0)),
            ],
            scratch_shapes=[
                pltpu.VMEM((2, rows, HD), bf16),
                pltpu.VMEM((2, rows, HD), bf16),
                pltpu.VMEM((2, 1, rows), f32),
                pltpu.VMEM((2, rows, HD), f32),
                pltpu.VMEM((len(pieces),) + pieces[0].shape, bf16),
                pltpu.SemaphoreType.DMA((len(pieces),)),
            ],
        ),
        out_shape=[
            jax.ShapeDtypeStruct(queries.shape, bf16),
            jax.ShapeDtypeStruct((tiles * span_len // 2, 2 * HD), bf16),
            jax.ShapeDtypeStruct((tiles * span_len // 2, 2 * HD), bf16),
        ],
        compiler_params=pltpu.CompilerParams(vmem_limit_bytes=40 * 1024 * 1024),
        cost_estimate=pl.CostEstimate(
            flops=visits * rows * span_len * HD * 10,
            bytes_accessed=kv_size * 4 + queries.size * 16,
            transcendentals=visits * rows * span_len * 2,
        ),
        name="attention_backward",
    )(spans, queries, grads, exact, lse, *table, *pieces)


def product(left, right, left_dim, right_dim, out=f32):
    result = lax.dot_general(left, right, (((left_dim,), (right_dim,)), ((), ())), preferred_element_type=f32)
    return result.astype(out)


def on_device(
    hidden_in,
    out_grad,
    span_order,
    w_query,
    w_key,
    w_value,
    w_output,
    w_gate,
    w_up,
    w_down,
    norm_scales,
):
    local_rows = hidden_in.shape[0]
    head_count = lax.axis_size("head")
    block_count = lax.axis_size("blk")
    block_index = lax.axis_index("blk")
    head_index = lax.axis_index("head")
    group_rows = local_rows * head_count
    span_len = group_rows // 2
    model_rows, query_width = w_query.shape
    model_width = hidden_in.shape[1]
    query_heads = query_width // HD
    half_units = w_gate.shape[1] // 2

    chip_masks = bits(block_count)[1:]
    pair, top = chip_masks[0], chip_masks[-1]
    far_masks = chip_masks[:0:-1]
    head_axes = [(0, mask) for mask in bits(head_count)]
    unit_axes = head_axes + [(pair, 0)]
    unit_side = (block_index // pair) % 2
    bit_count = len(chip_masks) + 1

    def side(mask):
        return (block_index // mask) % 2

    def send(value, mask, *after):
        return swap(tie(value, *after), (mask, 0))

    def segment(body, inputs, after=(), flying=()):
        inputs, after = lax.optimization_barrier((tuple(inputs), after))
        shapes = jax.eval_shape(body, *inputs)

        def nothing(*_):
            return jax.tree.map(lambda x: jnp.zeros(x.shape, x.dtype), shapes)

        results = lax.cond(span_order[0] >= 0, body, nothing, *inputs)
        return lax.optimization_barrier((results, flying))

    def far_spread(value, *after):
        held = {0: value}
        for mask in far_masks:
            for have in list(held):
                held[have ^ mask] = send(held[have], mask, *after)
        return held

    def near_spread(held, *after):
        return held | {have ^ pair: send(block, pair, *(after if have == 0 else ())) for have, block in held.items()}

    def split_dims(partial):
        return partial.reshape((2,) * bit_count + (-1, partial.shape[-1]))

    def halve(value, dim, mask, *after):
        moved = send(pick(value, dim, 1 - side(mask)), mask, *after)
        return plus(pick(value, dim, side(mask)), moved)

    slot = jnp.arange(head_count, dtype=jnp.int32) ^ head_index
    in_block = (slot[:, None] * local_rows + jnp.arange(local_rows, dtype=jnp.int32)[None, :]).reshape(-1)
    head_side = head_index // (head_count // 2)
    own_spans = jnp.stack([span_order[2 * block_index + head_side], span_order[2 * block_index + 1 - head_side]])
    row_spans = jnp.repeat(own_spans, span_len)
    position = row_spans * span_len + in_block % span_len
    even_masks = [0]
    for mask in chip_masks[::-1]:
        even_masks = even_masks + [have ^ mask for have in even_masks]
    slot_masks = even_masks + [mask ^ 1 for mask in even_masks]
    tile_blocks = jnp.array(slot_masks, jnp.int32) ^ block_index
    tile_slots = (2 * tile_blocks[:, None] + jnp.stack([head_side, 1 - head_side])[None, :]).reshape(-1)
    flip = (head_index % (head_count // 2)) * local_rows
    spans = jnp.concatenate([span_order[tile_slots], own_spans, flip[None]]).astype(jnp.int32)
    table = rotation(position)

    scale_count = norm_scales.shape[0]
    kv_at = head_index * query_heads // (H // KVH) * HD
    kv_local = jnp.concatenate(
        [
            lax.dynamic_slice_in_dim(w_key, kv_at, HD, 1),
            lax.dynamic_slice_in_dim(w_value, kv_at, HD, 1),
        ],
        1,
    )
    scale_local = jnp.pad(norm_scales, ((0, 16 - scale_count), (0, 2 * HD - model_rows)))
    kv_local = jnp.concatenate([kv_local, scale_local], 0)

    def half(local, index):
        return lax.dynamic_slice_in_dim(local, index * half_units, half_units, 1)

    def unit_slices():
        weights = (w_gate, w_up, w_down.T)
        return (
            half(w_gate, unit_side),
            jnp.concatenate([half(w, unit_side) for w in weights[1:]], 1),
            jnp.concatenate([half(w, 1 - unit_side) for w in weights[:2]], 1),
            half(weights[2], 1 - unit_side),
        )

    hidden_near = [swap(hidden_in, axis) for axis in head_axes]
    kv_chips = far_spread(kv_local)
    kv_chips.pop(0)
    kv_chips[pair] = send(kv_local, pair)
    (query_output_local, unit_local), (hidden_near, kv_chips) = segment(
        lambda w_query, w_output: (jnp.concatenate([w_query, w_output.T], 1), unit_slices()),
        (w_query, w_output),
        (table,),
        (hidden_near, kv_chips),
    )
    first_mine, second_mine, first_theirs, second_theirs = unit_local

    def first_rows(hidden_near, kv_chips):
        held = {0: kv_local} | kv_chips
        held |= {mask ^ pair: swap(block, (pair, 0)) for mask, block in kv_chips.items() if mask != pair}
        parts = {0: [hidden_in]} | {1 << at: [part] for at, part in enumerate(hidden_near)}
        for subset in range(1, head_count):
            if subset not in parts:
                ways = route(subset, len(head_axes), False)
                cuts = shares(local_rows, len(ways)) if len(ways) > 1 else [(0, local_rows)]
                parts[subset] = [
                    swap(parts[subset ^ (1 << way)][0][low:high], head_axes[way]) for way, (low, high) in zip(ways, cuts)
                ]
        def normed_keys(held, parts):
            came = ()
            for mask, block in list(held.items()):
                held[mask ^ 1] = swap(tie(block, *came), (1, 0))
                came = (held[mask ^ 1],)
            scale_blocks = place_scales(held, model_rows, block_index)
            scale_rows = scale_blocks.reshape(block_count, 16, 2 * HD)[:, :scale_count, :model_rows]
            scale_rows = scale_rows.transpose(1, 0, 2).reshape(scale_count, model_width).astype(f32)
            arrays = [part for slot in sorted(parts) for part in parts[slot]]
            normed_full, inverse_full = whole_call(
                functools.partial(norm_full_kernel, len(arrays)),
                [((group_rows, model_width), bf16), ((group_rows, 1), f32)],
                *arrays,
                scale_rows,
                name="norm_full",
            )
            kv_held = {mask: (block, 0) for mask, block in held.items()}
            kv_rows, kv_weight = project(normed_full, [kv_held], [2 * HD], table, 1, block_index, "key_rows")
            return kv_rows, kv_weight, scale_rows, normed_full, inverse_full

        held, parts = lax.optimization_barrier((held, parts))
        query_output = {mask: send(query_output_local, mask, held[pair ^ top]) for mask in (*far_masks, pair)}
        results, query_output = segment(normed_keys, (held, parts), (), query_output)
        return results, parts, query_output

    first_results, hidden_parts, query_output_chips = first_rows(hidden_near, kv_chips)
    kv_rows, kv_weight, scale_rows, normed_full, inverse_full = first_results
    hidden_slots = [part for slot in sorted(hidden_parts) for part in hidden_parts[slot]]
    row_shape = (local_rows, model_width)
    scale_shape = (1, model_width)

    if len(far_masks) > 1:
        query_output_chips = far_spread(query_output_local) | {pair: query_output_chips[pair]}
    query_output_chips[0] = query_output_local
    kv_far = far_spread(kv_rows)
    kv_far.pop(0)
    kv_near = send(kv_rows, pair)
    query_output_last = {
        mask ^ pair: send(block, pair, kv_rows) for mask, block in query_output_chips.items() if mask & ~pair
    }

    def beside_keys(kv_rows):
        cores, came = {}, ()
        for mask, block in ({-1: kv_rows} | query_output_chips).items():
            cores[mask] = swap(tie(block, *came), (1, 0))
            came = (cores[mask],)
        return cores

    cores, (kv_far, kv_near, query_output_last) = segment(
        beside_keys, (kv_rows,), (), (kv_far, kv_near, query_output_last)
    )

    def keys_and_queries(kv_far, kv_near, query_output_last):
        across = {mask ^ pair: swap(block, (pair, 0)) for mask, block in kv_far.items()}
        chips = query_output_chips | query_output_last
        held = query_output_last | {-1 - mask: piece for mask, piece in ({pair: kv_near} | kv_far | across).items()}
        came, others = (), dict(cores)
        for mask, block in held.items():
            others[mask] = swap(tie(block, *came), (1, 0))
            came = (others[mask],)
        pieces = {(-1 - mask) ^ 1: piece for mask, piece in others.items() if mask < 0}
        chips |= {mask ^ 1: block for mask, block in others.items() if mask >= 0}
        queries, query_weight, output_weight = project(
            normed_full,
            [{mask: (block, column) for mask, block in chips.items()} for column in (0, query_width)],
            [query_width, query_width],
            table,
            query_heads,
            block_index,
            "query_rows",
        )
        return across | pieces, query_weight, output_weight, queries

    first_near = far_spread(first_mine, kv_far[top])
    (kv_others, query_weight, output_weight, queries), first_near = segment(
        keys_and_queries, (kv_far, kv_near, query_output_last), (), first_near
    )
    kv_held = {0: kv_rows, pair: kv_near} | kv_far | kv_others
    kv_pieces = [kv_held[mask] for mask in slot_masks]

    def row_sum(partial, axes, light=False):
        shaped = partial.reshape(1 << len(axes), local_rows, model_width)
        return scatter_rows([shaped[i] for i in range(1 << len(axes))], axes, light)

    def attend(queries, first_near, second_mine):
        mixed, exact, lse = attention_forward(spans, queries, kv_pieces, span_len)
        cores = in_turn(first_near | {-1: second_mine})
        second_core = cores.pop(-1)
        first_core = {mask ^ 1: block for mask, block in cores.items()}
        mixed = tie(mixed, first_core, second_core)
        terms = row_sum(product(mixed, output_weight, 1, 1, bf16), head_axes)
        rows = whole_call(
            functools.partial(after_attention_kernel, len(terms)),
            [(row_shape, f32), (row_shape, f32), (row_shape, bf16)],
            *terms,
            hidden_in,
            scale_rows,
            name="after_attention",
        )
        return (mixed, exact, lse, *rows, first_core, second_core)

    second_near = far_spread(second_mine, queries)
    first_cross = send(first_theirs, pair, queries)
    (mixed, exact, lse, attn_out, resid, ffn_in, first_core, second_core), (second_near, first_cross) = segment(
        attend, (queries, first_near, second_mine), (), (second_near, first_cross)
    )
    second_far = {mask: block for mask, block in second_near.items() if mask}

    def join_units(ffn_in, first_cross, second_far):
        parts = {0: [ffn_in]}
        parts |= gather_hop(parts, unit_axes, True, hops(len(unit_axes), True)[0])

        def later_hops(parts):
            parts = gather_rows(None, unit_axes, True, parts)
            third = [part for t in parts if t.bit_count() > 1 and t != len(parts) - 1 for part in parts[t]]
            first_core = swap(tie(first_cross, *parts[len(parts) // 2]), (1, 0))
            second_cores = {
                mask ^ 1: swap(tie(block, *third, first_core), (1, 0)) for mask, block in second_far.items()
            }
            return join_rows(parts), first_core, second_cores

        second_cross = send(second_theirs, pair, parts)
        return segment(later_hops, (parts,), (), second_cross)

    first_across = far_spread(first_cross, ffn_in)
    ((ffn_full, cross_core, far_cores), second_cross), first_across = segment(
        join_units, (ffn_in, first_cross, second_far), (), first_across
    )
    second_held = second_near | {1: second_core} | far_cores

    def gate_and_up(ffn_full, first_across):
        cores = {1: cross_core} | {mask ^ 1: swap(block, (1, 0)) for mask, block in first_across.items() if mask}
        across = {mask ^ pair: block for mask, block in (first_across | cores).items()}
        gate_held = {mask: (block, 0) for mask, block in (first_near | first_core | across).items()}
        up_held = {mask: (block, 0) for mask, block in second_held.items()}
        up_held |= {mask: (block, half_units) for mask, block in across.items()}
        units = hidden_units(ffn_full, [gate_held, up_held], half_units, block_index)
        return units, swap(second_cross, (1, 0))

    second_across = far_spread(second_cross, ffn_full)
    ((hidden, active, slope, gate_weight, up_weight), second_cross_core), second_across = segment(
        gate_and_up, (ffn_full, first_across), (), second_across
    )
    down_held = {mask: (block, half_units) for mask, block in second_held.items()}
    down_held |= {mask ^ pair: (block, 0) for mask, block in second_across.items()}
    down_held |= {
        mask ^ pair ^ 1: (swap(block, (1, 0)) if mask else second_cross_core, 0)
        for mask, block in second_across.items()
    }
    ffn_part, down_weight = down_rows(hidden, down_held, block_index)
    ffn_terms = row_sum(ffn_part, unit_axes)
    layer_out, grad_ffn_out, scale_grad3 = whole_call(
        functools.partial(after_ffn_kernel, len(ffn_terms)),
        [(row_shape, bf16), (row_shape, bf16), (scale_shape, f32)],
        *ffn_terms,
        resid,
        out_grad,
        scale_rows,
        name="after_ffn",
    )

    def unit_core(partial):
        summed = halve(split_dims(partial), bit_count - 1, 1).astype(bf16)
        return pick(summed, 0, 1 - side(top)), pick(summed, 0, side(top))

    def unit_sides(kept, came):
        part = plus(kept, came).astype(bf16)
        for mask in far_masks[1:]:
            part = halve(part, 0, mask).astype(bf16)
        return pick(part, 0, 1 - unit_side), pick(part, 0, unit_side)

    def unit_whole(own, other):
        low = jnp.where(unit_side == 0, own, other)
        high = jnp.where(unit_side == 0, other, own)
        return jnp.concatenate([low, high], 1).astype(f32)

    def core_sum(partial):
        return halve(split_dims(partial), bit_count - 1, 1).astype(bf16)

    grad_ffn_full = join_rows(gather_rows(grad_ffn_out, unit_axes))
    grad_down = product(grad_ffn_full, hidden, 0, 0, bf16)
    grad_hidden = product(tie(grad_ffn_full, grad_down), down_weight, 1, 0)
    grad_gate_act = (grad_hidden * slope).astype(bf16)
    grad_up_act = (grad_hidden * active).astype(bf16)
    down_away, down_kept = unit_core(grad_down)
    down_came = send(down_away, top)

    def weight_back(act):
        return product(ffn_full, act, 0, 0, bf16)

    back_plan = scatter_plan(len(unit_axes), True)
    split_at = len(back_plan) - 2

    def beside_hops(bodies):
        results = []

        def beside(number):
            def run(moved):
                if number >= len(bodies):
                    return None, moved
                result, moved = segment(bodies[number], tuple(results[-1:]), (), moved)
                results.append(result)
                return result, moved

            return run

        return beside, results

    def ffn_back_first(grad_gate_act, grad_up_act):
        grad_ffn_part = two_products(grad_gate_act, gate_weight, grad_up_act, up_weight)
        shaped = grad_ffn_part.reshape(-1, local_rows, model_width)
        pieces, came = {t: [shaped[t]] for t in range(shaped.shape[0])}, ()
        beside, results = beside_hops([lambda: weight_back(tie(grad_gate_act, grad_ffn_part)), unit_core])
        for number, subsets in enumerate(back_plan[:split_at]):
            pieces, came, _ = scatter_hop(pieces, unit_axes, True, subsets, came, beside(number))
        return pieces, results[1]

    (ffn_pieces, (gate_away, gate_kept)), down_came = segment(
        ffn_back_first, (grad_gate_act, grad_up_act), (down_away, down_kept), down_came
    )

    def ffn_back_last(ffn_pieces, grad_up_act, down_came):
        pieces, came = ffn_pieces, ()
        beside, results = beside_hops(
            [lambda: weight_back(grad_up_act), lambda partial: (unit_core(partial), unit_sides(down_kept, down_came))]
        )
        for number, subsets in enumerate(back_plan[split_at:]):
            pieces, came, _ = scatter_hop(pieces, unit_axes, True, subsets, came, beside(number))
        rows = whole_call(
            functools.partial(after_ffn_back_kernel, len(pieces[0])),
            [(row_shape, f32), (row_shape, bf16), (scale_shape, f32), (scale_shape, f32)],
            *pieces[0],
            resid,
            attn_out,
            out_grad,
            scale_rows,
            name="after_ffn_back",
        )
        return (*rows, *results[1])

    gate_came = send(gate_away, top, down_came)
    (grad_resid, grad_attn, scale_grad2, scale_grad1, (up_away, up_kept), (down_far, down_own)), gate_came = segment(
        ffn_back_last, (ffn_pieces, grad_up_act, down_came), (gate_away, gate_kept), gate_came
    )

    def attend_back(grad_attn):
        grad_attn_full = join_rows(gather_rows(grad_attn, head_axes))
        grad_mixed = product(grad_attn_full, output_weight, 1, 0, bf16)
        grad_query_lin, kv_near, kv_far = attention_backward(
            spans, queries, grad_mixed, exact, lse, table, kv_pieces, span_len
        )
        kv_terms = plus(kv_near, swap(kv_far, (1, 0))).astype(bf16).reshape(-1, group_rows, 2 * HD)
        middle = kv_terms.shape[0] // 2
        return grad_attn_full, grad_query_lin, kv_terms[:middle], kv_terms[middle:]

    up_came = send(up_away, top, grad_attn)
    down_other = send(down_far, pair, grad_attn)
    (grad_attn_full, grad_query_lin, kv_kept, kv_away), (up_came, down_other) = segment(
        attend_back, (grad_attn,), (up_away, up_kept, down_far, down_own), (up_came, down_other)
    )

    def projections_back(grad_query_lin, gate_came):
        core = core_sum(outer((normed_full, grad_query_lin), (grad_attn_full, mixed)))
        away, kept = pick(core, bit_count - 2, 1 - unit_side), pick(core, bit_count - 2, unit_side)
        return away, kept, unit_sides(gate_kept, gate_came)

    kv_came = send(kv_away, pair)
    (query_output_away, query_output_kept, (gate_far, gate_own)), kv_came = segment(
        projections_back, (grad_query_lin, gate_came), (), kv_came
    )
    kv_terms = plus(kv_kept, kv_came).astype(bf16)
    for mask in chip_masks[1:-1]:
        middle = kv_terms.shape[0] // 2
        kv_terms = plus(kv_terms[:middle], swap(kv_terms[middle:], (mask, 0))).astype(bf16)

    def beside_last_keys(up_came, down_other):
        return unit_sides(up_kept, up_came), unit_whole(down_own, down_other).T

    kv_came = send(kv_terms[1], top)
    gate_other = send(gate_far, pair, kv_terms)
    ((up_far, up_own), out_down), (kv_came, gate_other) = segment(
        beside_last_keys, (up_came, down_other), (kv_terms,), (kv_came, gate_other)
    )

    def normed_rows_back(kv_kept, kv_came):
        (grad_kv_lin,) = whole_call(
            key_value_grad_kernel,
            [((group_rows, 2 * HD), bf16)],
            kv_kept,
            kv_came,
            *table,
            name="key_value_grad",
        )
        terms = core_sum(outer((normed_full, grad_kv_lin)))
        away, kept = pick(terms, bit_count - 2, 1 - unit_side), pick(terms, bit_count - 2, unit_side)

        def products_back(grad_kv_lin):
            grad_normed_part, scale_grad0 = normed_back(
                grad_query_lin, query_weight, grad_kv_lin, kv_weight, inverse_full, hidden_slots
            )
            scale_grad = jnp.concatenate([scale_grad0, scale_grad1, scale_grad2, scale_grad3], 0)
            scale_grad = scale_grad.reshape(scale_count, block_count, model_rows).transpose(1, 0, 2)
            scale_grad = scale_grad.reshape((2,) * bit_count + scale_grad.shape[1:])
            for at, mask in enumerate([1] + chip_masks[:-1]):
                scale_grad = halve(scale_grad, bit_count - 1 - at, mask)
            scale_grad = jnp.pad(scale_grad.astype(bf16), ((0, 0), (0, 16 - scale_count), (0, 2 * HD - model_rows)))
            return grad_normed_part, scale_grad

        wkv_came = send(away, pair)
        (grad_normed_part, scale_grad), wkv_came = segment(products_back, (grad_kv_lin,), (away, kept), wkv_came)
        wkv_terms = plus(kept, wkv_came).astype(bf16)
        for at, mask in list(enumerate(chip_masks))[1:-1]:
            wkv_terms = halve(wkv_terms, bit_count - 2 - at, mask).astype(bf16)

        def sums_back(grad_normed_part):
            terms = row_sum(grad_normed_part, head_axes)
            (grad_in,) = whole_call(
                functools.partial(after_all_kernel, len(terms)),
                [(row_shape, f32)],
                *terms,
                hidden_in,
                grad_resid,
                scale_rows,
                name="after_all",
            )
            return grad_in

        wkv_terms = jnp.concatenate([wkv_terms, scale_grad], 1)
        away, kept = lax.optimization_barrier((pick(wkv_terms, 0, 1 - side(top)), pick(wkv_terms, 0, side(top))))
        wkv_came = send(away, top)
        query_output_came = send(query_output_away, pair, away)
        grad_in, (wkv_came, query_output_came) = segment(
            sums_back, (grad_normed_part,), (away, kept), (wkv_came, query_output_came)
        )
        return (grad_in, plus(kept, wkv_came).astype(bf16)), query_output_came

    (grad_in, grad_wkv), query_output_came = segment(
        normed_rows_back, (kv_terms[0], kv_came), (up_far, up_own, out_down)
    )[0]
    query_output_terms = plus(query_output_kept, query_output_came).astype(bf16)
    for at, mask in list(enumerate(chip_masks))[1:-1]:
        query_output_terms = halve(query_output_terms, bit_count - 2 - at, mask).astype(bf16)
    query_output_away = pick(query_output_terms, 0, 1 - side(top))
    query_output_came = send(query_output_away, top)
    up_other = send(up_far, pair, grad_wkv)

    def head_rows(grad_wkv):
        parts = gather_rows(grad_wkv, head_axes)
        wkv_ordered = jnp.zeros((head_count,) + grad_wkv.shape, bf16)
        for mask, pieces in parts.items():
            first = 0
            for piece in pieces:
                wkv_ordered = lax.dynamic_update_slice(wkv_ordered, piece[None], (head_index ^ mask, first, 0))
                first += piece.shape[0]
        wkv_ordered = wkv_ordered.astype(f32)
        scale_total = wkv_ordered[:, model_rows : model_rows + scale_count, :model_rows].sum(0)
        wkv_ordered = wkv_ordered[:, :model_rows].reshape(KVH, head_count // KVH, model_rows, 2, HD).sum(1)
        out_key = wkv_ordered[:, :, 0].transpose(1, 0, 2).reshape(model_rows, KVH * HD)
        out_value = wkv_ordered[:, :, 1].transpose(1, 0, 2).reshape(model_rows, KVH * HD)
        return out_key, out_value, scale_total, unit_whole(gate_own, gate_other)

    (out_key, out_value, scale_total, out_gate), (query_output_came, up_other) = segment(
        head_rows, (grad_wkv,), (query_output_away,), (query_output_came, up_other)
    )
    out_query_output = plus(pick(query_output_terms, 0, side(top)), query_output_came)
    out_query = out_query_output[:, :query_width]
    out_output = out_query_output[:, query_width:].T
    out_up = unit_whole(up_own, up_other)

    return (
        layer_out,
        grad_in,
        out_query,
        out_key,
        out_value,
        out_output,
        out_gate,
        out_up,
        out_down,
        scale_total,
    )


def solution(mesh):
    placed = (
        P(("blk", "head"), None),
        P(("blk", "head"), None),
        P(),
        P("blk", "head"),
        P("blk", None),
        P("blk", None),
        P("head", "blk"),
        P("blk", "head"),
        P("blk", "head"),
        P("head", "blk"),
        P(None, "blk"),
    )
    return jax.shard_map(
        on_device,
        mesh=mesh,
        in_specs=placed,
        out_specs=(
            P(("blk", "head"), None),
            P(("blk", "head"), None),
            P("blk", "head"),
            P("blk", None),
            P("blk", None),
            P("head", "blk"),
            P("blk", "head"),
            P("blk", "head"),
            P("head", "blk"),
            P(None, "blk"),
        ),
        check_vma=False,
    )
```

```python
import functools
import math

import jax
import jax.numpy as jnp
from jax import lax
from jax.experimental import pallas as pl
from jax.experimental.pallas import tpu as pltpu
from jax.sharding import PartitionSpec as P

H = 8
KVH = 4
HD = 256

norm_eps = 1e-06
cap_value = 50.0
theta_base = 10000.0
f32 = jnp.float32
bf16 = jnp.bfloat16


def inverse_rms(value):
    return lax.rsqrt(jnp.mean(value * value, axis=-1, keepdims=True) + norm_eps)


def rms_back(value, scale, grad):
    inverse = inverse_rms(value)
    scaled = grad * scale
    inner = jnp.mean(scaled * value, axis=-1, keepdims=True)
    grad_value = inverse * scaled - value * (inverse * inverse * inverse) * inner
    grad_scale = jnp.sum(grad * value * inverse, axis=0, keepdims=True)
    return (grad_value, grad_scale)


def rotation(position):
    entry = jnp.arange(HD, dtype=jnp.int32)
    quarter = HD // 4
    pair_index = entry // (2 * quarter) * quarter + entry % quarter
    frequency = jnp.power(theta_base, -2.0 * pair_index.astype(f32) / HD)
    angles = position.astype(f32)[:, None] * frequency[None, :]
    sign = jnp.where(entry % (2 * quarter) < quarter, -1.0, 1.0)
    return jnp.cos(angles), jnp.sin(angles) * sign[None, :]


def rotated(value, cosine, sine, sign):
    half = HD // 2
    parts = []
    for at in range(0, HD, half):
        piece = value[:, at : at + half]
        partner = pltpu.roll(piece, half // 2, 1)
        parts.append(piece * cosine[:, at : at + half] + partner * (sign * sine[:, at : at + half]))
    return jnp.concatenate(parts, 1)


def swap(value, axis):
    blk_mask, head_mask = axis
    block_count, head_count = lax.axis_size("blk"), lax.axis_size("head")
    if blk_mask == 0:
        return lax.ppermute(value, "head", [(i, i ^ head_mask) for i in range(head_count)])
    return lax.ppermute(value, "blk", [(i, i ^ blk_mask) for i in range(block_count)])


def bits(count):
    return [1 << i for i in range(count.bit_length() - 1)]


def route(subset, total, light):
    members = [i for i in range(total) if subset >> i & 1]
    if light and len(members) > 1 and members[-1] == total - 1:
        members = members[:-1]
        return members if len(members) == total - 1 else members[:1]
    if len(members) >= 2 and len(members) == total - light:
        return members
    if not light and len(members) == 2 and members[1] - members[0] != 1:
        return members[1:]
    return members[:1]


def hops(total, light):
    size = lambda t: bin(t).count("1")
    last = 1 << (total - 1)
    subsets = range(1, 1 << total)
    if not light:
        return [[t for t in subsets if size(t) == n] for n in range(1, total + 1)]
    result = [[t for t in subsets if size(t) == 1]]
    for high in (0, last):
        for n in range(2, total + 1):
            result.append([t for t in subsets if size(t) == n and t & last == high])
    return [hop for hop in result if hop]


def shares(row_total, parts):
    unit = row_total // 16
    cuts = [unit * i // parts * 16 for i in range(parts + 1)]
    cuts[-1] = row_total
    return list(zip(cuts[:-1], cuts[1:]))


def gather_hop(parts, axes, light, subsets, before=()):
    rows = parts[0][0].shape[0]
    came = {}
    for subset in subsets:
        ways = route(subset, len(axes), light)
        cuts = shares(rows, len(ways)) if len(ways) > 1 else [(0, rows)]
        came[subset] = []
        for way, (low, high) in zip(ways, cuts):
            source = parts[subset ^ (1 << way)][0]
            came[subset].append(swap(tie(source[low:high] if len(ways) > 1 else source, *before), axes[way]))
    return came


def gather_rows(value, axes, light=False, parts=None):
    last = 1 << (len(axes) - 1)
    parts, before = parts or {0: [value]}, ()
    for subsets in hops(len(axes), light):
        if all(t in parts for t in subsets):
            continue
        if light and last in parts:
            before = [x for x in before if x is not parts[last][0]]
            before += parts[last] * any(t & last for t in subsets)
        came = gather_hop(parts, axes, light, subsets, before)
        parts = parts | came
        before = [part for pieces in came.values() for part in pieces]
    return parts


def join_kernel(plan, *refs):
    step = pl.program_id(0)
    out = refs[-1]
    for at, (slot, first, rows) in enumerate(plan):

        @pl.when(step == slot)
        def _():
            out[first : first + rows, :] = refs[at][...]


def join_rows(parts):
    plan, arrays = [], []
    for slot in sorted(parts):
        first = 0
        for array in parts[slot]:
            plan.append((slot, first, array.shape[0]))
            arrays.append(array)
            first += array.shape[0]
    rows, columns = parts[0][0].shape
    return pl.pallas_call(
        functools.partial(join_kernel, plan),
        grid=(len(parts),),
        in_specs=[pl.BlockSpec(a.shape, lambda m: (0, 0), pipeline_mode=pl.Buffered(1)) for a in arrays],
        out_specs=pl.BlockSpec((rows, columns), lambda m: (m, 0)),
        out_shape=jax.ShapeDtypeStruct((len(parts) * rows, columns), arrays[0].dtype),
        compiler_params=pltpu.CompilerParams(vmem_limit_bytes=16 * 1024 * 1024),
        cost_estimate=pl.CostEstimate(flops=0, bytes_accessed=4 * len(parts) * rows * columns, transcendentals=0),
        name="join_rows",
    )(*arrays)


def two_products_kernel(a_ref, u_ref, b_ref, v_ref, *outs):
    nt = (((1,), (1,)), ((), ()))
    total = lax.dot_general(a_ref[...], u_ref[...], nt, preferred_element_type=f32)
    total += lax.dot_general(b_ref[...], v_ref[...], nt, preferred_element_type=f32)
    put_pieces(outs, total)


def put_pieces(outs, value):
    rows = outs[0].shape[0]
    for at, out in enumerate(outs):
        out[...] = value[at * rows : (at + 1) * rows].astype(out.dtype)


def two_products(a, u, b, v, count):
    rows, depth = a.shape
    columns = u.shape[0]
    step = 256
    resident = pl.BlockSpec((rows, depth), lambda n: (0, 0), pipeline_mode=pl.Buffered(1))
    return pl.pallas_call(
        two_products_kernel,
        grid=(columns // step,),
        in_specs=[resident, pl.BlockSpec((step, depth), lambda n: (n, 0))] * 2,
        out_specs=[pl.BlockSpec((rows // count, step), lambda n: (0, n))] * count,
        out_shape=[jax.ShapeDtypeStruct((rows // count, columns), bf16)] * count,
        compiler_params=pltpu.CompilerParams(vmem_limit_bytes=20 * 1024 * 1024),
        cost_estimate=pl.CostEstimate(
            flops=4 * rows * columns * depth,
            bytes_accessed=4 * (rows * depth + columns * depth) + 2 * rows * columns,
            transcendentals=0,
        ),
        name="two_products",
    )(a, u, b, v)


def joined(left, right):
    return (left.astype(f32) + right.astype(f32)).astype(bf16)


def scatter_plan(total, light):
    plan = [list(hop) for hop in hops(total, light)[::-1]]
    last = 1 << (total - 1)
    if light:
        plan[-1].remove(last)
        plan[next(i for i, hop in enumerate(plan) if not any(t & last for t in hop))].append(last)
    return plan


def scatter_hop(pieces, axes, light, subsets, before=(), beside=None):
    last = 1 << (len(axes) - 1)
    pieces = dict(pieces)
    rows = pieces[0][0].shape[0]
    sent, result = [], None
    for subset in subsets:
        (piece,) = pieces.pop(subset)
        ways = route(subset, len(axes), light)
        cuts = shares(rows, len(ways)) if len(ways) > 1 else [(0, rows)]
        for way, (low, high) in zip(ways, cuts):
            part = piece if len(ways) == 1 else piece[low:high]
            sent.append((subset, subset ^ (1 << way), low, high, swap(tie(part, *before), axes[way])))
    if beside:
        result, came = beside([item[4] for item in sent])
        sent = [item[:4] + (moved,) for item, moved in zip(sent, came)]
    for subset, target, low, high, moved in sent:
        if target == 0:
            pieces[0] = pieces[0] + [moved]
        elif high - low == rows:
            pieces[target] = [joined(pieces[target][0], moved)]
        else:
            old = pieces[target][0]
            cut = [old[:low], joined(old[low:high], moved), old[high:]]
            pieces[target] = [jnp.concatenate([c for c in cut if c.shape[0]], 0)]
    came = [item[4] for item in sent if not (light and item[0] == last)]
    return pieces, came, result


def scatter_rows(pieces, axes, light=False):
    pieces, came = {t: [piece] for t, piece in enumerate(pieces)}, ()
    for subsets in scatter_plan(len(axes), light):
        pieces, came, _ = scatter_hop(pieces, axes, light, subsets, came)
    return pieces[0]


def tie(value, *after):
    return lax.optimization_barrier((value, *after))[0] if after else value


def tie_all(held, *after):
    return {mask: tie(block, *after) for mask, block in held.items()}


def scale_kernel(count, index_ref, *refs):
    step = pl.program_id(0)
    for at in range(count):

        @pl.when(step == at)
        def _():
            refs[count][...] = refs[at][...]


def place_scales(held, rows, block_index):
    count = len(held)
    shape = (16, held[0].shape[1])
    return pl.pallas_call(
        functools.partial(scale_kernel, count),
        grid_spec=pltpu.PrefetchScalarGridSpec(
            num_scalar_prefetch=1,
            grid=(count,),
            in_specs=[pl.BlockSpec(shape, lambda m, b: (rows // 16, 0), pipeline_mode=pl.Buffered(1))] * count,
            out_specs=pl.BlockSpec(shape, lambda m, b: (b[0] ^ m, 0)),
        ),
        out_shape=jax.ShapeDtypeStruct((count * 16, shape[1]), bf16),
        cost_estimate=pl.CostEstimate(flops=0, bytes_accessed=4 * count * 16 * shape[1], transcendentals=0),
        name="place_scales",
    )(block_index[None].astype(jnp.int32), *[held[mask] for mask in range(count)])


def placed_kernel(body, plans, counts, steps, index_ref, *refs):
    refs = list(refs)
    arrays, loads, inputs, outs, wholes, weights, loaded = [[refs.pop(0) for _ in range(count)] for count in counts]
    in_sems, out_sems = refs
    step = pl.program_id(0)
    came, at = [], 0
    for source, target in zip(loads, loaded):
        came.append([pltpu.make_async_copy(source, target, in_sems.at[at])])
        at += 1
    gone = [None] * len(loads)
    for weight, plan in zip(weights, plans):
        copies = []
        rows = weight.shape[0] // len(plan)
        for mask, (source, column) in enumerate(plan):
            row = pl.multiple_of((index_ref[0] ^ mask) * rows, 16)
            block = arrays[source].at[pl.ds(0, rows)]
            if arrays[source].shape[1] != weight.shape[1]:
                block = arrays[source].at[pl.ds(0, rows), pl.ds(column, weight.shape[1])]
            copies.append(pltpu.make_async_copy(block, weight.at[pl.ds(row, rows)], in_sems.at[at]))
            at += 1
        came.append(copies)
    gone += [
        pltpu.make_async_copy(weight, whole, out_sems.at[n]) for n, (weight, whole) in enumerate(zip(weights, wholes))
    ]

    @pl.when(step == 0)
    def _():
        for copies in came:
            for copy in copies:
                copy.start()
        for copies, copy_out in zip(came, gone):
            for copy in copies:
                copy.wait()
            if copy_out is not None:
                copy_out.start()

    body(step, loaded + inputs, outs, weights)

    @pl.when(step == steps - 1)
    def _():
        for copy_out in gone[len(loads) :]:
            copy_out.wait()


def placed(body, steps, held, columns, loads, inputs, in_specs, outs, out_specs, block_index, name, flops, vmem):
    arrays, plans = [], []
    for blocks, width in zip(held, columns):
        plan = []
        for mask in range(len(blocks)):
            array, column = blocks[mask]
            if width % 128 or column % 128:
                array, column = array[:, column : column + width], 0
            where = next((n for n, known in enumerate(arrays) if known is array), len(arrays))
            if where == len(arrays):
                arrays.append(array)
            plan.append((where, column))
        plans.append(plan)
    rows = min(array.shape[0] for array in arrays) // 16 * 16
    rows = rows - (16 if name == "key_rows" else 0)
    shapes = [(len(plan) * rows, width) for plan, width in zip(plans, columns)]
    anywhere = pl.BlockSpec(memory_space=pltpu.HBM)
    counts = (len(arrays), len(loads), len(inputs), len(outs), len(plans), len(plans), len(loads))
    return pl.pallas_call(
        functools.partial(placed_kernel, body, plans, counts, steps),
        grid_spec=pltpu.PrefetchScalarGridSpec(
            num_scalar_prefetch=1,
            grid=(steps,),
            in_specs=[anywhere] * (len(arrays) + len(loads)) + in_specs,
            out_specs=out_specs + [anywhere] * len(plans),
            scratch_shapes=[pltpu.VMEM(shape, bf16) for shape in shapes]
            + [pltpu.VMEM(array.shape, array.dtype) for array in loads]
            + [
                pltpu.SemaphoreType.DMA((sum(len(plan) for plan in plans) + len(loads),)),
                pltpu.SemaphoreType.DMA((len(plans),)),
            ],
        ),
        out_shape=outs + [jax.ShapeDtypeStruct(shape, bf16) for shape in shapes],
        compiler_params=pltpu.CompilerParams(vmem_limit_bytes=vmem * 1024 * 1024),
        cost_estimate=pl.CostEstimate(
            flops=flops, bytes_accessed=4 * sum(h * w for h, w in shapes), transcendentals=0
        ),
        name=name,
    )(block_index[None].astype(jnp.int32), *arrays, *loads, *inputs)


def in_turn(held):
    came = []
    for block in held.values():
        came.append(swap(tie(block, *came[-2:-1]), (1, 0)))
    return dict(zip(held, came))


def both_cores(held):
    return held | {mask ^ 1: swap(block, (1, 0)) for mask, block in held.items()}


def pick(value, dim, index):
    return lax.dynamic_index_in_dim(value, index, dim, keepdims=False)


def plus(left, right):
    return left.astype(f32) + right.astype(f32)


def whole_call(body, outs, *inputs, name):
    size = sum(x.size * x.dtype.itemsize for x in inputs)
    return pl.pallas_call(
        body,
        out_shape=[jax.ShapeDtypeStruct(shape, dtype) for shape, dtype in outs],
        compiler_params=pltpu.CompilerParams(vmem_limit_bytes=28 * 1024 * 1024),
        cost_estimate=pl.CostEstimate(flops=0, bytes_accessed=2 * size, transcendentals=0),
        name=name,
    )(*inputs)


def summed(refs):
    total = refs[0][...].astype(f32)
    for ref in refs[1:]:
        total = total + ref[...].astype(f32)
    return total


def norm_full_kernel(count, *refs):
    parts, (scale, normed, inverse) = refs[:count], refs[count:]
    first = 0
    for part in parts:
        value = part[...].astype(f32)
        here = slice(first, first + part.shape[0])
        first += part.shape[0]
        factor = inverse_rms(value)
        inverse[here, :] = factor
        normed[here, :] = (value * factor * scale[0:1, :]).astype(bf16)


def after_attention_kernel(count, *refs):
    terms, (hidden, scales, attn_out, resid_out, ffn_in) = refs[:count], refs[count:]
    attn = summed(terms)
    attn_out[...] = attn
    resid = hidden[...].astype(f32) + attn * inverse_rms(attn) * scales[1:2, :]
    resid_out[...] = resid
    ffn_in[...] = (resid * inverse_rms(resid) * scales[2:3, :]).astype(bf16)


def after_ffn_kernel(count, *refs):
    terms, (resid, out_grad, scales, layer_out, grad_out, grad_scale) = refs[:count], refs[count:]
    ffn_out = summed(terms)
    grad, grad_scale[...] = rms_back(ffn_out, scales[3:4, :], out_grad[...].astype(f32))
    grad_out[...] = grad.astype(bf16)
    layer_out[...] = (resid[...] + ffn_out * inverse_rms(ffn_out) * scales[3:4, :]).astype(bf16)


def after_ffn_back_kernel(count, *refs):
    terms, (resid, attn, out_grad, scales, grad_resid, grad_attn, grad_scale2, grad_scale1) = refs[:count], refs[count:]
    grad, grad_scale2[...] = rms_back(resid[...], scales[2:3, :], summed(terms))
    grad = out_grad[...].astype(f32) + grad
    grad_resid[...] = grad
    back, grad_scale1[...] = rms_back(attn[...], scales[1:2, :], grad)
    grad_attn[...] = back.astype(bf16)


def after_all_kernel(count, *refs):
    terms, (hidden, grad_resid, scales, grad_in) = refs[:count], refs[count:]
    grad, _ = rms_back(hidden[...].astype(f32), scales[0:1, :], summed(terms))
    grad_in[...] = grad_resid[...] + grad


def key_value_grad_kernel(kept, came, cosine, sine, out):
    total = kept[...].astype(f32) + came[...].astype(f32)
    out[:, :HD] = rotated(total[:, :HD], cosine[...], sine[...], -1.0).astype(bf16)
    out[:, HD:] = total[:, HD:].astype(bf16)


def project(rows, held, columns, table, turning, block_index, name):
    count, depth = rows.shape
    heads = columns[0] // HD
    fixed = lambda n, b: (0, 0)
    once = pl.Buffered(1)

    def body(step, inputs, outs, weights):
        rows_ref, cosine_ref, sine_ref = inputs
        (out_ref,) = outs
        here = pl.ds(pl.multiple_of(step * HD, HD), HD)
        value = jnp.dot(rows_ref[...], weights[0][:, here], preferred_element_type=f32)

        @pl.when(step < turning)
        def _():
            out_ref[...] = rotated(value, cosine_ref[...], sine_ref[...], 1.0).astype(bf16)

        @pl.when(step >= turning)
        def _():
            out_ref[...] = value.astype(bf16)

    return placed(
        body,
        heads,
        held,
        columns,
        [rows],
        list(table),
        [
            pl.BlockSpec((count, HD), fixed, pipeline_mode=once),
            pl.BlockSpec((count, HD), fixed, pipeline_mode=once),
        ],
        [jax.ShapeDtypeStruct((count, columns[0]), bf16)],
        [pl.BlockSpec((count, HD), lambda n, b: (0, n))],
        block_index,
        name,
        2 * rows.size * columns[0],
        20,
    )


def hidden_units(rows, held, width, block_index):
    count, depth = rows.shape
    step = 256

    def body(number, inputs, outs, weights):
        hidden_ref, active_ref, slope_ref = outs
        gate = jnp.dot(inputs[0][...], weights[0][...], preferred_element_type=f32)
        up = jnp.dot(inputs[0][...], weights[1][...], preferred_element_type=f32)
        inner = math.sqrt(2.0 / math.pi)
        square = gate * gate
        tangent = jnp.tanh(inner * gate * (1.0 + 0.044715 * square))
        share = 0.5 * (1.0 + tangent)
        active = gate * share
        slope = share + (0.5 * inner) * gate * (1.0 - tangent * tangent) * (1.0 + (3 * 0.044715) * square)
        hidden_ref[...] = (active * up).astype(bf16)
        active_ref[...] = active
        slope_ref[...] = slope * up

    return placed(
        body,
        count // step,
        held,
        [width, width],
        [],
        [rows],
        [pl.BlockSpec((step, depth), lambda n, b: (n, 0))],
        [jax.ShapeDtypeStruct((count, width), dtype) for dtype in (bf16, f32, f32)],
        [pl.BlockSpec((step, width), lambda n, b: (n, 0))] * 3,
        block_index,
        "hidden_units",
        4 * rows.size * width,
        40,
    )


def down_rows(hidden, held, block_index, pieces):
    count, width = hidden.shape
    depth = len(held) * held[0][0].shape[0]
    step = 768 if depth % 768 == 0 else 256

    def body(number, inputs, outs, weights):
        here = pl.ds(pl.multiple_of(number * step, step), step)
        value = lax.dot_general(
            inputs[0][...], weights[0][here, :], (((1,), (1,)), ((), ())), preferred_element_type=f32
        )
        put_pieces(outs, value)

    return placed(
        body,
        depth // step,
        [held],
        [width],
        [hidden],
        [],
        [],
        [jax.ShapeDtypeStruct((count // pieces, depth), bf16)] * pieces,
        [pl.BlockSpec((count // pieces, step), lambda n, b: (0, n))] * pieces,
        block_index,
        "down_rows",
        2 * hidden.size * depth,
        24,
    )


def outer_kernel(*refs):
    pairs, out = refs[:-1], refs[-1]
    width = 0
    for left, right in zip(pairs[::2], pairs[1::2]):
        columns = right.shape[1]
        value = lax.dot_general(left[...], right[...], (((0,), (0,)), ((), ())), preferred_element_type=f32)
        out[:, width : width + columns] = value.astype(bf16)
        width += columns


def outer(*pairs):
    rows, depth = pairs[0][0].shape
    width = sum(right.shape[1] for _, right in pairs)
    step = depth // 2
    specs = []
    for _, right in pairs:
        specs.append(pl.BlockSpec((rows, step), lambda n: (0, n)))
        specs.append(pl.BlockSpec(right.shape, lambda n: (0, 0), pipeline_mode=pl.Buffered(1)))
    return pl.pallas_call(
        outer_kernel,
        grid=(depth // step,),
        in_specs=specs,
        out_specs=pl.BlockSpec((step, width), lambda n: (n, 0)),
        out_shape=jax.ShapeDtypeStruct((depth, width), bf16),
        compiler_params=pltpu.CompilerParams(vmem_limit_bytes=24 * 1024 * 1024),
        cost_estimate=pl.CostEstimate(
            flops=2 * rows * depth * width, bytes_accessed=2 * (rows * depth * len(pairs) + depth * width), transcendentals=0
        ),
        name="outer",
    )(*[x for pair in pairs for x in pair])


def normed_back_kernel(count, q_ref, wq_ref, kv_ref, wkv_ref, inverse_ref, *refs):
    hidden, (*outs, scale_ref) = refs[:count], refs[count:]
    nt = (((1,), (1,)), ((), ()))
    total = lax.dot_general(q_ref[...], wq_ref[...], nt, preferred_element_type=f32)
    total += lax.dot_general(kv_ref[...], wkv_ref[...], nt, preferred_element_type=f32)
    put_pieces(outs, total)
    grad_scale, first = jnp.zeros((1, total.shape[1]), f32), 0
    for part in hidden:
        here = slice(first, first + part.shape[0])
        first += part.shape[0]
        unit = part[...].astype(f32) * inverse_ref[here, :]
        grad_scale += jnp.sum(total[here, :] * unit, axis=0, keepdims=True)
    scale_ref[...] = grad_scale


def normed_back(grad_query, query_weight, grad_kv, kv_weight, inverse, hidden, pieces):
    rows, width = grad_query.shape
    kv_width = grad_kv.shape[1]
    columns = query_weight.shape[0]
    step = 768 if columns % 768 == 0 else 256
    fixed = lambda n: (0, 0)
    once = pl.Buffered(1)
    return pl.pallas_call(
        functools.partial(normed_back_kernel, len(hidden)),
        grid=(columns // step,),
        in_specs=[
            pl.BlockSpec((rows, width), fixed, pipeline_mode=once),
            pl.BlockSpec((step, width), lambda n: (n, 0)),
            pl.BlockSpec((rows, kv_width), fixed, pipeline_mode=once),
            pl.BlockSpec((step, kv_width), lambda n: (n, 0)),
            pl.BlockSpec((rows, 1), fixed, pipeline_mode=once),
        ]
        + [pl.BlockSpec((part.shape[0], step), lambda n: (0, n)) for part in hidden],
        out_specs=[pl.BlockSpec((rows // pieces, step), lambda n: (0, n))] * pieces
        + [pl.BlockSpec((1, step), lambda n: (0, n))],
        out_shape=[jax.ShapeDtypeStruct((rows // pieces, columns), bf16)] * pieces
        + [jax.ShapeDtypeStruct((1, columns), f32)],
        compiler_params=pltpu.CompilerParams(vmem_limit_bytes=20 * 1024 * 1024),
        cost_estimate=pl.CostEstimate(
            flops=2 * rows * columns * (width + kv_width), bytes_accessed=4 * rows * columns, transcendentals=0
        ),
        name="normed_back",
    )(grad_query, query_weight, grad_kv, kv_weight, inverse, *hidden)


def scores(query, key, score_scale):
    raw = lax.dot_general(query, key, (((1,), (1,)), ((), ())), preferred_element_type=f32)
    return jnp.tanh(raw * (score_scale / cap_value))


def load_pieces(step, pieces, kv_all, sems):
    copies = [pltpu.make_async_copy(piece, kv_all.at[at], sems.at[at]) for at, piece in enumerate(pieces)]

    @pl.when(step == 0)
    def _():
        for copy in copies:
            copy.start()

    for at, copy in enumerate(copies):

        @pl.when(step == 2 * at)
        def _():
            copy.wait()


def forward_kernel(group, span_len, tiles, spans_ref, q_ref, *refs):
    pieces, (mixed_ref, exact_ref, lse_ref, q_all, acc, total, kv_all, sems) = refs[: tiles // 2], refs[tiles // 2 :]
    step = pl.program_id(0)
    load_pieces(step, pieces, kv_all, sems)
    score_scale = 1.0 / math.sqrt(HD)
    rows = group * span_len

    @pl.when(step == 0)
    def _():
        for half in range(2):
            for g in range(group):
                q_all[half, g * span_len : (g + 1) * span_len, :] = q_ref[
                    half * span_len : (half + 1) * span_len, g * HD : (g + 1) * HD
                ]
        acc[...] = jnp.zeros_like(acc)
        total[...] = jnp.zeros_like(total)

    tile_span = spans_ref[step]
    here = pl.ds(pl.multiple_of((step % 2) * span_len, span_len), span_len)
    key = kv_all[step // 2, here, :HD]
    value = kv_all[step // 2, here, HD:]

    def visit(half, diagonal):
        weights = jnp.exp(cap_value * scores(q_all[half], key, score_scale))
        if diagonal:
            flip = spans_ref[tiles + 2]
            shape = (rows, span_len)
            q_pos = (lax.broadcasted_iota(jnp.int32, shape, 0) % span_len) ^ flip
            k_pos = lax.broadcasted_iota(jnp.int32, shape, 1) ^ flip
            weights = jnp.where(k_pos <= q_pos, weights, 0.0)
        part = weights[:, :128]
        for at in range(128, span_len, 128):
            part = part + weights[:, at : at + 128]
        total[half] += part
        acc[half] += jnp.dot(weights.astype(bf16), value, preferred_element_type=f32)

    for half in range(2):
        own = spans_ref[tiles + half]

        @pl.when(tile_span < own)
        def _():
            visit(half, False)

        @pl.when(tile_span == own)
        def _():
            visit(half, True)

    @pl.when(step == tiles - 1)
    def _():
        for half in range(2):
            sums = jnp.sum(total[half], axis=1, keepdims=True)
            exact = acc[half] / sums
            lse_ref[half] = jnp.log(jnp.sum(total[half].T, axis=0, keepdims=True))
            for g in range(group):
                piece = exact[g * span_len : (g + 1) * span_len]
                place = (slice(half * span_len, (half + 1) * span_len), slice(g * HD, (g + 1) * HD))
                exact_ref[place] = piece
                mixed_ref[place] = piece.astype(bf16)


def backward_kernel(group, span_len, tiles, spans_ref, q_ref, g_ref, exact_ref, lse_ref, cosine_ref, sine_ref, *refs):
    pieces, rest = refs[: tiles // 2], refs[tiles // 2 :]
    dq_ref, near_ref, far_ref, q_all, g_all, delta, dq_acc, kv_all, sems = rest
    step = pl.program_id(0)
    load_pieces(step, pieces, kv_all, sems)
    score_scale = 1.0 / math.sqrt(HD)
    rows = group * span_len

    @pl.when(step == 0)
    def _():
        for half in range(2):
            for g in range(group):
                place = (slice(half * span_len, (half + 1) * span_len), slice(g * HD, (g + 1) * HD))
                here = slice(g * span_len, (g + 1) * span_len)
                q_all[half, here, :] = q_ref[place]
                g_all[half, here, :] = g_ref[place]
                product = g_ref[place].astype(f32) * exact_ref[place]
                folded = product[:, :128] + product[:, 128:]
                delta[half, :, here] = jnp.sum(folded.T, axis=0, keepdims=True)
        dq_acc[...] = jnp.zeros_like(dq_acc)

    tile_span = spans_ref[step]
    here = pl.ds(pl.multiple_of((step % 2) * span_len, span_len), span_len)
    key = kv_all[step // 2, here, :HD]
    value = kv_all[step // 2, here, HD:]

    def visit(half, diagonal):
        query = q_all[half]
        grad = g_all[half]
        tangent = scores(key, query, score_scale)
        probability = jnp.exp(cap_value * tangent - lse_ref[half])
        if diagonal:
            flip = spans_ref[tiles + 2]
            shape = (span_len, rows)
            q_pos = (lax.broadcasted_iota(jnp.int32, shape, 1) % span_len) ^ flip
            k_pos = lax.broadcasted_iota(jnp.int32, shape, 0) ^ flip
            probability = jnp.where(k_pos <= q_pos, probability, 0.0)
        grad_prob = lax.dot_general(value, grad, (((1,), (1,)), ((), ())), preferred_element_type=f32)
        grad_raw = probability * (grad_prob - delta[half]) * ((1.0 - tangent * tangent) * score_scale)
        grad_raw = grad_raw.astype(bf16)
        dv = jnp.dot(probability.astype(bf16), grad, preferred_element_type=f32)
        dk = jnp.dot(grad_raw, query, preferred_element_type=f32)
        dq_acc[half] += lax.dot_general(grad_raw, key, (((0,), (0,)), ((), ())), preferred_element_type=f32)
        return dk, dv

    def put(dk, dv):
        @pl.when(step < tiles // 2)
        def _():
            near_ref[:, :HD] = dk.astype(bf16)
            near_ref[:, HD:] = dv.astype(bf16)

        @pl.when(step >= tiles // 2)
        def _():
            far_ref[:, :HD] = dk.astype(bf16)
            far_ref[:, HD:] = dv.astype(bf16)

    low, high = spans_ref[tiles], spans_ref[tiles + 1]
    first, second = tile_span <= low, tile_span <= high

    @pl.when(jnp.logical_not(jnp.logical_or(first, second)))
    def _():
        put(jnp.zeros((span_len, HD), f32), jnp.zeros((span_len, HD), f32))

    for half, own, other in ((0, low, high), (1, high, low)):
        for diagonal in (False, True):
            here = tile_span == own if diagonal else tile_span < own

            @pl.when(jnp.logical_and(here, tile_span > other))
            def _(half=half, diagonal=diagonal):
                put(*visit(half, diagonal))

    for half, own, other in ((0, low, high), (1, high, low)):
        for diagonal in (False, True):
            here = tile_span == own if diagonal else tile_span < own

            @pl.when(jnp.logical_and(here, own < other))
            def _(half=half, diagonal=diagonal):
                dk_low, dv_low = visit(half, diagonal)
                dk_high, dv_high = visit(1 - half, False)
                put(dk_low + dk_high, dv_low + dv_high)

    @pl.when(step == tiles - 1)
    def _():
        for half in range(2):
            for g in range(group):
                here = slice(half * span_len, (half + 1) * span_len)
                turned = rotated(
                    dq_acc[half, g * span_len : (g + 1) * span_len], cosine_ref[here, :], sine_ref[here, :], -1.0
                )
                dq_ref[here, g * HD : (g + 1) * HD] = turned.astype(bf16)


def attention_forward(spans, queries, pieces, span_len):
    tiles = 2 * len(pieces)
    kv_size = len(pieces) * pieces[0].size
    width = queries.shape[1]
    group = width // HD
    rows = group * span_len
    whole = lambda s, t: (0, 0)
    visits = tiles + 1
    return pl.pallas_call(
        functools.partial(forward_kernel, group, span_len, tiles),
        grid_spec=pltpu.PrefetchScalarGridSpec(
            num_scalar_prefetch=1,
            grid=(tiles,),
            in_specs=[
                pl.BlockSpec(queries.shape, whole),
            ]
            + [pl.BlockSpec(memory_space=pltpu.HBM)] * len(pieces),
            out_specs=[
                pl.BlockSpec(queries.shape, whole),
                pl.BlockSpec(queries.shape, whole),
                pl.BlockSpec((2, 1, rows), lambda s, t: (0, 0, 0)),
            ],
            scratch_shapes=[
                pltpu.VMEM((2, rows, HD), bf16),
                pltpu.VMEM((2, rows, HD), f32),
                pltpu.VMEM((2, rows, 128), f32),
                pltpu.VMEM((len(pieces),) + pieces[0].shape, bf16),
                pltpu.SemaphoreType.DMA((len(pieces),)),
            ],
        ),
        out_shape=[
            jax.ShapeDtypeStruct(queries.shape, bf16),
            jax.ShapeDtypeStruct(queries.shape, f32),
            jax.ShapeDtypeStruct((2, 1, rows), f32),
        ],
        compiler_params=pltpu.CompilerParams(vmem_limit_bytes=14 * 1024 * 1024 + 2 * kv_size),
        cost_estimate=pl.CostEstimate(
            flops=visits * rows * span_len * HD * 4,
            bytes_accessed=kv_size * 2 + queries.size * 12,
            transcendentals=visits * rows * span_len * 2,
        ),
        name="attention_forward",
    )(spans, queries, *pieces)


def attention_backward(spans, queries, grads, exact, lse, table, pieces, span_len):
    tiles = 2 * len(pieces)
    kv_size = len(pieces) * pieces[0].size
    width = queries.shape[1]
    group = width // HD
    rows = group * span_len
    whole = lambda s, t: (0, 0)
    visits = tiles + 1
    return pl.pallas_call(
        functools.partial(backward_kernel, group, span_len, tiles),
        grid_spec=pltpu.PrefetchScalarGridSpec(
            num_scalar_prefetch=1,
            grid=(tiles,),
            in_specs=[
                pl.BlockSpec(queries.shape, whole),
                pl.BlockSpec(queries.shape, whole),
                pl.BlockSpec(queries.shape, whole),
                pl.BlockSpec((2, 1, rows), lambda s, t: (0, 0, 0)),
                pl.BlockSpec(table[0].shape, whole),
                pl.BlockSpec(table[0].shape, whole),
            ]
            + [pl.BlockSpec(memory_space=pltpu.HBM)] * len(pieces),
            out_specs=[
                pl.BlockSpec(queries.shape, whole),
                pl.BlockSpec((span_len, 2 * HD), lambda s, t: (jnp.minimum(s, tiles // 2 - 1), 0)),
                pl.BlockSpec((span_len, 2 * HD), lambda s, t: (jnp.maximum(s - tiles // 2, 0), 0)),
            ],
            scratch_shapes=[
                pltpu.VMEM((2, rows, HD), bf16),
                pltpu.VMEM((2, rows, HD), bf16),
                pltpu.VMEM((2, 1, rows), f32),
                pltpu.VMEM((2, rows, HD), f32),
                pltpu.VMEM((len(pieces),) + pieces[0].shape, bf16),
                pltpu.SemaphoreType.DMA((len(pieces),)),
            ],
        ),
        out_shape=[
            jax.ShapeDtypeStruct(queries.shape, bf16),
            jax.ShapeDtypeStruct((tiles * span_len // 2, 2 * HD), bf16),
            jax.ShapeDtypeStruct((tiles * span_len // 2, 2 * HD), bf16),
        ],
        compiler_params=pltpu.CompilerParams(vmem_limit_bytes=18 * 1024 * 1024 + 2 * kv_size),
        cost_estimate=pl.CostEstimate(
            flops=visits * rows * span_len * HD * 10,
            bytes_accessed=kv_size * 4 + queries.size * 16,
            transcendentals=visits * rows * span_len * 2,
        ),
        name="attention_backward",
    )(spans, queries, grads, exact, lse, *table, *pieces)


def product(left, right, left_dim, right_dim, out=f32):
    result = lax.dot_general(left, right, (((left_dim,), (right_dim,)), ((), ())), preferred_element_type=f32)
    return result.astype(out)


def on_device(
    hidden_in,
    out_grad,
    span_order,
    w_query,
    w_key,
    w_value,
    w_output,
    w_gate,
    w_up,
    w_down,
    norm_scales,
):
    local_rows = hidden_in.shape[0]
    head_count = lax.axis_size("head")
    block_count = lax.axis_size("blk")
    block_index = lax.axis_index("blk")
    head_index = lax.axis_index("head")
    group_rows = local_rows * head_count
    span_len = group_rows // 2
    model_rows, query_width = w_query.shape
    model_width = hidden_in.shape[1]
    query_heads = query_width // HD
    half_units = w_gate.shape[1] // 2

    chip_masks = bits(block_count)[1:]
    pair, top = chip_masks[0], chip_masks[-1]
    far_masks = chip_masks[:0:-1]
    head_axes = [(0, mask) for mask in bits(head_count)]
    unit_axes = head_axes + [(pair, 0)]
    unit_side = (block_index // pair) % 2
    bit_count = len(chip_masks) + 1

    def side(mask):
        return (block_index // mask) % 2

    def send(value, mask, *after):
        return swap(tie(value, *after), (mask, 0))

    def segment(body, inputs, after=(), flying=()):
        inputs, after = lax.optimization_barrier((tuple(inputs), after))
        shapes = jax.eval_shape(body, *inputs)

        def nothing(*_):
            return jax.tree.map(lambda x: jnp.zeros(x.shape, x.dtype), shapes)

        results = lax.cond(span_order[0] >= 0, body, nothing, *inputs)
        return lax.optimization_barrier((results, flying))

    def far_spread(value, *after):
        held = {0: value}
        for mask in far_masks:
            for have in list(held):
                held[have ^ mask] = send(held[have], mask, *after)
        return held

    def near_spread(held, *after):
        return held | {have ^ pair: send(block, pair, *(after if have == 0 else ())) for have, block in held.items()}

    def split_dims(partial):
        return partial.reshape((2,) * bit_count + (-1, partial.shape[-1]))

    def halve(value, dim, mask, *after):
        moved = send(pick(value, dim, 1 - side(mask)), mask, *after)
        return plus(pick(value, dim, side(mask)), moved)

    slot = jnp.arange(head_count, dtype=jnp.int32) ^ head_index
    in_block = (slot[:, None] * local_rows + jnp.arange(local_rows, dtype=jnp.int32)[None, :]).reshape(-1)
    head_side = head_index // (head_count // 2)
    own_spans = jnp.stack([span_order[2 * block_index + head_side], span_order[2 * block_index + 1 - head_side]])
    row_spans = jnp.repeat(own_spans, span_len)
    position = row_spans * span_len + in_block % span_len
    even_masks = [0]
    for mask in chip_masks[::-1]:
        even_masks = even_masks + [have ^ mask for have in even_masks]
    slot_masks = even_masks + [mask ^ 1 for mask in even_masks]
    tile_blocks = jnp.array(slot_masks, jnp.int32) ^ block_index
    tile_slots = (2 * tile_blocks[:, None] + jnp.stack([head_side, 1 - head_side])[None, :]).reshape(-1)
    flip = (head_index % (head_count // 2)) * local_rows
    spans = jnp.concatenate([span_order[tile_slots], own_spans, flip[None]]).astype(jnp.int32)
    table = rotation(position)

    scale_count = norm_scales.shape[0]
    kv_at = head_index * query_heads // (H // KVH) * HD
    kv_local = jnp.concatenate(
        [
            lax.dynamic_slice_in_dim(w_key, kv_at, HD, 1),
            lax.dynamic_slice_in_dim(w_value, kv_at, HD, 1),
        ],
        1,
    )
    scale_local = jnp.pad(norm_scales, ((0, 16 - scale_count), (0, 2 * HD - model_rows)))
    kv_local = jnp.concatenate([kv_local, scale_local], 0)

    def half(local, index):
        return lax.dynamic_slice_in_dim(local, index * half_units, half_units, 1)

    def unit_slices():
        weights = (w_gate, w_up, w_down.T)
        return (
            half(w_gate, unit_side),
            jnp.concatenate([half(w, unit_side) for w in weights[1:]], 1),
            jnp.concatenate([half(w, 1 - unit_side) for w in weights[:2]], 1),
            half(weights[2], 1 - unit_side),
        )

    hidden_near = [swap(hidden_in, axis) for axis in head_axes]
    kv_chips = far_spread(kv_local)
    kv_chips.pop(0)
    kv_chips[pair] = send(kv_local, pair)
    (query_output_local, unit_local), (hidden_near, kv_chips) = segment(
        lambda w_query, w_output: (jnp.concatenate([w_query, w_output.T], 1), unit_slices()),
        (w_query, w_output),
        (table,),
        (hidden_near, kv_chips),
    )
    first_mine, second_mine, first_theirs, second_theirs = unit_local

    def first_rows(hidden_near, kv_chips):
        held = {0: kv_local} | kv_chips
        held |= {mask ^ pair: swap(block, (pair, 0)) for mask, block in kv_chips.items() if mask != pair}
        parts = {0: [hidden_in]} | {1 << at: [part] for at, part in enumerate(hidden_near)}
        for subset in range(1, head_count):
            if subset not in parts:
                ways = route(subset, len(head_axes), False)
                cuts = shares(local_rows, len(ways)) if len(ways) > 1 else [(0, local_rows)]
                parts[subset] = [
                    swap(parts[subset ^ (1 << way)][0][low:high], head_axes[way]) for way, (low, high) in zip(ways, cuts)
                ]
        def normed_keys(held, parts):
            came = ()
            for mask, block in list(held.items()):
                held[mask ^ 1] = swap(tie(block, *came), (1, 0))
                came = (held[mask ^ 1],)
            scale_blocks = place_scales(held, model_rows, block_index)
            scale_rows = scale_blocks.reshape(block_count, 16, 2 * HD)[:, :scale_count, :model_rows]
            scale_rows = scale_rows.transpose(1, 0, 2).reshape(scale_count, model_width).astype(f32)
            arrays = [part for slot in sorted(parts) for part in parts[slot]]
            normed_full, inverse_full = whole_call(
                functools.partial(norm_full_kernel, len(arrays)),
                [((group_rows, model_width), bf16), ((group_rows, 1), f32)],
                *arrays,
                scale_rows,
                name="norm_full",
            )
            kv_held = {mask: (block, 0) for mask, block in held.items()}
            kv_rows, kv_weight = project(normed_full, [kv_held], [2 * HD], table, 1, block_index, "key_rows")
            return kv_rows, kv_weight, scale_rows, normed_full, inverse_full

        first = held[pair ^ top], *[part for slot, pieces in parts.items() if slot.bit_count() > 1 for part in pieces]
        query_output = {mask: send(query_output_local, mask, *first) for mask in (*far_masks, pair)}
        results, query_output = segment(normed_keys, (held, parts), (), query_output)
        return results, parts, query_output

    first_results, hidden_parts, query_output_chips = first_rows(hidden_near, kv_chips)
    kv_rows, kv_weight, scale_rows, normed_full, inverse_full = first_results
    hidden_slots = [part for slot in sorted(hidden_parts) for part in hidden_parts[slot]]
    row_shape = (local_rows, model_width)
    scale_shape = (1, model_width)

    if len(far_masks) > 1:
        query_output_chips = far_spread(query_output_local) | {pair: query_output_chips[pair]}
    query_output_chips[0] = query_output_local
    kv_far = far_spread(kv_rows)
    kv_far.pop(0)
    kv_near = send(kv_rows, pair)
    query_output_last = {
        mask ^ pair: send(block, pair, kv_rows) for mask, block in query_output_chips.items() if mask & ~pair
    }

    def beside_keys(kv_rows):
        cores, came = {}, ()
        for mask, block in ({-1: kv_rows} | query_output_chips).items():
            cores[mask] = swap(tie(block, *came), (1, 0))
            came = (cores[mask],)
        return cores

    cores, (kv_far, kv_near, query_output_last) = segment(
        beside_keys, (kv_rows,), (), (kv_far, kv_near, query_output_last)
    )

    def keys_and_queries(kv_far, kv_near, query_output_last):
        across = {mask ^ pair: swap(block, (pair, 0)) for mask, block in kv_far.items()}
        chips = query_output_chips | query_output_last
        held = query_output_last | {-1 - mask: piece for mask, piece in ({pair: kv_near} | kv_far).items()}
        came, others = (), dict(cores)
        for mask, block in held.items():
            others[mask] = swap(tie(block, *came), (1, 0))
            came = (others[mask],)
        chips |= {mask ^ 1: block for mask, block in others.items() if mask >= 0}
        queries, query_weight, output_weight = project(
            normed_full,
            [{mask: (block, column) for mask, block in chips.items()} for column in (0, query_width)],
            [query_width, query_width],
            table,
            query_heads,
            block_index,
            "query_rows",
        )
        came += (queries,)
        for mask, block in across.items():
            others[-1 - mask] = swap(tie(block, *came), (1, 0))
            came = (others[-1 - mask],)
        pieces = {(-1 - mask) ^ 1: piece for mask, piece in others.items() if mask < 0}
        return across | pieces, query_weight, output_weight, queries

    first_near = far_spread(first_mine, kv_far[top])
    (kv_others, query_weight, output_weight, queries), first_near = segment(
        keys_and_queries, (kv_far, kv_near, query_output_last), (), first_near
    )
    kv_held = {0: kv_rows, pair: kv_near} | kv_far | kv_others
    kv_pieces = [kv_held[mask] for mask in slot_masks]

    def row_sum(partial, axes, light=False):
        shaped = partial.reshape(1 << len(axes), local_rows, model_width)
        return scatter_rows([shaped[i] for i in range(1 << len(axes))], axes, light)

    def attend(queries, first_near, second_mine):
        mixed, exact, lse = attention_forward(spans, queries, kv_pieces, span_len)
        cores = in_turn(first_near | {-1: second_mine})
        second_core = cores.pop(-1)
        first_core = {mask ^ 1: block for mask, block in cores.items()}
        mixed = tie(mixed, first_core, second_core)
        terms = row_sum(product(mixed, output_weight, 1, 1, bf16), head_axes)
        rows = whole_call(
            functools.partial(after_attention_kernel, len(terms)),
            [(row_shape, f32), (row_shape, f32), (row_shape, bf16)],
            *terms,
            hidden_in,
            scale_rows,
            name="after_attention",
        )
        return (mixed, exact, lse, *rows, first_core, second_core)

    second_near = far_spread(second_mine, queries)
    first_cross = send(first_theirs, pair, queries)
    (mixed, exact, lse, attn_out, resid, ffn_in, first_core, second_core), (second_near, first_cross) = segment(
        attend, (queries, first_near, second_mine), (), (second_near, first_cross)
    )
    second_far = {mask: block for mask, block in second_near.items() if mask}

    def join_units(ffn_in, first_cross, second_far):
        parts = {0: [ffn_in]}
        plan = hops(len(unit_axes), True)
        parts |= gather_hop(parts, unit_axes, True, plan[0])
        flat = [part for t in plan[0][:-1] for part in parts[t]]
        parts |= gather_hop(parts, unit_axes, True, plan[1], flat)

        def later_hops(parts):
            parts = gather_rows(None, unit_axes, True, parts)
            third = [part for t in parts if t.bit_count() > 1 and t != len(parts) - 1 for part in parts[t]]
            first_core = swap(tie(first_cross, *parts[len(parts) // 2]), (1, 0))
            second_cores = {
                mask ^ 1: swap(tie(block, *third, first_core), (1, 0)) for mask, block in second_far.items()
            }
            return join_rows(parts), first_core, second_cores

        second_cross = send(second_theirs, pair, parts)
        return segment(later_hops, (parts,), (), second_cross)

    first_across = far_spread(first_cross, ffn_in)
    ((ffn_full, cross_core, far_cores), second_cross), first_across = segment(
        join_units, (ffn_in, first_cross, second_far), (), first_across
    )
    second_held = second_near | {1: second_core} | far_cores

    def gate_and_up(ffn_full, first_across):
        cores = {1: cross_core} | {mask ^ 1: swap(block, (1, 0)) for mask, block in first_across.items() if mask}
        across = {mask ^ pair: block for mask, block in (first_across | cores).items()}
        gate_held = {mask: (block, 0) for mask, block in (first_near | first_core | across).items()}
        up_held = {mask: (block, 0) for mask, block in second_held.items()}
        up_held |= {mask: (block, half_units) for mask, block in across.items()}
        units = hidden_units(ffn_full, [gate_held, up_held], half_units, block_index)
        return units, swap(second_cross, (1, 0))

    second_across = far_spread(second_cross, ffn_full)
    ((hidden, active, slope, gate_weight, up_weight), second_cross_core), second_across = segment(
        gate_and_up, (ffn_full, first_across), (), second_across
    )
    down_held = {mask: (block, half_units) for mask, block in second_held.items()}
    down_held |= {mask ^ pair: (block, 0) for mask, block in second_across.items()}
    down_held |= {
        mask ^ pair ^ 1: (swap(block, (1, 0)) if mask else second_cross_core, 0)
        for mask, block in second_across.items()
    }
    *ffn_parts, down_weight = down_rows(hidden, down_held, block_index, 1 << len(unit_axes))
    ffn_terms = scatter_rows(ffn_parts, unit_axes)
    layer_out, grad_ffn_out, scale_grad3 = whole_call(
        functools.partial(after_ffn_kernel, len(ffn_terms)),
        [(row_shape, bf16), (row_shape, bf16), (scale_shape, f32)],
        *ffn_terms,
        resid,
        out_grad,
        scale_rows,
        name="after_ffn",
    )

    def unit_core(partial):
        summed = halve(split_dims(partial), bit_count - 1, 1).astype(bf16)
        return pick(summed, 0, 1 - side(top)), pick(summed, 0, side(top))

    def unit_sides(kept, came):
        part = plus(kept, came).astype(bf16)
        for mask in far_masks[1:]:
            part = halve(part, 0, mask).astype(bf16)
        return pick(part, 0, 1 - unit_side), pick(part, 0, unit_side)

    def unit_whole(own, other):
        low = jnp.where(unit_side == 0, own, other)
        high = jnp.where(unit_side == 0, other, own)
        return jnp.concatenate([low, high], 1).astype(f32)

    def core_sum(partial):
        return halve(split_dims(partial), bit_count - 1, 1).astype(bf16)

    grad_ffn_full = join_rows(gather_rows(grad_ffn_out, unit_axes))
    grad_down = product(grad_ffn_full, hidden, 0, 0, bf16)
    grad_hidden = product(tie(grad_ffn_full, grad_down), down_weight, 1, 0)
    grad_gate_act = (grad_hidden * slope).astype(bf16)
    grad_up_act = (grad_hidden * active).astype(bf16)
    down_away, down_kept = unit_core(grad_down)
    down_came = send(down_away, top)

    def weight_back(act):
        return product(ffn_full, act, 0, 0, bf16)

    back_plan = scatter_plan(len(unit_axes), True)
    split_at = next(i for i, hop in enumerate(back_plan) if 1 << (len(unit_axes) - 1) in hop)

    def beside_hops(bodies):
        results = []

        def beside(number):
            def run(moved):
                if number >= len(bodies):
                    return None, moved
                result, moved = segment(bodies[number], tuple(results[-1:]), (), moved)
                results.append(result)
                return result, moved

            return run

        return beside, results

    def ffn_back_first(grad_gate_act, grad_up_act):
        parts = two_products(grad_gate_act, gate_weight, grad_up_act, up_weight, 1 << len(unit_axes))
        pieces, came = {t: [part] for t, part in enumerate(parts)}, ()
        beside, results = beside_hops([lambda: weight_back(tie(grad_gate_act, *parts)), unit_core])
        for number, subsets in enumerate(back_plan[:split_at]):
            pieces, came, _ = scatter_hop(pieces, unit_axes, True, subsets, came, beside(number))
        return pieces, results[1]

    (ffn_pieces, (gate_away, gate_kept)), down_came = segment(
        ffn_back_first, (grad_gate_act, grad_up_act), (down_away, down_kept), down_came
    )

    def ffn_back_last(ffn_pieces, grad_up_act, down_came):
        last = 1 << (len(unit_axes) - 1)

        def over_head(pieces, grad_up_act):
            came = ()
            beside, results = beside_hops(
                [lambda: weight_back(grad_up_act), lambda partial: (unit_core(partial), unit_sides(down_kept, down_came))]
            )
            for number, subsets in enumerate(back_plan[split_at:]):
                subsets = [t for t in subsets if t != last]
                pieces, came, _ = scatter_hop(pieces, unit_axes, True, subsets, came, beside(number))
            return pieces[0], results[1]

        pieces = dict(ffn_pieces)
        across = swap(pieces.pop(last)[0], unit_axes[-1])
        (terms, results), across = segment(over_head, (pieces, grad_up_act), (), across)
        rows = whole_call(
            functools.partial(after_ffn_back_kernel, len(terms) + 1),
            [(row_shape, f32), (row_shape, bf16), (scale_shape, f32), (scale_shape, f32)],
            *terms,
            across,
            resid,
            attn_out,
            out_grad,
            scale_rows,
            name="after_ffn_back",
        )
        return (*rows, *results)

    gate_came = [send(gate_away[0], top, down_came), None]
    (grad_resid, grad_attn, scale_grad2, scale_grad1, (up_away, up_kept), (down_far, down_own)), gate_came[0] = segment(
        ffn_back_last, (ffn_pieces, grad_up_act, down_came), (gate_away, gate_kept), gate_came[0]
    )

    def attend_back(grad_attn):
        grad_attn_full = join_rows(gather_rows(grad_attn, head_axes))
        grad_mixed = product(grad_attn_full, output_weight, 1, 0, bf16)
        grad_query_lin, kv_near, kv_far = attention_backward(
            spans, queries, grad_mixed, exact, lse, table, kv_pieces, span_len
        )
        kv_terms = plus(kv_near, swap(kv_far, (1, 0))).astype(bf16).reshape(-1, group_rows, 2 * HD)
        middle = kv_terms.shape[0] // 2
        return grad_attn_full, grad_query_lin, kv_terms[:middle], kv_terms[middle:]

    gate_came[1] = send(gate_away[1], top, grad_attn)
    up_came = [send(up_away[0], top, grad_attn), None]
    down_other = send(down_far, pair, grad_attn)
    (grad_attn_full, grad_query_lin, kv_kept, kv_away), (gate_came[1], up_came[0], down_other) = segment(
        attend_back, (grad_attn,), (up_away, up_kept, down_far, down_own), (gate_came[1], up_came[0], down_other)
    )

    def projections_back(grad_query_lin, gate_came):
        core = core_sum(outer((normed_full, grad_query_lin), (grad_attn_full, mixed)))
        away, kept = pick(core, bit_count - 2, 1 - unit_side), pick(core, bit_count - 2, unit_side)
        return (away[0], away[1]), kept, unit_sides(gate_kept, jnp.stack(gate_came))

    kv_came = send(kv_away, pair)
    (query_output_away, query_output_kept, (gate_far, gate_own)), kv_came = segment(
        projections_back, (grad_query_lin, gate_came), (), kv_came
    )
    kv_terms = plus(kv_kept, kv_came).astype(bf16)
    for mask in chip_masks[1:-1]:
        middle = kv_terms.shape[0] // 2
        kv_terms = plus(kv_terms[:middle], swap(kv_terms[middle:], (mask, 0))).astype(bf16)

    def beside_last_keys(down_other):
        return unit_whole(down_own, down_other).T

    kv_came = send(kv_terms[1], top)
    gate_other = send(gate_far, pair, kv_terms)
    out_down, (kv_came, gate_other) = segment(beside_last_keys, (down_other,), (kv_terms,), (kv_came, gate_other))

    def normed_rows_back(kv_kept, kv_came):
        normed_plan = scatter_plan(len(head_axes), False)

        def first_sums_back(kv_kept, kv_came):
            (grad_kv_lin,) = whole_call(
                key_value_grad_kernel,
                [((group_rows, 2 * HD), bf16)],
                kv_kept,
                kv_came,
                *table,
                name="key_value_grad",
            )
            *parts, scale_grad0 = normed_back(
                grad_query_lin, query_weight, grad_kv_lin, kv_weight, inverse_full, hidden_slots, head_count
            )

            def key_weights_back(grad_kv_lin, scale_grad0):
                scale_grad = jnp.concatenate([scale_grad0, scale_grad1, scale_grad2, scale_grad3], 0).astype(bf16)
                scale_grad = scale_grad.reshape(scale_count, block_count, model_rows).transpose(1, 0, 2)
                scale_grad = jnp.pad(scale_grad, ((0, 0), (0, 16 - scale_count), (0, 2 * HD - model_rows)))
                partial = outer((normed_full, grad_kv_lin)).reshape(block_count, model_rows, 2 * HD)
                terms = core_sum(jnp.concatenate([partial, scale_grad], 1).reshape(-1, 2 * HD))
                return pick(terms, bit_count - 2, 1 - unit_side), pick(terms, bit_count - 2, unit_side)

            def beside(moved):
                return segment(key_weights_back, (grad_kv_lin, scale_grad0), (), moved)

            pieces = {t: [part] for t, part in enumerate(parts)}
            pieces, _, terms = scatter_hop(pieces, head_axes, False, normed_plan[0], (), beside)
            return pieces, terms

        query_output_came = send(query_output_away[0], pair, kv_came)
        (pieces, (away, kept)), query_output_came = segment(first_sums_back, (kv_kept, kv_came), (), query_output_came)

        def sums_back(pieces):
            came = ()
            for subsets in normed_plan[1:]:
                pieces, came, _ = scatter_hop(pieces, head_axes, False, subsets, came)
            (grad_in,) = whole_call(
                functools.partial(after_all_kernel, len(pieces[0])),
                [(row_shape, f32)],
                *pieces[0],
                hidden_in,
                grad_resid,
                scale_rows,
                name="after_all",
            )
            return grad_in

        wkv_came = send(away, pair)
        grad_in, wkv_came = segment(sums_back, (pieces,), (away, kept), wkv_came)
        wkv_terms = plus(kept, wkv_came).astype(bf16)
        for at, mask in list(enumerate(chip_masks))[1:-1]:
            wkv_terms = halve(wkv_terms, bit_count - 2 - at, mask).astype(bf16)
        return grad_in, pick(wkv_terms, 0, 1 - side(top)), pick(wkv_terms, 0, side(top)), query_output_came

    up_came[1] = send(up_away[1], top, kv_came)
    query_output_came = [None, None]
    (grad_in, wkv_away, wkv_kept, query_output_came[0]), up_came[1] = segment(
        normed_rows_back, (kv_terms[0], kv_came), (out_down, *query_output_away), up_came[1]
    )
    wkv_came = send(wkv_away, top)
    query_output_came[1] = send(query_output_away[1], pair, wkv_away)

    def beside_key_weights(up_came, gate_other):
        return unit_sides(up_kept, jnp.stack(up_came)), unit_whole(gate_own, gate_other)

    ((up_far, up_own), out_gate), (wkv_came, query_output_came[1]) = segment(
        beside_key_weights, (up_came, gate_other), (wkv_away, wkv_kept), (wkv_came, query_output_came[1])
    )
    grad_wkv = plus(wkv_kept, wkv_came).astype(bf16)
    query_output_terms = plus(query_output_kept, jnp.stack(query_output_came)).astype(bf16)
    for at, mask in list(enumerate(chip_masks))[1:-1]:
        query_output_terms = halve(query_output_terms, bit_count - 2 - at, mask).astype(bf16)
    query_output_away = pick(query_output_terms, 0, 1 - side(top))
    query_output_came = send(query_output_away, top)
    up_other = send(up_far, pair, grad_wkv)

    def head_rows(grad_wkv):
        parts = gather_rows(grad_wkv, head_axes)
        wkv_ordered = jnp.zeros((head_count,) + grad_wkv.shape, bf16)
        for mask, pieces in parts.items():
            first = 0
            for piece in pieces:
                wkv_ordered = lax.dynamic_update_slice(wkv_ordered, piece[None], (head_index ^ mask, first, 0))
                first += piece.shape[0]
        wkv_ordered = wkv_ordered.astype(f32)
        scale_total = wkv_ordered[:, model_rows : model_rows + scale_count, :model_rows].sum(0)
        wkv_ordered = wkv_ordered[:, :model_rows].reshape(KVH, head_count // KVH, model_rows, 2, HD).sum(1)
        out_key = wkv_ordered[:, :, 0].transpose(1, 0, 2).reshape(model_rows, KVH * HD)
        out_value = wkv_ordered[:, :, 1].transpose(1, 0, 2).reshape(model_rows, KVH * HD)
        return out_key, out_value, scale_total

    (out_key, out_value, scale_total), (query_output_came, up_other) = segment(
        head_rows, (grad_wkv,), (query_output_away, up_far), (query_output_came, up_other)
    )
    out_query_output = plus(pick(query_output_terms, 0, side(top)), query_output_came)
    out_query = out_query_output[:, :query_width]
    out_output = out_query_output[:, query_width:].T
    out_up = unit_whole(up_own, up_other)

    return (
        layer_out,
        grad_in,
        out_query,
        out_key,
        out_value,
        out_output,
        out_gate,
        out_up,
        out_down,
        scale_total,
    )


def solution(mesh):
    placed = (
        P(("blk", "head"), None),
        P(("blk", "head"), None),
        P(),
        P("blk", "head"),
        P("blk", None),
        P("blk", None),
        P("head", "blk"),
        P("blk", "head"),
        P("blk", "head"),
        P("head", "blk"),
        P(None, "blk"),
    )
    return jax.shard_map(
        on_device,
        mesh=mesh,
        in_specs=placed,
        out_specs=(
            P(("blk", "head"), None),
            P(("blk", "head"), None),
            P("blk", "head"),
            P("blk", None),
            P("blk", None),
            P("head", "blk"),
            P("blk", "head"),
            P("blk", "head"),
            P("head", "blk"),
            P(None, "blk"),
        ),
        check_vma=False,
    )
```

```python
import functools
import math

import jax
import jax.numpy as jnp
from jax import lax
from jax.experimental import pallas as pl
from jax.experimental.pallas import tpu as pltpu
from jax.sharding import PartitionSpec as P

H = 8
KVH = 4
HD = 256

norm_eps = 1e-06
cap_value = 50.0
theta_base = 10000.0
f32 = jnp.float32
bf16 = jnp.bfloat16


def inverse_rms(value):
    return lax.rsqrt(jnp.mean(value * value, axis=-1, keepdims=True) + norm_eps)


def rms_back(value, scale, grad):
    inverse = inverse_rms(value)
    scaled = grad * scale
    inner = jnp.mean(scaled * value, axis=-1, keepdims=True)
    grad_value = inverse * scaled - value * (inverse * inverse * inverse) * inner
    grad_scale = jnp.sum(grad * value * inverse, axis=0, keepdims=True)
    return (grad_value, grad_scale)


def rotation(position):
    entry = jnp.arange(HD, dtype=jnp.int32)
    quarter = HD // 4
    pair_index = entry // (2 * quarter) * quarter + entry % quarter
    frequency = jnp.power(theta_base, -2.0 * pair_index.astype(f32) / HD)
    angles = position.astype(f32)[:, None] * frequency[None, :]
    sign = jnp.where(entry % (2 * quarter) < quarter, -1.0, 1.0)
    return jnp.cos(angles), jnp.sin(angles) * sign[None, :]


def rotated(value, cosine, sine, sign):
    half = HD // 2
    parts = []
    for at in range(0, HD, half):
        piece = value[:, at : at + half]
        partner = pltpu.roll(piece, half // 2, 1)
        parts.append(piece * cosine[:, at : at + half] + partner * (sign * sine[:, at : at + half]))
    return jnp.concatenate(parts, 1)


def swap(value, axis):
    blk_mask, head_mask = axis
    block_count, head_count = lax.axis_size("blk"), lax.axis_size("head")
    if blk_mask == 0:
        return lax.ppermute(value, "head", [(i, i ^ head_mask) for i in range(head_count)])
    return lax.ppermute(value, "blk", [(i, i ^ blk_mask) for i in range(block_count)])


def bits(count):
    return [1 << i for i in range(count.bit_length() - 1)]


def route(subset, total, light):
    members = [i for i in range(total) if subset >> i & 1]
    if light and len(members) > 1 and members[-1] == total - 1:
        members = members[:-1]
        return members if len(members) == total - 1 else members[:1]
    if len(members) >= 2 and len(members) == total - light:
        return members
    if not light and len(members) == 2 and members[1] - members[0] != 1:
        return members[1:]
    return members[:1]


def hops(total, light):
    size = lambda t: bin(t).count("1")
    last = 1 << (total - 1)
    subsets = range(1, 1 << total)
    if not light:
        return [[t for t in subsets if size(t) == n] for n in range(1, total + 1)]
    result = [[t for t in subsets if size(t) == 1]]
    for high in (0, last):
        for n in range(2, total + 1):
            result.append([t for t in subsets if size(t) == n and t & last == high])
    return [hop for hop in result if hop]


def shares(row_total, parts):
    unit = row_total // 16
    cuts = [unit * i // parts * 16 for i in range(parts + 1)]
    cuts[-1] = row_total
    return list(zip(cuts[:-1], cuts[1:]))


def gather_hop(parts, axes, light, subsets, before=()):
    rows = parts[0][0].shape[0]
    came = {}
    for subset in subsets:
        ways = route(subset, len(axes), light)
        cuts = shares(rows, len(ways)) if len(ways) > 1 else [(0, rows)]
        came[subset] = []
        for way, (low, high) in zip(ways, cuts):
            source = parts[subset ^ (1 << way)][0]
            came[subset].append(swap(tie(source[low:high] if len(ways) > 1 else source, *before), axes[way]))
    return came


def gather_rows(value, axes, light=False, parts=None):
    last = 1 << (len(axes) - 1)
    parts, before = parts or {0: [value]}, ()
    for subsets in hops(len(axes), light):
        if all(t in parts for t in subsets):
            continue
        if light and last in parts:
            before = [x for x in before if x is not parts[last][0]]
            before += parts[last] * any(t & last for t in subsets)
        came = gather_hop(parts, axes, light, subsets, before)
        parts = parts | came
        before = [part for pieces in came.values() for part in pieces]
    return parts


def join_kernel(plan, *refs):
    step = pl.program_id(0)
    out = refs[-1]
    for at, (slot, first, rows) in enumerate(plan):

        @pl.when(step == slot)
        def _():
            out[first : first + rows, :] = refs[at][...]


def join_rows(parts):
    plan, arrays = [], []
    for slot in sorted(parts):
        first = 0
        for array in parts[slot]:
            plan.append((slot, first, array.shape[0]))
            arrays.append(array)
            first += array.shape[0]
    rows, columns = parts[0][0].shape
    return pl.pallas_call(
        functools.partial(join_kernel, plan),
        grid=(len(parts),),
        in_specs=[pl.BlockSpec(a.shape, lambda m: (0, 0), pipeline_mode=pl.Buffered(1)) for a in arrays],
        out_specs=pl.BlockSpec((rows, columns), lambda m: (m, 0)),
        out_shape=jax.ShapeDtypeStruct((len(parts) * rows, columns), arrays[0].dtype),
        compiler_params=pltpu.CompilerParams(vmem_limit_bytes=16 * 1024 * 1024),
        cost_estimate=pl.CostEstimate(flops=0, bytes_accessed=4 * len(parts) * rows * columns, transcendentals=0),
        name="join_rows",
    )(*arrays)


def two_products_kernel(a_ref, u_ref, b_ref, v_ref, *outs):
    nt = (((1,), (1,)), ((), ()))
    total = lax.dot_general(a_ref[...], u_ref[...], nt, preferred_element_type=f32)
    total += lax.dot_general(b_ref[...], v_ref[...], nt, preferred_element_type=f32)
    put_pieces(outs, total)


def put_pieces(outs, value):
    rows = outs[0].shape[0]
    for at, out in enumerate(outs):
        out[...] = value[at * rows : (at + 1) * rows].astype(out.dtype)


def two_products(a, u, b, v, count):
    rows, depth = a.shape
    columns = u.shape[0]
    step = 256
    resident = pl.BlockSpec((rows, depth), lambda n: (0, 0), pipeline_mode=pl.Buffered(1))
    return pl.pallas_call(
        two_products_kernel,
        grid=(columns // step,),
        in_specs=[resident, pl.BlockSpec((step, depth), lambda n: (n, 0))] * 2,
        out_specs=[pl.BlockSpec((rows // count, step), lambda n: (0, n))] * count,
        out_shape=[jax.ShapeDtypeStruct((rows // count, columns), bf16)] * count,
        compiler_params=pltpu.CompilerParams(vmem_limit_bytes=20 * 1024 * 1024),
        cost_estimate=pl.CostEstimate(
            flops=4 * rows * columns * depth,
            bytes_accessed=4 * (rows * depth + columns * depth) + 2 * rows * columns,
            transcendentals=0,
        ),
        name="two_products",
    )(a, u, b, v)


def joined(left, right):
    return (left.astype(f32) + right.astype(f32)).astype(bf16)


def scatter_plan(total, light):
    plan = [list(hop) for hop in hops(total, light)[::-1]]
    last = 1 << (total - 1)
    if light:
        plan[-1].remove(last)
        plan[next(i for i, hop in enumerate(plan) if not any(t & last for t in hop))].append(last)
    return plan


def scatter_hop(pieces, axes, light, subsets, before=(), beside=None):
    last = 1 << (len(axes) - 1)
    pieces = dict(pieces)
    rows = pieces[0][0].shape[0]
    sent, result = [], None
    for subset in subsets:
        (piece,) = pieces.pop(subset)
        ways = route(subset, len(axes), light)
        cuts = shares(rows, len(ways)) if len(ways) > 1 else [(0, rows)]
        for way, (low, high) in zip(ways, cuts):
            part = piece if len(ways) == 1 else piece[low:high]
            sent.append((subset, subset ^ (1 << way), low, high, swap(tie(part, *before), axes[way])))
    if beside:
        result, came = beside([item[4] for item in sent])
        sent = [item[:4] + (moved,) for item, moved in zip(sent, came)]
    for subset, target, low, high, moved in sent:
        if target == 0:
            pieces[0] = pieces[0] + [moved]
        elif high - low == rows:
            pieces[target] = [joined(pieces[target][0], moved)]
        else:
            old = pieces[target][0]
            cut = [old[:low], joined(old[low:high], moved), old[high:]]
            pieces[target] = [jnp.concatenate([c for c in cut if c.shape[0]], 0)]
    came = [item[4] for item in sent if not (light and item[0] == last)]
    return pieces, came, result


def scatter_rows(pieces, axes, light=False):
    pieces, came = {t: [piece] for t, piece in enumerate(pieces)}, ()
    for subsets in scatter_plan(len(axes), light):
        pieces, came, _ = scatter_hop(pieces, axes, light, subsets, came)
    return pieces[0]


def tie(value, *after):
    return lax.optimization_barrier((value, *after))[0] if after else value


def tie_all(held, *after):
    return {mask: tie(block, *after) for mask, block in held.items()}


def scale_kernel(count, index_ref, *refs):
    for mask in range(count):
        row = pl.multiple_of((index_ref[0] ^ mask) * 16, 16)
        refs[count][pl.ds(row, 16), :] = refs[mask][...]


def place_scales(held, rows, block_index):
    count = len(held)
    shape = (16, held[0].shape[1])
    return pl.pallas_call(
        functools.partial(scale_kernel, count),
        grid_spec=pltpu.PrefetchScalarGridSpec(
            num_scalar_prefetch=1,
            grid=(1,),
            in_specs=[pl.BlockSpec(shape, lambda n, b: (rows // 16, 0))] * count,
            out_specs=pl.BlockSpec((count * 16, shape[1]), lambda n, b: (0, 0)),
        ),
        out_shape=jax.ShapeDtypeStruct((count * 16, shape[1]), bf16),
        cost_estimate=pl.CostEstimate(flops=0, bytes_accessed=4 * count * 16 * shape[1], transcendentals=0),
        name="place_scales",
    )(block_index[None].astype(jnp.int32), *[held[mask] for mask in range(count)])


def head_kernel(plan, rows, scale_count, index_ref, *refs):
    parts, (key_ref, value_ref, scale_ref) = refs[: len(plan)], refs[len(plan) :]
    step = pl.program_id(0)

    @pl.when(step == 0)
    def _():
        scale_ref[...] = jnp.zeros_like(scale_ref)

    for part, (slot, first) in zip(parts, plan):
        count = part.shape[0]

        @pl.when(step == slot)
        def _():
            last = min(first + count, rows)
            here, taken = slice(first, last), slice(0, last - first)
            key_ref[here, :] = part[taken, :HD].astype(f32)
            value_ref[here, :] = part[taken, HD:].astype(f32)
            if first + count > rows:
                scale_ref[...] += part[rows - first : rows - first + scale_count, :].astype(f32)


def place_heads(parts, rows, scale_count, head_index):
    plan, arrays = [], []
    for slot in sorted(parts):
        first = 0
        for array in parts[slot]:
            plan.append((slot, first))
            arrays.append(array)
            first += array.shape[0]
    columns = pl.BlockSpec((rows, HD), lambda m, h: (0, h[0] ^ m))
    fixed = lambda m, h: (0, 0)
    return pl.pallas_call(
        functools.partial(head_kernel, plan, rows, scale_count),
        grid_spec=pltpu.PrefetchScalarGridSpec(
            num_scalar_prefetch=1,
            grid=(len(parts),),
            in_specs=[pl.BlockSpec(a.shape, fixed, pipeline_mode=pl.Buffered(1)) for a in arrays],
            out_specs=[columns, columns, pl.BlockSpec((scale_count, 2 * HD), fixed)],
        ),
        out_shape=[jax.ShapeDtypeStruct((rows, len(parts) * HD), f32)] * 2
        + [jax.ShapeDtypeStruct((scale_count, 2 * HD), f32)],
        cost_estimate=pl.CostEstimate(flops=0, bytes_accessed=8 * len(parts) * rows * HD, transcendentals=0),
        name="place_heads",
    )(head_index[None].astype(jnp.int32), *arrays)


def placed_kernel(body, plans, counts, steps, index_ref, *refs):
    refs = list(refs)
    arrays, loads, inputs, outs, wholes, weights, loaded = [[refs.pop(0) for _ in range(count)] for count in counts]
    in_sems, out_sems = refs
    step = pl.program_id(0)
    came, at = [], 0
    for source, target in zip(loads, loaded):
        came.append([pltpu.make_async_copy(source, target, in_sems.at[at])])
        at += 1
    gone = [None] * len(loads)
    for weight, plan in zip(weights, plans):
        copies = []
        rows = weight.shape[0] // len(plan)
        for mask, (source, column) in enumerate(plan):
            row = pl.multiple_of((index_ref[0] ^ mask) * rows, 16)
            block = arrays[source].at[pl.ds(0, rows)]
            if arrays[source].shape[1] != weight.shape[1]:
                block = arrays[source].at[pl.ds(0, rows), pl.ds(column, weight.shape[1])]
            copies.append(pltpu.make_async_copy(block, weight.at[pl.ds(row, rows)], in_sems.at[at]))
            at += 1
        came.append(copies)
    gone += [
        pltpu.make_async_copy(weight, whole, out_sems.at[n]) for n, (weight, whole) in enumerate(zip(weights, wholes))
    ]

    @pl.when(step == 0)
    def _():
        for copies in came:
            for copy in copies:
                copy.start()
        for copies, copy_out in zip(came, gone):
            for copy in copies:
                copy.wait()
            if copy_out is not None:
                copy_out.start()

    body(step, loaded + inputs, outs, weights)

    @pl.when(step == steps - 1)
    def _():
        for copy_out in gone[len(loads) :]:
            copy_out.wait()


def placed(body, steps, held, columns, loads, inputs, in_specs, outs, out_specs, block_index, name, flops, vmem):
    arrays, plans = [], []
    for blocks, width in zip(held, columns):
        plan = []
        for mask in range(len(blocks)):
            array, column = blocks[mask]
            if width % 128 or column % 128:
                array, column = array[:, column : column + width], 0
            where = next((n for n, known in enumerate(arrays) if known is array), len(arrays))
            if where == len(arrays):
                arrays.append(array)
            plan.append((where, column))
        plans.append(plan)
    rows = min(array.shape[0] for array in arrays) // 16 * 16
    rows = rows - (16 if name == "key_rows" else 0)
    shapes = [(len(plan) * rows, width) for plan, width in zip(plans, columns)]
    anywhere = pl.BlockSpec(memory_space=pltpu.HBM)
    counts = (len(arrays), len(loads), len(inputs), len(outs), len(plans), len(plans), len(loads))
    return pl.pallas_call(
        functools.partial(placed_kernel, body, plans, counts, steps),
        grid_spec=pltpu.PrefetchScalarGridSpec(
            num_scalar_prefetch=1,
            grid=(steps,),
            in_specs=[anywhere] * (len(arrays) + len(loads)) + in_specs,
            out_specs=out_specs + [anywhere] * len(plans),
            scratch_shapes=[pltpu.VMEM(shape, bf16) for shape in shapes]
            + [pltpu.VMEM(array.shape, array.dtype) for array in loads]
            + [
                pltpu.SemaphoreType.DMA((sum(len(plan) for plan in plans) + len(loads),)),
                pltpu.SemaphoreType.DMA((len(plans),)),
            ],
        ),
        out_shape=outs + [jax.ShapeDtypeStruct(shape, bf16) for shape in shapes],
        compiler_params=pltpu.CompilerParams(vmem_limit_bytes=vmem * 1024 * 1024),
        cost_estimate=pl.CostEstimate(
            flops=flops, bytes_accessed=4 * sum(h * w for h, w in shapes), transcendentals=0
        ),
        name=name,
    )(block_index[None].astype(jnp.int32), *arrays, *loads, *inputs)


def in_turn(held):
    came = []
    for block in held.values():
        came.append(swap(tie(block, *came[-2:-1]), (1, 0)))
    return dict(zip(held, came))


def both_cores(held):
    return held | {mask ^ 1: swap(block, (1, 0)) for mask, block in held.items()}


def pick(value, dim, index):
    return lax.dynamic_index_in_dim(value, index, dim, keepdims=False)


def plus(left, right):
    return left.astype(f32) + right.astype(f32)


def whole_call(body, outs, *inputs, name):
    size = sum(x.size * x.dtype.itemsize for x in inputs)
    return pl.pallas_call(
        body,
        out_shape=[jax.ShapeDtypeStruct(shape, dtype) for shape, dtype in outs],
        compiler_params=pltpu.CompilerParams(vmem_limit_bytes=28 * 1024 * 1024),
        cost_estimate=pl.CostEstimate(flops=0, bytes_accessed=2 * size, transcendentals=0),
        name=name,
    )(*inputs)


def summed(refs):
    total = refs[0][...].astype(f32)
    for ref in refs[1:]:
        total = total + ref[...].astype(f32)
    return total


def norm_full_kernel(count, *refs):
    parts, (scale, normed, inverse) = refs[:count], refs[count:]
    first = 0
    for part in parts:
        value = part[...].astype(f32)
        here = slice(first, first + part.shape[0])
        first += part.shape[0]
        factor = inverse_rms(value)
        inverse[here, :] = factor
        normed[here, :] = (value * factor * scale[0:1, :]).astype(bf16)


def after_attention_kernel(count, *refs):
    terms, (hidden, scales, attn_out, resid_out, ffn_in) = refs[:count], refs[count:]
    attn = summed(terms)
    attn_out[...] = attn
    resid = hidden[...].astype(f32) + attn * inverse_rms(attn) * scales[1:2, :]
    resid_out[...] = resid
    ffn_in[...] = (resid * inverse_rms(resid) * scales[2:3, :]).astype(bf16)


def after_ffn_kernel(count, *refs):
    terms, (resid, out_grad, scales, layer_out, grad_out, grad_scale) = refs[:count], refs[count:]
    ffn_out = summed(terms)
    grad, grad_scale[...] = rms_back(ffn_out, scales[3:4, :], out_grad[...].astype(f32))
    grad_out[...] = grad.astype(bf16)
    layer_out[...] = (resid[...] + ffn_out * inverse_rms(ffn_out) * scales[3:4, :]).astype(bf16)


def after_ffn_back_kernel(count, *refs):
    terms, (resid, attn, out_grad, scales, grad_resid, grad_attn, grad_scale2, grad_scale1) = refs[:count], refs[count:]
    grad, grad_scale2[...] = rms_back(resid[...], scales[2:3, :], summed(terms))
    grad = out_grad[...].astype(f32) + grad
    grad_resid[...] = grad
    back, grad_scale1[...] = rms_back(attn[...], scales[1:2, :], grad)
    grad_attn[...] = back.astype(bf16)


def after_all_kernel(count, *refs):
    terms, (hidden, grad_resid, scales, grad_in) = refs[:count], refs[count:]
    grad, _ = rms_back(hidden[...].astype(f32), scales[0:1, :], summed(terms))
    grad_in[...] = grad_resid[...] + grad


def key_value_grad_kernel(kept, came, cosine, sine, out):
    total = kept[...].astype(f32) + came[...].astype(f32)
    out[:, :HD] = rotated(total[:, :HD], cosine[...], sine[...], -1.0).astype(bf16)
    out[:, HD:] = total[:, HD:].astype(bf16)


def project(rows, held, columns, table, turning, block_index, name):
    count, depth = rows.shape
    heads = columns[0] // HD
    fixed = lambda n, b: (0, 0)
    once = pl.Buffered(1)

    def body(step, inputs, outs, weights):
        rows_ref, cosine_ref, sine_ref = inputs
        (out_ref,) = outs
        here = pl.ds(pl.multiple_of(step * HD, HD), HD)
        value = jnp.dot(rows_ref[...], weights[0][:, here], preferred_element_type=f32)

        @pl.when(step < turning)
        def _():
            out_ref[...] = rotated(value, cosine_ref[...], sine_ref[...], 1.0).astype(bf16)

        @pl.when(step >= turning)
        def _():
            out_ref[...] = value.astype(bf16)

    return placed(
        body,
        heads,
        held,
        columns,
        [rows],
        list(table),
        [
            pl.BlockSpec((count, HD), fixed, pipeline_mode=once),
            pl.BlockSpec((count, HD), fixed, pipeline_mode=once),
        ],
        [jax.ShapeDtypeStruct((count, columns[0]), bf16)],
        [pl.BlockSpec((count, HD), lambda n, b: (0, n))],
        block_index,
        name,
        2 * rows.size * columns[0],
        20,
    )


def hidden_units(rows, held, width, block_index):
    count, depth = rows.shape
    step = 256

    def body(number, inputs, outs, weights):
        hidden_ref, active_ref, slope_ref = outs
        gate = jnp.dot(inputs[0][...], weights[0][...], preferred_element_type=f32)
        up = jnp.dot(inputs[0][...], weights[1][...], preferred_element_type=f32)
        inner = math.sqrt(2.0 / math.pi)
        square = gate * gate
        tangent = jnp.tanh(inner * gate * (1.0 + 0.044715 * square))
        share = 0.5 * (1.0 + tangent)
        active = gate * share
        slope = share + (0.5 * inner) * gate * (1.0 - tangent * tangent) * (1.0 + (3 * 0.044715) * square)
        hidden_ref[...] = (active * up).astype(bf16)
        active_ref[...] = active
        slope_ref[...] = slope * up

    return placed(
        body,
        count // step,
        held,
        [width, width],
        [],
        [rows],
        [pl.BlockSpec((step, depth), lambda n, b: (n, 0))],
        [jax.ShapeDtypeStruct((count, width), dtype) for dtype in (bf16, f32, f32)],
        [pl.BlockSpec((step, width), lambda n, b: (n, 0))] * 3,
        block_index,
        "hidden_units",
        4 * rows.size * width,
        40,
    )


def down_rows(hidden, held, block_index, pieces):
    count, width = hidden.shape
    depth = len(held) * held[0][0].shape[0]
    step = 768 if depth % 768 == 0 else 256

    def body(number, inputs, outs, weights):
        here = pl.ds(pl.multiple_of(number * step, step), step)
        value = lax.dot_general(
            inputs[0][...], weights[0][here, :], (((1,), (1,)), ((), ())), preferred_element_type=f32
        )
        put_pieces(outs, value)

    return placed(
        body,
        depth // step,
        [held],
        [width],
        [hidden],
        [],
        [],
        [jax.ShapeDtypeStruct((count // pieces, depth), bf16)] * pieces,
        [pl.BlockSpec((count // pieces, step), lambda n, b: (0, n))] * pieces,
        block_index,
        "down_rows",
        2 * hidden.size * depth,
        24,
    )


def outer_kernel(*refs):
    pairs, out = refs[:-1], refs[-1]
    width = 0
    for left, right in zip(pairs[::2], pairs[1::2]):
        columns = right.shape[1]
        value = lax.dot_general(left[...], right[...], (((0,), (0,)), ((), ())), preferred_element_type=f32)
        out[:, width : width + columns] = value.astype(bf16)
        width += columns


def outer(*pairs):
    rows, depth = pairs[0][0].shape
    width = sum(right.shape[1] for _, right in pairs)
    step = depth // 2
    specs = []
    for _, right in pairs:
        specs.append(pl.BlockSpec((rows, step), lambda n: (0, n)))
        specs.append(pl.BlockSpec(right.shape, lambda n: (0, 0), pipeline_mode=pl.Buffered(1)))
    return pl.pallas_call(
        outer_kernel,
        grid=(depth // step,),
        in_specs=specs,
        out_specs=pl.BlockSpec((step, width), lambda n: (n, 0)),
        out_shape=jax.ShapeDtypeStruct((depth, width), bf16),
        compiler_params=pltpu.CompilerParams(vmem_limit_bytes=24 * 1024 * 1024),
        cost_estimate=pl.CostEstimate(
            flops=2 * rows * depth * width, bytes_accessed=2 * (rows * depth * len(pairs) + depth * width), transcendentals=0
        ),
        name="outer",
    )(*[x for pair in pairs for x in pair])


def normed_back_kernel(count, q_ref, wq_ref, kv_ref, wkv_ref, inverse_ref, *refs):
    hidden, (*outs, scale_ref) = refs[:count], refs[count:]
    nt = (((1,), (1,)), ((), ()))
    total = lax.dot_general(q_ref[...], wq_ref[...], nt, preferred_element_type=f32)
    total += lax.dot_general(kv_ref[...], wkv_ref[...], nt, preferred_element_type=f32)
    put_pieces(outs, total)
    grad_scale, first = jnp.zeros((1, total.shape[1]), f32), 0
    for part in hidden:
        here = slice(first, first + part.shape[0])
        first += part.shape[0]
        unit = part[...].astype(f32) * inverse_ref[here, :]
        grad_scale += jnp.sum(total[here, :] * unit, axis=0, keepdims=True)
    scale_ref[...] = grad_scale


def normed_back(grad_query, query_weight, grad_kv, kv_weight, inverse, hidden, pieces):
    rows, width = grad_query.shape
    kv_width = grad_kv.shape[1]
    columns = query_weight.shape[0]
    step = 768 if columns % 768 == 0 else 256
    fixed = lambda n: (0, 0)
    once = pl.Buffered(1)
    return pl.pallas_call(
        functools.partial(normed_back_kernel, len(hidden)),
        grid=(columns // step,),
        in_specs=[
            pl.BlockSpec((rows, width), fixed, pipeline_mode=once),
            pl.BlockSpec((step, width), lambda n: (n, 0)),
            pl.BlockSpec((rows, kv_width), fixed, pipeline_mode=once),
            pl.BlockSpec((step, kv_width), lambda n: (n, 0)),
            pl.BlockSpec((rows, 1), fixed, pipeline_mode=once),
        ]
        + [pl.BlockSpec((part.shape[0], step), lambda n: (0, n)) for part in hidden],
        out_specs=[pl.BlockSpec((rows // pieces, step), lambda n: (0, n))] * pieces
        + [pl.BlockSpec((1, step), lambda n: (0, n))],
        out_shape=[jax.ShapeDtypeStruct((rows // pieces, columns), bf16)] * pieces
        + [jax.ShapeDtypeStruct((1, columns), f32)],
        compiler_params=pltpu.CompilerParams(vmem_limit_bytes=20 * 1024 * 1024),
        cost_estimate=pl.CostEstimate(
            flops=2 * rows * columns * (width + kv_width), bytes_accessed=4 * rows * columns, transcendentals=0
        ),
        name="normed_back",
    )(grad_query, query_weight, grad_kv, kv_weight, inverse, *hidden)


def scores(query, key, score_scale):
    raw = lax.dot_general(query, key, (((1,), (1,)), ((), ())), preferred_element_type=f32)
    return jnp.tanh(raw * (score_scale / cap_value))


def load_pieces(step, pieces, kv_all, sems):
    copies = [pltpu.make_async_copy(piece, kv_all.at[at], sems.at[at]) for at, piece in enumerate(pieces)]

    @pl.when(step == 0)
    def _():
        for copy in copies:
            copy.start()

    for at, copy in enumerate(copies):

        @pl.when(step == 2 * at)
        def _():
            copy.wait()


def forward_kernel(group, span_len, tiles, spans_ref, q_ref, *refs):
    pieces, (mixed_ref, exact_ref, lse_ref, q_all, acc, total, kv_all, sems) = refs[: tiles // 2], refs[tiles // 2 :]
    step = pl.program_id(0)
    load_pieces(step, pieces, kv_all, sems)
    score_scale = 1.0 / math.sqrt(HD)
    rows = group * span_len

    @pl.when(step == 0)
    def _():
        for half in range(2):
            for g in range(group):
                q_all[half, g * span_len : (g + 1) * span_len, :] = q_ref[
                    half * span_len : (half + 1) * span_len, g * HD : (g + 1) * HD
                ]
        acc[...] = jnp.zeros_like(acc)
        total[...] = jnp.zeros_like(total)

    tile_span = spans_ref[step]
    here = pl.ds(pl.multiple_of((step % 2) * span_len, span_len), span_len)
    key = kv_all[step // 2, here, :HD]
    value = kv_all[step // 2, here, HD:]

    def visit(half, diagonal):
        weights = jnp.exp(cap_value * scores(q_all[half], key, score_scale))
        if diagonal:
            flip = spans_ref[tiles + 2]
            shape = (rows, span_len)
            q_pos = (lax.broadcasted_iota(jnp.int32, shape, 0) % span_len) ^ flip
            k_pos = lax.broadcasted_iota(jnp.int32, shape, 1) ^ flip
            weights = jnp.where(k_pos <= q_pos, weights, 0.0)
        part = weights[:, :128]
        for at in range(128, span_len, 128):
            part = part + weights[:, at : at + 128]
        total[half] += part
        acc[half] += jnp.dot(weights.astype(bf16), value, preferred_element_type=f32)

    for half in range(2):
        own = spans_ref[tiles + half]

        @pl.when(tile_span < own)
        def _():
            visit(half, False)

        @pl.when(tile_span == own)
        def _():
            visit(half, True)

    @pl.when(step == tiles - 1)
    def _():
        for half in range(2):
            sums = jnp.sum(total[half], axis=1, keepdims=True)
            exact = acc[half] / sums
            lse_ref[half] = jnp.log(jnp.sum(total[half].T, axis=0, keepdims=True))
            for g in range(group):
                piece = exact[g * span_len : (g + 1) * span_len]
                place = (slice(half * span_len, (half + 1) * span_len), slice(g * HD, (g + 1) * HD))
                exact_ref[place] = piece
                mixed_ref[place] = piece.astype(bf16)


def backward_kernel(group, span_len, tiles, spans_ref, q_ref, g_ref, exact_ref, lse_ref, cosine_ref, sine_ref, *refs):
    pieces, rest = refs[: tiles // 2], refs[tiles // 2 :]
    dq_ref, near_ref, far_ref, q_all, g_all, delta, dq_acc, kv_all, sems = rest
    step = pl.program_id(0)
    load_pieces(step, pieces, kv_all, sems)
    score_scale = 1.0 / math.sqrt(HD)
    rows = group * span_len

    @pl.when(step == 0)
    def _():
        for half in range(2):
            for g in range(group):
                place = (slice(half * span_len, (half + 1) * span_len), slice(g * HD, (g + 1) * HD))
                here = slice(g * span_len, (g + 1) * span_len)
                q_all[half, here, :] = q_ref[place]
                g_all[half, here, :] = g_ref[place]
                product = g_ref[place].astype(f32) * exact_ref[place]
                folded = product[:, :128] + product[:, 128:]
                delta[half, :, here] = jnp.sum(folded.T, axis=0, keepdims=True)
        dq_acc[...] = jnp.zeros_like(dq_acc)

    tile_span = spans_ref[step]
    here = pl.ds(pl.multiple_of((step % 2) * span_len, span_len), span_len)
    key = kv_all[step // 2, here, :HD]
    value = kv_all[step // 2, here, HD:]

    def visit(half, diagonal):
        query = q_all[half]
        grad = g_all[half]
        tangent = scores(key, query, score_scale)
        probability = jnp.exp(cap_value * tangent - lse_ref[half])
        if diagonal:
            flip = spans_ref[tiles + 2]
            shape = (span_len, rows)
            q_pos = (lax.broadcasted_iota(jnp.int32, shape, 1) % span_len) ^ flip
            k_pos = lax.broadcasted_iota(jnp.int32, shape, 0) ^ flip
            probability = jnp.where(k_pos <= q_pos, probability, 0.0)
        grad_prob = lax.dot_general(value, grad, (((1,), (1,)), ((), ())), preferred_element_type=f32)
        grad_raw = probability * (grad_prob - delta[half]) * ((1.0 - tangent * tangent) * score_scale)
        grad_raw = grad_raw.astype(bf16)
        dv = jnp.dot(probability.astype(bf16), grad, preferred_element_type=f32)
        dk = jnp.dot(grad_raw, query, preferred_element_type=f32)
        dq_acc[half] += lax.dot_general(grad_raw, key, (((0,), (0,)), ((), ())), preferred_element_type=f32)
        return dk, dv

    def put(dk, dv):
        @pl.when(step < tiles // 2)
        def _():
            near_ref[:, :HD] = dk.astype(bf16)
            near_ref[:, HD:] = dv.astype(bf16)

        @pl.when(step >= tiles // 2)
        def _():
            far_ref[:, :HD] = dk.astype(bf16)
            far_ref[:, HD:] = dv.astype(bf16)

    low, high = spans_ref[tiles], spans_ref[tiles + 1]
    first, second = tile_span <= low, tile_span <= high

    @pl.when(jnp.logical_not(jnp.logical_or(first, second)))
    def _():
        put(jnp.zeros((span_len, HD), f32), jnp.zeros((span_len, HD), f32))

    for half, own, other in ((0, low, high), (1, high, low)):
        for diagonal in (False, True):
            here = tile_span == own if diagonal else tile_span < own

            @pl.when(jnp.logical_and(here, tile_span > other))
            def _(half=half, diagonal=diagonal):
                put(*visit(half, diagonal))

    for half, own, other in ((0, low, high), (1, high, low)):
        for diagonal in (False, True):
            here = tile_span == own if diagonal else tile_span < own

            @pl.when(jnp.logical_and(here, own < other))
            def _(half=half, diagonal=diagonal):
                dk_low, dv_low = visit(half, diagonal)
                dk_high, dv_high = visit(1 - half, False)
                put(dk_low + dk_high, dv_low + dv_high)

    @pl.when(step == tiles - 1)
    def _():
        for half in range(2):
            for g in range(group):
                here = slice(half * span_len, (half + 1) * span_len)
                turned = rotated(
                    dq_acc[half, g * span_len : (g + 1) * span_len], cosine_ref[here, :], sine_ref[here, :], -1.0
                )
                dq_ref[here, g * HD : (g + 1) * HD] = turned.astype(bf16)


def attention_forward(spans, queries, pieces, span_len):
    tiles = 2 * len(pieces)
    kv_size = len(pieces) * pieces[0].size
    width = queries.shape[1]
    group = width // HD
    rows = group * span_len
    whole = lambda s, t: (0, 0)
    visits = tiles + 1
    return pl.pallas_call(
        functools.partial(forward_kernel, group, span_len, tiles),
        grid_spec=pltpu.PrefetchScalarGridSpec(
            num_scalar_prefetch=1,
            grid=(tiles,),
            in_specs=[
                pl.BlockSpec(queries.shape, whole),
            ]
            + [pl.BlockSpec(memory_space=pltpu.HBM)] * len(pieces),
            out_specs=[
                pl.BlockSpec(queries.shape, whole),
                pl.BlockSpec(queries.shape, whole),
                pl.BlockSpec((2, 1, rows), lambda s, t: (0, 0, 0)),
            ],
            scratch_shapes=[
                pltpu.VMEM((2, rows, HD), bf16),
                pltpu.VMEM((2, rows, HD), f32),
                pltpu.VMEM((2, rows, 128), f32),
                pltpu.VMEM((len(pieces),) + pieces[0].shape, bf16),
                pltpu.SemaphoreType.DMA((len(pieces),)),
            ],
        ),
        out_shape=[
            jax.ShapeDtypeStruct(queries.shape, bf16),
            jax.ShapeDtypeStruct(queries.shape, f32),
            jax.ShapeDtypeStruct((2, 1, rows), f32),
        ],
        compiler_params=pltpu.CompilerParams(vmem_limit_bytes=14 * 1024 * 1024 + 2 * kv_size),
        cost_estimate=pl.CostEstimate(
            flops=visits * rows * span_len * HD * 4,
            bytes_accessed=kv_size * 2 + queries.size * 12,
            transcendentals=visits * rows * span_len * 2,
        ),
        name="attention_forward",
    )(spans, queries, *pieces)


def attention_backward(spans, queries, grads, exact, lse, table, pieces, span_len):
    tiles = 2 * len(pieces)
    kv_size = len(pieces) * pieces[0].size
    width = queries.shape[1]
    group = width // HD
    rows = group * span_len
    whole = lambda s, t: (0, 0)
    visits = tiles + 1
    return pl.pallas_call(
        functools.partial(backward_kernel, group, span_len, tiles),
        grid_spec=pltpu.PrefetchScalarGridSpec(
            num_scalar_prefetch=1,
            grid=(tiles,),
            in_specs=[
                pl.BlockSpec(queries.shape, whole),
                pl.BlockSpec(queries.shape, whole),
                pl.BlockSpec(queries.shape, whole),
                pl.BlockSpec((2, 1, rows), lambda s, t: (0, 0, 0)),
                pl.BlockSpec(table[0].shape, whole),
                pl.BlockSpec(table[0].shape, whole),
            ]
            + [pl.BlockSpec(memory_space=pltpu.HBM)] * len(pieces),
            out_specs=[
                pl.BlockSpec(queries.shape, whole),
                pl.BlockSpec((span_len, 2 * HD), lambda s, t: (jnp.minimum(s, tiles // 2 - 1), 0)),
                pl.BlockSpec((span_len, 2 * HD), lambda s, t: (jnp.maximum(s - tiles // 2, 0), 0)),
            ],
            scratch_shapes=[
                pltpu.VMEM((2, rows, HD), bf16),
                pltpu.VMEM((2, rows, HD), bf16),
                pltpu.VMEM((2, 1, rows), f32),
                pltpu.VMEM((2, rows, HD), f32),
                pltpu.VMEM((len(pieces),) + pieces[0].shape, bf16),
                pltpu.SemaphoreType.DMA((len(pieces),)),
            ],
        ),
        out_shape=[
            jax.ShapeDtypeStruct(queries.shape, bf16),
            jax.ShapeDtypeStruct((tiles * span_len // 2, 2 * HD), bf16),
            jax.ShapeDtypeStruct((tiles * span_len // 2, 2 * HD), bf16),
        ],
        compiler_params=pltpu.CompilerParams(vmem_limit_bytes=18 * 1024 * 1024 + 2 * kv_size),
        cost_estimate=pl.CostEstimate(
            flops=visits * rows * span_len * HD * 10,
            bytes_accessed=kv_size * 4 + queries.size * 16,
            transcendentals=visits * rows * span_len * 2,
        ),
        name="attention_backward",
    )(spans, queries, grads, exact, lse, *table, *pieces)


def product(left, right, left_dim, right_dim, out=f32):
    result = lax.dot_general(left, right, (((left_dim,), (right_dim,)), ((), ())), preferred_element_type=f32)
    return result.astype(out)


def on_device(
    hidden_in,
    out_grad,
    span_order,
    w_query,
    w_key,
    w_value,
    w_output,
    w_gate,
    w_up,
    w_down,
    norm_scales,
):
    local_rows = hidden_in.shape[0]
    head_count = lax.axis_size("head")
    block_count = lax.axis_size("blk")
    block_index = lax.axis_index("blk")
    head_index = lax.axis_index("head")
    group_rows = local_rows * head_count
    span_len = group_rows // 2
    model_rows, query_width = w_query.shape
    model_width = hidden_in.shape[1]
    query_heads = query_width // HD
    half_units = w_gate.shape[1] // 2

    chip_masks = bits(block_count)[1:]
    pair, top = chip_masks[0], chip_masks[-1]
    far_masks = chip_masks[:0:-1]
    head_axes = [(0, mask) for mask in bits(head_count)]
    unit_axes = head_axes + [(pair, 0)]
    unit_side = (block_index // pair) % 2
    bit_count = len(chip_masks) + 1

    def side(mask):
        return (block_index // mask) % 2

    def send(value, mask, *after):
        return swap(tie(value, *after), (mask, 0))

    def segment(body, inputs, after=(), flying=()):
        inputs, after = lax.optimization_barrier((tuple(inputs), after))
        shapes = jax.eval_shape(body, *inputs)

        def nothing(*_):
            return jax.tree.map(lambda x: jnp.zeros(x.shape, x.dtype), shapes)

        results = lax.cond(span_order[0] >= 0, body, nothing, *inputs)
        return lax.optimization_barrier((results, flying))

    def far_spread(value, *after):
        held = {0: value}
        for mask in far_masks:
            for have in list(held):
                held[have ^ mask] = send(held[have], mask, *after)
        return held

    def near_spread(held, *after):
        return held | {have ^ pair: send(block, pair, *(after if have == 0 else ())) for have, block in held.items()}

    def split_dims(partial):
        return partial.reshape((2,) * bit_count + (-1, partial.shape[-1]))

    def halve(value, dim, mask, *after):
        moved = send(pick(value, dim, 1 - side(mask)), mask, *after)
        return plus(pick(value, dim, side(mask)), moved)

    slot = jnp.arange(head_count, dtype=jnp.int32) ^ head_index
    in_block = (slot[:, None] * local_rows + jnp.arange(local_rows, dtype=jnp.int32)[None, :]).reshape(-1)
    head_side = head_index // (head_count // 2)
    own_spans = jnp.stack([span_order[2 * block_index + head_side], span_order[2 * block_index + 1 - head_side]])
    row_spans = jnp.repeat(own_spans, span_len)
    position = row_spans * span_len + in_block % span_len
    even_masks = [0]
    for mask in chip_masks[::-1]:
        even_masks = even_masks + [have ^ mask for have in even_masks]
    slot_masks = even_masks + [mask ^ 1 for mask in even_masks]
    tile_blocks = jnp.array(slot_masks, jnp.int32) ^ block_index
    tile_slots = (2 * tile_blocks[:, None] + jnp.stack([head_side, 1 - head_side])[None, :]).reshape(-1)
    flip = (head_index % (head_count // 2)) * local_rows
    spans = jnp.concatenate([span_order[tile_slots], own_spans, flip[None]]).astype(jnp.int32)
    table = rotation(position)

    scale_count = norm_scales.shape[0]
    kv_at = head_index * query_heads // (H // KVH) * HD
    kv_local = jnp.concatenate(
        [
            lax.dynamic_slice_in_dim(w_key, kv_at, HD, 1),
            lax.dynamic_slice_in_dim(w_value, kv_at, HD, 1),
        ],
        1,
    )
    scale_local = jnp.pad(norm_scales, ((0, 16 - scale_count), (0, 2 * HD - model_rows)))
    kv_local = jnp.concatenate([kv_local, scale_local], 0)

    def half(local, index):
        return lax.dynamic_slice_in_dim(local, index * half_units, half_units, 1)

    def unit_slices():
        weights = (w_gate, w_up, w_down.T)
        return (
            half(w_gate, unit_side),
            jnp.concatenate([half(w, unit_side) for w in weights[1:]], 1),
            jnp.concatenate([half(w, 1 - unit_side) for w in weights[:2]], 1),
            half(weights[2], 1 - unit_side),
        )

    hidden_near = [swap(hidden_in, axis) for axis in head_axes]
    kv_chips = far_spread(kv_local)
    kv_chips.pop(0)
    kv_chips[pair] = send(kv_local, pair)
    (query_output_local, unit_local), (hidden_near, kv_chips) = segment(
        lambda w_query, w_output: (jnp.concatenate([w_query, w_output.T], 1), unit_slices()),
        (w_query, w_output),
        (table,),
        (hidden_near, kv_chips),
    )
    first_mine, second_mine, first_theirs, second_theirs = unit_local

    def first_rows(hidden_near, kv_chips):
        held = {0: kv_local} | kv_chips
        held |= {mask ^ pair: swap(block, (pair, 0)) for mask, block in kv_chips.items() if mask != pair}
        parts = {0: [hidden_in]} | {1 << at: [part] for at, part in enumerate(hidden_near)}
        for subset in range(1, head_count):
            if subset not in parts:
                ways = route(subset, len(head_axes), False)
                cuts = shares(local_rows, len(ways)) if len(ways) > 1 else [(0, local_rows)]
                parts[subset] = [
                    swap(parts[subset ^ (1 << way)][0][low:high], head_axes[way]) for way, (low, high) in zip(ways, cuts)
                ]
        def normed_keys(held, parts):
            came = ()
            for mask, block in list(held.items()):
                held[mask ^ 1] = swap(tie(block, *came), (1, 0))
                came = (held[mask ^ 1],)
            scale_blocks = place_scales(held, model_rows, block_index)
            scale_rows = scale_blocks.reshape(block_count, 16, 2 * HD)[:, :scale_count, :model_rows]
            scale_rows = scale_rows.transpose(1, 0, 2).reshape(scale_count, model_width).astype(f32)
            arrays = [part for slot in sorted(parts) for part in parts[slot]]
            normed_full, inverse_full = whole_call(
                functools.partial(norm_full_kernel, len(arrays)),
                [((group_rows, model_width), bf16), ((group_rows, 1), f32)],
                *arrays,
                scale_rows,
                name="norm_full",
            )
            kv_held = {mask: (block, 0) for mask, block in held.items()}
            kv_rows, kv_weight = project(normed_full, [kv_held], [2 * HD], table, 1, block_index, "key_rows")
            return kv_rows, kv_weight, scale_rows, normed_full, inverse_full

        first = held[pair ^ top], *[part for slot, pieces in parts.items() if slot.bit_count() > 1 for part in pieces]
        query_output = {mask: send(query_output_local, mask, *first) for mask in (*far_masks, pair)}
        results, query_output = segment(normed_keys, (held, parts), (), query_output)
        return results, parts, query_output

    first_results, hidden_parts, query_output_chips = first_rows(hidden_near, kv_chips)
    kv_rows, kv_weight, scale_rows, normed_full, inverse_full = first_results
    hidden_slots = [part for slot in sorted(hidden_parts) for part in hidden_parts[slot]]
    row_shape = (local_rows, model_width)
    scale_shape = (1, model_width)

    if len(far_masks) > 1:
        query_output_chips = far_spread(query_output_local) | {pair: query_output_chips[pair]}
    query_output_chips[0] = query_output_local
    kv_far = far_spread(kv_rows)
    kv_far.pop(0)
    kv_near = send(kv_rows, pair)
    query_output_last = {
        mask ^ pair: send(block, pair, kv_rows) for mask, block in query_output_chips.items() if mask & ~pair
    }

    def beside_keys(kv_rows):
        cores, came = {}, ()
        for mask, block in ({-1: kv_rows} | query_output_chips).items():
            cores[mask] = swap(tie(block, *came), (1, 0))
            came = (cores[mask],)
        return cores

    cores, (kv_far, kv_near, query_output_last) = segment(
        beside_keys, (kv_rows,), (), (kv_far, kv_near, query_output_last)
    )

    def keys_and_queries(kv_far, kv_near, query_output_last):
        across = {mask ^ pair: swap(block, (pair, 0)) for mask, block in kv_far.items()}
        chips = query_output_chips | query_output_last
        held = query_output_last | {-1 - mask: piece for mask, piece in ({pair: kv_near} | kv_far).items()}
        came, others = (), dict(cores)
        for mask, block in held.items():
            others[mask] = swap(tie(block, *came), (1, 0))
            came = (others[mask],)
        chips |= {mask ^ 1: block for mask, block in others.items() if mask >= 0}
        queries, query_weight, output_weight = project(
            normed_full,
            [{mask: (block, column) for mask, block in chips.items()} for column in (0, query_width)],
            [query_width, query_width],
            table,
            query_heads,
            block_index,
            "query_rows",
        )
        came += (queries,)
        for mask, block in across.items():
            others[-1 - mask] = swap(tie(block, *came), (1, 0))
            came = (others[-1 - mask],)
        pieces = {(-1 - mask) ^ 1: piece for mask, piece in others.items() if mask < 0}
        return across | pieces, query_weight, output_weight, queries

    first_near = far_spread(first_mine, kv_far[top])
    (kv_others, query_weight, output_weight, queries), first_near = segment(
        keys_and_queries, (kv_far, kv_near, query_output_last), (), first_near
    )
    kv_held = {0: kv_rows, pair: kv_near} | kv_far | kv_others
    kv_pieces = [kv_held[mask] for mask in slot_masks]

    def row_sum(partial, axes, light=False):
        shaped = partial.reshape(1 << len(axes), local_rows, model_width)
        return scatter_rows([shaped[i] for i in range(1 << len(axes))], axes, light)

    def attend(queries, first_near, second_mine):
        mixed, exact, lse = attention_forward(spans, queries, kv_pieces, span_len)
        cores = in_turn(first_near | {-1: second_mine})
        second_core = cores.pop(-1)
        first_core = {mask ^ 1: block for mask, block in cores.items()}
        mixed = tie(mixed, first_core, second_core)
        terms = row_sum(product(mixed, output_weight, 1, 1, bf16), head_axes)
        rows = whole_call(
            functools.partial(after_attention_kernel, len(terms)),
            [(row_shape, f32), (row_shape, f32), (row_shape, bf16)],
            *terms,
            hidden_in,
            scale_rows,
            name="after_attention",
        )
        return (mixed, exact, lse, *rows, first_core, second_core)

    second_near = far_spread(second_mine, queries)
    first_cross = send(first_theirs, pair, queries)
    (mixed, exact, lse, attn_out, resid, ffn_in, first_core, second_core), (second_near, first_cross) = segment(
        attend, (queries, first_near, second_mine), (), (second_near, first_cross)
    )
    second_far = {mask: block for mask, block in second_near.items() if mask}

    def join_units(ffn_in, first_cross, second_far):
        parts = {0: [ffn_in]}
        plan = hops(len(unit_axes), True)
        parts |= gather_hop(parts, unit_axes, True, plan[0])
        flat = [part for t in plan[0][:-1] for part in parts[t]]
        parts |= gather_hop(parts, unit_axes, True, plan[1], flat)

        def later_hops(parts):
            parts = gather_rows(None, unit_axes, True, parts)
            third = [part for t in parts if t.bit_count() > 1 and t != len(parts) - 1 for part in parts[t]]
            first_core = swap(tie(first_cross, *parts[len(parts) // 2]), (1, 0))
            second_cores = {
                mask ^ 1: swap(tie(block, *third, first_core), (1, 0)) for mask, block in second_far.items()
            }
            return join_rows(parts), first_core, second_cores

        second_cross = send(second_theirs, pair, parts)
        return segment(later_hops, (parts,), (), second_cross)

    first_across = far_spread(first_cross, ffn_in)
    ((ffn_full, cross_core, far_cores), second_cross), first_across = segment(
        join_units, (ffn_in, first_cross, second_far), (), first_across
    )
    second_held = second_near | {1: second_core} | far_cores

    def gate_and_up(ffn_full, first_across):
        cores = {1: cross_core} | {mask ^ 1: swap(block, (1, 0)) for mask, block in first_across.items() if mask}
        across = {mask ^ pair: block for mask, block in (first_across | cores).items()}
        gate_held = {mask: (block, 0) for mask, block in (first_near | first_core | across).items()}
        up_held = {mask: (block, 0) for mask, block in second_held.items()}
        up_held |= {mask: (block, half_units) for mask, block in across.items()}
        units = hidden_units(ffn_full, [gate_held, up_held], half_units, block_index)
        return units, swap(second_cross, (1, 0))

    second_across = far_spread(second_cross, ffn_full)
    ((hidden, active, slope, gate_weight, up_weight), second_cross_core), second_across = segment(
        gate_and_up, (ffn_full, first_across), (), second_across
    )
    down_held = {mask: (block, half_units) for mask, block in second_held.items()}
    down_held |= {mask ^ pair: (block, 0) for mask, block in second_across.items()}
    down_held |= {
        mask ^ pair ^ 1: (swap(block, (1, 0)) if mask else second_cross_core, 0)
        for mask, block in second_across.items()
    }
    *ffn_parts, down_weight = down_rows(hidden, down_held, block_index, 1 << len(unit_axes))
    ffn_terms = scatter_rows(ffn_parts, unit_axes)
    layer_out, grad_ffn_out, scale_grad3 = whole_call(
        functools.partial(after_ffn_kernel, len(ffn_terms)),
        [(row_shape, bf16), (row_shape, bf16), (scale_shape, f32)],
        *ffn_terms,
        resid,
        out_grad,
        scale_rows,
        name="after_ffn",
    )

    def unit_core(partial):
        summed = halve(split_dims(partial), bit_count - 1, 1).astype(bf16)
        return pick(summed, 0, 1 - side(top)), pick(summed, 0, side(top))

    def unit_sides(kept, came):
        part = plus(kept, came).astype(bf16)
        for mask in far_masks[1:]:
            part = halve(part, 0, mask).astype(bf16)
        return pick(part, 0, 1 - unit_side), pick(part, 0, unit_side)

    def unit_whole(own, other):
        low = jnp.where(unit_side == 0, own, other)
        high = jnp.where(unit_side == 0, other, own)
        return jnp.concatenate([low, high], 1).astype(f32)

    def core_sum(partial):
        return halve(split_dims(partial), bit_count - 1, 1).astype(bf16)

    grad_ffn_full = join_rows(gather_rows(grad_ffn_out, unit_axes))
    grad_down = product(grad_ffn_full, hidden, 0, 0, bf16)
    grad_hidden = product(tie(grad_ffn_full, grad_down), down_weight, 1, 0)
    grad_gate_act = (grad_hidden * slope).astype(bf16)
    grad_up_act = (grad_hidden * active).astype(bf16)
    down_away, down_kept = unit_core(grad_down)
    down_came = send(down_away, top)

    def weight_back(act):
        return product(ffn_full, act, 0, 0, bf16)

    back_plan = scatter_plan(len(unit_axes), True)
    split_at = next(i for i, hop in enumerate(back_plan) if 1 << (len(unit_axes) - 1) in hop)

    def beside_hops(bodies):
        results = []

        def beside(number):
            def run(moved):
                if number >= len(bodies):
                    return None, moved
                result, moved = segment(bodies[number], tuple(results[-1:]), (), moved)
                results.append(result)
                return result, moved

            return run

        return beside, results

    def ffn_back_first(grad_gate_act, grad_up_act):
        parts = two_products(grad_gate_act, gate_weight, grad_up_act, up_weight, 1 << len(unit_axes))
        pieces, came = {t: [part] for t, part in enumerate(parts)}, ()
        beside, results = beside_hops([lambda: weight_back(tie(grad_gate_act, *parts)), unit_core])
        for number, subsets in enumerate(back_plan[:split_at]):
            pieces, came, _ = scatter_hop(pieces, unit_axes, True, subsets, came, beside(number))
        return pieces, results[1]

    (ffn_pieces, (gate_away, gate_kept)), down_came = segment(
        ffn_back_first, (grad_gate_act, grad_up_act), (down_away, down_kept), down_came
    )

    def ffn_back_last(ffn_pieces, grad_up_act, down_came):
        last = 1 << (len(unit_axes) - 1)

        def over_head(pieces, grad_up_act):
            came = ()
            beside, results = beside_hops(
                [lambda: weight_back(grad_up_act), lambda partial: (unit_core(partial), unit_sides(down_kept, down_came))]
            )
            for number, subsets in enumerate(back_plan[split_at:]):
                subsets = [t for t in subsets if t != last]
                pieces, came, _ = scatter_hop(pieces, unit_axes, True, subsets, came, beside(number))
            return pieces[0], results[1]

        pieces = dict(ffn_pieces)
        across = swap(pieces.pop(last)[0], unit_axes[-1])
        (terms, results), across = segment(over_head, (pieces, grad_up_act), (), across)
        rows = whole_call(
            functools.partial(after_ffn_back_kernel, len(terms) + 1),
            [(row_shape, f32), (row_shape, bf16), (scale_shape, f32), (scale_shape, f32)],
            *terms,
            across,
            resid,
            attn_out,
            out_grad,
            scale_rows,
            name="after_ffn_back",
        )
        return (*rows, *results)

    gate_came = [send(gate_away[0], top, down_came), None]
    (grad_resid, grad_attn, scale_grad2, scale_grad1, (up_away, up_kept), (down_far, down_own)), gate_came[0] = segment(
        ffn_back_last, (ffn_pieces, grad_up_act, down_came), (gate_away, gate_kept), gate_came[0]
    )

    def attend_back(grad_attn):
        grad_attn_full = join_rows(gather_rows(grad_attn, head_axes))
        grad_mixed = product(grad_attn_full, output_weight, 1, 0, bf16)
        grad_query_lin, kv_near, kv_far = attention_backward(
            spans, queries, grad_mixed, exact, lse, table, kv_pieces, span_len
        )
        kv_terms = plus(kv_near, swap(kv_far, (1, 0))).astype(bf16).reshape(-1, group_rows, 2 * HD)
        middle = kv_terms.shape[0] // 2
        return grad_attn_full, grad_query_lin, kv_terms[:middle], kv_terms[middle:]

    gate_came[1] = send(gate_away[1], top, grad_attn)
    up_came = [send(up_away[0], top, grad_attn), None]
    down_other = send(down_far, pair, grad_attn)
    (grad_attn_full, grad_query_lin, kv_kept, kv_away), (gate_came[1], up_came[0], down_other) = segment(
        attend_back, (grad_attn,), (up_away, up_kept, down_far, down_own), (gate_came[1], up_came[0], down_other)
    )

    def projections_back(grad_query_lin, gate_came):
        core = core_sum(outer((normed_full, grad_query_lin), (grad_attn_full, mixed)))
        away, kept = pick(core, bit_count - 2, 1 - unit_side), pick(core, bit_count - 2, unit_side)
        parts = [(pick(away, 0, index), pick(kept, 0, index)) for index in (1 - side(top), side(top))]
        return parts, unit_sides(gate_kept, jnp.stack(gate_came))

    kv_came = send(kv_away, pair)
    (((onward_away, onward_kept), (staying_away, staying_kept)), (gate_far, gate_own)), kv_came = segment(
        projections_back, (grad_query_lin, gate_came), (), kv_came
    )
    kv_terms = plus(kv_kept, kv_came).astype(bf16)
    for mask in chip_masks[1:-1]:
        middle = kv_terms.shape[0] // 2
        kv_terms = plus(kv_terms[:middle], swap(kv_terms[middle:], (mask, 0))).astype(bf16)

    def beside_last_keys(down_other):
        return unit_whole(down_own, down_other).T

    kv_came = send(kv_terms[1], top)
    gate_other = send(gate_far, pair, kv_terms)
    out_down, (kv_came, gate_other) = segment(beside_last_keys, (down_other,), (kv_terms,), (kv_came, gate_other))

    def normed_rows_back(kv_kept, kv_came):
        normed_plan = scatter_plan(len(head_axes), False)

        def first_sums_back(kv_kept, kv_came):
            (grad_kv_lin,) = whole_call(
                key_value_grad_kernel,
                [((group_rows, 2 * HD), bf16)],
                kv_kept,
                kv_came,
                *table,
                name="key_value_grad",
            )
            *parts, scale_grad0 = normed_back(
                grad_query_lin, query_weight, grad_kv_lin, kv_weight, inverse_full, hidden_slots, head_count
            )

            def key_weights_back(grad_kv_lin, scale_grad0):
                scale_grad = jnp.concatenate([scale_grad0, scale_grad1, scale_grad2, scale_grad3], 0).astype(bf16)
                scale_grad = scale_grad.reshape(scale_count, block_count, model_rows).transpose(1, 0, 2)
                scale_grad = jnp.pad(scale_grad, ((0, 0), (0, 16 - scale_count), (0, 2 * HD - model_rows)))
                partial = outer((normed_full, grad_kv_lin)).reshape(block_count, model_rows, 2 * HD)
                terms = core_sum(jnp.concatenate([partial, scale_grad], 1).reshape(-1, 2 * HD))
                return pick(terms, bit_count - 2, 1 - unit_side), pick(terms, bit_count - 2, unit_side)

            def beside(moved):
                return segment(key_weights_back, (grad_kv_lin, scale_grad0), (), moved)

            pieces = {t: [part] for t, part in enumerate(parts)}
            pieces, _, terms = scatter_hop(pieces, head_axes, False, normed_plan[0], (), beside)
            return pieces, terms

        onward_came = send(onward_away, pair, kv_came)
        (pieces, (away, kept)), onward_came = segment(first_sums_back, (kv_kept, kv_came), (), onward_came)
        onward = plus(onward_kept, onward_came).astype(bf16)
        for at, mask in list(enumerate(chip_masks))[1:-1]:
            onward = halve(onward, bit_count - 3 - at, mask).astype(bf16)
        onward_query, onward_output = lax.optimization_barrier((onward[:, :query_width], onward[:, query_width:]))

        def sums_back(pieces):
            came = ()
            for subsets in normed_plan[1:]:
                pieces, came, _ = scatter_hop(pieces, head_axes, False, subsets, came)
            (grad_in,) = whole_call(
                functools.partial(after_all_kernel, len(pieces[0])),
                [(row_shape, f32)],
                *pieces[0],
                hidden_in,
                grad_resid,
                scale_rows,
                name="after_all",
            )
            return grad_in

        wkv_came = send(away, pair)
        query_came = send(onward_query, top)
        grad_in, (wkv_came, query_came) = segment(sums_back, (pieces,), (away, kept), (wkv_came, query_came))
        wkv_terms = plus(kept, wkv_came).astype(bf16)
        for at, mask in list(enumerate(chip_masks))[1:-1]:
            wkv_terms = halve(wkv_terms, bit_count - 2 - at, mask).astype(bf16)
        return grad_in, pick(wkv_terms, 0, 1 - side(top)), pick(wkv_terms, 0, side(top)), query_came, onward_output

    up_came[1] = send(up_away[1], top, kv_came)
    (grad_in, wkv_away, wkv_kept, query_came, onward_output), up_came[1] = segment(
        normed_rows_back, (kv_terms[0], kv_came), (out_down, onward_away), up_came[1]
    )
    wkv_came = send(wkv_away, top)
    staying_came = send(staying_away, pair, wkv_away)

    def beside_key_weights(up_came, gate_other):
        return unit_sides(up_kept, jnp.stack(up_came)), unit_whole(gate_own, gate_other)

    ((up_far, up_own), out_gate), (wkv_came, staying_came) = segment(
        beside_key_weights, (up_came, gate_other), (wkv_away, wkv_kept), (wkv_came, staying_came)
    )
    grad_wkv = plus(wkv_kept, wkv_came).astype(bf16)
    output_came = send(onward_output, top, grad_wkv)
    up_other = send(up_far, pair, grad_wkv)

    def head_rows(grad_wkv, staying_kept, staying_came, query_came):
        staying = plus(staying_kept, staying_came).astype(bf16)
        for at, mask in list(enumerate(chip_masks))[1:-1]:
            staying = halve(staying, bit_count - 3 - at, mask).astype(bf16)
        out_query = plus(staying[:, :query_width], query_came)
        staying_output = staying[:, query_width:]
        parts = gather_rows(grad_wkv, head_axes)
        if head_count == KVH:
            out_key, out_value, scale_total = place_heads(parts, model_rows, scale_count, head_index)
            return out_key, out_value, scale_total[:, :model_rows], out_query, staying_output
        wkv_ordered = jnp.zeros((head_count,) + grad_wkv.shape, bf16)
        for mask, pieces in parts.items():
            first = 0
            for piece in pieces:
                wkv_ordered = lax.dynamic_update_slice(wkv_ordered, piece[None], (head_index ^ mask, first, 0))
                first += piece.shape[0]
        wkv_ordered = wkv_ordered.astype(f32)
        scale_total = wkv_ordered[:, model_rows : model_rows + scale_count, :model_rows].sum(0)
        wkv_ordered = wkv_ordered[:, :model_rows].reshape(KVH, head_count // KVH, model_rows, 2, HD).sum(1)
        out_key = wkv_ordered[:, :, 0].transpose(1, 0, 2).reshape(model_rows, KVH * HD)
        out_value = wkv_ordered[:, :, 1].transpose(1, 0, 2).reshape(model_rows, KVH * HD)
        return out_key, out_value, scale_total, out_query, staying_output

    (out_key, out_value, scale_total, out_query, staying_output), (output_came, up_other) = segment(
        head_rows, (grad_wkv, staying_kept, staying_came, query_came), (onward_output, up_far), (output_came, up_other)
    )
    out_output = plus(staying_output, output_came).T
    out_up = unit_whole(up_own, up_other)

    return (
        layer_out,
        grad_in,
        out_query,
        out_key,
        out_value,
        out_output,
        out_gate,
        out_up,
        out_down,
        scale_total,
    )


def solution(mesh):
    placed = (
        P(("blk", "head"), None),
        P(("blk", "head"), None),
        P(),
        P("blk", "head"),
        P("blk", None),
        P("blk", None),
        P("head", "blk"),
        P("blk", "head"),
        P("blk", "head"),
        P("head", "blk"),
        P(None, "blk"),
    )
    return jax.shard_map(
        on_device,
        mesh=mesh,
        in_specs=placed,
        out_specs=(
            P(("blk", "head"), None),
            P(("blk", "head"), None),
            P("blk", "head"),
            P("blk", None),
            P("blk", None),
            P("head", "blk"),
            P("blk", "head"),
            P("blk", "head"),
            P("head", "blk"),
            P(None, "blk"),
        ),
        check_vma=False,
    )
```

```python
import functools
import math

import jax
import jax.numpy as jnp
from jax import lax
from jax.experimental import pallas as pl
from jax.experimental.pallas import tpu as pltpu
from jax.sharding import PartitionSpec as P

H = 8
KVH = 4
HD = 256

norm_eps = 1e-06
cap_value = 50.0
theta_base = 10000.0
f32 = jnp.float32
bf16 = jnp.bfloat16


def inverse_rms(value):
    return lax.rsqrt(jnp.mean(value * value, axis=-1, keepdims=True) + norm_eps)


def rms_back(value, scale, grad):
    inverse = inverse_rms(value)
    scaled = grad * scale
    inner = jnp.mean(scaled * value, axis=-1, keepdims=True)
    grad_value = inverse * scaled - value * (inverse * inverse * inverse) * inner
    grad_scale = jnp.sum(grad * value * inverse, axis=0, keepdims=True)
    return (grad_value, grad_scale)


def rotation(position):
    entry = jnp.arange(HD, dtype=jnp.int32)
    quarter = HD // 4
    pair_index = entry // (2 * quarter) * quarter + entry % quarter
    frequency = jnp.power(theta_base, -2.0 * pair_index.astype(f32) / HD)
    angles = position.astype(f32)[:, None] * frequency[None, :]
    sign = jnp.where(entry % (2 * quarter) < quarter, -1.0, 1.0)
    return jnp.cos(angles), jnp.sin(angles) * sign[None, :]


def rotated(value, cosine, sine, sign):
    half = HD // 2
    parts = []
    for at in range(0, HD, half):
        piece = value[:, at : at + half]
        partner = pltpu.roll(piece, half // 2, 1)
        parts.append(piece * cosine[:, at : at + half] + partner * (sign * sine[:, at : at + half]))
    return jnp.concatenate(parts, 1)


def swap(value, axis):
    blk_mask, head_mask = axis
    block_count, head_count = lax.axis_size("blk"), lax.axis_size("head")
    if blk_mask == 0:
        return lax.ppermute(value, "head", [(i, i ^ head_mask) for i in range(head_count)])
    return lax.ppermute(value, "blk", [(i, i ^ blk_mask) for i in range(block_count)])


def bits(count):
    return [1 << i for i in range(count.bit_length() - 1)]


def route(subset, total, light):
    members = [i for i in range(total) if subset >> i & 1]
    if light and len(members) > 1 and members[-1] == total - 1:
        members = members[:-1]
        return members if len(members) == total - 1 else members[:1]
    if len(members) >= 2 and len(members) == total - light:
        return members
    if not light and len(members) == 2 and members[1] - members[0] != 1:
        return members[1:]
    return members[:1]


def hops(total, light):
    size = lambda t: bin(t).count("1")
    last = 1 << (total - 1)
    subsets = range(1, 1 << total)
    if not light:
        return [[t for t in subsets if size(t) == n] for n in range(1, total + 1)]
    result = [[t for t in subsets if size(t) == 1]]
    for high in (0, last):
        for n in range(2, total + 1):
            result.append([t for t in subsets if size(t) == n and t & last == high])
    return [hop for hop in result if hop]


def shares(row_total, parts):
    unit = row_total // 16
    cuts = [unit * i // parts * 16 for i in range(parts + 1)]
    cuts[-1] = row_total
    return list(zip(cuts[:-1], cuts[1:]))


def gather_hop(parts, axes, light, subsets, before=()):
    rows = parts[0][0].shape[0]
    came = {}
    for subset in subsets:
        ways = route(subset, len(axes), light)
        cuts = shares(rows, len(ways)) if len(ways) > 1 else [(0, rows)]
        came[subset] = []
        for way, (low, high) in zip(ways, cuts):
            source = parts[subset ^ (1 << way)][0]
            came[subset].append(swap(tie(source[low:high] if len(ways) > 1 else source, *before), axes[way]))
    return came


def gather_rows(value, axes, light=False, parts=None):
    last = 1 << (len(axes) - 1)
    parts, before = parts or {0: [value]}, ()
    for subsets in hops(len(axes), light):
        if all(t in parts for t in subsets):
            continue
        if light and last in parts:
            before = [x for x in before if x is not parts[last][0]]
            before += parts[last] * any(t & last for t in subsets)
        came = gather_hop(parts, axes, light, subsets, before)
        parts = parts | came
        before = [part for pieces in came.values() for part in pieces]
    return parts


def join_kernel(plan, *refs):
    step = pl.program_id(0)
    out = refs[-1]
    for at, (slot, first, rows) in enumerate(plan):

        @pl.when(step == slot)
        def _():
            out[first : first + rows, :] = refs[at][...]


def join_rows(parts):
    plan, arrays = [], []
    for slot in sorted(parts):
        first = 0
        for array in parts[slot]:
            plan.append((slot, first, array.shape[0]))
            arrays.append(array)
            first += array.shape[0]
    rows, columns = parts[0][0].shape
    return pl.pallas_call(
        functools.partial(join_kernel, plan),
        grid=(len(parts),),
        in_specs=[pl.BlockSpec(a.shape, lambda m: (0, 0), pipeline_mode=pl.Buffered(1)) for a in arrays],
        out_specs=pl.BlockSpec((rows, columns), lambda m: (m, 0)),
        out_shape=jax.ShapeDtypeStruct((len(parts) * rows, columns), arrays[0].dtype),
        compiler_params=pltpu.CompilerParams(vmem_limit_bytes=16 * 1024 * 1024),
        cost_estimate=pl.CostEstimate(flops=0, bytes_accessed=4 * len(parts) * rows * columns, transcendentals=0),
        name="join_rows",
    )(*arrays)


def two_products_kernel(a_ref, u_ref, b_ref, v_ref, *outs):
    nt = (((1,), (1,)), ((), ()))
    total = lax.dot_general(a_ref[...], u_ref[...], nt, preferred_element_type=f32)
    total += lax.dot_general(b_ref[...], v_ref[...], nt, preferred_element_type=f32)
    put_pieces(outs, total)


def put_pieces(outs, value):
    rows = outs[0].shape[0]
    for at, out in enumerate(outs):
        out[...] = value[at * rows : (at + 1) * rows].astype(out.dtype)


def two_products(a, u, b, v, count):
    rows, depth = a.shape
    columns = u.shape[0]
    step = 256
    resident = pl.BlockSpec((rows, depth), lambda n: (0, 0), pipeline_mode=pl.Buffered(1))
    return pl.pallas_call(
        two_products_kernel,
        grid=(columns // step,),
        in_specs=[resident, pl.BlockSpec((step, depth), lambda n: (n, 0))] * 2,
        out_specs=[pl.BlockSpec((rows // count, step), lambda n: (0, n))] * count,
        out_shape=[jax.ShapeDtypeStruct((rows // count, columns), bf16)] * count,
        compiler_params=pltpu.CompilerParams(vmem_limit_bytes=20 * 1024 * 1024),
        cost_estimate=pl.CostEstimate(
            flops=4 * rows * columns * depth,
            bytes_accessed=4 * (rows * depth + columns * depth) + 2 * rows * columns,
            transcendentals=0,
        ),
        name="two_products",
    )(a, u, b, v)


def joined(left, right):
    return (left.astype(f32) + right.astype(f32)).astype(bf16)


def scatter_plan(total, light):
    plan = [list(hop) for hop in hops(total, light)[::-1]]
    last = 1 << (total - 1)
    if light:
        plan[-1].remove(last)
        plan[next(i for i, hop in enumerate(plan) if not any(t & last for t in hop))].append(last)
    return plan


def scatter_hop(pieces, axes, light, subsets, before=(), beside=None):
    last = 1 << (len(axes) - 1)
    pieces = dict(pieces)
    rows = pieces[0][0].shape[0]
    sent, result = [], None
    for subset in subsets:
        (piece,) = pieces.pop(subset)
        ways = route(subset, len(axes), light)
        cuts = shares(rows, len(ways)) if len(ways) > 1 else [(0, rows)]
        for way, (low, high) in zip(ways, cuts):
            part = piece if len(ways) == 1 else piece[low:high]
            sent.append((subset, subset ^ (1 << way), low, high, swap(tie(part, *before), axes[way])))
    if beside:
        result, came = beside([item[4] for item in sent])
        sent = [item[:4] + (moved,) for item, moved in zip(sent, came)]
    for subset, target, low, high, moved in sent:
        if target == 0:
            pieces[0] = pieces[0] + [moved]
        elif high - low == rows:
            pieces[target] = [joined(pieces[target][0], moved)]
        else:
            old = pieces[target][0]
            cut = [old[:low], joined(old[low:high], moved), old[high:]]
            pieces[target] = [jnp.concatenate([c for c in cut if c.shape[0]], 0)]
    came = [item[4] for item in sent if not (light and item[0] == last)]
    return pieces, came, result


def scatter_rows(pieces, axes, light=False):
    pieces, came = {t: [piece] for t, piece in enumerate(pieces)}, ()
    for subsets in scatter_plan(len(axes), light):
        pieces, came, _ = scatter_hop(pieces, axes, light, subsets, came)
    return pieces[0]


def tie(value, *after):
    return lax.optimization_barrier((value, *after))[0] if after else value


def tie_all(held, *after):
    return {mask: tie(block, *after) for mask, block in held.items()}


def scale_kernel(count, index_ref, *refs):
    for mask in range(count):
        row = pl.multiple_of((index_ref[0] ^ mask) * 16, 16)
        refs[count][pl.ds(row, 16), :] = refs[mask][...]


def place_scales(held, rows, block_index):
    count = len(held)
    shape = (16, held[0].shape[1])
    return pl.pallas_call(
        functools.partial(scale_kernel, count),
        grid_spec=pltpu.PrefetchScalarGridSpec(
            num_scalar_prefetch=1,
            grid=(1,),
            in_specs=[pl.BlockSpec(shape, lambda n, b: (rows // 16, 0))] * count,
            out_specs=pl.BlockSpec((count * 16, shape[1]), lambda n, b: (0, 0)),
        ),
        out_shape=jax.ShapeDtypeStruct((count * 16, shape[1]), bf16),
        cost_estimate=pl.CostEstimate(flops=0, bytes_accessed=4 * count * 16 * shape[1], transcendentals=0),
        name="place_scales",
    )(block_index[None].astype(jnp.int32), *[held[mask] for mask in range(count)])


def head_kernel(plan, rows, scale_count, index_ref, *refs):
    parts, (key_ref, value_ref, scale_ref) = refs[: len(plan)], refs[len(plan) :]
    step = pl.program_id(0)

    @pl.when(step == 0)
    def _():
        scale_ref[...] = jnp.zeros_like(scale_ref)

    for part, (slot, first) in zip(parts, plan):
        count = part.shape[0]

        @pl.when(step == slot)
        def _():
            last = min(first + count, rows)
            here, taken = slice(first, last), slice(0, last - first)
            key_ref[here, :] = part[taken, :HD].astype(f32)
            value_ref[here, :] = part[taken, HD:].astype(f32)
            if first + count > rows:
                scale_ref[...] += part[rows - first : rows - first + 16, :].astype(f32)[:scale_count]


def place_heads(parts, rows, scale_count, head_index):
    plan, arrays = [], []
    for slot in sorted(parts):
        first = 0
        for array in parts[slot]:
            plan.append((slot, first))
            arrays.append(array)
            first += array.shape[0]
    columns = pl.BlockSpec((rows, HD), lambda m, h: (0, h[0] ^ m))
    fixed = lambda m, h: (0, 0)
    return pl.pallas_call(
        functools.partial(head_kernel, plan, rows, scale_count),
        grid_spec=pltpu.PrefetchScalarGridSpec(
            num_scalar_prefetch=1,
            grid=(len(parts),),
            in_specs=[pl.BlockSpec(a.shape, fixed, pipeline_mode=pl.Buffered(1)) for a in arrays],
            out_specs=[columns, columns, pl.BlockSpec((scale_count, 2 * HD), fixed)],
        ),
        out_shape=[jax.ShapeDtypeStruct((rows, len(parts) * HD), f32)] * 2
        + [jax.ShapeDtypeStruct((scale_count, 2 * HD), f32)],
        cost_estimate=pl.CostEstimate(flops=0, bytes_accessed=8 * len(parts) * rows * HD, transcendentals=0),
        name="place_heads",
    )(head_index[None].astype(jnp.int32), *arrays)


def placed_kernel(body, plans, counts, steps, index_ref, *refs):
    refs = list(refs)
    arrays, loads, inputs, outs, wholes, weights, loaded = [[refs.pop(0) for _ in range(count)] for count in counts]
    in_sems, out_sems = refs
    step = pl.program_id(0)
    came, at = [], 0
    for source, target in zip(loads, loaded):
        came.append([pltpu.make_async_copy(source, target, in_sems.at[at])])
        at += 1
    gone = [None] * len(loads)
    for weight, plan in zip(weights, plans):
        copies = []
        rows = weight.shape[0] // len(plan)
        for mask, (source, column) in enumerate(plan):
            row = pl.multiple_of((index_ref[0] ^ mask) * rows, 16)
            block = arrays[source].at[pl.ds(0, rows)]
            if arrays[source].shape[1] != weight.shape[1]:
                block = arrays[source].at[pl.ds(0, rows), pl.ds(column, weight.shape[1])]
            copies.append(pltpu.make_async_copy(block, weight.at[pl.ds(row, rows)], in_sems.at[at]))
            at += 1
        came.append(copies)
    gone += [
        pltpu.make_async_copy(weight, whole, out_sems.at[n]) for n, (weight, whole) in enumerate(zip(weights, wholes))
    ]

    @pl.when(step == 0)
    def _():
        for copies in came:
            for copy in copies:
                copy.start()
        for copies, copy_out in zip(came, gone):
            for copy in copies:
                copy.wait()
            if copy_out is not None:
                copy_out.start()

    body(step, loaded + inputs, outs, weights)

    @pl.when(step == steps - 1)
    def _():
        for copy_out in gone[len(loads) :]:
            copy_out.wait()


def placed(body, steps, held, columns, loads, inputs, in_specs, outs, out_specs, block_index, name, flops, vmem):
    arrays, plans = [], []
    for blocks, width in zip(held, columns):
        plan = []
        for mask in range(len(blocks)):
            array, column = blocks[mask]
            if width % 128 or column % 128:
                array, column = array[:, column : column + width], 0
            where = next((n for n, known in enumerate(arrays) if known is array), len(arrays))
            if where == len(arrays):
                arrays.append(array)
            plan.append((where, column))
        plans.append(plan)
    rows = min(array.shape[0] for array in arrays) // 16 * 16
    rows = rows - (16 if name == "key_rows" else 0)
    shapes = [(len(plan) * rows, width) for plan, width in zip(plans, columns)]
    anywhere = pl.BlockSpec(memory_space=pltpu.HBM)
    counts = (len(arrays), len(loads), len(inputs), len(outs), len(plans), len(plans), len(loads))
    return pl.pallas_call(
        functools.partial(placed_kernel, body, plans, counts, steps),
        grid_spec=pltpu.PrefetchScalarGridSpec(
            num_scalar_prefetch=1,
            grid=(steps,),
            in_specs=[anywhere] * (len(arrays) + len(loads)) + in_specs,
            out_specs=out_specs + [anywhere] * len(plans),
            scratch_shapes=[pltpu.VMEM(shape, bf16) for shape in shapes]
            + [pltpu.VMEM(array.shape, array.dtype) for array in loads]
            + [
                pltpu.SemaphoreType.DMA((sum(len(plan) for plan in plans) + len(loads),)),
                pltpu.SemaphoreType.DMA((len(plans),)),
            ],
        ),
        out_shape=outs + [jax.ShapeDtypeStruct(shape, bf16) for shape in shapes],
        compiler_params=pltpu.CompilerParams(vmem_limit_bytes=vmem * 1024 * 1024),
        cost_estimate=pl.CostEstimate(
            flops=flops, bytes_accessed=4 * sum(h * w for h, w in shapes), transcendentals=0
        ),
        name=name,
    )(block_index[None].astype(jnp.int32), *arrays, *loads, *inputs)


def in_turn(held):
    came = []
    for block in held.values():
        came.append(swap(tie(block, *came[-2:-1]), (1, 0)))
    return dict(zip(held, came))


def both_cores(held):
    return held | {mask ^ 1: swap(block, (1, 0)) for mask, block in held.items()}


def pick(value, dim, index):
    return lax.dynamic_index_in_dim(value, index, dim, keepdims=False)


def plus(left, right):
    return left.astype(f32) + right.astype(f32)


def whole_call(body, outs, *inputs, name):
    size = sum(x.size * x.dtype.itemsize for x in inputs)
    return pl.pallas_call(
        body,
        out_shape=[jax.ShapeDtypeStruct(shape, dtype) for shape, dtype in outs],
        compiler_params=pltpu.CompilerParams(vmem_limit_bytes=28 * 1024 * 1024),
        cost_estimate=pl.CostEstimate(flops=0, bytes_accessed=2 * size, transcendentals=0),
        name=name,
    )(*inputs)


def summed(refs):
    total = refs[0][...].astype(f32)
    for ref in refs[1:]:
        total = total + ref[...].astype(f32)
    return total


def norm_full_kernel(count, *refs):
    parts, (scale, normed, inverse) = refs[:count], refs[count:]
    first = 0
    for part in parts:
        value = part[...].astype(f32)
        here = slice(first, first + part.shape[0])
        first += part.shape[0]
        factor = inverse_rms(value)
        inverse[here, :] = factor
        normed[here, :] = (value * factor * scale[0:1, :]).astype(bf16)


def after_attention_kernel(count, *refs):
    terms, (hidden, scales, attn_out, resid_out, ffn_in) = refs[:count], refs[count:]
    attn = summed(terms)
    attn_out[...] = attn
    resid = hidden[...].astype(f32) + attn * inverse_rms(attn) * scales[1:2, :]
    resid_out[...] = resid
    ffn_in[...] = (resid * inverse_rms(resid) * scales[2:3, :]).astype(bf16)


def after_ffn_kernel(count, *refs):
    terms, (resid, out_grad, scales, layer_out, grad_out, grad_scale) = refs[:count], refs[count:]
    ffn_out = summed(terms)
    grad, grad_scale[...] = rms_back(ffn_out, scales[3:4, :], out_grad[...].astype(f32))
    grad_out[...] = grad.astype(bf16)
    layer_out[...] = (resid[...] + ffn_out * inverse_rms(ffn_out) * scales[3:4, :]).astype(bf16)


def after_ffn_back_kernel(count, *refs):
    terms, (resid, attn, out_grad, scales, grad_resid, grad_attn, grad_scale2, grad_scale1) = refs[:count], refs[count:]
    grad, grad_scale2[...] = rms_back(resid[...], scales[2:3, :], summed(terms))
    grad = out_grad[...].astype(f32) + grad
    grad_resid[...] = grad
    back, grad_scale1[...] = rms_back(attn[...], scales[1:2, :], grad)
    grad_attn[...] = back.astype(bf16)


def after_all_kernel(count, *refs):
    terms, (hidden, grad_resid, scales, grad_in) = refs[:count], refs[count:]
    grad, _ = rms_back(hidden[...].astype(f32), scales[0:1, :], summed(terms))
    grad_in[...] = grad_resid[...] + grad


def key_value_grad_kernel(kept, came, cosine, sine, out):
    total = kept[...].astype(f32) + came[...].astype(f32)
    out[:, :HD] = rotated(total[:, :HD], cosine[...], sine[...], -1.0).astype(bf16)
    out[:, HD:] = total[:, HD:].astype(bf16)


def project(rows, held, columns, table, turning, block_index, name):
    count, depth = rows.shape
    heads = columns[0] // HD
    fixed = lambda n, b: (0, 0)
    once = pl.Buffered(1)

    def body(step, inputs, outs, weights):
        rows_ref, cosine_ref, sine_ref = inputs
        (out_ref,) = outs
        here = pl.ds(pl.multiple_of(step * HD, HD), HD)
        value = jnp.dot(rows_ref[...], weights[0][:, here], preferred_element_type=f32)

        @pl.when(step < turning)
        def _():
            out_ref[...] = rotated(value, cosine_ref[...], sine_ref[...], 1.0).astype(bf16)

        @pl.when(step >= turning)
        def _():
            out_ref[...] = value.astype(bf16)

    return placed(
        body,
        heads,
        held,
        columns,
        [rows],
        list(table),
        [
            pl.BlockSpec((count, HD), fixed, pipeline_mode=once),
            pl.BlockSpec((count, HD), fixed, pipeline_mode=once),
        ],
        [jax.ShapeDtypeStruct((count, columns[0]), bf16)],
        [pl.BlockSpec((count, HD), lambda n, b: (0, n))],
        block_index,
        name,
        2 * rows.size * columns[0],
        20,
    )


def hidden_units(rows, held, width, block_index):
    count, depth = rows.shape
    step = 256

    def body(number, inputs, outs, weights):
        hidden_ref, active_ref, slope_ref = outs
        gate = jnp.dot(inputs[0][...], weights[0][...], preferred_element_type=f32)
        up = jnp.dot(inputs[0][...], weights[1][...], preferred_element_type=f32)
        inner = math.sqrt(2.0 / math.pi)
        square = gate * gate
        tangent = jnp.tanh(inner * gate * (1.0 + 0.044715 * square))
        share = 0.5 * (1.0 + tangent)
        active = gate * share
        slope = share + (0.5 * inner) * gate * (1.0 - tangent * tangent) * (1.0 + (3 * 0.044715) * square)
        hidden_ref[...] = (active * up).astype(bf16)
        active_ref[...] = active
        slope_ref[...] = slope * up

    return placed(
        body,
        count // step,
        held,
        [width, width],
        [],
        [rows],
        [pl.BlockSpec((step, depth), lambda n, b: (n, 0))],
        [jax.ShapeDtypeStruct((count, width), dtype) for dtype in (bf16, f32, f32)],
        [pl.BlockSpec((step, width), lambda n, b: (n, 0))] * 3,
        block_index,
        "hidden_units",
        4 * rows.size * width,
        40,
    )


def down_rows(hidden, held, block_index, pieces):
    count, width = hidden.shape
    depth = len(held) * held[0][0].shape[0]
    step = 768 if depth % 768 == 0 else 256

    def body(number, inputs, outs, weights):
        here = pl.ds(pl.multiple_of(number * step, step), step)
        value = lax.dot_general(
            inputs[0][...], weights[0][here, :], (((1,), (1,)), ((), ())), preferred_element_type=f32
        )
        put_pieces(outs, value)

    return placed(
        body,
        depth // step,
        [held],
        [width],
        [hidden],
        [],
        [],
        [jax.ShapeDtypeStruct((count // pieces, depth), bf16)] * pieces,
        [pl.BlockSpec((count // pieces, step), lambda n, b: (0, n))] * pieces,
        block_index,
        "down_rows",
        2 * hidden.size * depth,
        24,
    )


def outer_kernel(*refs):
    pairs, out = refs[:-1], refs[-1]
    width = 0
    for left, right in zip(pairs[::2], pairs[1::2]):
        columns = right.shape[1]
        value = lax.dot_general(left[...], right[...], (((0,), (0,)), ((), ())), preferred_element_type=f32)
        out[:, width : width + columns] = value.astype(bf16)
        width += columns


def outer(*pairs):
    rows, depth = pairs[0][0].shape
    width = sum(right.shape[1] for _, right in pairs)
    step = depth // 2
    specs = []
    for _, right in pairs:
        specs.append(pl.BlockSpec((rows, step), lambda n: (0, n)))
        specs.append(pl.BlockSpec(right.shape, lambda n: (0, 0), pipeline_mode=pl.Buffered(1)))
    return pl.pallas_call(
        outer_kernel,
        grid=(depth // step,),
        in_specs=specs,
        out_specs=pl.BlockSpec((step, width), lambda n: (n, 0)),
        out_shape=jax.ShapeDtypeStruct((depth, width), bf16),
        compiler_params=pltpu.CompilerParams(vmem_limit_bytes=24 * 1024 * 1024),
        cost_estimate=pl.CostEstimate(
            flops=2 * rows * depth * width, bytes_accessed=2 * (rows * depth * len(pairs) + depth * width), transcendentals=0
        ),
        name="outer",
    )(*[x for pair in pairs for x in pair])


def normed_back_kernel(count, q_ref, wq_ref, kv_ref, wkv_ref, inverse_ref, *refs):
    hidden, (*outs, scale_ref) = refs[:count], refs[count:]
    nt = (((1,), (1,)), ((), ()))
    total = lax.dot_general(q_ref[...], wq_ref[...], nt, preferred_element_type=f32)
    total += lax.dot_general(kv_ref[...], wkv_ref[...], nt, preferred_element_type=f32)
    put_pieces(outs, total)
    grad_scale, first = jnp.zeros((1, total.shape[1]), f32), 0
    for part in hidden:
        here = slice(first, first + part.shape[0])
        first += part.shape[0]
        unit = part[...].astype(f32) * inverse_ref[here, :]
        grad_scale += jnp.sum(total[here, :] * unit, axis=0, keepdims=True)
    scale_ref[...] = grad_scale


def normed_back(grad_query, query_weight, grad_kv, kv_weight, inverse, hidden, pieces):
    rows, width = grad_query.shape
    kv_width = grad_kv.shape[1]
    columns = query_weight.shape[0]
    step = 768 if columns % 768 == 0 else 256
    fixed = lambda n: (0, 0)
    once = pl.Buffered(1)
    return pl.pallas_call(
        functools.partial(normed_back_kernel, len(hidden)),
        grid=(columns // step,),
        in_specs=[
            pl.BlockSpec((rows, width), fixed, pipeline_mode=once),
            pl.BlockSpec((step, width), lambda n: (n, 0)),
            pl.BlockSpec((rows, kv_width), fixed, pipeline_mode=once),
            pl.BlockSpec((step, kv_width), lambda n: (n, 0)),
            pl.BlockSpec((rows, 1), fixed, pipeline_mode=once),
        ]
        + [pl.BlockSpec((part.shape[0], step), lambda n: (0, n)) for part in hidden],
        out_specs=[pl.BlockSpec((rows // pieces, step), lambda n: (0, n))] * pieces
        + [pl.BlockSpec((1, step), lambda n: (0, n))],
        out_shape=[jax.ShapeDtypeStruct((rows // pieces, columns), bf16)] * pieces
        + [jax.ShapeDtypeStruct((1, columns), f32)],
        compiler_params=pltpu.CompilerParams(vmem_limit_bytes=20 * 1024 * 1024),
        cost_estimate=pl.CostEstimate(
            flops=2 * rows * columns * (width + kv_width), bytes_accessed=4 * rows * columns, transcendentals=0
        ),
        name="normed_back",
    )(grad_query, query_weight, grad_kv, kv_weight, inverse, *hidden)


def scores(query, key, score_scale):
    raw = lax.dot_general(query, key, (((1,), (1,)), ((), ())), preferred_element_type=f32)
    return jnp.tanh(raw * (score_scale / cap_value))


def load_pieces(step, pieces, kv_all, sems):
    copies = [pltpu.make_async_copy(piece, kv_all.at[at], sems.at[at]) for at, piece in enumerate(pieces)]

    @pl.when(step == 0)
    def _():
        for copy in copies:
            copy.start()

    for at, copy in enumerate(copies):

        @pl.when(step == 2 * at)
        def _():
            copy.wait()


def forward_kernel(group, span_len, tiles, spans_ref, q_ref, *refs):
    pieces, (mixed_ref, exact_ref, lse_ref, q_all, acc, total, kv_all, sems) = refs[: tiles // 2], refs[tiles // 2 :]
    step = pl.program_id(0)
    load_pieces(step, pieces, kv_all, sems)
    score_scale = 1.0 / math.sqrt(HD)
    rows = group * span_len

    @pl.when(step == 0)
    def _():
        for half in range(2):
            for g in range(group):
                q_all[half, g * span_len : (g + 1) * span_len, :] = q_ref[
                    half * span_len : (half + 1) * span_len, g * HD : (g + 1) * HD
                ]
        acc[...] = jnp.zeros_like(acc)
        total[...] = jnp.zeros_like(total)

    tile_span = spans_ref[step]
    here = pl.ds(pl.multiple_of((step % 2) * span_len, span_len), span_len)
    key = kv_all[step // 2, here, :HD]
    value = kv_all[step // 2, here, HD:]

    def visit(half, diagonal):
        weights = jnp.exp(cap_value * scores(q_all[half], key, score_scale))
        if diagonal:
            flip = spans_ref[tiles + 2]
            shape = (rows, span_len)
            q_pos = (lax.broadcasted_iota(jnp.int32, shape, 0) % span_len) ^ flip
            k_pos = lax.broadcasted_iota(jnp.int32, shape, 1) ^ flip
            weights = jnp.where(k_pos <= q_pos, weights, 0.0)
        part = weights[:, :128]
        for at in range(128, span_len, 128):
            part = part + weights[:, at : at + 128]
        total[half] += part
        acc[half] += jnp.dot(weights.astype(bf16), value, preferred_element_type=f32)

    for half in range(2):
        own = spans_ref[tiles + half]

        @pl.when(tile_span < own)
        def _():
            visit(half, False)

        @pl.when(tile_span == own)
        def _():
            visit(half, True)

    @pl.when(step == tiles - 1)
    def _():
        for half in range(2):
            sums = jnp.sum(total[half], axis=1, keepdims=True)
            exact = acc[half] / sums
            lse_ref[half] = jnp.log(jnp.sum(total[half].T, axis=0, keepdims=True))
            for g in range(group):
                piece = exact[g * span_len : (g + 1) * span_len]
                place = (slice(half * span_len, (half + 1) * span_len), slice(g * HD, (g + 1) * HD))
                exact_ref[place] = piece
                mixed_ref[place] = piece.astype(bf16)


def backward_kernel(group, span_len, tiles, spans_ref, q_ref, g_ref, exact_ref, lse_ref, cosine_ref, sine_ref, *refs):
    pieces, rest = refs[: tiles // 2], refs[tiles // 2 :]
    dq_ref, near_ref, far_ref, q_all, g_all, delta, dq_acc, kv_all, sems = rest
    step = pl.program_id(0)
    load_pieces(step, pieces, kv_all, sems)
    score_scale = 1.0 / math.sqrt(HD)
    rows = group * span_len

    @pl.when(step == 0)
    def _():
        for half in range(2):
            for g in range(group):
                place = (slice(half * span_len, (half + 1) * span_len), slice(g * HD, (g + 1) * HD))
                here = slice(g * span_len, (g + 1) * span_len)
                q_all[half, here, :] = q_ref[place]
                g_all[half, here, :] = g_ref[place]
                product = g_ref[place].astype(f32) * exact_ref[place]
                folded = product[:, :128] + product[:, 128:]
                delta[half, :, here] = jnp.sum(folded.T, axis=0, keepdims=True)
        dq_acc[...] = jnp.zeros_like(dq_acc)

    tile_span = spans_ref[step]
    here = pl.ds(pl.multiple_of((step % 2) * span_len, span_len), span_len)
    key = kv_all[step // 2, here, :HD]
    value = kv_all[step // 2, here, HD:]

    def visit(half, diagonal):
        query = q_all[half]
        grad = g_all[half]
        tangent = scores(key, query, score_scale)
        probability = jnp.exp(cap_value * tangent - lse_ref[half])
        if diagonal:
            flip = spans_ref[tiles + 2]
            shape = (span_len, rows)
            q_pos = (lax.broadcasted_iota(jnp.int32, shape, 1) % span_len) ^ flip
            k_pos = lax.broadcasted_iota(jnp.int32, shape, 0) ^ flip
            probability = jnp.where(k_pos <= q_pos, probability, 0.0)
        grad_prob = lax.dot_general(value, grad, (((1,), (1,)), ((), ())), preferred_element_type=f32)
        grad_raw = probability * (grad_prob - delta[half]) * ((1.0 - tangent * tangent) * score_scale)
        grad_raw = grad_raw.astype(bf16)
        dv = jnp.dot(probability.astype(bf16), grad, preferred_element_type=f32)
        dk = jnp.dot(grad_raw, query, preferred_element_type=f32)
        dq_acc[half] += lax.dot_general(grad_raw, key, (((0,), (0,)), ((), ())), preferred_element_type=f32)
        return dk, dv

    def put(dk, dv):
        @pl.when(step < tiles // 2)
        def _():
            near_ref[:, :HD] = dk.astype(bf16)
            near_ref[:, HD:] = dv.astype(bf16)

        @pl.when(step >= tiles // 2)
        def _():
            far_ref[:, :HD] = dk.astype(bf16)
            far_ref[:, HD:] = dv.astype(bf16)

    low, high = spans_ref[tiles], spans_ref[tiles + 1]
    first, second = tile_span <= low, tile_span <= high

    @pl.when(jnp.logical_not(jnp.logical_or(first, second)))
    def _():
        put(jnp.zeros((span_len, HD), f32), jnp.zeros((span_len, HD), f32))

    for half, own, other in ((0, low, high), (1, high, low)):
        for diagonal in (False, True):
            here = tile_span == own if diagonal else tile_span < own

            @pl.when(jnp.logical_and(here, tile_span > other))
            def _(half=half, diagonal=diagonal):
                put(*visit(half, diagonal))

    for half, own, other in ((0, low, high), (1, high, low)):
        for diagonal in (False, True):
            here = tile_span == own if diagonal else tile_span < own

            @pl.when(jnp.logical_and(here, own < other))
            def _(half=half, diagonal=diagonal):
                dk_low, dv_low = visit(half, diagonal)
                dk_high, dv_high = visit(1 - half, False)
                put(dk_low + dk_high, dv_low + dv_high)

    @pl.when(step == tiles - 1)
    def _():
        for half in range(2):
            for g in range(group):
                here = slice(half * span_len, (half + 1) * span_len)
                turned = rotated(
                    dq_acc[half, g * span_len : (g + 1) * span_len], cosine_ref[here, :], sine_ref[here, :], -1.0
                )
                dq_ref[here, g * HD : (g + 1) * HD] = turned.astype(bf16)


def attention_forward(spans, queries, pieces, span_len):
    tiles = 2 * len(pieces)
    kv_size = len(pieces) * pieces[0].size
    width = queries.shape[1]
    group = width // HD
    rows = group * span_len
    whole = lambda s, t: (0, 0)
    visits = tiles + 1
    return pl.pallas_call(
        functools.partial(forward_kernel, group, span_len, tiles),
        grid_spec=pltpu.PrefetchScalarGridSpec(
            num_scalar_prefetch=1,
            grid=(tiles,),
            in_specs=[
                pl.BlockSpec(queries.shape, whole),
            ]
            + [pl.BlockSpec(memory_space=pltpu.HBM)] * len(pieces),
            out_specs=[
                pl.BlockSpec(queries.shape, whole),
                pl.BlockSpec(queries.shape, whole),
                pl.BlockSpec((2, 1, rows), lambda s, t: (0, 0, 0)),
            ],
            scratch_shapes=[
                pltpu.VMEM((2, rows, HD), bf16),
                pltpu.VMEM((2, rows, HD), f32),
                pltpu.VMEM((2, rows, 128), f32),
                pltpu.VMEM((len(pieces),) + pieces[0].shape, bf16),
                pltpu.SemaphoreType.DMA((len(pieces),)),
            ],
        ),
        out_shape=[
            jax.ShapeDtypeStruct(queries.shape, bf16),
            jax.ShapeDtypeStruct(queries.shape, f32),
            jax.ShapeDtypeStruct((2, 1, rows), f32),
        ],
        compiler_params=pltpu.CompilerParams(vmem_limit_bytes=14 * 1024 * 1024 + 2 * kv_size),
        cost_estimate=pl.CostEstimate(
            flops=visits * rows * span_len * HD * 4,
            bytes_accessed=kv_size * 2 + queries.size * 12,
            transcendentals=visits * rows * span_len * 2,
        ),
        name="attention_forward",
    )(spans, queries, *pieces)


def attention_backward(spans, queries, grads, exact, lse, table, pieces, span_len):
    tiles = 2 * len(pieces)
    kv_size = len(pieces) * pieces[0].size
    width = queries.shape[1]
    group = width // HD
    rows = group * span_len
    whole = lambda s, t: (0, 0)
    visits = tiles + 1
    return pl.pallas_call(
        functools.partial(backward_kernel, group, span_len, tiles),
        grid_spec=pltpu.PrefetchScalarGridSpec(
            num_scalar_prefetch=1,
            grid=(tiles,),
            in_specs=[
                pl.BlockSpec(queries.shape, whole),
                pl.BlockSpec(queries.shape, whole),
                pl.BlockSpec(queries.shape, whole),
                pl.BlockSpec((2, 1, rows), lambda s, t: (0, 0, 0)),
                pl.BlockSpec(table[0].shape, whole),
                pl.BlockSpec(table[0].shape, whole),
            ]
            + [pl.BlockSpec(memory_space=pltpu.HBM)] * len(pieces),
            out_specs=[
                pl.BlockSpec(queries.shape, whole),
                pl.BlockSpec((span_len, 2 * HD), lambda s, t: (jnp.minimum(s, tiles // 2 - 1), 0)),
                pl.BlockSpec((span_len, 2 * HD), lambda s, t: (jnp.maximum(s - tiles // 2, 0), 0)),
            ],
            scratch_shapes=[
                pltpu.VMEM((2, rows, HD), bf16),
                pltpu.VMEM((2, rows, HD), bf16),
                pltpu.VMEM((2, 1, rows), f32),
                pltpu.VMEM((2, rows, HD), f32),
                pltpu.VMEM((len(pieces),) + pieces[0].shape, bf16),
                pltpu.SemaphoreType.DMA((len(pieces),)),
            ],
        ),
        out_shape=[
            jax.ShapeDtypeStruct(queries.shape, bf16),
            jax.ShapeDtypeStruct((tiles * span_len // 2, 2 * HD), bf16),
            jax.ShapeDtypeStruct((tiles * span_len // 2, 2 * HD), bf16),
        ],
        compiler_params=pltpu.CompilerParams(vmem_limit_bytes=18 * 1024 * 1024 + 2 * kv_size),
        cost_estimate=pl.CostEstimate(
            flops=visits * rows * span_len * HD * 10,
            bytes_accessed=kv_size * 4 + queries.size * 16,
            transcendentals=visits * rows * span_len * 2,
        ),
        name="attention_backward",
    )(spans, queries, grads, exact, lse, *table, *pieces)


def product(left, right, left_dim, right_dim, out=f32):
    result = lax.dot_general(left, right, (((left_dim,), (right_dim,)), ((), ())), preferred_element_type=f32)
    return result.astype(out)


def on_device(
    hidden_in,
    out_grad,
    span_order,
    w_query,
    w_key,
    w_value,
    w_output,
    w_gate,
    w_up,
    w_down,
    norm_scales,
):
    local_rows = hidden_in.shape[0]
    head_count = lax.axis_size("head")
    block_count = lax.axis_size("blk")
    block_index = lax.axis_index("blk")
    head_index = lax.axis_index("head")
    group_rows = local_rows * head_count
    span_len = group_rows // 2
    model_rows, query_width = w_query.shape
    model_width = hidden_in.shape[1]
    query_heads = query_width // HD
    half_units = w_gate.shape[1] // 2

    chip_masks = bits(block_count)[1:]
    pair, top = chip_masks[0], chip_masks[-1]
    far_masks = chip_masks[:0:-1]
    head_axes = [(0, mask) for mask in bits(head_count)]
    unit_axes = head_axes + [(pair, 0)]
    unit_side = (block_index // pair) % 2
    bit_count = len(chip_masks) + 1

    def side(mask):
        return (block_index // mask) % 2

    def send(value, mask, *after):
        return swap(tie(value, *after), (mask, 0))

    def segment(body, inputs, after=(), flying=()):
        inputs, after = lax.optimization_barrier((tuple(inputs), after))
        shapes = jax.eval_shape(body, *inputs)

        def nothing(*_):
            return jax.tree.map(lambda x: jnp.zeros(x.shape, x.dtype), shapes)

        results = lax.cond(span_order[0] >= 0, body, nothing, *inputs)
        return lax.optimization_barrier((results, flying))

    def far_spread(value, *after):
        held = {0: value}
        for mask in far_masks:
            for have in list(held):
                held[have ^ mask] = send(held[have], mask, *after)
        return held

    def near_spread(held, *after):
        return held | {have ^ pair: send(block, pair, *(after if have == 0 else ())) for have, block in held.items()}

    def split_dims(partial):
        return partial.reshape((2,) * bit_count + (-1, partial.shape[-1]))

    def halve(value, dim, mask, *after):
        moved = send(pick(value, dim, 1 - side(mask)), mask, *after)
        return plus(pick(value, dim, side(mask)), moved)

    slot = jnp.arange(head_count, dtype=jnp.int32) ^ head_index
    in_block = (slot[:, None] * local_rows + jnp.arange(local_rows, dtype=jnp.int32)[None, :]).reshape(-1)
    head_side = head_index // (head_count // 2)
    own_spans = jnp.stack([span_order[2 * block_index + head_side], span_order[2 * block_index + 1 - head_side]])
    row_spans = jnp.repeat(own_spans, span_len)
    position = row_spans * span_len + in_block % span_len
    even_masks = [0]
    for mask in chip_masks[::-1]:
        even_masks = even_masks + [have ^ mask for have in even_masks]
    slot_masks = even_masks + [mask ^ 1 for mask in even_masks]
    tile_blocks = jnp.array(slot_masks, jnp.int32) ^ block_index
    tile_slots = (2 * tile_blocks[:, None] + jnp.stack([head_side, 1 - head_side])[None, :]).reshape(-1)
    flip = (head_index % (head_count // 2)) * local_rows
    spans = jnp.concatenate([span_order[tile_slots], own_spans, flip[None]]).astype(jnp.int32)
    table = rotation(position)

    scale_count = norm_scales.shape[0]
    kv_at = head_index * query_heads // (H // KVH) * HD
    kv_local = jnp.concatenate(
        [
            lax.dynamic_slice_in_dim(w_key, kv_at, HD, 1),
            lax.dynamic_slice_in_dim(w_value, kv_at, HD, 1),
        ],
        1,
    )
    scale_local = jnp.pad(norm_scales, ((0, 16 - scale_count), (0, 2 * HD - model_rows)))
    kv_local = jnp.concatenate([kv_local, scale_local], 0)

    def half(local, index):
        return lax.dynamic_slice_in_dim(local, index * half_units, half_units, 1)

    def unit_slices():
        weights = (w_gate, w_up, w_down.T)
        return (
            half(w_gate, unit_side),
            jnp.concatenate([half(w, unit_side) for w in weights[1:]], 1),
            jnp.concatenate([half(w, 1 - unit_side) for w in weights[:2]], 1),
            half(weights[2], 1 - unit_side),
        )

    hidden_near = [swap(hidden_in, axis) for axis in head_axes]
    kv_chips = far_spread(kv_local)
    kv_chips.pop(0)
    kv_chips[pair] = send(kv_local, pair)
    (query_output_local, unit_local), (hidden_near, kv_chips) = segment(
        lambda w_query, w_output: (jnp.concatenate([w_query, w_output.T], 1), unit_slices()),
        (w_query, w_output),
        (table,),
        (hidden_near, kv_chips),
    )
    first_mine, second_mine, first_theirs, second_theirs = unit_local

    def first_rows(hidden_near, kv_chips):
        held = {0: kv_local} | kv_chips
        held |= {mask ^ pair: swap(block, (pair, 0)) for mask, block in kv_chips.items() if mask != pair}
        parts = {0: [hidden_in]} | {1 << at: [part] for at, part in enumerate(hidden_near)}
        for subset in range(1, head_count):
            if subset not in parts:
                ways = route(subset, len(head_axes), False)
                cuts = shares(local_rows, len(ways)) if len(ways) > 1 else [(0, local_rows)]
                parts[subset] = [
                    swap(parts[subset ^ (1 << way)][0][low:high], head_axes[way]) for way, (low, high) in zip(ways, cuts)
                ]
        def normed_keys(held, parts):
            came = ()
            for mask, block in list(held.items()):
                held[mask ^ 1] = swap(tie(block, *came), (1, 0))
                came = (held[mask ^ 1],)
            scale_blocks = place_scales(held, model_rows, block_index)
            scale_rows = scale_blocks.reshape(block_count, 16, 2 * HD)[:, :scale_count, :model_rows]
            scale_rows = scale_rows.transpose(1, 0, 2).reshape(scale_count, model_width).astype(f32)
            arrays = [part for slot in sorted(parts) for part in parts[slot]]
            normed_full, inverse_full = whole_call(
                functools.partial(norm_full_kernel, len(arrays)),
                [((group_rows, model_width), bf16), ((group_rows, 1), f32)],
                *arrays,
                scale_rows,
                name="norm_full",
            )
            kv_held = {mask: (block, 0) for mask, block in held.items()}
            kv_rows, kv_weight = project(normed_full, [kv_held], [2 * HD], table, 1, block_index, "key_rows")
            return kv_rows, kv_weight, scale_rows, normed_full, inverse_full

        first = held[pair ^ top], *[part for slot, pieces in parts.items() if slot.bit_count() > 1 for part in pieces]
        query_output = {mask: send(query_output_local, mask, *first) for mask in (*far_masks, pair)}
        results, query_output = segment(normed_keys, (held, parts), (), query_output)
        return results, parts, query_output

    first_results, hidden_parts, query_output_chips = first_rows(hidden_near, kv_chips)
    kv_rows, kv_weight, scale_rows, normed_full, inverse_full = first_results
    hidden_slots = [part for slot in sorted(hidden_parts) for part in hidden_parts[slot]]
    row_shape = (local_rows, model_width)
    scale_shape = (1, model_width)

    if len(far_masks) > 1:
        query_output_chips = far_spread(query_output_local) | {pair: query_output_chips[pair]}
    query_output_chips[0] = query_output_local
    kv_far = far_spread(kv_rows)
    kv_far.pop(0)
    kv_near = send(kv_rows, pair)
    query_output_last = {
        mask ^ pair: send(block, pair, kv_rows) for mask, block in query_output_chips.items() if mask & ~pair
    }

    def beside_keys(kv_rows):
        cores, came = {}, ()
        for mask, block in ({-1: kv_rows} | query_output_chips).items():
            cores[mask] = swap(tie(block, *came), (1, 0))
            came = (cores[mask],)
        return cores

    cores, (kv_far, kv_near, query_output_last) = segment(
        beside_keys, (kv_rows,), (), (kv_far, kv_near, query_output_last)
    )

    def keys_and_queries(kv_far, kv_near, query_output_last):
        across = {mask ^ pair: swap(block, (pair, 0)) for mask, block in kv_far.items()}
        chips = query_output_chips | query_output_last
        held = query_output_last | {-1 - mask: piece for mask, piece in ({pair: kv_near} | kv_far).items()}
        came, others = (), dict(cores)
        for mask, block in held.items():
            others[mask] = swap(tie(block, *came), (1, 0))
            came = (others[mask],)
        chips |= {mask ^ 1: block for mask, block in others.items() if mask >= 0}
        queries, query_weight, output_weight = project(
            normed_full,
            [{mask: (block, column) for mask, block in chips.items()} for column in (0, query_width)],
            [query_width, query_width],
            table,
            query_heads,
            block_index,
            "query_rows",
        )
        came += (queries,)
        for mask, block in across.items():
            others[-1 - mask] = swap(tie(block, *came), (1, 0))
            came = (others[-1 - mask],)
        pieces = {(-1 - mask) ^ 1: piece for mask, piece in others.items() if mask < 0}
        return across | pieces, query_weight, output_weight, queries

    first_near = far_spread(first_mine, kv_far[top])
    (kv_others, query_weight, output_weight, queries), first_near = segment(
        keys_and_queries, (kv_far, kv_near, query_output_last), (), first_near
    )
    kv_held = {0: kv_rows, pair: kv_near} | kv_far | kv_others
    kv_pieces = [kv_held[mask] for mask in slot_masks]

    def row_sum(partial, axes, light=False):
        shaped = partial.reshape(1 << len(axes), local_rows, model_width)
        return scatter_rows([shaped[i] for i in range(1 << len(axes))], axes, light)

    def attend(queries, first_near, second_mine):
        mixed, exact, lse = attention_forward(spans, queries, kv_pieces, span_len)
        cores = in_turn(first_near | {-1: second_mine})
        second_core = cores.pop(-1)
        first_core = {mask ^ 1: block for mask, block in cores.items()}
        mixed = tie(mixed, first_core, second_core)
        terms = row_sum(product(mixed, output_weight, 1, 1, bf16), head_axes)
        rows = whole_call(
            functools.partial(after_attention_kernel, len(terms)),
            [(row_shape, f32), (row_shape, f32), (row_shape, bf16)],
            *terms,
            hidden_in,
            scale_rows,
            name="after_attention",
        )
        return (mixed, exact, lse, *rows, first_core, second_core)

    second_near = far_spread(second_mine, queries)
    first_cross = send(first_theirs, pair, queries)
    (mixed, exact, lse, attn_out, resid, ffn_in, first_core, second_core), (second_near, first_cross) = segment(
        attend, (queries, first_near, second_mine), (), (second_near, first_cross)
    )
    second_far = {mask: block for mask, block in second_near.items() if mask}

    def join_units(ffn_in, first_cross, second_far):
        parts = {0: [ffn_in]}
        plan = hops(len(unit_axes), True)
        parts |= gather_hop(parts, unit_axes, True, plan[0])
        flat = [part for t in plan[0][:-1] for part in parts[t]]
        parts |= gather_hop(parts, unit_axes, True, plan[1], flat)

        def later_hops(parts):
            parts = gather_rows(None, unit_axes, True, parts)
            third = [part for t in parts if t.bit_count() > 1 and t != len(parts) - 1 for part in parts[t]]
            first_core = swap(tie(first_cross, *parts[len(parts) // 2]), (1, 0))
            second_cores = {
                mask ^ 1: swap(tie(block, *third, first_core), (1, 0)) for mask, block in second_far.items()
            }
            return join_rows(parts), first_core, second_cores

        second_cross = send(second_theirs, pair, parts)
        return segment(later_hops, (parts,), (), second_cross)

    first_across = far_spread(first_cross, ffn_in)
    ((ffn_full, cross_core, far_cores), second_cross), first_across = segment(
        join_units, (ffn_in, first_cross, second_far), (), first_across
    )
    second_held = second_near | {1: second_core} | far_cores

    def gate_and_up(ffn_full, first_across):
        cores = {1: cross_core} | {mask ^ 1: swap(block, (1, 0)) for mask, block in first_across.items() if mask}
        across = {mask ^ pair: block for mask, block in (first_across | cores).items()}
        gate_held = {mask: (block, 0) for mask, block in (first_near | first_core | across).items()}
        up_held = {mask: (block, 0) for mask, block in second_held.items()}
        up_held |= {mask: (block, half_units) for mask, block in across.items()}
        units = hidden_units(ffn_full, [gate_held, up_held], half_units, block_index)
        return units, swap(second_cross, (1, 0))

    second_across = far_spread(second_cross, ffn_full)
    ((hidden, active, slope, gate_weight, up_weight), second_cross_core), second_across = segment(
        gate_and_up, (ffn_full, first_across), (), second_across
    )
    down_held = {mask: (block, half_units) for mask, block in second_held.items()}
    down_held |= {mask ^ pair: (block, 0) for mask, block in second_across.items()}
    down_held |= {
        mask ^ pair ^ 1: (swap(block, (1, 0)) if mask else second_cross_core, 0)
        for mask, block in second_across.items()
    }
    *ffn_parts, down_weight = down_rows(hidden, down_held, block_index, 1 << len(unit_axes))
    ffn_terms = scatter_rows(ffn_parts, unit_axes)
    layer_out, grad_ffn_out, scale_grad3 = whole_call(
        functools.partial(after_ffn_kernel, len(ffn_terms)),
        [(row_shape, bf16), (row_shape, bf16), (scale_shape, f32)],
        *ffn_terms,
        resid,
        out_grad,
        scale_rows,
        name="after_ffn",
    )

    def unit_core(partial):
        summed = halve(split_dims(partial), bit_count - 1, 1).astype(bf16)
        return pick(summed, 0, 1 - side(top)), pick(summed, 0, side(top))

    def unit_sides(kept, came):
        part = plus(kept, came).astype(bf16)
        for mask in far_masks[1:]:
            part = halve(part, 0, mask).astype(bf16)
        return pick(part, 0, 1 - unit_side), pick(part, 0, unit_side)

    def unit_whole(own, other):
        low = jnp.where(unit_side == 0, own, other)
        high = jnp.where(unit_side == 0, other, own)
        return jnp.concatenate([low, high], 1).astype(f32)

    def core_sum(partial):
        return halve(split_dims(partial), bit_count - 1, 1).astype(bf16)

    grad_ffn_full = join_rows(gather_rows(grad_ffn_out, unit_axes))
    grad_down = product(grad_ffn_full, hidden, 0, 0, bf16)
    grad_hidden = product(tie(grad_ffn_full, grad_down), down_weight, 1, 0)
    grad_gate_act = (grad_hidden * slope).astype(bf16)
    grad_up_act = (grad_hidden * active).astype(bf16)
    down_away, down_kept = unit_core(grad_down)
    down_came = send(down_away, top)

    def weight_back(act):
        return product(ffn_full, act, 0, 0, bf16)

    back_plan = scatter_plan(len(unit_axes), True)
    split_at = next(i for i, hop in enumerate(back_plan) if 1 << (len(unit_axes) - 1) in hop)

    def beside_hops(bodies):
        results = []

        def beside(number):
            def run(moved):
                if number >= len(bodies):
                    return None, moved
                result, moved = segment(bodies[number], tuple(results[-1:]), (), moved)
                results.append(result)
                return result, moved

            return run

        return beside, results

    def ffn_back_first(grad_gate_act, grad_up_act):
        parts = two_products(grad_gate_act, gate_weight, grad_up_act, up_weight, 1 << len(unit_axes))
        pieces, came = {t: [part] for t, part in enumerate(parts)}, ()
        beside, results = beside_hops([lambda: weight_back(tie(grad_gate_act, *parts)), unit_core])
        for number, subsets in enumerate(back_plan[:split_at]):
            pieces, came, _ = scatter_hop(pieces, unit_axes, True, subsets, came, beside(number))
        return pieces, results[1]

    (ffn_pieces, (gate_away, gate_kept)), down_came = segment(
        ffn_back_first, (grad_gate_act, grad_up_act), (down_away, down_kept), down_came
    )

    def ffn_back_last(ffn_pieces, grad_up_act, down_came):
        last = 1 << (len(unit_axes) - 1)

        def over_head(pieces, grad_up_act):
            came = ()
            beside, results = beside_hops(
                [lambda: weight_back(grad_up_act), lambda partial: (unit_core(partial), unit_sides(down_kept, down_came))]
            )
            for number, subsets in enumerate(back_plan[split_at:]):
                subsets = [t for t in subsets if t != last]
                pieces, came, _ = scatter_hop(pieces, unit_axes, True, subsets, came, beside(number))
            return pieces[0], results[1]

        pieces = dict(ffn_pieces)
        across = swap(pieces.pop(last)[0], unit_axes[-1])
        (terms, results), across = segment(over_head, (pieces, grad_up_act), (), across)
        rows = whole_call(
            functools.partial(after_ffn_back_kernel, len(terms) + 1),
            [(row_shape, f32), (row_shape, bf16), (scale_shape, f32), (scale_shape, f32)],
            *terms,
            across,
            resid,
            attn_out,
            out_grad,
            scale_rows,
            name="after_ffn_back",
        )
        return (*rows, *results)

    gate_came = [send(gate_away[0], top, down_came), None]
    (grad_resid, grad_attn, scale_grad2, scale_grad1, (up_away, up_kept), (down_far, down_own)), gate_came[0] = segment(
        ffn_back_last, (ffn_pieces, grad_up_act, down_came), (gate_away, gate_kept), gate_came[0]
    )

    def attend_back(grad_attn):
        grad_attn_full = join_rows(gather_rows(grad_attn, head_axes))
        grad_mixed = product(grad_attn_full, output_weight, 1, 0, bf16)
        grad_query_lin, kv_near, kv_far = attention_backward(
            spans, queries, grad_mixed, exact, lse, table, kv_pieces, span_len
        )
        kv_terms = plus(kv_near, swap(kv_far, (1, 0))).astype(bf16).reshape(-1, group_rows, 2 * HD)
        middle = kv_terms.shape[0] // 2
        return grad_attn_full, grad_query_lin, kv_terms[:middle], kv_terms[middle:]

    gate_came[1] = send(gate_away[1], top, grad_attn)
    up_came = [send(up_away[0], top, grad_attn), None]
    down_other = send(down_far, pair, grad_attn)
    (grad_attn_full, grad_query_lin, kv_kept, kv_away), (gate_came[1], up_came[0], down_other) = segment(
        attend_back, (grad_attn,), (up_away, up_kept, down_far, down_own), (gate_came[1], up_came[0], down_other)
    )

    def projections_back(grad_query_lin, gate_came):
        core = core_sum(outer((normed_full, grad_query_lin), (grad_attn_full, mixed)))
        away, kept = pick(core, bit_count - 2, 1 - unit_side), pick(core, bit_count - 2, unit_side)
        parts = [(pick(away, 0, index), pick(kept, 0, index)) for index in (1 - side(top), side(top))]
        return parts, unit_sides(gate_kept, jnp.stack(gate_came))

    kv_came = send(kv_away, pair)
    (((onward_away, onward_kept), (staying_away, staying_kept)), (gate_far, gate_own)), kv_came = segment(
        projections_back, (grad_query_lin, gate_came), (), kv_came
    )
    kv_terms = plus(kv_kept, kv_came).astype(bf16)
    for mask in chip_masks[1:-1]:
        middle = kv_terms.shape[0] // 2
        kv_terms = plus(kv_terms[:middle], swap(kv_terms[middle:], (mask, 0))).astype(bf16)

    def beside_last_keys(down_other):
        return unit_whole(down_own, down_other).T

    kv_came = send(kv_terms[1], top)
    gate_other = send(gate_far, pair, kv_terms)
    out_down, (kv_came, gate_other) = segment(beside_last_keys, (down_other,), (kv_terms,), (kv_came, gate_other))

    def normed_rows_back(kv_kept, kv_came):
        normed_plan = scatter_plan(len(head_axes), False)

        def first_sums_back(kv_kept, kv_came):
            (grad_kv_lin,) = whole_call(
                key_value_grad_kernel,
                [((group_rows, 2 * HD), bf16)],
                kv_kept,
                kv_came,
                *table,
                name="key_value_grad",
            )
            *parts, scale_grad0 = normed_back(
                grad_query_lin, query_weight, grad_kv_lin, kv_weight, inverse_full, hidden_slots, head_count
            )

            def key_weights_back(grad_kv_lin, scale_grad0):
                scale_grad = jnp.concatenate([scale_grad0, scale_grad1, scale_grad2, scale_grad3], 0).astype(bf16)
                scale_grad = scale_grad.reshape(scale_count, block_count, model_rows).transpose(1, 0, 2)
                scale_grad = jnp.pad(scale_grad, ((0, 0), (0, 16 - scale_count), (0, 2 * HD - model_rows)))
                partial = outer((normed_full, grad_kv_lin)).reshape(block_count, model_rows, 2 * HD)
                terms = core_sum(jnp.concatenate([partial, scale_grad], 1).reshape(-1, 2 * HD))
                return pick(terms, bit_count - 2, 1 - unit_side), pick(terms, bit_count - 2, unit_side)

            def beside(moved):
                return segment(key_weights_back, (grad_kv_lin, scale_grad0), (), moved)

            pieces = {t: [part] for t, part in enumerate(parts)}
            pieces, _, terms = scatter_hop(pieces, head_axes, False, normed_plan[0], (), beside)
            return pieces, terms

        onward_came = send(onward_away, pair, kv_came)
        (pieces, (away, kept)), onward_came = segment(first_sums_back, (kv_kept, kv_came), (), onward_came)
        onward = plus(onward_kept, onward_came).astype(bf16)
        for at, mask in list(enumerate(chip_masks))[1:-1]:
            onward = halve(onward, bit_count - 3 - at, mask).astype(bf16)
        onward_query, onward_output = lax.optimization_barrier((onward[:, :query_width], onward[:, query_width:]))

        def sums_back(pieces):
            came = ()
            for subsets in normed_plan[1:]:
                pieces, came, _ = scatter_hop(pieces, head_axes, False, subsets, came)
            (grad_in,) = whole_call(
                functools.partial(after_all_kernel, len(pieces[0])),
                [(row_shape, f32)],
                *pieces[0],
                hidden_in,
                grad_resid,
                scale_rows,
                name="after_all",
            )
            return grad_in

        wkv_came = send(away, pair)
        output_came = send(onward_output, top)
        grad_in, (wkv_came, output_came) = segment(sums_back, (pieces,), (away, kept), (wkv_came, output_came))
        wkv_terms = plus(kept, wkv_came).astype(bf16)
        for at, mask in list(enumerate(chip_masks))[1:-1]:
            wkv_terms = halve(wkv_terms, bit_count - 2 - at, mask).astype(bf16)
        return grad_in, pick(wkv_terms, 0, 1 - side(top)), pick(wkv_terms, 0, side(top)), output_came, onward_query

    up_came[1] = send(up_away[1], top, kv_came)
    (grad_in, wkv_away, wkv_kept, output_came, onward_query), up_came[1] = segment(
        normed_rows_back, (kv_terms[0], kv_came), (out_down, onward_away), up_came[1]
    )
    wkv_came = send(wkv_away, top)
    staying_came = send(staying_away, pair, wkv_away)

    def beside_key_weights(up_came, gate_other):
        return unit_sides(up_kept, jnp.stack(up_came)), unit_whole(gate_own, gate_other)

    ((up_far, up_own), out_gate), (wkv_came, staying_came) = segment(
        beside_key_weights, (up_came, gate_other), (wkv_away, wkv_kept), (wkv_came, staying_came)
    )
    grad_wkv = plus(wkv_kept, wkv_came).astype(bf16)
    query_came = send(onward_query, top, grad_wkv)
    up_other = send(up_far, pair, grad_wkv)

    def head_rows(grad_wkv, staying_kept, staying_came, output_came):
        staying = plus(staying_kept, staying_came).astype(bf16)
        for at, mask in list(enumerate(chip_masks))[1:-1]:
            staying = halve(staying, bit_count - 3 - at, mask).astype(bf16)
        out_output = plus(staying[:, query_width:], output_came).T
        staying_query = staying[:, :query_width]
        parts = gather_rows(grad_wkv, head_axes)
        if head_count == KVH:
            out_key, out_value, scale_total = place_heads(parts, model_rows, scale_count, head_index)
            return out_key, out_value, scale_total[:, :model_rows], out_output, staying_query
        wkv_ordered = jnp.zeros((head_count,) + grad_wkv.shape, bf16)
        for mask, pieces in parts.items():
            first = 0
            for piece in pieces:
                wkv_ordered = lax.dynamic_update_slice(wkv_ordered, piece[None], (head_index ^ mask, first, 0))
                first += piece.shape[0]
        wkv_ordered = wkv_ordered.astype(f32)
        scale_total = wkv_ordered[:, model_rows : model_rows + scale_count, :model_rows].sum(0)
        wkv_ordered = wkv_ordered[:, :model_rows].reshape(KVH, head_count // KVH, model_rows, 2, HD).sum(1)
        out_key = wkv_ordered[:, :, 0].transpose(1, 0, 2).reshape(model_rows, KVH * HD)
        out_value = wkv_ordered[:, :, 1].transpose(1, 0, 2).reshape(model_rows, KVH * HD)
        return out_key, out_value, scale_total, out_output, staying_query

    (out_key, out_value, scale_total, out_output, staying_query), (query_came, up_other) = segment(
        head_rows, (grad_wkv, staying_kept, staying_came, output_came), (onward_query, up_far), (query_came, up_other)
    )
    out_query = plus(staying_query, query_came)
    out_up = unit_whole(up_own, up_other)

    return (
        layer_out,
        grad_in,
        out_query,
        out_key,
        out_value,
        out_output,
        out_gate,
        out_up,
        out_down,
        scale_total,
    )


def solution(mesh):
    placed = (
        P(("blk", "head"), None),
        P(("blk", "head"), None),
        P(),
        P("blk", "head"),
        P("blk", None),
        P("blk", None),
        P("head", "blk"),
        P("blk", "head"),
        P("blk", "head"),
        P("head", "blk"),
        P(None, "blk"),
    )
    return jax.shard_map(
        on_device,
        mesh=mesh,
        in_specs=placed,
        out_specs=(
            P(("blk", "head"), None),
            P(("blk", "head"), None),
            P("blk", "head"),
            P("blk", None),
            P("blk", None),
            P("head", "blk"),
            P("blk", "head"),
            P("blk", "head"),
            P("head", "blk"),
            P(None, "blk"),
        ),
        check_vma=False,
    )
```

```python
import functools
import math

import jax
import jax.numpy as jnp
from jax import lax
from jax.experimental import pallas as pl
from jax.experimental.pallas import tpu as pltpu
from jax.sharding import PartitionSpec as P

H = 8
KVH = 4
HD = 256

norm_eps = 1e-06
cap_value = 50.0
theta_base = 10000.0
f32 = jnp.float32
bf16 = jnp.bfloat16


def inverse_rms(value):
    return lax.rsqrt(jnp.mean(value * value, axis=-1, keepdims=True) + norm_eps)


def rms_back(value, scale, grad):
    inverse = inverse_rms(value)
    scaled = grad * scale
    inner = jnp.mean(scaled * value, axis=-1, keepdims=True)
    grad_value = inverse * scaled - value * (inverse * inverse * inverse) * inner
    grad_scale = jnp.sum(grad * value * inverse, axis=0, keepdims=True)
    return (grad_value, grad_scale)


def rotation(position):
    entry = jnp.arange(HD, dtype=jnp.int32)
    quarter = HD // 4
    pair_index = entry // (2 * quarter) * quarter + entry % quarter
    frequency = jnp.power(theta_base, -2.0 * pair_index.astype(f32) / HD)
    angles = position.astype(f32)[:, None] * frequency[None, :]
    sign = jnp.where(entry % (2 * quarter) < quarter, -1.0, 1.0)
    return jnp.cos(angles), jnp.sin(angles) * sign[None, :]


def rotated(value, cosine, sine, sign):
    half = HD // 2
    parts = []
    for at in range(0, HD, half):
        piece = value[:, at : at + half]
        partner = pltpu.roll(piece, half // 2, 1)
        parts.append(piece * cosine[:, at : at + half] + partner * (sign * sine[:, at : at + half]))
    return jnp.concatenate(parts, 1)


def swap(value, axis):
    blk_mask, head_mask = axis
    block_count, head_count = lax.axis_size("blk"), lax.axis_size("head")
    if blk_mask == 0:
        return lax.ppermute(value, "head", [(i, i ^ head_mask) for i in range(head_count)])
    return lax.ppermute(value, "blk", [(i, i ^ blk_mask) for i in range(block_count)])


def bits(count):
    return [1 << i for i in range(count.bit_length() - 1)]


def route(subset, total, light):
    members = [i for i in range(total) if subset >> i & 1]
    if light and len(members) > 1 and members[-1] == total - 1:
        members = members[:-1]
        return members if len(members) == total - 1 else members[:1]
    if len(members) >= 2 and len(members) == total - light:
        return members
    if not light and len(members) == 2 and members[1] - members[0] != 1:
        return members[1:]
    return members[:1]


def hops(total, light):
    size = lambda t: bin(t).count("1")
    last = 1 << (total - 1)
    subsets = range(1, 1 << total)
    if not light:
        return [[t for t in subsets if size(t) == n] for n in range(1, total + 1)]
    result = [[t for t in subsets if size(t) == 1]]
    for high in (0, last):
        for n in range(2, total + 1):
            result.append([t for t in subsets if size(t) == n and t & last == high])
    return [hop for hop in result if hop]


def shares(row_total, parts):
    unit = row_total // 16
    cuts = [unit * i // parts * 16 for i in range(parts + 1)]
    cuts[-1] = row_total
    return list(zip(cuts[:-1], cuts[1:]))


def gather_hop(parts, axes, light, subsets, before=()):
    rows = parts[0][0].shape[0]
    came = {}
    for subset in subsets:
        ways = route(subset, len(axes), light)
        cuts = shares(rows, len(ways)) if len(ways) > 1 else [(0, rows)]
        came[subset] = []
        for way, (low, high) in zip(ways, cuts):
            source = parts[subset ^ (1 << way)][0]
            came[subset].append(swap(tie(source[low:high] if len(ways) > 1 else source, *before), axes[way]))
    return came


def gather_rows(value, axes, light=False, parts=None):
    last = 1 << (len(axes) - 1)
    parts, before = parts or {0: [value]}, ()
    for subsets in hops(len(axes), light):
        if all(t in parts for t in subsets):
            continue
        if light and last in parts:
            before = [x for x in before if x is not parts[last][0]]
            before += parts[last] * any(t & last for t in subsets)
        came = gather_hop(parts, axes, light, subsets, before)
        parts = parts | came
        before = [part for pieces in came.values() for part in pieces]
    return parts


def join_kernel(plan, *refs):
    step = pl.program_id(0)
    out = refs[-1]
    for at, (slot, first, rows) in enumerate(plan):

        @pl.when(step == slot)
        def _():
            out[first : first + rows, :] = refs[at][...]


def join_rows(parts):
    plan, arrays = [], []
    for slot in sorted(parts):
        first = 0
        for array in parts[slot]:
            plan.append((slot, first, array.shape[0]))
            arrays.append(array)
            first += array.shape[0]
    rows, columns = parts[0][0].shape
    return pl.pallas_call(
        functools.partial(join_kernel, plan),
        grid=(len(parts),),
        in_specs=[pl.BlockSpec(a.shape, lambda m: (0, 0), pipeline_mode=pl.Buffered(1)) for a in arrays],
        out_specs=pl.BlockSpec((rows, columns), lambda m: (m, 0)),
        out_shape=jax.ShapeDtypeStruct((len(parts) * rows, columns), arrays[0].dtype),
        compiler_params=pltpu.CompilerParams(vmem_limit_bytes=16 * 1024 * 1024),
        cost_estimate=pl.CostEstimate(flops=0, bytes_accessed=4 * len(parts) * rows * columns, transcendentals=0),
        name="join_rows",
    )(*arrays)


def two_products_kernel(a_ref, u_ref, b_ref, v_ref, *outs):
    nt = (((1,), (1,)), ((), ()))
    total = lax.dot_general(a_ref[...], u_ref[...], nt, preferred_element_type=f32)
    total += lax.dot_general(b_ref[...], v_ref[...], nt, preferred_element_type=f32)
    put_pieces(outs, total)


def put_pieces(outs, value):
    rows = outs[0].shape[0]
    for at, out in enumerate(outs):
        out[...] = value[at * rows : (at + 1) * rows].astype(out.dtype)


def two_products(a, u, b, v, count):
    rows, depth = a.shape
    columns = u.shape[0]
    step = 256
    resident = pl.BlockSpec((rows, depth), lambda n: (0, 0), pipeline_mode=pl.Buffered(1))
    return pl.pallas_call(
        two_products_kernel,
        grid=(columns // step,),
        in_specs=[resident, pl.BlockSpec((step, depth), lambda n: (n, 0))] * 2,
        out_specs=[pl.BlockSpec((rows // count, step), lambda n: (0, n))] * count,
        out_shape=[jax.ShapeDtypeStruct((rows // count, columns), bf16)] * count,
        compiler_params=pltpu.CompilerParams(vmem_limit_bytes=20 * 1024 * 1024),
        cost_estimate=pl.CostEstimate(
            flops=4 * rows * columns * depth,
            bytes_accessed=4 * (rows * depth + columns * depth) + 2 * rows * columns,
            transcendentals=0,
        ),
        name="two_products",
    )(a, u, b, v)


def joined(left, right):
    return (left.astype(f32) + right.astype(f32)).astype(bf16)


def scatter_plan(total, light):
    plan = [list(hop) for hop in hops(total, light)[::-1]]
    last = 1 << (total - 1)
    if light:
        plan[-1].remove(last)
        plan[next(i for i, hop in enumerate(plan) if not any(t & last for t in hop))].append(last)
    return plan


def scatter_hop(pieces, axes, light, subsets, before=(), beside=None):
    last = 1 << (len(axes) - 1)
    pieces = dict(pieces)
    rows = pieces[0][0].shape[0]
    sent, result = [], None
    for subset in subsets:
        (piece,) = pieces.pop(subset)
        ways = route(subset, len(axes), light)
        cuts = shares(rows, len(ways)) if len(ways) > 1 else [(0, rows)]
        for way, (low, high) in zip(ways, cuts):
            part = piece if len(ways) == 1 else piece[low:high]
            sent.append((subset, subset ^ (1 << way), low, high, swap(tie(part, *before), axes[way])))
    if beside:
        result, came = beside([item[4] for item in sent])
        sent = [item[:4] + (moved,) for item, moved in zip(sent, came)]
    for subset, target, low, high, moved in sent:
        if target == 0:
            pieces[0] = pieces[0] + [moved]
        elif high - low == rows:
            pieces[target] = [joined(pieces[target][0], moved)]
        else:
            old = pieces[target][0]
            cut = [old[:low], joined(old[low:high], moved), old[high:]]
            pieces[target] = [jnp.concatenate([c for c in cut if c.shape[0]], 0)]
    came = [item[4] for item in sent if not (light and item[0] == last)]
    return pieces, came, result


def scatter_rows(pieces, axes, light=False):
    pieces, came = {t: [piece] for t, piece in enumerate(pieces)}, ()
    for subsets in scatter_plan(len(axes), light):
        pieces, came, _ = scatter_hop(pieces, axes, light, subsets, came)
    return pieces[0]


def tie(value, *after):
    return lax.optimization_barrier((value, *after))[0] if after else value


def tie_all(held, *after):
    return {mask: tie(block, *after) for mask, block in held.items()}


def scale_kernel(count, index_ref, *refs):
    for mask in range(count):
        row = pl.multiple_of((index_ref[0] ^ mask) * 16, 16)
        refs[count][pl.ds(row, 16), :] = refs[mask][...]


def place_scales(held, rows, block_index):
    count = len(held)
    shape = (16, held[0].shape[1])
    return pl.pallas_call(
        functools.partial(scale_kernel, count),
        grid_spec=pltpu.PrefetchScalarGridSpec(
            num_scalar_prefetch=1,
            grid=(1,),
            in_specs=[pl.BlockSpec(shape, lambda n, b: (rows // 16, 0))] * count,
            out_specs=pl.BlockSpec((count * 16, shape[1]), lambda n, b: (0, 0)),
        ),
        out_shape=jax.ShapeDtypeStruct((count * 16, shape[1]), bf16),
        cost_estimate=pl.CostEstimate(flops=0, bytes_accessed=4 * count * 16 * shape[1], transcendentals=0),
        name="place_scales",
    )(block_index[None].astype(jnp.int32), *[held[mask] for mask in range(count)])


def head_kernel(plan, rows, scale_count, index_ref, *refs):
    parts, (key_ref, value_ref, scale_ref) = refs[: len(plan)], refs[len(plan) :]
    step = pl.program_id(0)

    @pl.when(step == 0)
    def _():
        scale_ref[...] = jnp.zeros_like(scale_ref)

    for part, (slot, first) in zip(parts, plan):
        count = part.shape[0]

        @pl.when(step == slot)
        def _():
            last = min(first + count, rows)
            here, taken = slice(first, last), slice(0, last - first)
            key_ref[here, :] = part[taken, :HD].astype(f32)
            value_ref[here, :] = part[taken, HD:].astype(f32)
            if first + count > rows:
                scale_ref[...] += part[rows - first : rows - first + 16, :].astype(f32)[:scale_count]


def place_heads(parts, rows, scale_count, head_index):
    plan, arrays = [], []
    for slot in sorted(parts):
        first = 0
        for array in parts[slot]:
            plan.append((slot, first))
            arrays.append(array)
            first += array.shape[0]
    columns = pl.BlockSpec((rows, HD), lambda m, h: (0, h[0] ^ m))
    fixed = lambda m, h: (0, 0)
    return pl.pallas_call(
        functools.partial(head_kernel, plan, rows, scale_count),
        grid_spec=pltpu.PrefetchScalarGridSpec(
            num_scalar_prefetch=1,
            grid=(len(parts),),
            in_specs=[pl.BlockSpec(a.shape, fixed, pipeline_mode=pl.Buffered(1)) for a in arrays],
            out_specs=[columns, columns, pl.BlockSpec((scale_count, 2 * HD), fixed)],
        ),
        out_shape=[jax.ShapeDtypeStruct((rows, len(parts) * HD), f32)] * 2
        + [jax.ShapeDtypeStruct((scale_count, 2 * HD), f32)],
        cost_estimate=pl.CostEstimate(flops=0, bytes_accessed=8 * len(parts) * rows * HD, transcendentals=0),
        name="place_heads",
    )(head_index[None].astype(jnp.int32), *arrays)


def placed_kernel(body, plans, counts, steps, index_ref, *refs):
    refs = list(refs)
    arrays, loads, inputs, outs, wholes, weights, loaded = [[refs.pop(0) for _ in range(count)] for count in counts]
    in_sems, out_sems = refs
    step = pl.program_id(0)
    came, at = [], 0
    for source, target in zip(loads, loaded):
        came.append([pltpu.make_async_copy(source, target, in_sems.at[at])])
        at += 1
    gone = [None] * len(loads)
    for weight, plan in zip(weights, plans):
        copies = []
        rows = weight.shape[0] // len(plan)
        for mask, (source, column) in enumerate(plan):
            row = pl.multiple_of((index_ref[0] ^ mask) * rows, 16)
            block = arrays[source].at[pl.ds(0, rows)]
            if arrays[source].shape[1] != weight.shape[1]:
                block = arrays[source].at[pl.ds(0, rows), pl.ds(column, weight.shape[1])]
            copies.append(pltpu.make_async_copy(block, weight.at[pl.ds(row, rows)], in_sems.at[at]))
            at += 1
        came.append(copies)
    gone += [
        pltpu.make_async_copy(weight, whole, out_sems.at[n]) for n, (weight, whole) in enumerate(zip(weights, wholes))
    ]

    @pl.when(step == 0)
    def _():
        for copies in came:
            for copy in copies:
                copy.start()
        for copies, copy_out in zip(came, gone):
            for copy in copies:
                copy.wait()
            if copy_out is not None:
                copy_out.start()

    body(step, loaded + inputs, outs, weights)

    @pl.when(step == steps - 1)
    def _():
        for copy_out in gone[len(loads) :]:
            copy_out.wait()


def placed(body, steps, held, columns, loads, inputs, in_specs, outs, out_specs, block_index, name, flops, vmem):
    arrays, plans = [], []
    for blocks, width in zip(held, columns):
        plan = []
        for mask in range(len(blocks)):
            array, column = blocks[mask]
            if width % 128 or column % 128:
                array, column = array[:, column : column + width], 0
            where = next((n for n, known in enumerate(arrays) if known is array), len(arrays))
            if where == len(arrays):
                arrays.append(array)
            plan.append((where, column))
        plans.append(plan)
    rows = min(array.shape[0] for array in arrays) // 16 * 16
    rows = rows - (16 if name == "key_rows" else 0)
    shapes = [(len(plan) * rows, width) for plan, width in zip(plans, columns)]
    anywhere = pl.BlockSpec(memory_space=pltpu.HBM)
    counts = (len(arrays), len(loads), len(inputs), len(outs), len(plans), len(plans), len(loads))
    return pl.pallas_call(
        functools.partial(placed_kernel, body, plans, counts, steps),
        grid_spec=pltpu.PrefetchScalarGridSpec(
            num_scalar_prefetch=1,
            grid=(steps,),
            in_specs=[anywhere] * (len(arrays) + len(loads)) + in_specs,
            out_specs=out_specs + [anywhere] * len(plans),
            scratch_shapes=[pltpu.VMEM(shape, bf16) for shape in shapes]
            + [pltpu.VMEM(array.shape, array.dtype) for array in loads]
            + [
                pltpu.SemaphoreType.DMA((sum(len(plan) for plan in plans) + len(loads),)),
                pltpu.SemaphoreType.DMA((len(plans),)),
            ],
        ),
        out_shape=outs + [jax.ShapeDtypeStruct(shape, bf16) for shape in shapes],
        compiler_params=pltpu.CompilerParams(vmem_limit_bytes=vmem * 1024 * 1024),
        cost_estimate=pl.CostEstimate(
            flops=flops, bytes_accessed=4 * sum(h * w for h, w in shapes), transcendentals=0
        ),
        name=name,
    )(block_index[None].astype(jnp.int32), *arrays, *loads, *inputs)


def in_turn(held):
    came = []
    for block in held.values():
        came.append(swap(tie(block, *came[-2:-1]), (1, 0)))
    return dict(zip(held, came))


def both_cores(held):
    return held | {mask ^ 1: swap(block, (1, 0)) for mask, block in held.items()}


def pick(value, dim, index):
    return lax.dynamic_index_in_dim(value, index, dim, keepdims=False)


def plus(left, right):
    return left.astype(f32) + right.astype(f32)


def whole_call(body, outs, *inputs, name):
    size = sum(x.size * x.dtype.itemsize for x in inputs)
    return pl.pallas_call(
        body,
        out_shape=[jax.ShapeDtypeStruct(shape, dtype) for shape, dtype in outs],
        compiler_params=pltpu.CompilerParams(vmem_limit_bytes=28 * 1024 * 1024),
        cost_estimate=pl.CostEstimate(flops=0, bytes_accessed=2 * size, transcendentals=0),
        name=name,
    )(*inputs)


def summed(refs):
    total = refs[0][...].astype(f32)
    for ref in refs[1:]:
        total = total + ref[...].astype(f32)
    return total


def norm_full_kernel(count, *refs):
    parts, (scale, normed, inverse) = refs[:count], refs[count:]
    first = 0
    for part in parts:
        value = part[...].astype(f32)
        here = slice(first, first + part.shape[0])
        first += part.shape[0]
        factor = inverse_rms(value)
        inverse[here, :] = factor
        normed[here, :] = (value * factor * scale[0:1, :]).astype(bf16)


def after_attention_kernel(count, *refs):
    terms, (hidden, scales, attn_out, resid_out, ffn_in) = refs[:count], refs[count:]
    attn = summed(terms)
    attn_out[...] = attn
    resid = hidden[...].astype(f32) + attn * inverse_rms(attn) * scales[1:2, :]
    resid_out[...] = resid
    ffn_in[...] = (resid * inverse_rms(resid) * scales[2:3, :]).astype(bf16)


def after_ffn_kernel(count, *refs):
    terms, (resid, out_grad, scales, layer_out, grad_out, grad_scale) = refs[:count], refs[count:]
    ffn_out = summed(terms)
    grad, grad_scale[...] = rms_back(ffn_out, scales[3:4, :], out_grad[...].astype(f32))
    grad_out[...] = grad.astype(bf16)
    layer_out[...] = (resid[...] + ffn_out * inverse_rms(ffn_out) * scales[3:4, :]).astype(bf16)


def after_ffn_back_kernel(count, *refs):
    terms, (resid, attn, out_grad, scales, grad_resid, grad_attn, grad_scale2, grad_scale1) = refs[:count], refs[count:]
    grad, grad_scale2[...] = rms_back(resid[...], scales[2:3, :], summed(terms))
    grad = out_grad[...].astype(f32) + grad
    grad_resid[...] = grad
    back, grad_scale1[...] = rms_back(attn[...], scales[1:2, :], grad)
    grad_attn[...] = back.astype(bf16)


def after_all_kernel(count, *refs):
    terms, (hidden, grad_resid, scales, grad_in) = refs[:count], refs[count:]
    grad, _ = rms_back(hidden[...].astype(f32), scales[0:1, :], summed(terms))
    grad_in[...] = grad_resid[...] + grad


def key_value_grad_kernel(kept, came, cosine, sine, out):
    total = kept[...].astype(f32) + came[...].astype(f32)
    out[:, :HD] = rotated(total[:, :HD], cosine[...], sine[...], -1.0).astype(bf16)
    out[:, HD:] = total[:, HD:].astype(bf16)


def project(rows, held, columns, table, turning, block_index, name):
    count, depth = rows.shape
    heads = columns[0] // HD
    fixed = lambda n, b: (0, 0)
    once = pl.Buffered(1)

    def body(step, inputs, outs, weights):
        rows_ref, cosine_ref, sine_ref = inputs
        (out_ref,) = outs
        here = pl.ds(pl.multiple_of(step * HD, HD), HD)
        value = jnp.dot(rows_ref[...], weights[0][:, here], preferred_element_type=f32)

        @pl.when(step < turning)
        def _():
            out_ref[...] = rotated(value, cosine_ref[...], sine_ref[...], 1.0).astype(bf16)

        @pl.when(step >= turning)
        def _():
            out_ref[...] = value.astype(bf16)

    return placed(
        body,
        heads,
        held,
        columns,
        [rows],
        list(table),
        [
            pl.BlockSpec((count, HD), fixed, pipeline_mode=once),
            pl.BlockSpec((count, HD), fixed, pipeline_mode=once),
        ],
        [jax.ShapeDtypeStruct((count, columns[0]), bf16)],
        [pl.BlockSpec((count, HD), lambda n, b: (0, n))],
        block_index,
        name,
        2 * rows.size * columns[0],
        20,
    )


def hidden_units(rows, held, width, block_index):
    count, depth = rows.shape
    step = 256

    def body(number, inputs, outs, weights):
        hidden_ref, active_ref, slope_ref = outs
        gate = jnp.dot(inputs[0][...], weights[0][...], preferred_element_type=f32)
        up = jnp.dot(inputs[0][...], weights[1][...], preferred_element_type=f32)
        inner = math.sqrt(2.0 / math.pi)
        square = gate * gate
        tangent = jnp.tanh(inner * gate * (1.0 + 0.044715 * square))
        share = 0.5 * (1.0 + tangent)
        active = gate * share
        slope = share + (0.5 * inner) * gate * (1.0 - tangent * tangent) * (1.0 + (3 * 0.044715) * square)
        hidden_ref[...] = (active * up).astype(bf16)
        active_ref[...] = active
        slope_ref[...] = slope * up

    return placed(
        body,
        count // step,
        held,
        [width, width],
        [],
        [rows],
        [pl.BlockSpec((step, depth), lambda n, b: (n, 0))],
        [jax.ShapeDtypeStruct((count, width), dtype) for dtype in (bf16, f32, f32)],
        [pl.BlockSpec((step, width), lambda n, b: (n, 0))] * 3,
        block_index,
        "hidden_units",
        4 * rows.size * width,
        40,
    )


def down_rows(hidden, held, block_index, pieces):
    count, width = hidden.shape
    depth = len(held) * held[0][0].shape[0]
    step = 768 if depth % 768 == 0 else 256

    def body(number, inputs, outs, weights):
        here = pl.ds(pl.multiple_of(number * step, step), step)
        value = lax.dot_general(
            inputs[0][...], weights[0][here, :], (((1,), (1,)), ((), ())), preferred_element_type=f32
        )
        put_pieces(outs, value)

    return placed(
        body,
        depth // step,
        [held],
        [width],
        [hidden],
        [],
        [],
        [jax.ShapeDtypeStruct((count // pieces, depth), bf16)] * pieces,
        [pl.BlockSpec((count // pieces, step), lambda n, b: (0, n))] * pieces,
        block_index,
        "down_rows",
        2 * hidden.size * depth,
        24,
    )


def outer_kernel(*refs):
    pairs, out = refs[:-1], refs[-1]
    width = 0
    for left, right in zip(pairs[::2], pairs[1::2]):
        columns = right.shape[1]
        value = lax.dot_general(left[...], right[...], (((0,), (0,)), ((), ())), preferred_element_type=f32)
        out[:, width : width + columns] = value.astype(bf16)
        width += columns


def outer(*pairs):
    rows, depth = pairs[0][0].shape
    width = sum(right.shape[1] for _, right in pairs)
    step = depth // 2
    specs = []
    for _, right in pairs:
        specs.append(pl.BlockSpec((rows, step), lambda n: (0, n)))
        specs.append(pl.BlockSpec(right.shape, lambda n: (0, 0), pipeline_mode=pl.Buffered(1)))
    return pl.pallas_call(
        outer_kernel,
        grid=(depth // step,),
        in_specs=specs,
        out_specs=pl.BlockSpec((step, width), lambda n: (n, 0)),
        out_shape=jax.ShapeDtypeStruct((depth, width), bf16),
        compiler_params=pltpu.CompilerParams(vmem_limit_bytes=24 * 1024 * 1024),
        cost_estimate=pl.CostEstimate(
            flops=2 * rows * depth * width, bytes_accessed=2 * (rows * depth * len(pairs) + depth * width), transcendentals=0
        ),
        name="outer",
    )(*[x for pair in pairs for x in pair])


def normed_back_kernel(count, q_ref, wq_ref, kv_ref, wkv_ref, inverse_ref, *refs):
    hidden, (*outs, scale_ref) = refs[:count], refs[count:]
    nt = (((1,), (1,)), ((), ()))
    total = lax.dot_general(q_ref[...], wq_ref[...], nt, preferred_element_type=f32)
    total += lax.dot_general(kv_ref[...], wkv_ref[...], nt, preferred_element_type=f32)
    put_pieces(outs, total)
    grad_scale, first = jnp.zeros((1, total.shape[1]), f32), 0
    for part in hidden:
        here = slice(first, first + part.shape[0])
        first += part.shape[0]
        unit = part[...].astype(f32) * inverse_ref[here, :]
        grad_scale += jnp.sum(total[here, :] * unit, axis=0, keepdims=True)
    scale_ref[...] = grad_scale


def normed_back(grad_query, query_weight, grad_kv, kv_weight, inverse, hidden, pieces):
    rows, width = grad_query.shape
    kv_width = grad_kv.shape[1]
    columns = query_weight.shape[0]
    step = 768 if columns % 768 == 0 else 256
    fixed = lambda n: (0, 0)
    once = pl.Buffered(1)
    return pl.pallas_call(
        functools.partial(normed_back_kernel, len(hidden)),
        grid=(columns // step,),
        in_specs=[
            pl.BlockSpec((rows, width), fixed, pipeline_mode=once),
            pl.BlockSpec((step, width), lambda n: (n, 0)),
            pl.BlockSpec((rows, kv_width), fixed, pipeline_mode=once),
            pl.BlockSpec((step, kv_width), lambda n: (n, 0)),
            pl.BlockSpec((rows, 1), fixed, pipeline_mode=once),
        ]
        + [pl.BlockSpec((part.shape[0], step), lambda n: (0, n)) for part in hidden],
        out_specs=[pl.BlockSpec((rows // pieces, step), lambda n: (0, n))] * pieces
        + [pl.BlockSpec((1, step), lambda n: (0, n))],
        out_shape=[jax.ShapeDtypeStruct((rows // pieces, columns), bf16)] * pieces
        + [jax.ShapeDtypeStruct((1, columns), f32)],
        compiler_params=pltpu.CompilerParams(vmem_limit_bytes=20 * 1024 * 1024),
        cost_estimate=pl.CostEstimate(
            flops=2 * rows * columns * (width + kv_width), bytes_accessed=4 * rows * columns, transcendentals=0
        ),
        name="normed_back",
    )(grad_query, query_weight, grad_kv, kv_weight, inverse, *hidden)


def scores(query, key, score_scale):
    raw = lax.dot_general(query, key, (((1,), (1,)), ((), ())), preferred_element_type=f32)
    return jnp.tanh(raw * (score_scale / cap_value))


def load_pieces(step, pieces, kv_all, sems):
    copies = [pltpu.make_async_copy(piece, kv_all.at[at], sems.at[at]) for at, piece in enumerate(pieces)]

    @pl.when(step == 0)
    def _():
        for copy in copies:
            copy.start()

    for at, copy in enumerate(copies):

        @pl.when(step == 2 * at)
        def _():
            copy.wait()


def forward_kernel(group, span_len, tiles, spans_ref, q_ref, *refs):
    pieces, (mixed_ref, exact_ref, lse_ref, q_all, acc, total, kv_all, sems) = refs[: tiles // 2], refs[tiles // 2 :]
    step = pl.program_id(0)
    load_pieces(step, pieces, kv_all, sems)
    score_scale = 1.0 / math.sqrt(HD)
    rows = group * span_len

    @pl.when(step == 0)
    def _():
        for half in range(2):
            for g in range(group):
                q_all[half, g * span_len : (g + 1) * span_len, :] = q_ref[
                    half * span_len : (half + 1) * span_len, g * HD : (g + 1) * HD
                ]
        acc[...] = jnp.zeros_like(acc)
        total[...] = jnp.zeros_like(total)

    tile_span = spans_ref[step]
    here = pl.ds(pl.multiple_of((step % 2) * span_len, span_len), span_len)
    key = kv_all[step // 2, here, :HD]
    value = kv_all[step // 2, here, HD:]

    def visit(half, diagonal):
        weights = jnp.exp(cap_value * scores(q_all[half], key, score_scale))
        if diagonal:
            flip = spans_ref[tiles + 2]
            shape = (rows, span_len)
            q_pos = (lax.broadcasted_iota(jnp.int32, shape, 0) % span_len) ^ flip
            k_pos = lax.broadcasted_iota(jnp.int32, shape, 1) ^ flip
            weights = jnp.where(k_pos <= q_pos, weights, 0.0)
        part = weights[:, :128]
        for at in range(128, span_len, 128):
            part = part + weights[:, at : at + 128]
        total[half] += part
        acc[half] += jnp.dot(weights.astype(bf16), value, preferred_element_type=f32)

    for half in range(2):
        own = spans_ref[tiles + half]

        @pl.when(tile_span < own)
        def _():
            visit(half, False)

        @pl.when(tile_span == own)
        def _():
            visit(half, True)

    @pl.when(step == tiles - 1)
    def _():
        for half in range(2):
            sums = jnp.sum(total[half], axis=1, keepdims=True)
            exact = acc[half] / sums
            lse_ref[half] = jnp.log(jnp.sum(total[half].T, axis=0, keepdims=True))
            for g in range(group):
                piece = exact[g * span_len : (g + 1) * span_len]
                place = (slice(half * span_len, (half + 1) * span_len), slice(g * HD, (g + 1) * HD))
                exact_ref[place] = piece
                mixed_ref[place] = piece.astype(bf16)


def backward_kernel(group, span_len, tiles, spans_ref, q_ref, g_ref, exact_ref, lse_ref, cosine_ref, sine_ref, *refs):
    pieces, rest = refs[: tiles // 2], refs[tiles // 2 :]
    dq_ref, near_ref, far_ref, q_all, g_all, delta, dq_acc, kv_all, sems = rest
    step = pl.program_id(0)
    load_pieces(step, pieces, kv_all, sems)
    score_scale = 1.0 / math.sqrt(HD)
    rows = group * span_len

    @pl.when(step == 0)
    def _():
        for half in range(2):
            for g in range(group):
                place = (slice(half * span_len, (half + 1) * span_len), slice(g * HD, (g + 1) * HD))
                here = slice(g * span_len, (g + 1) * span_len)
                q_all[half, here, :] = q_ref[place]
                g_all[half, here, :] = g_ref[place]
                product = g_ref[place].astype(f32) * exact_ref[place]
                folded = product[:, :128] + product[:, 128:]
                delta[half, :, here] = jnp.sum(folded.T, axis=0, keepdims=True)
        dq_acc[...] = jnp.zeros_like(dq_acc)

    tile_span = spans_ref[step]
    here = pl.ds(pl.multiple_of((step % 2) * span_len, span_len), span_len)
    key = kv_all[step // 2, here, :HD]
    value = kv_all[step // 2, here, HD:]

    def visit(half, diagonal):
        query = q_all[half]
        grad = g_all[half]
        tangent = scores(key, query, score_scale)
        probability = jnp.exp(cap_value * tangent - lse_ref[half])
        if diagonal:
            flip = spans_ref[tiles + 2]
            shape = (span_len, rows)
            q_pos = (lax.broadcasted_iota(jnp.int32, shape, 1) % span_len) ^ flip
            k_pos = lax.broadcasted_iota(jnp.int32, shape, 0) ^ flip
            probability = jnp.where(k_pos <= q_pos, probability, 0.0)
        grad_prob = lax.dot_general(value, grad, (((1,), (1,)), ((), ())), preferred_element_type=f32)
        grad_raw = probability * (grad_prob - delta[half]) * ((1.0 - tangent * tangent) * score_scale)
        grad_raw = grad_raw.astype(bf16)
        dv = jnp.dot(probability.astype(bf16), grad, preferred_element_type=f32)
        dk = jnp.dot(grad_raw, query, preferred_element_type=f32)
        dq_acc[half] += lax.dot_general(grad_raw, key, (((0,), (0,)), ((), ())), preferred_element_type=f32)
        return dk, dv

    def put(dk, dv):
        @pl.when(step < tiles // 2)
        def _():
            near_ref[:, :HD] = dk.astype(bf16)
            near_ref[:, HD:] = dv.astype(bf16)

        @pl.when(step >= tiles // 2)
        def _():
            far_ref[:, :HD] = dk.astype(bf16)
            far_ref[:, HD:] = dv.astype(bf16)

    low, high = spans_ref[tiles], spans_ref[tiles + 1]
    first, second = tile_span <= low, tile_span <= high

    @pl.when(jnp.logical_not(jnp.logical_or(first, second)))
    def _():
        put(jnp.zeros((span_len, HD), f32), jnp.zeros((span_len, HD), f32))

    for half, own, other in ((0, low, high), (1, high, low)):
        for diagonal in (False, True):
            here = tile_span == own if diagonal else tile_span < own

            @pl.when(jnp.logical_and(here, tile_span > other))
            def _(half=half, diagonal=diagonal):
                put(*visit(half, diagonal))

    for half, own, other in ((0, low, high), (1, high, low)):
        for diagonal in (False, True):
            here = tile_span == own if diagonal else tile_span < own

            @pl.when(jnp.logical_and(here, own < other))
            def _(half=half, diagonal=diagonal):
                dk_low, dv_low = visit(half, diagonal)
                dk_high, dv_high = visit(1 - half, False)
                put(dk_low + dk_high, dv_low + dv_high)

    @pl.when(step == tiles - 1)
    def _():
        for half in range(2):
            for g in range(group):
                here = slice(half * span_len, (half + 1) * span_len)
                turned = rotated(
                    dq_acc[half, g * span_len : (g + 1) * span_len], cosine_ref[here, :], sine_ref[here, :], -1.0
                )
                dq_ref[here, g * HD : (g + 1) * HD] = turned.astype(bf16)


def attention_forward(spans, queries, pieces, span_len):
    tiles = 2 * len(pieces)
    kv_size = len(pieces) * pieces[0].size
    width = queries.shape[1]
    group = width // HD
    rows = group * span_len
    whole = lambda s, t: (0, 0)
    visits = tiles + 1
    return pl.pallas_call(
        functools.partial(forward_kernel, group, span_len, tiles),
        grid_spec=pltpu.PrefetchScalarGridSpec(
            num_scalar_prefetch=1,
            grid=(tiles,),
            in_specs=[
                pl.BlockSpec(queries.shape, whole),
            ]
            + [pl.BlockSpec(memory_space=pltpu.HBM)] * len(pieces),
            out_specs=[
                pl.BlockSpec(queries.shape, whole),
                pl.BlockSpec(queries.shape, whole),
                pl.BlockSpec((2, 1, rows), lambda s, t: (0, 0, 0)),
            ],
            scratch_shapes=[
                pltpu.VMEM((2, rows, HD), bf16),
                pltpu.VMEM((2, rows, HD), f32),
                pltpu.VMEM((2, rows, 128), f32),
                pltpu.VMEM((len(pieces),) + pieces[0].shape, bf16),
                pltpu.SemaphoreType.DMA((len(pieces),)),
            ],
        ),
        out_shape=[
            jax.ShapeDtypeStruct(queries.shape, bf16),
            jax.ShapeDtypeStruct(queries.shape, f32),
            jax.ShapeDtypeStruct((2, 1, rows), f32),
        ],
        compiler_params=pltpu.CompilerParams(vmem_limit_bytes=14 * 1024 * 1024 + 2 * kv_size),
        cost_estimate=pl.CostEstimate(
            flops=visits * rows * span_len * HD * 4,
            bytes_accessed=kv_size * 2 + queries.size * 12,
            transcendentals=visits * rows * span_len * 2,
        ),
        name="attention_forward",
    )(spans, queries, *pieces)


def attention_backward(spans, queries, grads, exact, lse, table, pieces, span_len):
    tiles = 2 * len(pieces)
    kv_size = len(pieces) * pieces[0].size
    width = queries.shape[1]
    group = width // HD
    rows = group * span_len
    whole = lambda s, t: (0, 0)
    visits = tiles + 1
    return pl.pallas_call(
        functools.partial(backward_kernel, group, span_len, tiles),
        grid_spec=pltpu.PrefetchScalarGridSpec(
            num_scalar_prefetch=1,
            grid=(tiles,),
            in_specs=[
                pl.BlockSpec(queries.shape, whole),
                pl.BlockSpec(queries.shape, whole),
                pl.BlockSpec(queries.shape, whole),
                pl.BlockSpec((2, 1, rows), lambda s, t: (0, 0, 0)),
                pl.BlockSpec(table[0].shape, whole),
                pl.BlockSpec(table[0].shape, whole),
            ]
            + [pl.BlockSpec(memory_space=pltpu.HBM)] * len(pieces),
            out_specs=[
                pl.BlockSpec(queries.shape, whole),
                pl.BlockSpec((span_len, 2 * HD), lambda s, t: (jnp.minimum(s, tiles // 2 - 1), 0)),
                pl.BlockSpec((span_len, 2 * HD), lambda s, t: (jnp.maximum(s - tiles // 2, 0), 0)),
            ],
            scratch_shapes=[
                pltpu.VMEM((2, rows, HD), bf16),
                pltpu.VMEM((2, rows, HD), bf16),
                pltpu.VMEM((2, 1, rows), f32),
                pltpu.VMEM((2, rows, HD), f32),
                pltpu.VMEM((len(pieces),) + pieces[0].shape, bf16),
                pltpu.SemaphoreType.DMA((len(pieces),)),
            ],
        ),
        out_shape=[
            jax.ShapeDtypeStruct(queries.shape, bf16),
            jax.ShapeDtypeStruct((tiles * span_len // 2, 2 * HD), bf16),
            jax.ShapeDtypeStruct((tiles * span_len // 2, 2 * HD), bf16),
        ],
        compiler_params=pltpu.CompilerParams(vmem_limit_bytes=18 * 1024 * 1024 + 2 * kv_size),
        cost_estimate=pl.CostEstimate(
            flops=visits * rows * span_len * HD * 10,
            bytes_accessed=kv_size * 4 + queries.size * 16,
            transcendentals=visits * rows * span_len * 2,
        ),
        name="attention_backward",
    )(spans, queries, grads, exact, lse, *table, *pieces)


def product(left, right, left_dim, right_dim, out=f32):
    result = lax.dot_general(left, right, (((left_dim,), (right_dim,)), ((), ())), preferred_element_type=f32)
    return result.astype(out)


def on_device(
    hidden_in,
    out_grad,
    span_order,
    w_query,
    w_key,
    w_value,
    w_output,
    w_gate,
    w_up,
    w_down,
    norm_scales,
):
    local_rows = hidden_in.shape[0]
    head_count = lax.axis_size("head")
    block_count = lax.axis_size("blk")
    block_index = lax.axis_index("blk")
    head_index = lax.axis_index("head")
    group_rows = local_rows * head_count
    span_len = group_rows // 2
    model_rows, query_width = w_query.shape
    model_width = hidden_in.shape[1]
    query_heads = query_width // HD
    half_units = w_gate.shape[1] // 2

    chip_masks = bits(block_count)[1:]
    pair, top = chip_masks[0], chip_masks[-1]
    far_masks = chip_masks[:0:-1]
    head_axes = [(0, mask) for mask in bits(head_count)]
    unit_axes = head_axes + [(pair, 0)]
    unit_side = (block_index // pair) % 2
    bit_count = len(chip_masks) + 1

    def side(mask):
        return (block_index // mask) % 2

    def send(value, mask, *after):
        return swap(tie(value, *after), (mask, 0))

    def segment(body, inputs, after=(), flying=()):
        inputs, after = lax.optimization_barrier((tuple(inputs), after))
        shapes = jax.eval_shape(body, *inputs)

        def nothing(*_):
            return jax.tree.map(lambda x: jnp.zeros(x.shape, x.dtype), shapes)

        results = lax.cond(span_order[0] >= 0, body, nothing, *inputs)
        return lax.optimization_barrier((results, flying))

    def far_spread(value, *after):
        held = {0: value}
        for mask in far_masks:
            for have in list(held):
                held[have ^ mask] = send(held[have], mask, *after)
        return held

    def near_spread(held, *after):
        return held | {have ^ pair: send(block, pair, *(after if have == 0 else ())) for have, block in held.items()}

    def split_dims(partial):
        return partial.reshape((2,) * bit_count + (-1, partial.shape[-1]))

    def halve(value, dim, mask, *after):
        moved = send(pick(value, dim, 1 - side(mask)), mask, *after)
        return plus(pick(value, dim, side(mask)), moved)

    slot = jnp.arange(head_count, dtype=jnp.int32) ^ head_index
    in_block = (slot[:, None] * local_rows + jnp.arange(local_rows, dtype=jnp.int32)[None, :]).reshape(-1)
    head_side = head_index // (head_count // 2)
    own_spans = jnp.stack([span_order[2 * block_index + head_side], span_order[2 * block_index + 1 - head_side]])
    row_spans = jnp.repeat(own_spans, span_len)
    position = row_spans * span_len + in_block % span_len
    even_masks = [0]
    for mask in chip_masks[::-1]:
        even_masks = even_masks + [have ^ mask for have in even_masks]
    slot_masks = even_masks + [mask ^ 1 for mask in even_masks]
    tile_blocks = jnp.array(slot_masks, jnp.int32) ^ block_index
    tile_slots = (2 * tile_blocks[:, None] + jnp.stack([head_side, 1 - head_side])[None, :]).reshape(-1)
    flip = (head_index % (head_count // 2)) * local_rows
    spans = jnp.concatenate([span_order[tile_slots], own_spans, flip[None]]).astype(jnp.int32)
    table = rotation(position)

    scale_count = norm_scales.shape[0]
    kv_at = head_index * query_heads // (H // KVH) * HD
    kv_local = jnp.concatenate(
        [
            lax.dynamic_slice_in_dim(w_key, kv_at, HD, 1),
            lax.dynamic_slice_in_dim(w_value, kv_at, HD, 1),
        ],
        1,
    )
    scale_local = jnp.pad(norm_scales, ((0, 16 - scale_count), (0, 2 * HD - model_rows)))
    kv_local = jnp.concatenate([kv_local, scale_local], 0)

    def half(local, index):
        return lax.dynamic_slice_in_dim(local, index * half_units, half_units, 1)

    def unit_slices():
        weights = (w_gate, w_up, w_down.T)
        return (
            half(w_gate, unit_side),
            jnp.concatenate([half(w, unit_side) for w in weights[1:]], 1),
            jnp.concatenate([half(w, 1 - unit_side) for w in weights[:2]], 1),
            half(weights[2], 1 - unit_side),
        )

    hidden_near = [swap(hidden_in, axis) for axis in head_axes]
    kv_chips = far_spread(kv_local)
    kv_chips.pop(0)
    kv_chips[pair] = send(kv_local, pair)
    (query_output_local, unit_local), (hidden_near, kv_chips) = segment(
        lambda w_query, w_output: (jnp.concatenate([w_query, w_output.T], 1), unit_slices()),
        (w_query, w_output),
        (table,),
        (hidden_near, kv_chips),
    )
    first_mine, second_mine, first_theirs, second_theirs = unit_local

    def first_rows(hidden_near, kv_chips):
        held = {0: kv_local} | kv_chips
        held |= {mask ^ pair: swap(block, (pair, 0)) for mask, block in kv_chips.items() if mask != pair}
        parts = {0: [hidden_in]} | {1 << at: [part] for at, part in enumerate(hidden_near)}
        for subset in range(1, head_count):
            if subset not in parts:
                ways = route(subset, len(head_axes), False)
                cuts = shares(local_rows, len(ways)) if len(ways) > 1 else [(0, local_rows)]
                parts[subset] = [
                    swap(parts[subset ^ (1 << way)][0][low:high], head_axes[way]) for way, (low, high) in zip(ways, cuts)
                ]
        def normed_keys(held, parts):
            came = ()
            for mask, block in list(held.items()):
                held[mask ^ 1] = swap(tie(block, *came), (1, 0))
                came = (held[mask ^ 1],)
            scale_blocks = place_scales(held, model_rows, block_index)
            scale_rows = scale_blocks.reshape(block_count, 16, 2 * HD)[:, :scale_count, :model_rows]
            scale_rows = scale_rows.transpose(1, 0, 2).reshape(scale_count, model_width).astype(f32)
            arrays = [part for slot in sorted(parts) for part in parts[slot]]
            normed_full, inverse_full = whole_call(
                functools.partial(norm_full_kernel, len(arrays)),
                [((group_rows, model_width), bf16), ((group_rows, 1), f32)],
                *arrays,
                scale_rows,
                name="norm_full",
            )
            kv_held = {mask: (block, 0) for mask, block in held.items()}
            kv_rows, kv_weight = project(normed_full, [kv_held], [2 * HD], table, 1, block_index, "key_rows")
            return kv_rows, kv_weight, scale_rows, normed_full, inverse_full

        first = held[pair ^ top], *[part for slot, pieces in parts.items() if slot.bit_count() > 1 for part in pieces]
        query_output = {mask: send(query_output_local, mask, *first) for mask in (*far_masks, pair)}
        results, query_output = segment(normed_keys, (held, parts), (), query_output)
        return results, parts, query_output

    first_results, hidden_parts, query_output_chips = first_rows(hidden_near, kv_chips)
    kv_rows, kv_weight, scale_rows, normed_full, inverse_full = first_results
    hidden_slots = [part for slot in sorted(hidden_parts) for part in hidden_parts[slot]]
    row_shape = (local_rows, model_width)
    scale_shape = (1, model_width)

    if len(far_masks) > 1:
        query_output_chips = far_spread(query_output_local) | {pair: query_output_chips[pair]}
    query_output_chips[0] = query_output_local
    kv_far = far_spread(kv_rows)
    kv_far.pop(0)
    kv_near = send(kv_rows, pair)
    query_output_last = {
        mask ^ pair: send(block, pair, kv_rows) for mask, block in query_output_chips.items() if mask & ~pair
    }

    def beside_keys(kv_rows):
        cores, came = {}, ()
        for mask, block in ({-1: kv_rows} | query_output_chips).items():
            cores[mask] = swap(tie(block, *came), (1, 0))
            came = (cores[mask],)
        return cores

    cores, (kv_far, kv_near, query_output_last) = segment(
        beside_keys, (kv_rows,), (), (kv_far, kv_near, query_output_last)
    )

    def keys_and_queries(kv_far, kv_near, query_output_last):
        across = {mask ^ pair: swap(block, (pair, 0)) for mask, block in kv_far.items()}
        chips = query_output_chips | query_output_last
        held = query_output_last | {-1 - mask: piece for mask, piece in ({pair: kv_near} | kv_far).items()}
        came, others = (), dict(cores)
        for mask, block in held.items():
            others[mask] = swap(tie(block, *came), (1, 0))
            came = (others[mask],)
        chips |= {mask ^ 1: block for mask, block in others.items() if mask >= 0}
        queries, query_weight, output_weight = project(
            normed_full,
            [{mask: (block, column) for mask, block in chips.items()} for column in (0, query_width)],
            [query_width, query_width],
            table,
            query_heads,
            block_index,
            "query_rows",
        )
        came += (queries,)
        for mask, block in across.items():
            others[-1 - mask] = swap(tie(block, *came), (1, 0))
            came = (others[-1 - mask],)
        pieces = {(-1 - mask) ^ 1: piece for mask, piece in others.items() if mask < 0}
        return across | pieces, query_weight, output_weight, queries

    first_near = far_spread(first_mine, kv_far[top])
    (kv_others, query_weight, output_weight, queries), first_near = segment(
        keys_and_queries, (kv_far, kv_near, query_output_last), (), first_near
    )
    kv_held = {0: kv_rows, pair: kv_near} | kv_far | kv_others
    kv_pieces = [kv_held[mask] for mask in slot_masks]

    def row_sum(partial, axes, light=False):
        shaped = partial.reshape(1 << len(axes), local_rows, model_width)
        return scatter_rows([shaped[i] for i in range(1 << len(axes))], axes, light)

    def attend(queries, first_near, second_mine):
        mixed, exact, lse = attention_forward(spans, queries, kv_pieces, span_len)
        cores = in_turn(first_near | {-1: second_mine})
        second_core = cores.pop(-1)
        first_core = {mask ^ 1: block for mask, block in cores.items()}
        mixed = tie(mixed, first_core, second_core)
        terms = row_sum(product(mixed, output_weight, 1, 1, bf16), head_axes)
        rows = whole_call(
            functools.partial(after_attention_kernel, len(terms)),
            [(row_shape, f32), (row_shape, f32), (row_shape, bf16)],
            *terms,
            hidden_in,
            scale_rows,
            name="after_attention",
        )
        return (mixed, exact, lse, *rows, first_core, second_core)

    second_near = far_spread(second_mine, queries)
    first_cross = send(first_theirs, pair, queries)
    (mixed, exact, lse, attn_out, resid, ffn_in, first_core, second_core), (second_near, first_cross) = segment(
        attend, (queries, first_near, second_mine), (), (second_near, first_cross)
    )
    second_far = {mask: block for mask, block in second_near.items() if mask}

    def join_units(ffn_in, first_cross, second_far):
        parts = {0: [ffn_in]}
        plan = hops(len(unit_axes), True)
        parts |= gather_hop(parts, unit_axes, True, plan[0])
        flat = [part for t in plan[0][:-1] for part in parts[t]]
        parts |= gather_hop(parts, unit_axes, True, plan[1], flat)

        def later_hops(parts):
            parts = gather_rows(None, unit_axes, True, parts)
            third = [part for t in parts if t.bit_count() > 1 and t != len(parts) - 1 for part in parts[t]]
            first_core = swap(tie(first_cross, *parts[len(parts) // 2]), (1, 0))
            second_cores = {
                mask ^ 1: swap(tie(block, *third, first_core), (1, 0)) for mask, block in second_far.items()
            }
            return join_rows(parts), first_core, second_cores

        second_cross = send(second_theirs, pair, parts)
        return segment(later_hops, (parts,), (), second_cross)

    first_across = far_spread(first_cross, ffn_in)
    ((ffn_full, cross_core, far_cores), second_cross), first_across = segment(
        join_units, (ffn_in, first_cross, second_far), (), first_across
    )
    second_held = second_near | {1: second_core} | far_cores

    def gate_and_up(ffn_full, first_across):
        cores = {1: cross_core} | {mask ^ 1: swap(block, (1, 0)) for mask, block in first_across.items() if mask}
        across = {mask ^ pair: block for mask, block in (first_across | cores).items()}
        gate_held = {mask: (block, 0) for mask, block in (first_near | first_core | across).items()}
        up_held = {mask: (block, 0) for mask, block in second_held.items()}
        up_held |= {mask: (block, half_units) for mask, block in across.items()}
        units = hidden_units(ffn_full, [gate_held, up_held], half_units, block_index)
        return units, swap(second_cross, (1, 0))

    second_across = far_spread(second_cross, ffn_full)
    ((hidden, active, slope, gate_weight, up_weight), second_cross_core), second_across = segment(
        gate_and_up, (ffn_full, first_across), (), second_across
    )
    down_held = {mask: (block, half_units) for mask, block in second_held.items()}
    down_held |= {mask ^ pair: (block, 0) for mask, block in second_across.items()}
    down_held |= {
        mask ^ pair ^ 1: (swap(block, (1, 0)) if mask else second_cross_core, 0)
        for mask, block in second_across.items()
    }
    *ffn_parts, down_weight = down_rows(hidden, down_held, block_index, 1 << len(unit_axes))
    ffn_terms = scatter_rows(ffn_parts, unit_axes)
    layer_out, grad_ffn_out, scale_grad3 = whole_call(
        functools.partial(after_ffn_kernel, len(ffn_terms)),
        [(row_shape, bf16), (row_shape, bf16), (scale_shape, f32)],
        *ffn_terms,
        resid,
        out_grad,
        scale_rows,
        name="after_ffn",
    )

    def unit_core(partial):
        summed = halve(split_dims(partial), bit_count - 1, 1).astype(bf16)
        return pick(summed, 0, 1 - side(top)), pick(summed, 0, side(top))

    def unit_sides(kept, came):
        part = plus(kept, came).astype(bf16)
        for mask in far_masks[1:]:
            part = halve(part, 0, mask).astype(bf16)
        return pick(part, 0, 1 - unit_side), pick(part, 0, unit_side)

    def unit_whole(own, other):
        low = jnp.where(unit_side == 0, own, other)
        high = jnp.where(unit_side == 0, other, own)
        return jnp.concatenate([low, high], 1).astype(f32)

    def core_sum(partial):
        return halve(split_dims(partial), bit_count - 1, 1).astype(bf16)

    grad_ffn_full = join_rows(gather_rows(grad_ffn_out, unit_axes))
    grad_down = product(grad_ffn_full, hidden, 0, 0, bf16)
    down_dims = split_dims(grad_down)

    def down_half(far, core):
        return pick(pick(down_dims, bit_count - 1, core), 0, far)

    down_away = down_half(1 - side(top), 1 - side(1))
    down_away = plus(down_half(1 - side(top), side(1)), send(down_away, 1)).astype(bf16)
    down_came = send(down_away, top)
    down_other = send(down_half(side(top), 1 - side(1)), 1, down_away)

    def hidden_back(rows):
        grad_hidden = product(rows, down_weight, 1, 0)
        return (grad_hidden * slope).astype(bf16), (grad_hidden * active).astype(bf16)

    (grad_gate_act, grad_up_act), down_other = segment(hidden_back, (grad_ffn_full,), (down_away,), down_other)

    def weight_back(act):
        return product(ffn_full, act, 0, 0, bf16)

    back_plan = scatter_plan(len(unit_axes), True)
    split_at = next(i for i, hop in enumerate(back_plan) if 1 << (len(unit_axes) - 1) in hop)

    def beside_hops(bodies):
        results = []

        def beside(number):
            def run(moved):
                if number >= len(bodies):
                    return None, moved
                result, moved = segment(bodies[number], tuple(results[-1:]), (), moved)
                results.append(result)
                return result, moved

            return run

        return beside, results

    def ffn_back_first(grad_gate_act, grad_up_act):
        parts = two_products(grad_gate_act, gate_weight, grad_up_act, up_weight, 1 << len(unit_axes))
        pieces, came = {t: [part] for t, part in enumerate(parts)}, ()
        beside, results = beside_hops([lambda: weight_back(tie(grad_gate_act, *parts)), unit_core])
        for number, subsets in enumerate(back_plan[:split_at]):
            pieces, came, _ = scatter_hop(pieces, unit_axes, True, subsets, came, beside(number))
        return pieces, results[1]

    (ffn_pieces, (gate_away, gate_kept)), down_came = segment(
        ffn_back_first, (grad_gate_act, grad_up_act), (down_away,), down_came
    )

    def ffn_back_last(ffn_pieces, grad_up_act, down_came):
        last = 1 << (len(unit_axes) - 1)

        def over_head(pieces, grad_up_act):
            came = ()
            beside, results = beside_hops(
                [lambda: weight_back(grad_up_act), lambda partial: (unit_core(partial), unit_sides(plus(down_half(side(top), side(1)), down_other), down_came))]
            )
            for number, subsets in enumerate(back_plan[split_at:]):
                subsets = [t for t in subsets if t != last]
                pieces, came, _ = scatter_hop(pieces, unit_axes, True, subsets, came, beside(number))
            return pieces[0], results[1]

        pieces = dict(ffn_pieces)
        across = swap(pieces.pop(last)[0], unit_axes[-1])
        (terms, results), across = segment(over_head, (pieces, grad_up_act), (), across)
        rows = whole_call(
            functools.partial(after_ffn_back_kernel, len(terms) + 1),
            [(row_shape, f32), (row_shape, bf16), (scale_shape, f32), (scale_shape, f32)],
            *terms,
            across,
            resid,
            attn_out,
            out_grad,
            scale_rows,
            name="after_ffn_back",
        )
        return (*rows, *results)

    gate_came = [send(gate_away[0], top, down_came), None]
    (grad_resid, grad_attn, scale_grad2, scale_grad1, (up_away, up_kept), (down_far, down_own)), gate_came[0] = segment(
        ffn_back_last, (ffn_pieces, grad_up_act, down_came), (gate_away, gate_kept), gate_came[0]
    )

    def attend_back(grad_attn):
        grad_attn_full = join_rows(gather_rows(grad_attn, head_axes))
        grad_mixed = product(grad_attn_full, output_weight, 1, 0, bf16)
        grad_query_lin, kv_near, kv_far = attention_backward(
            spans, queries, grad_mixed, exact, lse, table, kv_pieces, span_len
        )
        kv_terms = plus(kv_near, swap(kv_far, (1, 0))).astype(bf16).reshape(-1, group_rows, 2 * HD)
        middle = kv_terms.shape[0] // 2
        return grad_attn_full, grad_query_lin, kv_terms[:middle], kv_terms[middle:]

    gate_came[1] = send(gate_away[1], top, grad_attn)
    up_came = [send(up_away[0], top, grad_attn), None]
    down_other = send(down_far, pair, grad_attn)
    (grad_attn_full, grad_query_lin, kv_kept, kv_away), (gate_came[1], up_came[0], down_other) = segment(
        attend_back, (grad_attn,), (up_away, up_kept, down_far, down_own), (gate_came[1], up_came[0], down_other)
    )

    def projections_back(grad_query_lin, gate_came):
        core = core_sum(outer((normed_full, grad_query_lin), (grad_attn_full, mixed)))
        away, kept = pick(core, bit_count - 2, 1 - unit_side), pick(core, bit_count - 2, unit_side)
        parts = [(pick(away, 0, index), pick(kept, 0, index)) for index in (1 - side(top), side(top))]
        return parts, unit_sides(gate_kept, jnp.stack(gate_came))

    kv_came = send(kv_away, pair)
    (((onward_away, onward_kept), (staying_away, staying_kept)), (gate_far, gate_own)), kv_came = segment(
        projections_back, (grad_query_lin, gate_came), (), kv_came
    )
    kv_terms = plus(kv_kept, kv_came).astype(bf16)
    for mask in chip_masks[1:-1]:
        middle = kv_terms.shape[0] // 2
        kv_terms = plus(kv_terms[:middle], swap(kv_terms[middle:], (mask, 0))).astype(bf16)

    def beside_last_keys(down_other):
        return unit_whole(down_own, down_other).T

    kv_came = send(kv_terms[1], top)
    gate_other = send(gate_far, pair, kv_terms)
    out_down, (kv_came, gate_other) = segment(beside_last_keys, (down_other,), (kv_terms,), (kv_came, gate_other))

    def normed_rows_back(kv_kept, kv_came):
        normed_plan = scatter_plan(len(head_axes), False)

        def first_sums_back(kv_kept, kv_came):
            (grad_kv_lin,) = whole_call(
                key_value_grad_kernel,
                [((group_rows, 2 * HD), bf16)],
                kv_kept,
                kv_came,
                *table,
                name="key_value_grad",
            )
            *parts, scale_grad0 = normed_back(
                grad_query_lin, query_weight, grad_kv_lin, kv_weight, inverse_full, hidden_slots, head_count
            )

            def key_weights_back(grad_kv_lin, scale_grad0):
                scale_grad = jnp.concatenate([scale_grad0, scale_grad1, scale_grad2, scale_grad3], 0).astype(bf16)
                scale_grad = scale_grad.reshape(scale_count, block_count, model_rows).transpose(1, 0, 2)
                scale_grad = jnp.pad(scale_grad, ((0, 0), (0, 16 - scale_count), (0, 2 * HD - model_rows)))
                partial = outer((normed_full, grad_kv_lin)).reshape(block_count, model_rows, 2 * HD)
                terms = core_sum(jnp.concatenate([partial, scale_grad], 1).reshape(-1, 2 * HD))
                return pick(terms, bit_count - 2, 1 - unit_side), pick(terms, bit_count - 2, unit_side)

            def beside(moved):
                return segment(key_weights_back, (grad_kv_lin, scale_grad0), (), moved)

            pieces = {t: [part] for t, part in enumerate(parts)}
            pieces, _, terms = scatter_hop(pieces, head_axes, False, normed_plan[0], (), beside)
            return pieces, terms

        onward_came = send(onward_away, pair, kv_came)
        (pieces, (away, kept)), onward_came = segment(first_sums_back, (kv_kept, kv_came), (), onward_came)
        onward = plus(onward_kept, onward_came).astype(bf16)
        for at, mask in list(enumerate(chip_masks))[1:-1]:
            onward = halve(onward, bit_count - 3 - at, mask).astype(bf16)
        onward_query, onward_output = lax.optimization_barrier((onward[:, :query_width], onward[:, query_width:]))

        def sums_back(pieces):
            came = ()
            for subsets in normed_plan[1:]:
                pieces, came, _ = scatter_hop(pieces, head_axes, False, subsets, came)
            (grad_in,) = whole_call(
                functools.partial(after_all_kernel, len(pieces[0])),
                [(row_shape, f32)],
                *pieces[0],
                hidden_in,
                grad_resid,
                scale_rows,
                name="after_all",
            )
            return grad_in

        wkv_came = send(away, pair)
        output_came = send(onward_output, top)
        grad_in, (wkv_came, output_came) = segment(sums_back, (pieces,), (away, kept), (wkv_came, output_came))
        wkv_terms = plus(kept, wkv_came).astype(bf16)
        for at, mask in list(enumerate(chip_masks))[1:-1]:
            wkv_terms = halve(wkv_terms, bit_count - 2 - at, mask).astype(bf16)
        return grad_in, pick(wkv_terms, 0, 1 - side(top)), pick(wkv_terms, 0, side(top)), output_came, onward_query

    up_came[1] = send(up_away[1], top, kv_came)
    (grad_in, wkv_away, wkv_kept, output_came, onward_query), up_came[1] = segment(
        normed_rows_back, (kv_terms[0], kv_came), (out_down, onward_away), up_came[1]
    )
    wkv_came = send(wkv_away, top)
    staying_came = send(staying_away, pair, wkv_away)

    def beside_key_weights(up_came, gate_other):
        return unit_sides(up_kept, jnp.stack(up_came)), unit_whole(gate_own, gate_other)

    ((up_far, up_own), out_gate), (wkv_came, staying_came) = segment(
        beside_key_weights, (up_came, gate_other), (wkv_away, wkv_kept), (wkv_came, staying_came)
    )
    grad_wkv = plus(wkv_kept, wkv_came).astype(bf16)
    query_came = send(onward_query, top, grad_wkv)
    up_other = send(up_far, pair, grad_wkv)

    def head_rows(grad_wkv, staying_kept, staying_came, output_came):
        staying = plus(staying_kept, staying_came).astype(bf16)
        for at, mask in list(enumerate(chip_masks))[1:-1]:
            staying = halve(staying, bit_count - 3 - at, mask).astype(bf16)
        out_output = plus(staying[:, query_width:], output_came).T
        staying_query = staying[:, :query_width]
        parts = gather_rows(grad_wkv, head_axes)
        if head_count == KVH:
            out_key, out_value, scale_total = place_heads(parts, model_rows, scale_count, head_index)
            return out_key, out_value, scale_total[:, :model_rows], out_output, staying_query
        wkv_ordered = jnp.zeros((head_count,) + grad_wkv.shape, bf16)
        for mask, pieces in parts.items():
            first = 0
            for piece in pieces:
                wkv_ordered = lax.dynamic_update_slice(wkv_ordered, piece[None], (head_index ^ mask, first, 0))
                first += piece.shape[0]
        wkv_ordered = wkv_ordered.astype(f32)
        scale_total = wkv_ordered[:, model_rows : model_rows + scale_count, :model_rows].sum(0)
        wkv_ordered = wkv_ordered[:, :model_rows].reshape(KVH, head_count // KVH, model_rows, 2, HD).sum(1)
        out_key = wkv_ordered[:, :, 0].transpose(1, 0, 2).reshape(model_rows, KVH * HD)
        out_value = wkv_ordered[:, :, 1].transpose(1, 0, 2).reshape(model_rows, KVH * HD)
        return out_key, out_value, scale_total, out_output, staying_query

    (out_key, out_value, scale_total, out_output, staying_query), (query_came, up_other) = segment(
        head_rows, (grad_wkv, staying_kept, staying_came, output_came), (onward_query, up_far), (query_came, up_other)
    )
    out_query = plus(staying_query, query_came)
    out_up = unit_whole(up_own, up_other)

    return (
        layer_out,
        grad_in,
        out_query,
        out_key,
        out_value,
        out_output,
        out_gate,
        out_up,
        out_down,
        scale_total,
    )


def solution(mesh):
    placed = (
        P(("blk", "head"), None),
        P(("blk", "head"), None),
        P(),
        P("blk", "head"),
        P("blk", None),
        P("blk", None),
        P("head", "blk"),
        P("blk", "head"),
        P("blk", "head"),
        P("head", "blk"),
        P(None, "blk"),
    )
    return jax.shard_map(
        on_device,
        mesh=mesh,
        in_specs=placed,
        out_specs=(
            P(("blk", "head"), None),
            P(("blk", "head"), None),
            P("blk", "head"),
            P("blk", None),
            P("blk", None),
            P("head", "blk"),
            P("blk", "head"),
            P("blk", "head"),
            P("head", "blk"),
            P(None, "blk"),
        ),
        check_vma=False,
    )
```

```python
import functools
import math

import jax
import jax.numpy as jnp
from jax import lax
from jax.experimental import pallas as pl
from jax.experimental.pallas import tpu as pltpu
from jax.sharding import PartitionSpec as P

H = 8
KVH = 4
HD = 256

norm_eps = 1e-06
cap_value = 50.0
theta_base = 10000.0
f32 = jnp.float32
bf16 = jnp.bfloat16


def inverse_rms(value):
    return lax.rsqrt(jnp.mean(value * value, axis=-1, keepdims=True) + norm_eps)


def rms_back(value, scale, grad):
    inverse = inverse_rms(value)
    scaled = grad * scale
    inner = jnp.mean(scaled * value, axis=-1, keepdims=True)
    grad_value = inverse * scaled - value * (inverse * inverse * inverse) * inner
    grad_scale = jnp.sum(grad * value * inverse, axis=0, keepdims=True)
    return (grad_value, grad_scale)


def rotation(position):
    entry = jnp.arange(HD, dtype=jnp.int32)
    quarter = HD // 4
    pair_index = entry // (2 * quarter) * quarter + entry % quarter
    frequency = jnp.power(theta_base, -2.0 * pair_index.astype(f32) / HD)
    angles = position.astype(f32)[:, None] * frequency[None, :]
    sign = jnp.where(entry % (2 * quarter) < quarter, -1.0, 1.0)
    return jnp.cos(angles), jnp.sin(angles) * sign[None, :]


def rotated(value, cosine, sine, sign):
    half = HD // 2
    parts = []
    for at in range(0, HD, half):
        piece = value[:, at : at + half]
        partner = pltpu.roll(piece, half // 2, 1)
        parts.append(piece * cosine[:, at : at + half] + partner * (sign * sine[:, at : at + half]))
    return jnp.concatenate(parts, 1)


def swap(value, axis):
    blk_mask, head_mask = axis
    block_count, head_count = lax.axis_size("blk"), lax.axis_size("head")
    if blk_mask == 0:
        return lax.ppermute(value, "head", [(i, i ^ head_mask) for i in range(head_count)])
    return lax.ppermute(value, "blk", [(i, i ^ blk_mask) for i in range(block_count)])


def bits(count):
    return [1 << i for i in range(count.bit_length() - 1)]


def route(subset, total, light):
    members = [i for i in range(total) if subset >> i & 1]
    if light and len(members) > 1 and members[-1] == total - 1:
        members = members[:-1]
        return members if len(members) == total - 1 else members[:1]
    if len(members) >= 2 and len(members) == total - light:
        return members
    if not light and len(members) == 2 and members[1] - members[0] != 1:
        return members[1:]
    return members[:1]


def hops(total, light):
    size = lambda t: bin(t).count("1")
    last = 1 << (total - 1)
    subsets = range(1, 1 << total)
    if not light:
        return [[t for t in subsets if size(t) == n] for n in range(1, total + 1)]
    result = [[t for t in subsets if size(t) == 1]]
    for high in (0, last):
        for n in range(2, total + 1):
            result.append([t for t in subsets if size(t) == n and t & last == high])
    return [hop for hop in result if hop]


def shares(row_total, parts):
    unit = row_total // 16
    cuts = [unit * i // parts * 16 for i in range(parts + 1)]
    cuts[-1] = row_total
    return list(zip(cuts[:-1], cuts[1:]))


def gather_hop(parts, axes, light, subsets, before=()):
    rows = parts[0][0].shape[0]
    came = {}
    for subset in subsets:
        ways = route(subset, len(axes), light)
        cuts = shares(rows, len(ways)) if len(ways) > 1 else [(0, rows)]
        came[subset] = []
        for way, (low, high) in zip(ways, cuts):
            source = parts[subset ^ (1 << way)][0]
            came[subset].append(swap(tie(source[low:high] if len(ways) > 1 else source, *before), axes[way]))
    return came


def gather_rows(value, axes, light=False, parts=None):
    last = 1 << (len(axes) - 1)
    parts, before = parts or {0: [value]}, ()
    for subsets in hops(len(axes), light):
        if all(t in parts for t in subsets):
            continue
        if light and last in parts:
            before = [x for x in before if x is not parts[last][0]]
            before += parts[last] * any(t & last for t in subsets)
        came = gather_hop(parts, axes, light, subsets, before)
        parts = parts | came
        before = [part for pieces in came.values() for part in pieces]
    return parts


def join_kernel(plan, *refs):
    step = pl.program_id(0)
    out = refs[-1]
    for at, (slot, first, rows) in enumerate(plan):

        @pl.when(step == slot)
        def _():
            out[first : first + rows, :] = refs[at][...]


def join_rows(parts):
    plan, arrays = [], []
    for slot in sorted(parts):
        first = 0
        for array in parts[slot]:
            plan.append((slot, first, array.shape[0]))
            arrays.append(array)
            first += array.shape[0]
    rows, columns = parts[0][0].shape
    return pl.pallas_call(
        functools.partial(join_kernel, plan),
        grid=(len(parts),),
        in_specs=[pl.BlockSpec(a.shape, lambda m: (0, 0), pipeline_mode=pl.Buffered(1)) for a in arrays],
        out_specs=pl.BlockSpec((rows, columns), lambda m: (m, 0)),
        out_shape=jax.ShapeDtypeStruct((len(parts) * rows, columns), arrays[0].dtype),
        compiler_params=pltpu.CompilerParams(vmem_limit_bytes=16 * 1024 * 1024),
        cost_estimate=pl.CostEstimate(flops=0, bytes_accessed=4 * len(parts) * rows * columns, transcendentals=0),
        name="join_rows",
    )(*arrays)


def two_products_kernel(a_ref, u_ref, b_ref, v_ref, *outs):
    nt = (((1,), (1,)), ((), ()))
    total = lax.dot_general(a_ref[...], u_ref[...], nt, preferred_element_type=f32)
    total += lax.dot_general(b_ref[...], v_ref[...], nt, preferred_element_type=f32)
    put_pieces(outs, total)


def put_pieces(outs, value):
    rows = outs[0].shape[0]
    for at, out in enumerate(outs):
        out[...] = value[at * rows : (at + 1) * rows].astype(out.dtype)


def two_products(a, u, b, v, count):
    rows, depth = a.shape
    columns = u.shape[0]
    step = 256
    resident = pl.BlockSpec((rows, depth), lambda n: (0, 0), pipeline_mode=pl.Buffered(1))
    return pl.pallas_call(
        two_products_kernel,
        grid=(columns // step,),
        in_specs=[resident, pl.BlockSpec((step, depth), lambda n: (n, 0))] * 2,
        out_specs=[pl.BlockSpec((rows // count, step), lambda n: (0, n))] * count,
        out_shape=[jax.ShapeDtypeStruct((rows // count, columns), bf16)] * count,
        compiler_params=pltpu.CompilerParams(vmem_limit_bytes=20 * 1024 * 1024),
        cost_estimate=pl.CostEstimate(
            flops=4 * rows * columns * depth,
            bytes_accessed=4 * (rows * depth + columns * depth) + 2 * rows * columns,
            transcendentals=0,
        ),
        name="two_products",
    )(a, u, b, v)


def joined(left, right):
    return (left.astype(f32) + right.astype(f32)).astype(bf16)


def scatter_plan(total, light):
    plan = [list(hop) for hop in hops(total, light)[::-1]]
    last = 1 << (total - 1)
    if light:
        plan[-1].remove(last)
        plan[next(i for i, hop in enumerate(plan) if not any(t & last for t in hop))].append(last)
    return plan


def scatter_hop(pieces, axes, light, subsets, before=(), beside=None):
    last = 1 << (len(axes) - 1)
    pieces = dict(pieces)
    rows = pieces[0][0].shape[0]
    sent, result = [], None
    for subset in subsets:
        (piece,) = pieces.pop(subset)
        ways = route(subset, len(axes), light)
        cuts = shares(rows, len(ways)) if len(ways) > 1 else [(0, rows)]
        for way, (low, high) in zip(ways, cuts):
            part = piece if len(ways) == 1 else piece[low:high]
            sent.append((subset, subset ^ (1 << way), low, high, swap(tie(part, *before), axes[way])))
    if beside:
        result, came = beside([item[4] for item in sent])
        sent = [item[:4] + (moved,) for item, moved in zip(sent, came)]
    for subset, target, low, high, moved in sent:
        if target == 0:
            pieces[0] = pieces[0] + [moved]
        elif high - low == rows:
            pieces[target] = [joined(pieces[target][0], moved)]
        else:
            old = pieces[target][0]
            cut = [old[:low], joined(old[low:high], moved), old[high:]]
            pieces[target] = [jnp.concatenate([c for c in cut if c.shape[0]], 0)]
    came = [item[4] for item in sent if not (light and item[0] == last)]
    return pieces, came, result


def scatter_rows(pieces, axes, light=False):
    pieces, came = {t: [piece] for t, piece in enumerate(pieces)}, ()
    for subsets in scatter_plan(len(axes), light):
        pieces, came, _ = scatter_hop(pieces, axes, light, subsets, came)
    return pieces[0]


def tie(value, *after):
    return lax.optimization_barrier((value, *after))[0] if after else value


def tie_all(held, *after):
    return {mask: tie(block, *after) for mask, block in held.items()}


def scale_kernel(count, index_ref, *refs):
    for mask in range(count):
        row = pl.multiple_of((index_ref[0] ^ mask) * 16, 16)
        refs[count][pl.ds(row, 16), :] = refs[mask][...]


def place_scales(held, rows, block_index):
    count = len(held)
    shape = (16, held[0].shape[1])
    return pl.pallas_call(
        functools.partial(scale_kernel, count),
        grid_spec=pltpu.PrefetchScalarGridSpec(
            num_scalar_prefetch=1,
            grid=(1,),
            in_specs=[pl.BlockSpec(shape, lambda n, b: (rows // 16, 0))] * count,
            out_specs=pl.BlockSpec((count * 16, shape[1]), lambda n, b: (0, 0)),
        ),
        out_shape=jax.ShapeDtypeStruct((count * 16, shape[1]), bf16),
        cost_estimate=pl.CostEstimate(flops=0, bytes_accessed=4 * count * 16 * shape[1], transcendentals=0),
        name="place_scales",
    )(block_index[None].astype(jnp.int32), *[held[mask] for mask in range(count)])


def head_kernel(plan, rows, scale_count, index_ref, *refs):
    parts, (key_ref, value_ref, scale_ref) = refs[: len(plan)], refs[len(plan) :]
    step = pl.program_id(0)

    @pl.when(step == 0)
    def _():
        scale_ref[...] = jnp.zeros_like(scale_ref)

    for part, (slot, first) in zip(parts, plan):
        count = part.shape[0]

        @pl.when(step == slot)
        def _():
            last = min(first + count, rows)
            here, taken = slice(first, last), slice(0, last - first)
            key_ref[here, :] = part[taken, :HD].astype(f32)
            value_ref[here, :] = part[taken, HD:].astype(f32)
            if first + count > rows:
                scale_ref[...] += part[rows - first : rows - first + 16, :].astype(f32)[:scale_count]


def place_heads(parts, rows, scale_count, head_index):
    plan, arrays = [], []
    for slot in sorted(parts):
        first = 0
        for array in parts[slot]:
            plan.append((slot, first))
            arrays.append(array)
            first += array.shape[0]
    columns = pl.BlockSpec((rows, HD), lambda m, h: (0, h[0] ^ m))
    fixed = lambda m, h: (0, 0)
    return pl.pallas_call(
        functools.partial(head_kernel, plan, rows, scale_count),
        grid_spec=pltpu.PrefetchScalarGridSpec(
            num_scalar_prefetch=1,
            grid=(len(parts),),
            in_specs=[pl.BlockSpec(a.shape, fixed, pipeline_mode=pl.Buffered(1)) for a in arrays],
            out_specs=[columns, columns, pl.BlockSpec((scale_count, 2 * HD), fixed)],
        ),
        out_shape=[jax.ShapeDtypeStruct((rows, len(parts) * HD), f32)] * 2
        + [jax.ShapeDtypeStruct((scale_count, 2 * HD), f32)],
        cost_estimate=pl.CostEstimate(flops=0, bytes_accessed=8 * len(parts) * rows * HD, transcendentals=0),
        name="place_heads",
    )(head_index[None].astype(jnp.int32), *arrays)


def placed_kernel(body, plans, counts, steps, index_ref, *refs):
    refs = list(refs)
    arrays, loads, inputs, outs, wholes, weights, loaded = [[refs.pop(0) for _ in range(count)] for count in counts]
    in_sems, out_sems = refs
    step = pl.program_id(0)
    came, at = [], 0
    for source, target in zip(loads, loaded):
        came.append([pltpu.make_async_copy(source, target, in_sems.at[at])])
        at += 1
    gone = [None] * len(loads)
    for weight, plan in zip(weights, plans):
        copies = []
        rows = weight.shape[0] // len(plan)
        for mask, (source, column) in enumerate(plan):
            row = pl.multiple_of((index_ref[0] ^ mask) * rows, 16)
            block = arrays[source].at[pl.ds(0, rows)]
            if arrays[source].shape[1] != weight.shape[1]:
                block = arrays[source].at[pl.ds(0, rows), pl.ds(column, weight.shape[1])]
            copies.append(pltpu.make_async_copy(block, weight.at[pl.ds(row, rows)], in_sems.at[at]))
            at += 1
        came.append(copies)
    gone += [
        pltpu.make_async_copy(weight, whole, out_sems.at[n]) for n, (weight, whole) in enumerate(zip(weights, wholes))
    ]

    @pl.when(step == 0)
    def _():
        for copies in came:
            for copy in copies:
                copy.start()
        for copies, copy_out in zip(came, gone):
            for copy in copies:
                copy.wait()
            if copy_out is not None:
                copy_out.start()

    body(step, loaded + inputs, outs, weights)

    @pl.when(step == steps - 1)
    def _():
        for copy_out in gone[len(loads) :]:
            copy_out.wait()


def placed(body, steps, held, columns, loads, inputs, in_specs, outs, out_specs, block_index, name, flops, vmem):
    arrays, plans = [], []
    for blocks, width in zip(held, columns):
        plan = []
        for mask in range(len(blocks)):
            array, column = blocks[mask]
            if width % 128 or column % 128:
                array, column = array[:, column : column + width], 0
            where = next((n for n, known in enumerate(arrays) if known is array), len(arrays))
            if where == len(arrays):
                arrays.append(array)
            plan.append((where, column))
        plans.append(plan)
    rows = min(array.shape[0] for array in arrays) // 16 * 16
    rows = rows - (16 if name == "key_rows" else 0)
    shapes = [(len(plan) * rows, width) for plan, width in zip(plans, columns)]
    anywhere = pl.BlockSpec(memory_space=pltpu.HBM)
    counts = (len(arrays), len(loads), len(inputs), len(outs), len(plans), len(plans), len(loads))
    return pl.pallas_call(
        functools.partial(placed_kernel, body, plans, counts, steps),
        grid_spec=pltpu.PrefetchScalarGridSpec(
            num_scalar_prefetch=1,
            grid=(steps,),
            in_specs=[anywhere] * (len(arrays) + len(loads)) + in_specs,
            out_specs=out_specs + [anywhere] * len(plans),
            scratch_shapes=[pltpu.VMEM(shape, bf16) for shape in shapes]
            + [pltpu.VMEM(array.shape, array.dtype) for array in loads]
            + [
                pltpu.SemaphoreType.DMA((sum(len(plan) for plan in plans) + len(loads),)),
                pltpu.SemaphoreType.DMA((len(plans),)),
            ],
        ),
        out_shape=outs + [jax.ShapeDtypeStruct(shape, bf16) for shape in shapes],
        compiler_params=pltpu.CompilerParams(vmem_limit_bytes=vmem * 1024 * 1024),
        cost_estimate=pl.CostEstimate(
            flops=flops, bytes_accessed=4 * sum(h * w for h, w in shapes), transcendentals=0
        ),
        name=name,
    )(block_index[None].astype(jnp.int32), *arrays, *loads, *inputs)


def in_turn(held):
    came = []
    for block in held.values():
        came.append(swap(tie(block, *came[-2:-1]), (1, 0)))
    return dict(zip(held, came))


def both_cores(held):
    return held | {mask ^ 1: swap(block, (1, 0)) for mask, block in held.items()}


def pick(value, dim, index):
    return lax.dynamic_index_in_dim(value, index, dim, keepdims=False)


def plus(left, right):
    return left.astype(f32) + right.astype(f32)


def whole_call(body, outs, *inputs, name):
    size = sum(x.size * x.dtype.itemsize for x in inputs)
    return pl.pallas_call(
        body,
        out_shape=[jax.ShapeDtypeStruct(shape, dtype) for shape, dtype in outs],
        compiler_params=pltpu.CompilerParams(vmem_limit_bytes=28 * 1024 * 1024),
        cost_estimate=pl.CostEstimate(flops=0, bytes_accessed=2 * size, transcendentals=0),
        name=name,
    )(*inputs)


def summed(refs):
    total = refs[0][...].astype(f32)
    for ref in refs[1:]:
        total = total + ref[...].astype(f32)
    return total


def norm_full_kernel(count, *refs):
    parts, (scale, normed, inverse) = refs[:count], refs[count:]
    first = 0
    for part in parts:
        value = part[...].astype(f32)
        here = slice(first, first + part.shape[0])
        first += part.shape[0]
        factor = inverse_rms(value)
        inverse[here, :] = factor
        normed[here, :] = (value * factor * scale[0:1, :]).astype(bf16)


def after_attention_kernel(count, *refs):
    terms, (hidden, scales, attn_out, resid_out, ffn_in) = refs[:count], refs[count:]
    attn = summed(terms)
    attn_out[...] = attn
    resid = hidden[...].astype(f32) + attn * inverse_rms(attn) * scales[1:2, :]
    resid_out[...] = resid
    ffn_in[...] = (resid * inverse_rms(resid) * scales[2:3, :]).astype(bf16)


def after_ffn_kernel(count, *refs):
    terms, (resid, out_grad, scales, layer_out, grad_out, grad_scale) = refs[:count], refs[count:]
    ffn_out = summed(terms)
    grad, grad_scale[...] = rms_back(ffn_out, scales[3:4, :], out_grad[...].astype(f32))
    grad_out[...] = grad.astype(bf16)
    layer_out[...] = (resid[...] + ffn_out * inverse_rms(ffn_out) * scales[3:4, :]).astype(bf16)


def after_ffn_back_kernel(count, *refs):
    terms, (resid, attn, out_grad, scales, grad_resid, grad_attn, grad_scale2, grad_scale1) = refs[:count], refs[count:]
    grad, grad_scale2[...] = rms_back(resid[...], scales[2:3, :], summed(terms))
    grad = out_grad[...].astype(f32) + grad
    grad_resid[...] = grad
    back, grad_scale1[...] = rms_back(attn[...], scales[1:2, :], grad)
    grad_attn[...] = back.astype(bf16)


def after_all_kernel(count, *refs):
    terms, (hidden, grad_resid, scales, grad_in) = refs[:count], refs[count:]
    grad, _ = rms_back(hidden[...].astype(f32), scales[0:1, :], summed(terms))
    grad_in[...] = grad_resid[...] + grad


def key_value_grad_kernel(kept, came, cosine, sine, out):
    total = kept[...].astype(f32) + came[...].astype(f32)
    out[:, :HD] = rotated(total[:, :HD], cosine[...], sine[...], -1.0).astype(bf16)
    out[:, HD:] = total[:, HD:].astype(bf16)


def project(rows, held, columns, table, turning, block_index, name):
    count, depth = rows.shape
    heads = columns[0] // HD
    fixed = lambda n, b: (0, 0)
    once = pl.Buffered(1)

    def body(step, inputs, outs, weights):
        rows_ref, cosine_ref, sine_ref = inputs
        (out_ref,) = outs
        here = pl.ds(pl.multiple_of(step * HD, HD), HD)
        value = jnp.dot(rows_ref[...], weights[0][:, here], preferred_element_type=f32)

        @pl.when(step < turning)
        def _():
            out_ref[...] = rotated(value, cosine_ref[...], sine_ref[...], 1.0).astype(bf16)

        @pl.when(step >= turning)
        def _():
            out_ref[...] = value.astype(bf16)

    return placed(
        body,
        heads,
        held,
        columns,
        [rows],
        list(table),
        [
            pl.BlockSpec((count, HD), fixed, pipeline_mode=once),
            pl.BlockSpec((count, HD), fixed, pipeline_mode=once),
        ],
        [jax.ShapeDtypeStruct((count, columns[0]), bf16)],
        [pl.BlockSpec((count, HD), lambda n, b: (0, n))],
        block_index,
        name,
        2 * rows.size * columns[0],
        20,
    )


def hidden_units(rows, held, width, block_index):
    count, depth = rows.shape
    step = 256

    def body(number, inputs, outs, weights):
        hidden_ref, active_ref, slope_ref = outs
        gate = jnp.dot(inputs[0][...], weights[0][...], preferred_element_type=f32)
        up = jnp.dot(inputs[0][...], weights[1][...], preferred_element_type=f32)
        inner = math.sqrt(2.0 / math.pi)
        square = gate * gate
        tangent = jnp.tanh(inner * gate * (1.0 + 0.044715 * square))
        share = 0.5 * (1.0 + tangent)
        active = gate * share
        slope = share + (0.5 * inner) * gate * (1.0 - tangent * tangent) * (1.0 + (3 * 0.044715) * square)
        hidden_ref[...] = (active * up).astype(bf16)
        active_ref[...] = active.astype(bf16)
        slope_ref[...] = (slope * up).astype(bf16)

    return placed(
        body,
        count // step,
        held,
        [width, width],
        [],
        [rows],
        [pl.BlockSpec((step, depth), lambda n, b: (n, 0))],
        [jax.ShapeDtypeStruct((count, width), bf16)] * 3,
        [pl.BlockSpec((step, width), lambda n, b: (n, 0))] * 3,
        block_index,
        "hidden_units",
        4 * rows.size * width,
        40,
    )


def down_rows(hidden, held, block_index, pieces):
    count, width = hidden.shape
    depth = len(held) * held[0][0].shape[0]
    step = 768 if depth % 768 == 0 else 256

    def body(number, inputs, outs, weights):
        here = pl.ds(pl.multiple_of(number * step, step), step)
        value = lax.dot_general(
            inputs[0][...], weights[0][here, :], (((1,), (1,)), ((), ())), preferred_element_type=f32
        )
        put_pieces(outs, value)

    return placed(
        body,
        depth // step,
        [held],
        [width],
        [hidden],
        [],
        [],
        [jax.ShapeDtypeStruct((count // pieces, depth), bf16)] * pieces,
        [pl.BlockSpec((count // pieces, step), lambda n, b: (0, n))] * pieces,
        block_index,
        "down_rows",
        2 * hidden.size * depth,
        24,
    )


def outer_kernel(*refs):
    pairs, out = refs[:-1], refs[-1]
    width = 0
    for left, right in zip(pairs[::2], pairs[1::2]):
        columns = right.shape[1]
        value = lax.dot_general(left[...], right[...], (((0,), (0,)), ((), ())), preferred_element_type=f32)
        out[:, width : width + columns] = value.astype(bf16)
        width += columns


def outer(*pairs):
    rows, depth = pairs[0][0].shape
    width = sum(right.shape[1] for _, right in pairs)
    step = depth // 2
    specs = []
    for _, right in pairs:
        specs.append(pl.BlockSpec((rows, step), lambda n: (0, n)))
        specs.append(pl.BlockSpec(right.shape, lambda n: (0, 0), pipeline_mode=pl.Buffered(1)))
    return pl.pallas_call(
        outer_kernel,
        grid=(depth // step,),
        in_specs=specs,
        out_specs=pl.BlockSpec((step, width), lambda n: (n, 0)),
        out_shape=jax.ShapeDtypeStruct((depth, width), bf16),
        compiler_params=pltpu.CompilerParams(vmem_limit_bytes=24 * 1024 * 1024),
        cost_estimate=pl.CostEstimate(
            flops=2 * rows * depth * width, bytes_accessed=2 * (rows * depth * len(pairs) + depth * width), transcendentals=0
        ),
        name="outer",
    )(*[x for pair in pairs for x in pair])


def normed_back_kernel(count, q_ref, wq_ref, kv_ref, wkv_ref, inverse_ref, *refs):
    hidden, (*outs, scale_ref) = refs[:count], refs[count:]
    nt = (((1,), (1,)), ((), ()))
    total = lax.dot_general(q_ref[...], wq_ref[...], nt, preferred_element_type=f32)
    total += lax.dot_general(kv_ref[...], wkv_ref[...], nt, preferred_element_type=f32)
    put_pieces(outs, total)
    grad_scale, first = jnp.zeros((1, total.shape[1]), f32), 0
    for part in hidden:
        here = slice(first, first + part.shape[0])
        first += part.shape[0]
        unit = part[...].astype(f32) * inverse_ref[here, :]
        grad_scale += jnp.sum(total[here, :] * unit, axis=0, keepdims=True)
    scale_ref[...] = grad_scale


def normed_back(grad_query, query_weight, grad_kv, kv_weight, inverse, hidden, pieces):
    rows, width = grad_query.shape
    kv_width = grad_kv.shape[1]
    columns = query_weight.shape[0]
    step = 768 if columns % 768 == 0 else 256
    fixed = lambda n: (0, 0)
    once = pl.Buffered(1)
    return pl.pallas_call(
        functools.partial(normed_back_kernel, len(hidden)),
        grid=(columns // step,),
        in_specs=[
            pl.BlockSpec((rows, width), fixed, pipeline_mode=once),
            pl.BlockSpec((step, width), lambda n: (n, 0)),
            pl.BlockSpec((rows, kv_width), fixed, pipeline_mode=once),
            pl.BlockSpec((step, kv_width), lambda n: (n, 0)),
            pl.BlockSpec((rows, 1), fixed, pipeline_mode=once),
        ]
        + [pl.BlockSpec((part.shape[0], step), lambda n: (0, n)) for part in hidden],
        out_specs=[pl.BlockSpec((rows // pieces, step), lambda n: (0, n))] * pieces
        + [pl.BlockSpec((1, step), lambda n: (0, n))],
        out_shape=[jax.ShapeDtypeStruct((rows // pieces, columns), bf16)] * pieces
        + [jax.ShapeDtypeStruct((1, columns), f32)],
        compiler_params=pltpu.CompilerParams(vmem_limit_bytes=20 * 1024 * 1024),
        cost_estimate=pl.CostEstimate(
            flops=2 * rows * columns * (width + kv_width), bytes_accessed=4 * rows * columns, transcendentals=0
        ),
        name="normed_back",
    )(grad_query, query_weight, grad_kv, kv_weight, inverse, *hidden)


def scores(query, key, score_scale):
    raw = lax.dot_general(query, key, (((1,), (1,)), ((), ())), preferred_element_type=f32)
    return jnp.tanh(raw * (score_scale / cap_value))


def load_pieces(step, pieces, kv_all, sems):
    copies = [pltpu.make_async_copy(piece, kv_all.at[at], sems.at[at]) for at, piece in enumerate(pieces)]

    @pl.when(step == 0)
    def _():
        for copy in copies:
            copy.start()

    for at, copy in enumerate(copies):

        @pl.when(step == 2 * at)
        def _():
            copy.wait()


def forward_kernel(group, span_len, tiles, spans_ref, q_ref, *refs):
    pieces, (mixed_ref, exact_ref, lse_ref, q_all, acc, total, kv_all, sems) = refs[: tiles // 2], refs[tiles // 2 :]
    step = pl.program_id(0)
    load_pieces(step, pieces, kv_all, sems)
    score_scale = 1.0 / math.sqrt(HD)
    rows = group * span_len

    @pl.when(step == 0)
    def _():
        for half in range(2):
            for g in range(group):
                q_all[half, g * span_len : (g + 1) * span_len, :] = q_ref[
                    half * span_len : (half + 1) * span_len, g * HD : (g + 1) * HD
                ]
        acc[...] = jnp.zeros_like(acc)
        total[...] = jnp.zeros_like(total)

    tile_span = spans_ref[step]
    here = pl.ds(pl.multiple_of((step % 2) * span_len, span_len), span_len)
    key = kv_all[step // 2, here, :HD]
    value = kv_all[step // 2, here, HD:]

    def visit(half, diagonal):
        weights = jnp.exp(cap_value * scores(q_all[half], key, score_scale))
        if diagonal:
            flip = spans_ref[tiles + 2]
            shape = (rows, span_len)
            q_pos = (lax.broadcasted_iota(jnp.int32, shape, 0) % span_len) ^ flip
            k_pos = lax.broadcasted_iota(jnp.int32, shape, 1) ^ flip
            weights = jnp.where(k_pos <= q_pos, weights, 0.0)
        part = weights[:, :128]
        for at in range(128, span_len, 128):
            part = part + weights[:, at : at + 128]
        total[half] += part
        acc[half] += jnp.dot(weights.astype(bf16), value, preferred_element_type=f32)

    for half in range(2):
        own = spans_ref[tiles + half]

        @pl.when(tile_span < own)
        def _():
            visit(half, False)

        @pl.when(tile_span == own)
        def _():
            visit(half, True)

    @pl.when(step == tiles - 1)
    def _():
        for half in range(2):
            sums = jnp.sum(total[half], axis=1, keepdims=True)
            exact = acc[half] / sums
            lse_ref[half] = jnp.log(jnp.sum(total[half].T, axis=0, keepdims=True))
            for g in range(group):
                piece = exact[g * span_len : (g + 1) * span_len]
                place = (slice(half * span_len, (half + 1) * span_len), slice(g * HD, (g + 1) * HD))
                exact_ref[place] = piece
                mixed_ref[place] = piece.astype(bf16)


def backward_kernel(group, span_len, tiles, spans_ref, q_ref, g_ref, exact_ref, lse_ref, cosine_ref, sine_ref, *refs):
    pieces, rest = refs[: tiles // 2], refs[tiles // 2 :]
    dq_ref, near_ref, far_ref, q_all, g_all, delta, dq_acc, kv_all, sems = rest
    step = pl.program_id(0)
    load_pieces(step, pieces, kv_all, sems)
    score_scale = 1.0 / math.sqrt(HD)
    rows = group * span_len

    @pl.when(step == 0)
    def _():
        for half in range(2):
            for g in range(group):
                place = (slice(half * span_len, (half + 1) * span_len), slice(g * HD, (g + 1) * HD))
                here = slice(g * span_len, (g + 1) * span_len)
                q_all[half, here, :] = q_ref[place]
                g_all[half, here, :] = g_ref[place]
                product = g_ref[place].astype(f32) * exact_ref[place]
                folded = product[:, :128] + product[:, 128:]
                delta[half, :, here] = jnp.sum(folded.T, axis=0, keepdims=True)
        dq_acc[...] = jnp.zeros_like(dq_acc)

    tile_span = spans_ref[step]
    here = pl.ds(pl.multiple_of((step % 2) * span_len, span_len), span_len)
    key = kv_all[step // 2, here, :HD]
    value = kv_all[step // 2, here, HD:]

    def visit(half, diagonal):
        query = q_all[half]
        grad = g_all[half]
        tangent = scores(key, query, score_scale)
        probability = jnp.exp(cap_value * tangent - lse_ref[half])
        if diagonal:
            flip = spans_ref[tiles + 2]
            shape = (span_len, rows)
            q_pos = (lax.broadcasted_iota(jnp.int32, shape, 1) % span_len) ^ flip
            k_pos = lax.broadcasted_iota(jnp.int32, shape, 0) ^ flip
            probability = jnp.where(k_pos <= q_pos, probability, 0.0)
        grad_prob = lax.dot_general(value, grad, (((1,), (1,)), ((), ())), preferred_element_type=f32)
        grad_raw = probability * (grad_prob - delta[half]) * ((1.0 - tangent * tangent) * score_scale)
        grad_raw = grad_raw.astype(bf16)
        dv = jnp.dot(probability.astype(bf16), grad, preferred_element_type=f32)
        dk = jnp.dot(grad_raw, query, preferred_element_type=f32)
        dq_acc[half] += lax.dot_general(grad_raw, key, (((0,), (0,)), ((), ())), preferred_element_type=f32)
        return dk, dv

    def put(dk, dv):
        @pl.when(step < tiles // 2)
        def _():
            near_ref[:, :HD] = dk.astype(bf16)
            near_ref[:, HD:] = dv.astype(bf16)

        @pl.when(step >= tiles // 2)
        def _():
            far_ref[:, :HD] = dk.astype(bf16)
            far_ref[:, HD:] = dv.astype(bf16)

    low, high = spans_ref[tiles], spans_ref[tiles + 1]
    first, second = tile_span <= low, tile_span <= high

    @pl.when(jnp.logical_not(jnp.logical_or(first, second)))
    def _():
        put(jnp.zeros((span_len, HD), f32), jnp.zeros((span_len, HD), f32))

    for half, own, other in ((0, low, high), (1, high, low)):
        for diagonal in (False, True):
            here = tile_span == own if diagonal else tile_span < own

            @pl.when(jnp.logical_and(here, tile_span > other))
            def _(half=half, diagonal=diagonal):
                put(*visit(half, diagonal))

    for half, own, other in ((0, low, high), (1, high, low)):
        for diagonal in (False, True):
            here = tile_span == own if diagonal else tile_span < own

            @pl.when(jnp.logical_and(here, own < other))
            def _(half=half, diagonal=diagonal):
                dk_low, dv_low = visit(half, diagonal)
                dk_high, dv_high = visit(1 - half, False)
                put(dk_low + dk_high, dv_low + dv_high)

    @pl.when(step == tiles - 1)
    def _():
        for half in range(2):
            for g in range(group):
                here = slice(half * span_len, (half + 1) * span_len)
                turned = rotated(
                    dq_acc[half, g * span_len : (g + 1) * span_len], cosine_ref[here, :], sine_ref[here, :], -1.0
                )
                dq_ref[here, g * HD : (g + 1) * HD] = turned.astype(bf16)


def attention_forward(spans, queries, pieces, span_len):
    tiles = 2 * len(pieces)
    kv_size = len(pieces) * pieces[0].size
    width = queries.shape[1]
    group = width // HD
    rows = group * span_len
    whole = lambda s, t: (0, 0)
    visits = tiles + 1
    return pl.pallas_call(
        functools.partial(forward_kernel, group, span_len, tiles),
        grid_spec=pltpu.PrefetchScalarGridSpec(
            num_scalar_prefetch=1,
            grid=(tiles,),
            in_specs=[
                pl.BlockSpec(queries.shape, whole),
            ]
            + [pl.BlockSpec(memory_space=pltpu.HBM)] * len(pieces),
            out_specs=[
                pl.BlockSpec(queries.shape, whole),
                pl.BlockSpec(queries.shape, whole),
                pl.BlockSpec((2, 1, rows), lambda s, t: (0, 0, 0)),
            ],
            scratch_shapes=[
                pltpu.VMEM((2, rows, HD), bf16),
                pltpu.VMEM((2, rows, HD), f32),
                pltpu.VMEM((2, rows, 128), f32),
                pltpu.VMEM((len(pieces),) + pieces[0].shape, bf16),
                pltpu.SemaphoreType.DMA((len(pieces),)),
            ],
        ),
        out_shape=[
            jax.ShapeDtypeStruct(queries.shape, bf16),
            jax.ShapeDtypeStruct(queries.shape, f32),
            jax.ShapeDtypeStruct((2, 1, rows), f32),
        ],
        compiler_params=pltpu.CompilerParams(vmem_limit_bytes=14 * 1024 * 1024 + 2 * kv_size),
        cost_estimate=pl.CostEstimate(
            flops=visits * rows * span_len * HD * 4,
            bytes_accessed=kv_size * 2 + queries.size * 12,
            transcendentals=visits * rows * span_len * 2,
        ),
        name="attention_forward",
    )(spans, queries, *pieces)


def attention_backward(spans, queries, grads, exact, lse, table, pieces, span_len):
    tiles = 2 * len(pieces)
    kv_size = len(pieces) * pieces[0].size
    width = queries.shape[1]
    group = width // HD
    rows = group * span_len
    whole = lambda s, t: (0, 0)
    visits = tiles + 1
    return pl.pallas_call(
        functools.partial(backward_kernel, group, span_len, tiles),
        grid_spec=pltpu.PrefetchScalarGridSpec(
            num_scalar_prefetch=1,
            grid=(tiles,),
            in_specs=[
                pl.BlockSpec(queries.shape, whole),
                pl.BlockSpec(queries.shape, whole),
                pl.BlockSpec(queries.shape, whole),
                pl.BlockSpec((2, 1, rows), lambda s, t: (0, 0, 0)),
                pl.BlockSpec(table[0].shape, whole),
                pl.BlockSpec(table[0].shape, whole),
            ]
            + [pl.BlockSpec(memory_space=pltpu.HBM)] * len(pieces),
            out_specs=[
                pl.BlockSpec(queries.shape, whole),
                pl.BlockSpec((span_len, 2 * HD), lambda s, t: (jnp.minimum(s, tiles // 2 - 1), 0)),
                pl.BlockSpec((span_len, 2 * HD), lambda s, t: (jnp.maximum(s - tiles // 2, 0), 0)),
            ],
            scratch_shapes=[
                pltpu.VMEM((2, rows, HD), bf16),
                pltpu.VMEM((2, rows, HD), bf16),
                pltpu.VMEM((2, 1, rows), f32),
                pltpu.VMEM((2, rows, HD), f32),
                pltpu.VMEM((len(pieces),) + pieces[0].shape, bf16),
                pltpu.SemaphoreType.DMA((len(pieces),)),
            ],
        ),
        out_shape=[
            jax.ShapeDtypeStruct(queries.shape, bf16),
            jax.ShapeDtypeStruct((tiles * span_len // 2, 2 * HD), bf16),
            jax.ShapeDtypeStruct((tiles * span_len // 2, 2 * HD), bf16),
        ],
        compiler_params=pltpu.CompilerParams(vmem_limit_bytes=18 * 1024 * 1024 + 2 * kv_size),
        cost_estimate=pl.CostEstimate(
            flops=visits * rows * span_len * HD * 10,
            bytes_accessed=kv_size * 4 + queries.size * 16,
            transcendentals=visits * rows * span_len * 2,
        ),
        name="attention_backward",
    )(spans, queries, grads, exact, lse, *table, *pieces)


def product(left, right, left_dim, right_dim, out=f32):
    result = lax.dot_general(left, right, (((left_dim,), (right_dim,)), ((), ())), preferred_element_type=f32)
    return result.astype(out)


def on_device(
    hidden_in,
    out_grad,
    span_order,
    w_query,
    w_key,
    w_value,
    w_output,
    w_gate,
    w_up,
    w_down,
    norm_scales,
):
    local_rows = hidden_in.shape[0]
    head_count = lax.axis_size("head")
    block_count = lax.axis_size("blk")
    block_index = lax.axis_index("blk")
    head_index = lax.axis_index("head")
    group_rows = local_rows * head_count
    span_len = group_rows // 2
    model_rows, query_width = w_query.shape
    model_width = hidden_in.shape[1]
    query_heads = query_width // HD
    half_units = w_gate.shape[1] // 2

    chip_masks = bits(block_count)[1:]
    pair, top = chip_masks[0], chip_masks[-1]
    far_masks = chip_masks[:0:-1]
    head_axes = [(0, mask) for mask in bits(head_count)]
    unit_axes = head_axes + [(pair, 0)]
    unit_side = (block_index // pair) % 2
    bit_count = len(chip_masks) + 1

    def side(mask):
        return (block_index // mask) % 2

    def send(value, mask, *after):
        return swap(tie(value, *after), (mask, 0))

    def segment(body, inputs, after=(), flying=()):
        inputs, after = lax.optimization_barrier((tuple(inputs), after))
        shapes = jax.eval_shape(body, *inputs)

        def nothing(*_):
            return jax.tree.map(lambda x: jnp.zeros(x.shape, x.dtype), shapes)

        results = lax.cond(span_order[0] >= 0, body, nothing, *inputs)
        return lax.optimization_barrier((results, flying))

    def far_spread(value, *after):
        held = {0: value}
        for mask in far_masks:
            for have in list(held):
                held[have ^ mask] = send(held[have], mask, *after)
        return held

    def near_spread(held, *after):
        return held | {have ^ pair: send(block, pair, *(after if have == 0 else ())) for have, block in held.items()}

    def split_dims(partial):
        return partial.reshape((2,) * bit_count + (-1, partial.shape[-1]))

    def halve(value, dim, mask, *after):
        moved = send(pick(value, dim, 1 - side(mask)), mask, *after)
        return plus(pick(value, dim, side(mask)), moved)

    slot = jnp.arange(head_count, dtype=jnp.int32) ^ head_index
    in_block = (slot[:, None] * local_rows + jnp.arange(local_rows, dtype=jnp.int32)[None, :]).reshape(-1)
    head_side = head_index // (head_count // 2)
    own_spans = jnp.stack([span_order[2 * block_index + head_side], span_order[2 * block_index + 1 - head_side]])
    row_spans = jnp.repeat(own_spans, span_len)
    position = row_spans * span_len + in_block % span_len
    even_masks = [0]
    for mask in chip_masks[::-1]:
        even_masks = even_masks + [have ^ mask for have in even_masks]
    slot_masks = even_masks + [mask ^ 1 for mask in even_masks]
    tile_blocks = jnp.array(slot_masks, jnp.int32) ^ block_index
    tile_slots = (2 * tile_blocks[:, None] + jnp.stack([head_side, 1 - head_side])[None, :]).reshape(-1)
    flip = (head_index % (head_count // 2)) * local_rows
    spans = jnp.concatenate([span_order[tile_slots], own_spans, flip[None]]).astype(jnp.int32)
    table = rotation(position)

    scale_count = norm_scales.shape[0]
    kv_at = head_index * query_heads // (H // KVH) * HD
    kv_local = jnp.concatenate(
        [
            lax.dynamic_slice_in_dim(w_key, kv_at, HD, 1),
            lax.dynamic_slice_in_dim(w_value, kv_at, HD, 1),
        ],
        1,
    )
    scale_local = jnp.pad(norm_scales, ((0, 16 - scale_count), (0, 2 * HD - model_rows)))
    kv_local = jnp.concatenate([kv_local, scale_local], 0)

    def half(local, index):
        return lax.dynamic_slice_in_dim(local, index * half_units, half_units, 1)

    def unit_slices():
        weights = (w_gate, w_up, w_down.T)
        return (
            half(w_gate, unit_side),
            jnp.concatenate([half(w, unit_side) for w in weights[1:]], 1),
            jnp.concatenate([half(w, 1 - unit_side) for w in weights[:2]], 1),
            half(weights[2], 1 - unit_side),
        )

    hidden_near = [swap(hidden_in, axis) for axis in head_axes]
    kv_chips = far_spread(kv_local)
    kv_chips.pop(0)
    kv_chips[pair] = send(kv_local, pair)
    (query_output_local, unit_local), (hidden_near, kv_chips) = segment(
        lambda w_query, w_output: (jnp.concatenate([w_query, w_output.T], 1), unit_slices()),
        (w_query, w_output),
        (table,),
        (hidden_near, kv_chips),
    )
    first_mine, second_mine, first_theirs, second_theirs = unit_local

    def first_rows(hidden_near, kv_chips):
        held = {0: kv_local} | kv_chips
        held |= {mask ^ pair: swap(block, (pair, 0)) for mask, block in kv_chips.items() if mask != pair}
        parts = {0: [hidden_in]} | {1 << at: [part] for at, part in enumerate(hidden_near)}
        for subset in range(1, head_count):
            if subset not in parts:
                ways = route(subset, len(head_axes), False)
                cuts = shares(local_rows, len(ways)) if len(ways) > 1 else [(0, local_rows)]
                parts[subset] = [
                    swap(parts[subset ^ (1 << way)][0][low:high], head_axes[way]) for way, (low, high) in zip(ways, cuts)
                ]
        def normed_keys(held, parts):
            came = ()
            for mask, block in list(held.items()):
                held[mask ^ 1] = swap(tie(block, *came), (1, 0))
                came = (held[mask ^ 1],)
            scale_blocks = place_scales(held, model_rows, block_index)
            scale_rows = scale_blocks.reshape(block_count, 16, 2 * HD)[:, :scale_count, :model_rows]
            scale_rows = scale_rows.transpose(1, 0, 2).reshape(scale_count, model_width).astype(f32)
            arrays = [part for slot in sorted(parts) for part in parts[slot]]
            normed_full, inverse_full = whole_call(
                functools.partial(norm_full_kernel, len(arrays)),
                [((group_rows, model_width), bf16), ((group_rows, 1), f32)],
                *arrays,
                scale_rows,
                name="norm_full",
            )
            kv_held = {mask: (block, 0) for mask, block in held.items()}
            kv_rows, kv_weight = project(normed_full, [kv_held], [2 * HD], table, 1, block_index, "key_rows")
            return kv_rows, kv_weight, scale_rows, normed_full, inverse_full

        first = held[pair ^ top], *[part for slot, pieces in parts.items() if slot.bit_count() > 1 for part in pieces]
        query_output = {mask: send(query_output_local, mask, *first) for mask in (*far_masks, pair)}
        results, query_output = segment(normed_keys, (held, parts), (), query_output)
        return results, parts, query_output

    first_results, hidden_parts, query_output_chips = first_rows(hidden_near, kv_chips)
    kv_rows, kv_weight, scale_rows, normed_full, inverse_full = first_results
    hidden_slots = [part for slot in sorted(hidden_parts) for part in hidden_parts[slot]]
    row_shape = (local_rows, model_width)
    scale_shape = (1, model_width)

    if len(far_masks) > 1:
        query_output_chips = far_spread(query_output_local) | {pair: query_output_chips[pair]}
    query_output_chips[0] = query_output_local
    kv_far = far_spread(kv_rows)
    kv_far.pop(0)
    kv_near = send(kv_rows, pair)
    query_output_last = {
        mask ^ pair: send(block, pair, kv_rows) for mask, block in query_output_chips.items() if mask & ~pair
    }

    def beside_keys(kv_rows):
        cores, came = {}, ()
        for mask, block in ({-1: kv_rows} | query_output_chips).items():
            cores[mask] = swap(tie(block, *came), (1, 0))
            came = (cores[mask],)
        return cores

    cores, (kv_far, kv_near, query_output_last) = segment(
        beside_keys, (kv_rows,), (), (kv_far, kv_near, query_output_last)
    )

    def keys_and_queries(kv_far, kv_near, query_output_last):
        across = {mask ^ pair: swap(block, (pair, 0)) for mask, block in kv_far.items()}
        chips = query_output_chips | query_output_last
        held = query_output_last | {-1 - mask: piece for mask, piece in ({pair: kv_near} | kv_far).items()}
        came, others = (), dict(cores)
        for mask, block in held.items():
            others[mask] = swap(tie(block, *came), (1, 0))
            came = (others[mask],)
        chips |= {mask ^ 1: block for mask, block in others.items() if mask >= 0}
        queries, query_weight, output_weight = project(
            normed_full,
            [{mask: (block, column) for mask, block in chips.items()} for column in (0, query_width)],
            [query_width, query_width],
            table,
            query_heads,
            block_index,
            "query_rows",
        )
        came += (queries,)
        for mask, block in across.items():
            others[-1 - mask] = swap(tie(block, *came), (1, 0))
            came = (others[-1 - mask],)
        pieces = {(-1 - mask) ^ 1: piece for mask, piece in others.items() if mask < 0}
        return across | pieces, query_weight, output_weight, queries

    first_near = far_spread(first_mine, kv_far[top])
    (kv_others, query_weight, output_weight, queries), first_near = segment(
        keys_and_queries, (kv_far, kv_near, query_output_last), (), first_near
    )
    kv_held = {0: kv_rows, pair: kv_near} | kv_far | kv_others
    kv_pieces = [kv_held[mask] for mask in slot_masks]

    def row_sum(partial, axes, light=False):
        shaped = partial.reshape(1 << len(axes), local_rows, model_width)
        return scatter_rows([shaped[i] for i in range(1 << len(axes))], axes, light)

    def attend(queries, first_near, second_mine):
        mixed, exact, lse = attention_forward(spans, queries, kv_pieces, span_len)
        cores = in_turn(first_near | {-1: second_mine})
        second_core = cores.pop(-1)
        first_core = {mask ^ 1: block for mask, block in cores.items()}
        mixed = tie(mixed, first_core, second_core)
        terms = row_sum(product(mixed, output_weight, 1, 1, bf16), head_axes)
        rows = whole_call(
            functools.partial(after_attention_kernel, len(terms)),
            [(row_shape, f32), (row_shape, f32), (row_shape, bf16)],
            *terms,
            hidden_in,
            scale_rows,
            name="after_attention",
        )
        return (mixed, exact, lse, *rows, first_core, second_core)

    second_near = far_spread(second_mine, queries)
    first_cross = send(first_theirs, pair, queries)
    (mixed, exact, lse, attn_out, resid, ffn_in, first_core, second_core), (second_near, first_cross) = segment(
        attend, (queries, first_near, second_mine), (), (second_near, first_cross)
    )
    second_far = {mask: block for mask, block in second_near.items() if mask}

    def join_units(ffn_in, first_cross, second_far):
        parts = {0: [ffn_in]}
        plan = hops(len(unit_axes), True)
        parts |= gather_hop(parts, unit_axes, True, plan[0])
        flat = [part for t in plan[0][:-1] for part in parts[t]]
        parts |= gather_hop(parts, unit_axes, True, plan[1], flat)

        def later_hops(parts):
            parts = gather_rows(None, unit_axes, True, parts)
            third = [part for t in parts if t.bit_count() > 1 and t != len(parts) - 1 for part in parts[t]]
            first_core = swap(tie(first_cross, *parts[len(parts) // 2]), (1, 0))
            second_cores = {
                mask ^ 1: swap(tie(block, *third, first_core), (1, 0)) for mask, block in second_far.items()
            }
            return join_rows(parts), first_core, second_cores

        second_cross = send(second_theirs, pair, parts)
        return segment(later_hops, (parts,), (), second_cross)

    first_across = far_spread(first_cross, ffn_in)
    ((ffn_full, cross_core, far_cores), second_cross), first_across = segment(
        join_units, (ffn_in, first_cross, second_far), (), first_across
    )
    second_held = second_near | {1: second_core} | far_cores

    def gate_and_up(ffn_full, first_across):
        cores = {1: cross_core} | {mask ^ 1: swap(block, (1, 0)) for mask, block in first_across.items() if mask}
        across = {mask ^ pair: block for mask, block in (first_across | cores).items()}
        gate_held = {mask: (block, 0) for mask, block in (first_near | first_core | across).items()}
        up_held = {mask: (block, 0) for mask, block in second_held.items()}
        up_held |= {mask: (block, half_units) for mask, block in across.items()}
        units = hidden_units(ffn_full, [gate_held, up_held], half_units, block_index)
        return units, swap(second_cross, (1, 0))

    second_across = far_spread(second_cross, ffn_full)
    ((hidden, active, slope, gate_weight, up_weight), second_cross_core), second_across = segment(
        gate_and_up, (ffn_full, first_across), (), second_across
    )
    down_held = {mask: (block, half_units) for mask, block in second_held.items()}
    down_held |= {mask ^ pair: (block, 0) for mask, block in second_across.items()}
    down_held |= {
        mask ^ pair ^ 1: (swap(block, (1, 0)) if mask else second_cross_core, 0)
        for mask, block in second_across.items()
    }
    *ffn_parts, down_weight = down_rows(hidden, down_held, block_index, 1 << len(unit_axes))
    ffn_terms = scatter_rows(ffn_parts, unit_axes)
    layer_out, grad_ffn_out, scale_grad3 = whole_call(
        functools.partial(after_ffn_kernel, len(ffn_terms)),
        [(row_shape, bf16), (row_shape, bf16), (scale_shape, f32)],
        *ffn_terms,
        resid,
        out_grad,
        scale_rows,
        name="after_ffn",
    )

    def unit_core(partial):
        summed = halve(split_dims(partial), bit_count - 1, 1).astype(bf16)
        return pick(summed, 0, 1 - side(top)), pick(summed, 0, side(top))

    def unit_sides(kept, came):
        part = plus(kept, came).astype(bf16)
        for mask in far_masks[1:]:
            part = halve(part, 0, mask).astype(bf16)
        return pick(part, 0, 1 - unit_side), pick(part, 0, unit_side)

    def unit_whole(own, other):
        low = jnp.where(unit_side == 0, own, other)
        high = jnp.where(unit_side == 0, other, own)
        return jnp.concatenate([low, high], 1).astype(f32)

    def core_sum(partial):
        return halve(split_dims(partial), bit_count - 1, 1).astype(bf16)

    grad_ffn_full = join_rows(gather_rows(grad_ffn_out, unit_axes))
    grad_down = product(grad_ffn_full, hidden, 0, 0, bf16)
    down_dims = split_dims(grad_down)

    def down_half(far, core):
        return pick(pick(down_dims, bit_count - 1, core), 0, far)

    down_away = down_half(1 - side(top), 1 - side(1))
    down_away = plus(down_half(1 - side(top), side(1)), send(down_away, 1)).astype(bf16)
    down_came = send(down_away, top)
    down_other = send(down_half(side(top), 1 - side(1)), 1, down_away)

    def hidden_back(rows):
        grad_hidden = product(rows, down_weight, 1, 0)
        return (grad_hidden * slope).astype(bf16), (grad_hidden * active).astype(bf16)

    (grad_gate_act, grad_up_act), down_other = segment(hidden_back, (grad_ffn_full,), (down_away,), down_other)

    def weight_back(act):
        return product(ffn_full, act, 0, 0, bf16)

    back_plan = scatter_plan(len(unit_axes), True)
    split_at = next(i for i, hop in enumerate(back_plan) if 1 << (len(unit_axes) - 1) in hop)

    def beside_hops(bodies):
        results = []

        def beside(number):
            def run(moved):
                if number >= len(bodies):
                    return None, moved
                result, moved = segment(bodies[number], tuple(results[-1:]), (), moved)
                results.append(result)
                return result, moved

            return run

        return beside, results

    def ffn_back_first(grad_gate_act, grad_up_act):
        parts = two_products(grad_gate_act, gate_weight, grad_up_act, up_weight, 1 << len(unit_axes))
        pieces, came = {t: [part] for t, part in enumerate(parts)}, ()
        beside, results = beside_hops([lambda: weight_back(tie(grad_gate_act, *parts)), unit_core])
        for number, subsets in enumerate(back_plan[:split_at]):
            pieces, came, _ = scatter_hop(pieces, unit_axes, True, subsets, came, beside(number))
        return pieces, results[1]

    (ffn_pieces, (gate_away, gate_kept)), down_came = segment(
        ffn_back_first, (grad_gate_act, grad_up_act), (down_away,), down_came
    )

    def ffn_back_last(ffn_pieces, grad_up_act, down_came):
        last = 1 << (len(unit_axes) - 1)

        def over_head(pieces, grad_up_act):
            came = ()
            beside, results = beside_hops(
                [lambda: weight_back(grad_up_act), lambda partial: (unit_core(partial), unit_sides(plus(down_half(side(top), side(1)), down_other), down_came))]
            )
            for number, subsets in enumerate(back_plan[split_at:]):
                subsets = [t for t in subsets if t != last]
                pieces, came, _ = scatter_hop(pieces, unit_axes, True, subsets, came, beside(number))
            return pieces[0], results[1]

        pieces = dict(ffn_pieces)
        across = swap(pieces.pop(last)[0], unit_axes[-1])
        (terms, results), across = segment(over_head, (pieces, grad_up_act), (), across)
        rows = whole_call(
            functools.partial(after_ffn_back_kernel, len(terms) + 1),
            [(row_shape, f32), (row_shape, bf16), (scale_shape, f32), (scale_shape, f32)],
            *terms,
            across,
            resid,
            attn_out,
            out_grad,
            scale_rows,
            name="after_ffn_back",
        )
        return (*rows, *results)

    gate_came = [send(gate_away[0], top, down_came), None]
    (grad_resid, grad_attn, scale_grad2, scale_grad1, (up_away, up_kept), (down_far, down_own)), gate_came[0] = segment(
        ffn_back_last, (ffn_pieces, grad_up_act, down_came), (gate_away, gate_kept), gate_came[0]
    )

    def attend_back(grad_attn):
        grad_attn_full = join_rows(gather_rows(grad_attn, head_axes))
        grad_mixed = product(grad_attn_full, output_weight, 1, 0, bf16)
        grad_query_lin, kv_near, kv_far = attention_backward(
            spans, queries, grad_mixed, exact, lse, table, kv_pieces, span_len
        )
        kv_terms = plus(kv_near, swap(kv_far, (1, 0))).astype(bf16).reshape(-1, group_rows, 2 * HD)
        middle = kv_terms.shape[0] // 2
        return grad_attn_full, grad_query_lin, kv_terms[:middle], kv_terms[middle:]

    gate_came[1] = send(gate_away[1], top, grad_attn)
    up_came = [send(up_away[0], top, grad_attn), None]
    down_other = send(down_far, pair, grad_attn)
    (grad_attn_full, grad_query_lin, kv_kept, kv_away), (gate_came[1], up_came[0], down_other) = segment(
        attend_back, (grad_attn,), (up_away, up_kept, down_far, down_own), (gate_came[1], up_came[0], down_other)
    )

    def projections_back(grad_query_lin, gate_came):
        core = core_sum(outer((normed_full, grad_query_lin), (grad_attn_full, mixed)))
        away, kept = pick(core, bit_count - 2, 1 - unit_side), pick(core, bit_count - 2, unit_side)
        parts = [(pick(away, 0, index), pick(kept, 0, index)) for index in (1 - side(top), side(top))]
        return parts, unit_sides(gate_kept, jnp.stack(gate_came))

    kv_came = send(kv_away, pair)
    (((onward_away, onward_kept), (staying_away, staying_kept)), (gate_far, gate_own)), kv_came = segment(
        projections_back, (grad_query_lin, gate_came), (), kv_came
    )
    kv_terms = plus(kv_kept, kv_came).astype(bf16)
    for mask in chip_masks[1:-1]:
        middle = kv_terms.shape[0] // 2
        kv_terms = plus(kv_terms[:middle], swap(kv_terms[middle:], (mask, 0))).astype(bf16)

    def beside_last_keys(down_other):
        return unit_whole(down_own, down_other).T

    kv_came = send(kv_terms[1], top)
    gate_other = send(gate_far, pair, kv_terms)
    out_down, (kv_came, gate_other) = segment(beside_last_keys, (down_other,), (kv_terms,), (kv_came, gate_other))

    def normed_rows_back(kv_kept, kv_came):
        normed_plan = scatter_plan(len(head_axes), False)

        def first_sums_back(kv_kept, kv_came):
            (grad_kv_lin,) = whole_call(
                key_value_grad_kernel,
                [((group_rows, 2 * HD), bf16)],
                kv_kept,
                kv_came,
                *table,
                name="key_value_grad",
            )
            *parts, scale_grad0 = normed_back(
                grad_query_lin, query_weight, grad_kv_lin, kv_weight, inverse_full, hidden_slots, head_count
            )

            def key_weights_back(grad_kv_lin, scale_grad0):
                scale_grad = jnp.concatenate([scale_grad0, scale_grad1, scale_grad2, scale_grad3], 0).astype(bf16)
                scale_grad = scale_grad.reshape(scale_count, block_count, model_rows).transpose(1, 0, 2)
                scale_grad = jnp.pad(scale_grad, ((0, 0), (0, 16 - scale_count), (0, 2 * HD - model_rows)))
                partial = outer((normed_full, grad_kv_lin)).reshape(block_count, model_rows, 2 * HD)
                terms = core_sum(jnp.concatenate([partial, scale_grad], 1).reshape(-1, 2 * HD))
                return pick(terms, bit_count - 2, 1 - unit_side), pick(terms, bit_count - 2, unit_side)

            def beside(moved):
                return segment(key_weights_back, (grad_kv_lin, scale_grad0), (), moved)

            pieces = {t: [part] for t, part in enumerate(parts)}
            pieces, _, terms = scatter_hop(pieces, head_axes, False, normed_plan[0], (), beside)
            return pieces, terms

        onward_came = send(onward_away, pair, kv_came)
        (pieces, (away, kept)), onward_came = segment(first_sums_back, (kv_kept, kv_came), (), onward_came)
        onward = plus(onward_kept, onward_came).astype(bf16)
        for at, mask in list(enumerate(chip_masks))[1:-1]:
            onward = halve(onward, bit_count - 3 - at, mask).astype(bf16)
        onward_query, onward_output = lax.optimization_barrier((onward[:, :query_width], onward[:, query_width:]))

        def sums_back(pieces):
            came = ()
            for subsets in normed_plan[1:]:
                pieces, came, _ = scatter_hop(pieces, head_axes, False, subsets, came)
            (grad_in,) = whole_call(
                functools.partial(after_all_kernel, len(pieces[0])),
                [(row_shape, f32)],
                *pieces[0],
                hidden_in,
                grad_resid,
                scale_rows,
                name="after_all",
            )
            return grad_in

        wkv_came = send(away, pair)
        output_came = send(onward_output, top)
        grad_in, (wkv_came, output_came) = segment(sums_back, (pieces,), (away, kept), (wkv_came, output_came))
        wkv_terms = plus(kept, wkv_came).astype(bf16)
        for at, mask in list(enumerate(chip_masks))[1:-1]:
            wkv_terms = halve(wkv_terms, bit_count - 2 - at, mask).astype(bf16)
        return grad_in, pick(wkv_terms, 0, 1 - side(top)), pick(wkv_terms, 0, side(top)), output_came, onward_query

    up_came[1] = send(up_away[1], top, kv_came)
    (grad_in, wkv_away, wkv_kept, output_came, onward_query), up_came[1] = segment(
        normed_rows_back, (kv_terms[0], kv_came), (out_down, onward_away), up_came[1]
    )
    wkv_came = send(wkv_away, top)
    staying_came = send(staying_away, pair, wkv_away)

    def beside_key_weights(up_came, gate_other):
        return unit_sides(up_kept, jnp.stack(up_came)), unit_whole(gate_own, gate_other)

    ((up_far, up_own), out_gate), (wkv_came, staying_came) = segment(
        beside_key_weights, (up_came, gate_other), (wkv_away, wkv_kept), (wkv_came, staying_came)
    )
    grad_wkv = plus(wkv_kept, wkv_came).astype(bf16)
    query_came = send(onward_query, top, grad_wkv)
    up_other = send(up_far, pair, grad_wkv)

    def head_rows(grad_wkv, staying_kept, staying_came, output_came):
        staying = plus(staying_kept, staying_came).astype(bf16)
        for at, mask in list(enumerate(chip_masks))[1:-1]:
            staying = halve(staying, bit_count - 3 - at, mask).astype(bf16)
        out_output = plus(staying[:, query_width:], output_came).T
        staying_query = staying[:, :query_width]
        parts = gather_rows(grad_wkv, head_axes)
        if head_count == KVH:
            out_key, out_value, scale_total = place_heads(parts, model_rows, scale_count, head_index)
            return out_key, out_value, scale_total[:, :model_rows], out_output, staying_query
        wkv_ordered = jnp.zeros((head_count,) + grad_wkv.shape, bf16)
        for mask, pieces in parts.items():
            first = 0
            for piece in pieces:
                wkv_ordered = lax.dynamic_update_slice(wkv_ordered, piece[None], (head_index ^ mask, first, 0))
                first += piece.shape[0]
        wkv_ordered = wkv_ordered.astype(f32)
        scale_total = wkv_ordered[:, model_rows : model_rows + scale_count, :model_rows].sum(0)
        wkv_ordered = wkv_ordered[:, :model_rows].reshape(KVH, head_count // KVH, model_rows, 2, HD).sum(1)
        out_key = wkv_ordered[:, :, 0].transpose(1, 0, 2).reshape(model_rows, KVH * HD)
        out_value = wkv_ordered[:, :, 1].transpose(1, 0, 2).reshape(model_rows, KVH * HD)
        return out_key, out_value, scale_total, out_output, staying_query

    (out_key, out_value, scale_total, out_output, staying_query), (query_came, up_other) = segment(
        head_rows, (grad_wkv, staying_kept, staying_came, output_came), (onward_query, up_far), (query_came, up_other)
    )
    out_query = plus(staying_query, query_came)
    out_up = unit_whole(up_own, up_other)

    return (
        layer_out,
        grad_in,
        out_query,
        out_key,
        out_value,
        out_output,
        out_gate,
        out_up,
        out_down,
        scale_total,
    )


def solution(mesh):
    placed = (
        P(("blk", "head"), None),
        P(("blk", "head"), None),
        P(),
        P("blk", "head"),
        P("blk", None),
        P("blk", None),
        P("head", "blk"),
        P("blk", "head"),
        P("blk", "head"),
        P("head", "blk"),
        P(None, "blk"),
    )
    return jax.shard_map(
        on_device,
        mesh=mesh,
        in_specs=placed,
        out_specs=(
            P(("blk", "head"), None),
            P(("blk", "head"), None),
            P("blk", "head"),
            P("blk", None),
            P("blk", None),
            P("head", "blk"),
            P("blk", "head"),
            P("blk", "head"),
            P("head", "blk"),
            P(None, "blk"),
        ),
        check_vma=False,
    )
```
